32 devices in a mesh: tile: 8 (over y, x, core), view: 4 (over z).
Axes of the slice: x: 2, y: 2, z: 4, core: 2. Of those that a mesh axis runs over, the one named last changes fastest.
Arguments:
- estimate: float32 [64, 64, 256], P('tile'), may hold values from 0.5 to 2
- measured: float32 [4, 64, 64, 256], P('view', 'tile'), may hold values from 0.3 to 3
- kernels: float32 [4, 3, 15], P('view'), may hold values from 0.1 to 1
- labels: int32 [64, 64, 256], P('tile'), may hold values from 0 to 15
- label_owner: int32 [8, 16, 1], P('tile'), may hold values from 0 to 7; in each aligned block of 16 rows (0 to 15, 16 to 31, ..., all dimensions but the last counted through in order) at most 5 rows name the same one
- label_index: int32 [8, 16], P('tile'), may hold values from 0 to 127
Outputs:
- new_estimate: float32 [64, 64, 256], P('tile')
- nucleus_moments: float32 [10, 1024], P(None, 'tile')
The draws below stay inside these ranges and needn't reach their ends.
Inputs may be any that keep to these rules, and one draw needn't show every extreme that they name: `label_owner`: among the 16 slots of one slab at most 5 name the same owner, a bound that some block reaches.
All inputs are finite; a program needn't handle non-finite values.
Results may differ from the reference program's by a relative error of at most 0.0003.
Values sent between devices are 32-bit elements; how exact they have to be, the bound alone decides.
No kernel may reach another device: no remote copies, remote signals or barrier semaphores. Data moves between devices by JAX's collectives and lax.ppermute only.
A program may use at most 64 MiB of HBM per device.

```python
import math
import jax
import jax.numpy as jnp
import numpy as np
from jax import lax

CZ = 8
NY = 64
NX = 256
TAPS = 15
CAP = 5
NUC_DEV = 128
VIEWS = 4
L_TILE = 16
NZ = 64
NUCLEI = 1024
N_TILE = 8


def draw_labels(key, part):
    key = jax.random.fold_in(key, 11)
    slabs = NZ // CZ
    half = L_TILE // 2
    cell_rows = max(4, NY // 16)
    cell_cols = max(4, NX // 8)
    grid_rows = max(1, NY // cell_rows)
    grid_cols = max(1, NX // cell_cols)
    volume = CZ * NY * NX
    stretch = volume // half
    key_z, key_y, key_x, key_order, key_spot = jax.random.split(key, 5)
    seeds_z = jax.random.randint(key_z, (slabs, grid_rows, grid_cols), 0, CZ, dtype=jnp.int32)
    seeds_y = jax.random.randint(key_y, (slabs, grid_rows, grid_cols), 0, cell_rows, dtype=jnp.int32)
    seeds_x = jax.random.randint(key_x, (slabs, grid_rows, grid_cols), 0, cell_cols, dtype=jnp.int32)
    order_keys = jax.random.split(key_order, slabs)
    orders = jax.vmap(lambda one_key: jax.random.permutation(one_key, half).astype(jnp.int32))(order_keys)
    spots = jax.random.randint(key_spot, (slabs, half), 0, stretch, dtype=jnp.int32)

    def one_slab(inputs):
        seed_z, seed_y, seed_x, order, spot = inputs
        plane = lax.broadcasted_iota(jnp.int32, (CZ, NY, NX), 0)
        row = lax.broadcasted_iota(jnp.int32, (CZ, NY, NX), 1)
        col = lax.broadcasted_iota(jnp.int32, (CZ, NY, NX), 2)
        home_r = jnp.minimum(row // cell_rows, grid_rows - 1)
        home_c = jnp.minimum(col // cell_cols, grid_cols - 1)
        best = jnp.full((CZ, NY, NX), 2 ** 30, jnp.int32)
        for shift in range(9):
            cand_r = home_r + (shift // 3 - 1)
            cand_c = home_c + (shift % 3 - 1)
            valid = (cand_r >= 0) & (cand_r < grid_rows) & (cand_c >= 0) & (cand_c < grid_cols)
            safe_r = jnp.clip(cand_r, 0, grid_rows - 1)
            safe_c = jnp.clip(cand_c, 0, grid_cols - 1)
            gap_z = plane - seed_z[safe_r, safe_c]
            gap_y = row - (safe_r * cell_rows + seed_y[safe_r, safe_c])
            gap_x = col - (safe_c * cell_cols + seed_x[safe_r, safe_c])
            dist = 4 * gap_z * gap_z + gap_y * gap_y + gap_x * gap_x
            score = jnp.where(valid, dist * 16 + shift, 2 ** 30)
            best = jnp.minimum(best, score)
        winner = best % 16
        cell = (home_r + winner // 3 - 1) * grid_cols + (home_c + winner % 3 - 1)
        slot = 2 * order[cell % half]
        flat = slot.reshape(-1)
        places = jnp.arange(half, dtype=jnp.int32) * stretch + spot
        flat = flat.at[places].set(2 * jnp.arange(half, dtype=jnp.int32) + 1)
        return flat.reshape(CZ, NY, NX).astype(jnp.int32)
    result = lax.map(one_slab, (seeds_z, seeds_y, seeds_x, orders, spots))
    return result.reshape(NZ, NY, NX).astype(jnp.int32)


def place_ends(entries, stream_key, least, high):
    shape = entries.shape
    place = [jax.random.randint(jax.random.fold_in(stream_key, axis), (), 0, shape[axis]) for axis in range(len(shape))]
    entries = entries.at[tuple(place)].set(least)
    longest = shape.index(max(shape))
    place[longest] = (place[longest] + 1) % shape[longest]
    return entries.at[tuple(place)].set(high)


def level_of(key, extent, pieces, low, top_value):
    level = 1.0
    for dim, parts in pieces:
        steps = jax.random.uniform(jax.random.fold_in(jax.random.fold_in(key, 6), dim), (parts,), jnp.float32, low / len(pieces), top_value / len(pieces))
        level = level * jnp.repeat(jnp.exp(steps), extent[dim] // parts).reshape((-1,) + (1,) * (len(extent) - 1 - dim))
    return level


def routed_block(rng, own, number, rows, count, top, reach, lean):
    ranking = jax.random.permutation(rng, count)
    packed, ordinary = load_shares(count, rows * top, reach, lean, True), load_shares(count, rows * top, reach, lean, False)
    places = jnp.arange(count)

    def named(sizes, turn):
        used = int((sizes > 0).sum())
        fixed = max(1, used // 4)
        moved = fixed + (places - fixed + turn * (used - fixed)) % max(1, count - fixed)
        return jnp.zeros((count,), jnp.int32).at[ranking[jnp.where(places < fixed, places, moved)]].set(jnp.asarray(sizes, jnp.int32))

    sizes = jnp.where(number % 4 == 0, named(packed, number // 4), named(ordinary, number - number // 4 - 1))
    mixed = jax.random.permutation(jax.random.fold_in(own, 3), count)
    donor, receiver = mixed[0:count // 2 * 2:2], mixed[1:count // 2 * 2:2]
    room = jnp.minimum(sizes[donor] - 1, reach - sizes[receiver]) // 2
    room = jnp.where((donor == ranking[0]) | (receiver == ranking[0]) | (sizes[receiver] == 0), 0, jnp.maximum(room, 0))
    moved = jax.random.randint(jax.random.fold_in(own, 4), (count // 2,), 0, 1 << 20) % (room + 1)
    sizes = sizes.at[donor].add(-moved).at[receiver].add(moved)
    items = jnp.searchsorted(jnp.cumsum(sizes), jnp.arange(rows * top), side="right").astype(jnp.int32)
    listing = items.reshape(top, rows).T
    listing = listing[jax.random.permutation(jax.random.fold_in(own, 1), rows)]
    turn = jax.random.randint(jax.random.fold_in(own, 2), (rows, 1), 0, top)
    return jnp.take_along_axis(listing, (jnp.arange(top)[None, :] + turn) % top, axis=1)


def load_shares(number_of, total, bound, lean, full):
    loads = [(1 << 20) // math.isqrt(standing ** lean) + 1 for standing in range(1, number_of + 1)]
    largest = bound if full else min(bound, max(-(-total // number_of), total * loads[0] // sum(loads)))
    least = 1 if total - largest >= number_of - 1 else 0
    counts, rest = [largest] + [least] * (number_of - 1), total - largest - least * (number_of - 1)
    while rest > 0:
        movable = [i for i in range(1, number_of) if counts[i] < largest] or [i for i in range(1, number_of) if counts[i] < bound]
        whole, left = sum([loads[i] for i in movable]), rest
        for i in movable:
            extra = min(bound - counts[i], max(1, left * loads[i] // whole), rest)
            counts[i] = counts[i] + extra
            rest = rest - extra
    return np.array(counts)


def setup_inputs(seed: int = 0) -> dict:
    splits = jax.random.split(jax.random.key(seed), 7)
    estimate = jnp.clip(jnp.exp(math.log(2.0) - 1.3862944 * jax.random.uniform(splits[0], (NZ, NY, NX), jnp.float32) ** level_of(splits[0], (NZ, NY, NX), ((0, 8),), -0.2, 0.2)), 0.5, 2.0)
    measured = jnp.clip(jnp.exp(math.log(3.0) - 2.3025851 * jax.random.uniform(splits[1], (VIEWS, NZ, NY, NX), jnp.float32) ** level_of(splits[1], (VIEWS, NZ, NY, NX), ((0, 4), (1, 8)), -0.2, 0.2)), 0.3, 3.0)
    kernels = jnp.clip(jnp.exp(math.log(1.0) - 2.3025851 * jax.random.uniform(splits[2], (VIEWS, 3, TAPS), jnp.float32) ** level_of(splits[2], (VIEWS, 3, TAPS), ((0, 4),), -0.2, 0.2)), 0.1, 1.0)
    labels = draw_labels(jax.random.fold_in(splits[6], 71), 0)
    label_owner_keys = jax.random.split(jax.random.fold_in(splits[4], 1), N_TILE * L_TILE // L_TILE)
    label_owner_turns = jax.random.permutation(jax.random.fold_in(splits[4], 3), N_TILE * L_TILE // L_TILE)
    label_owner = jax.vmap(lambda own, number: routed_block(jax.random.fold_in(splits[4], 2), own, number, L_TILE, N_TILE, 1, CAP, 2))(label_owner_keys, label_owner_turns).reshape((N_TILE, L_TILE, 1))
    label_index = place_ends(jax.random.randint(splits[5], (N_TILE, L_TILE), 0, NUC_DEV), jax.random.fold_in(splits[5], 1), 0, NUC_DEV - 1).astype(jnp.int32)
    return dict(estimate=estimate, measured=measured, kernels=kernels, labels=labels, label_owner=label_owner, label_index=label_index)


def blur_pass(field, taps, axis, flipped):
    radius = (TAPS - 1) // 2
    count = field.shape[axis]
    widths = [(0, 0), (0, 0), (0, 0)]
    widths[axis] = (radius, radius)
    padded = jnp.pad(field, widths)
    result = jnp.zeros_like(field)
    for step in range(TAPS):
        offset = 2 * radius - step if flipped else step
        result = result + taps[step] * lax.slice_in_dim(padded, offset, offset + count, axis=axis)
    return result


def blur_volume(field, taps, flipped):
    result = blur_pass(field, taps[2], 2, flipped)
    result = blur_pass(result, taps[1], 1, flipped)
    return blur_pass(result, taps[0], 0, flipped)


def reference(estimate, measured, kernels, labels, label_owner, label_index):
    weights = kernels / jnp.sum(kernels, axis=-1, keepdims=True)
    total = jnp.zeros_like(estimate)
    for view_number in range(VIEWS):
        forward = blur_volume(estimate, weights[view_number], False)
        ratio = measured[view_number] / forward
        total = total + blur_volume(ratio, weights[view_number], True)
    new_estimate = estimate * total / VIEWS
    global_table = (label_owner[:, :, 0] * NUC_DEV + label_index).astype(jnp.int32)
    slab_of = (jnp.arange(NZ, dtype=jnp.int32) // CZ).astype(jnp.int32)
    nucleus = global_table[slab_of[:, None, None], labels].ravel()
    depth = ((jnp.arange(NZ, dtype=jnp.int32).astype(jnp.float32) + 0.5) / NZ)[:, None, None]
    height = ((jnp.arange(NY, dtype=jnp.int32).astype(jnp.float32) + 0.5) / NY)[None, :, None]
    across = ((jnp.arange(NX, dtype=jnp.int32).astype(jnp.float32) + 0.5) / NX)[None, None, :]
    factors = [None, depth, height, across, depth * depth, height * height, across * across,
               depth * height, depth * across, height * across]
    sums = []
    for factor in factors:
        weighted = new_estimate if factor is None else new_estimate * factor
        sums.append(jax.ops.segment_sum(weighted.ravel(), nucleus, num_segments=NUCLEI))
    sums = jnp.stack(sums)
    mass = sums[0]
    scaled = mass * (L_TILE / (CZ * NY * NX))
    shape_part = sums[1:] / jnp.maximum(mass, 1.0)[None, :]
    return new_estimate, jnp.concatenate([scaled[None, :], shape_part], axis=0)
```

```python
import functools

import jax
import jax.numpy as jnp
from jax import lax
from jax.experimental import pallas as pl
from jax.experimental.pallas import tpu as pltpu
from jax.sharding import PartitionSpec as P

MOM = 10
ROWS = 8
NUC_DEV = 128
LANES = 128
F32 = jnp.float32
BF16 = jnp.bfloat16
ANY = pl.BlockSpec(memory_space=pl.ANY)
VMEM = pl.BlockSpec(memory_space=pltpu.VMEM)
SMEM = pl.BlockSpec(memory_space=pltpu.SMEM)
LIMIT = 32 * 1024 * 1024


def half_of(view):
    return (view ^ (view >> 1)) & 1


def split(value):
    upper = value.astype(BF16)
    return upper, (value - upper.astype(F32)).astype(BF16)


def band(taps, shape, offset):
    rows = lax.broadcasted_iota(jnp.int32, shape, 0)
    cols = lax.broadcasted_iota(jnp.int32, shape, 1)
    place = cols - rows + offset
    result = jnp.zeros(shape, F32)
    for step in range(taps.shape[1]):
        result = jnp.where(place == step, taps[:, step : step + 1], result)
    return result


def bands_kernel(core, taps_own, taps_other, wide, tall, back):
    half = half_of(lax.axis_index("view"))
    across = wide.shape[-1]
    rows, keep = tall.shape[1], back.shape[1]
    for which, ref in enumerate((taps_own, taps_other)):
        raw = ref[0]
        taps = raw / jnp.sum(raw, axis=-1, keepdims=True)
        taps_y, taps_x = taps[1:2], taps[2:3]
        radius = (raw.shape[1] - 1) // 2
        flipped_x = jnp.concatenate([taps_x[:, t : t + 1] for t in reversed(range(raw.shape[1]))], axis=1)
        flipped_y = jnp.concatenate([taps_y[:, t : t + 1] for t in reversed(range(raw.shape[1]))], axis=1)
        upper, lower = split(band(flipped_x, (across, across), radius))
        wide[which, 0, 0] = upper
        wide[which, 0, 1] = lower
        upper, lower = split(band(taps_x, (across, across), radius))
        wide[which, 1, 0] = upper
        wide[which, 1, 1] = lower
        upper, lower = split(band(taps_y, (rows, rows), radius))
        tall[which] = jnp.concatenate([upper, upper, lower], axis=1)
        shift = (2 * keep - rows) * half
        upper, lower = split(band(flipped_y, (keep, rows), radius + shift - keep * half))
        back[which] = jnp.concatenate([upper, upper, lower], axis=1)


def make_bands(core, taps_own, taps_other, across, rows, keep):
    return pl.pallas_call(
        functools.partial(bands_kernel, core),
        out_shape=(
            jax.ShapeDtypeStruct((2, 2, 2, across, across), BF16),
            jax.ShapeDtypeStruct((2, rows, 3 * rows), BF16),
            jax.ShapeDtypeStruct((2, keep, 3 * rows), BF16),
        ),
        in_specs=[VMEM, VMEM],
        out_specs=(VMEM, VMEM, VMEM),
        compiler_params=pltpu.CompilerParams(vmem_limit_bytes=LIMIT),
        name="bands",
    )(taps_own, taps_other)


def depth_sum(source, weights, planes, flipped, lead, row_at, rows, lane_at, lanes):
    taps = len(weights)
    totals = [None] * planes
    for place in range(planes + taps - 1):
        block = source(place)
        for plane in range(planes):
            step = plane + taps - 1 - place if flipped else place - plane
            if 0 <= step < taps:
                term = weights[step] * block
                totals[plane] = term if totals[plane] is None else totals[plane] + term
    return totals


def load_rims(parity, radius, planes, near, far, place, sems):
    @pl.when(parity == 0)
    def _():
        pltpu.make_async_copy(far, place(0, radius), sems.at[0]).start()
        pltpu.make_async_copy(near, place(radius + planes, radius), sems.at[1]).start()

    @pl.when(parity == 1)
    def _():
        pltpu.make_async_copy(near, place(0, radius), sems.at[0]).start()
        pltpu.make_async_copy(far, place(radius + planes, radius), sems.at[1]).start()

    return [
        pltpu.make_async_copy(far, place(0, radius), sems.at[0]),
        pltpu.make_async_copy(near, place(radius + planes, radius), sems.at[1]),
    ]


def forward_kernel(
    weights, estimate, near, far, measured, swapped, wide, tall, back,
    field, send_near, send_far,
    padded, seen, blur_hi, blur_lo, plane_hi, plane_lo, result, sems, out_sems,
):
    planes, radius = estimate.shape[0], near.shape[0]
    rows, across = near.shape[1], near.shape[2]
    keep = result.shape[2]
    taps = 2 * radius + 1
    parity = lax.axis_index("tile") % 2
    half = half_of(lax.axis_index("view"))
    start = pl.multiple_of((estimate.shape[1] - rows) * half, 16)
    own = pltpu.make_async_copy(
        estimate.at[:, pl.ds(start, rows)], padded.at[pl.ds(radius, planes)], sems.at[2]
    )
    own.start()
    rims = load_rims(
        parity, radius, planes, near, far, lambda at, count: padded.at[pl.ds(at, count)], sems
    )
    views = [
        pltpu.make_async_copy(measured.at[0, :, pl.ds(start, rows)], seen.at[0], sems.at[3]),
        pltpu.make_async_copy(swapped, seen.at[1], sems.at[4]),
    ]
    for copy in views:
        copy.start()
    own.wait()
    for copy in rims:
        copy.wait()
    for which in range(2):
        factors = [weights[which, 0, step] for step in range(taps)]
        for row in range(0, rows, 16):
            for lane in range(0, across, LANES):
                blocks = depth_sum(
                    lambda place: padded[place, row : row + 16, lane : lane + LANES],
                    factors, planes, False, None, row, 16, lane, LANES,
                )
                for plane, block in enumerate(blocks):
                    upper, lower = split(block)
                    at = plane * rows + row
                    blur_hi[which, at : at + 16, lane : lane + LANES] = upper
                    blur_lo[which, at : at + 16, lane : lane + LANES] = lower
    for copy in views:
        copy.wait()
    for which in range(2):
        upper, lower = wide[which, 0, 0], wide[which, 0, 1]
        lines = jnp.dot(blur_hi[which], upper, preferred_element_type=F32)
        lines += jnp.dot(blur_lo[which], upper, preferred_element_type=F32)
        lines += jnp.dot(blur_hi[which], lower, preferred_element_type=F32)
        for plane in range(planes):
            hi, lo = split(lines[plane * rows : (plane + 1) * rows])
            forward = jnp.dot(
                tall[which], jnp.concatenate([hi, lo, hi], axis=0), preferred_element_type=F32
            )
            ratio = seen[which, plane] / forward
            hi, lo = split(ratio)
            turned = jnp.dot(
                back[which], jnp.concatenate([hi, lo, hi], axis=0), preferred_element_type=F32
            )
            hi, lo = split(turned)
            plane_hi[which, plane * keep : (plane + 1) * keep] = hi
            plane_lo[which, plane * keep : (plane + 1) * keep] = lo
        upper, lower = wide[which, 1, 0], wide[which, 1, 1]
        lines = jnp.dot(plane_hi[which], upper, preferred_element_type=F32)
        lines += jnp.dot(plane_lo[which], upper, preferred_element_type=F32)
        lines += jnp.dot(plane_hi[which], lower, preferred_element_type=F32)
        result[which] = lines.reshape(planes, keep, across)
    outs = [
        pltpu.make_async_copy(result.at[:, pl.ds(parity, radius)], send_far, out_sems.at[0]),
        pltpu.make_async_copy(result.at[:, pl.ds(1 - parity, radius)], send_near, out_sems.at[1]),
        pltpu.make_async_copy(result, field, out_sems.at[2]),
    ]
    for copy in outs:
        copy.start()
    for copy in outs:
        copy.wait()


def ratio_fields(weights, estimate, near, far, measured, swapped, wide, tall, back):
    planes, radius, rows, across = estimate.shape[0], near.shape[0], near.shape[1], near.shape[2]
    keep = back.shape[1]
    return pl.pallas_call(
        forward_kernel,
        out_shape=(
            jax.ShapeDtypeStruct((2, planes, keep, across), F32),
            jax.ShapeDtypeStruct((2, radius, keep, across), F32),
            jax.ShapeDtypeStruct((2, radius, keep, across), F32),
        ),
        in_specs=[SMEM, ANY, ANY, ANY, ANY, ANY, VMEM, VMEM, VMEM],
        out_specs=(ANY, ANY, ANY),
        scratch_shapes=[
            pltpu.VMEM((planes + 2 * radius, rows, across), F32),
            pltpu.VMEM((2, planes, rows, across), F32),
            pltpu.VMEM((2, planes * rows, across), BF16),
            pltpu.VMEM((2, planes * rows, across), BF16),
            pltpu.VMEM((2, planes * keep, across), BF16),
            pltpu.VMEM((2, planes * keep, across), BF16),
            pltpu.VMEM((2, planes, keep, across), F32),
            pltpu.SemaphoreType.DMA((5,)),
            pltpu.SemaphoreType.DMA((3,)),
        ],
        compiler_params=pltpu.CompilerParams(vmem_limit_bytes=LIMIT),
        name="ratio_fields",
    )(weights, estimate, near, far, measured, swapped, wide, tall, back)


def backward_kernel(weights, field, near, far, correction, padded, sems):
    planes, radius, keep, across = field.shape[1], near.shape[1], field.shape[2], field.shape[3]
    taps = 2 * radius + 1
    parity = lax.axis_index("tile") % 2
    own = pltpu.make_async_copy(field, padded.at[:, pl.ds(radius, planes)], sems.at[2])
    own.start()
    rims = load_rims(
        parity, radius, planes, near, far, lambda at, count: padded.at[:, pl.ds(at, count)], sems
    )
    own.wait()
    for copy in rims:
        copy.wait()
    for row in range(0, keep, 16):
        for lane in range(0, across, LANES):
            totals = None
            for which in range(2):
                factors = [weights[which, 0, step] for step in range(taps)]
                blocks = depth_sum(
                    lambda place: padded[which, place, row : row + 16, lane : lane + LANES],
                    factors, planes, True, None, row, 16, lane, LANES,
                )
                totals = blocks if totals is None else [a + b for a, b in zip(totals, blocks)]
            for plane, block in enumerate(totals):
                correction[plane, row : row + 16, lane : lane + LANES] = block


def pair_correction(weights, field, near, far):
    _, planes, keep, across = field.shape
    radius = near.shape[1]
    return pl.pallas_call(
        backward_kernel,
        out_shape=jax.ShapeDtypeStruct((planes, keep, across), F32),
        in_specs=[SMEM, ANY, ANY, ANY],
        out_specs=VMEM,
        scratch_shapes=[
            pltpu.VMEM((2, planes + 2 * radius, keep, across), F32),
            pltpu.SemaphoreType.DMA((3,)),
        ],
        compiler_params=pltpu.CompilerParams(vmem_limit_bytes=LIMIT),
        name="pair_correction",
    )(weights, field, near, far)


def update_kernel(views, estimate, mine, other, result, held, sem):
    keep = mine.shape[1]
    half = half_of(lax.axis_index("view"))
    copy = pltpu.make_async_copy(
        estimate.at[:, pl.ds(pl.multiple_of(keep * half, 8), keep)], held, sem
    )
    copy.start()
    copy.wait()
    result[...] = held[...] * (mine[...] + other[...]) * (1.0 / views)


def update(views, estimate, mine, other):
    return pl.pallas_call(
        functools.partial(update_kernel, views),
        out_shape=jax.ShapeDtypeStruct(mine.shape, F32),
        in_specs=[ANY, VMEM, VMEM],
        out_specs=VMEM,
        scratch_shapes=[pltpu.VMEM(mine.shape, F32), pltpu.SemaphoreType.DMA],
        compiler_params=pltpu.CompilerParams(vmem_limit_bytes=LIMIT),
        name="update",
    )(estimate, mine, other)


def moments_kernel(
    views, depth_total, estimate, correction, labels, owner_row, owner_col, index_col,
    sent, held, marks, sums, sems,
):
    planes, keep, across = correction.shape
    height_total = estimate.shape[1]
    slots = owner_row.shape[1]
    half = half_of(lax.axis_index("view"))
    first = lax.axis_index("tile") * planes
    start = pl.multiple_of(keep * half, 8)
    copies = [
        pltpu.make_async_copy(estimate.at[:, pl.ds(start, keep)], held, sems.at[0]),
        pltpu.make_async_copy(labels.at[:, pl.ds(start, keep)], marks, sems.at[1]),
    ]
    for copy in copies:
        copy.start()
    for copy in copies:
        copy.wait()
    held[...] = held[...] * correction[...] * (1.0 / views)
    group = 16
    columns = lax.broadcasted_iota(jnp.int32, (across, LANES), 1)
    spot = (lax.broadcasted_iota(jnp.int32, (across, LANES), 0).astype(F32) + 0.5) / across
    one, line, square = jnp.ones_like(spot), spot, spot * spot

    def placed(*pairs):
        result = jnp.zeros((across, LANES), F32)
        for lane, value in pairs:
            result = jnp.where(columns == lane, value, result)
        return result

    factors = jnp.concatenate(
        [
            placed((0, one), (3, line), (6, square)),
            placed((2, one), (9, line)),
            placed((5, one)),
            placed((1, one), (8, line)),
            placed((7, one)),
            placed((4, one)),
        ],
        axis=0,
    )
    base = lax.broadcasted_iota(jnp.int32, (8, across), 0)

    def one_group(number, carry):
        def one_slot(inner, carry):
            slot = number * group + inner
            parts = [jnp.zeros((8, across), F32) for _ in range(6)]
            for row in range(0, keep, 8):
                high = ((base + (row + start)).astype(F32) + 0.5) / height_total
                flat = [jnp.zeros((8, across), F32) for _ in range(3)]
                for plane in range(planes):
                    deep = ((first + plane).astype(F32) + 0.5) / depth_total
                    hit = marks[plane, row : row + 8] == slot
                    value = jnp.where(hit, held[plane, row : row + 8], 0.0)
                    flat[0] = flat[0] + value
                    value = value * deep
                    flat[1] = flat[1] + value
                    flat[2] = flat[2] + value * deep
                scaled = flat[0] * high
                parts[0] = parts[0] + flat[0]
                parts[1] = parts[1] + scaled
                parts[2] = parts[2] + scaled * high
                parts[3] = parts[3] + flat[1]
                parts[4] = parts[4] + flat[1] * high
                parts[5] = parts[5] + flat[2]
            at = pl.multiple_of(inner * 8, 8)
            sums[pl.ds(at, 8), :] = jnp.concatenate(parts, axis=1)
            return carry

        lax.fori_loop(0, group, one_slot, 0)
        table = jnp.dot(
            sums[...], factors, precision=lax.Precision.HIGHEST, preferred_element_type=F32
        )
        table = jnp.sum(table.reshape(group, 8, LANES), axis=1)
        at = pl.multiple_of(number * group, group)
        ids = index_col[pl.ds(at, group), :].astype(F32)
        lanes = lax.broadcasted_iota(jnp.int32, (group, LANES), 1)
        table = jnp.where(lanes == MOM, ids, table)
        owner = owner_col[pl.ds(at, group), :]
        earlier = lax.broadcasted_iota(jnp.int32, (group, slots), 1) < (
            lax.broadcasted_iota(jnp.int32, (group, slots), 0) + number * group
        )
        same = (owner == owner_row[...]) & earlier
        rank = jnp.sum(same.astype(F32), axis=1, keepdims=True).astype(jnp.int32)
        place = owner * ROWS + rank
        spots = lax.broadcasted_iota(jnp.int32, (group, sent.shape[0]), 1)
        picked = (place == spots).astype(F32)
        sent[...] += lax.dot_general(
            picked, table, (((0,), (0,)), ((), ())),
            precision=lax.Precision.HIGHEST, preferred_element_type=F32,
        )
        return carry

    sent[...] = jnp.zeros_like(sent)
    lax.fori_loop(0, slots // group, one_group, 0)


def moment_rows(views, tiles, estimate, correction, labels, label_owner, label_index):
    slots = label_index.shape[1]
    planes, keep, across = correction.shape
    return pl.pallas_call(
        functools.partial(moments_kernel, views, tiles * planes),
        out_shape=jax.ShapeDtypeStruct((tiles * ROWS, LANES), F32),
        in_specs=[ANY, VMEM, ANY, VMEM, VMEM, VMEM],
        out_specs=VMEM,
        scratch_shapes=[
            pltpu.VMEM(correction.shape, F32),
            pltpu.VMEM(correction.shape, jnp.int32),
            pltpu.VMEM((16 * 8, 6 * across), F32),
            pltpu.SemaphoreType.DMA((2,)),
        ],
        compiler_params=pltpu.CompilerParams(vmem_limit_bytes=LIMIT),
        name="moment_rows",
    )(
        estimate, correction, labels,
        label_owner.reshape(1, slots), label_owner.reshape(slots, 1), label_index.reshape(slots, 1),
    )


def segments_kernel(rows, table):
    values = rows[...]
    ids = values[:, MOM : MOM + 1].astype(jnp.int32)
    spots = lax.broadcasted_iota(jnp.int32, (values.shape[0], NUC_DEV), 1)
    picked = (ids == spots).astype(F32)
    full = lax.dot_general(
        values, picked, (((0,), (0,)), ((), ())),
        precision=lax.Precision.HIGHEST, preferred_element_type=F32,
    )
    table[...] = full[: table.shape[0]]


def segment_table(rows):
    return pl.pallas_call(
        segments_kernel,
        out_shape=jax.ShapeDtypeStruct((16, NUC_DEV), F32),
        in_specs=[VMEM],
        out_specs=VMEM,
        compiler_params=pltpu.CompilerParams(vmem_limit_bytes=LIMIT),
        name="segment_table",
    )(rows)


def finish_kernel(scale, mine, other, first, second, third, fourth, whole, moments, sems):
    keep = mine.shape[1]
    half = half_of(lax.axis_index("view"))
    copies = [
        pltpu.make_async_copy(
            mine, whole.at[:, pl.ds(pl.multiple_of(keep * half, 8), keep)], sems.at[0]
        ),
        pltpu.make_async_copy(
            other, whole.at[:, pl.ds(pl.multiple_of(keep * (1 - half), 8), keep)], sems.at[1]
        ),
    ]
    for copy in copies:
        copy.start()
    table = (first[...] + second[...]) + (third[...] + fourth[...])
    mass = table[0:1]
    lines = lax.broadcasted_iota(jnp.int32, table.shape, 0)
    result = jnp.where(lines == 0, table * scale, table / jnp.maximum(mass, 1.0))
    moments[...] = result[:MOM]
    for copy in copies:
        copy.wait()


def finish(scale, mine, other, tables):
    planes, keep, across = mine.shape
    return pl.pallas_call(
        functools.partial(finish_kernel, scale),
        out_shape=(
            jax.ShapeDtypeStruct((planes, 2 * keep, across), F32),
            jax.ShapeDtypeStruct((MOM, NUC_DEV), F32),
        ),
        in_specs=[ANY, ANY, VMEM, VMEM, VMEM, VMEM],
        out_specs=(ANY, VMEM),
        scratch_shapes=[pltpu.SemaphoreType.DMA((2,))],
        compiler_params=pltpu.CompilerParams(vmem_limit_bytes=LIMIT),
        name="finish",
    )(mine, other, *tables)


def on_device(estimate, measured, kernels, labels, label_owner, label_index):
    tiles, views = lax.axis_size("tile"), lax.axis_size("view")
    planes, height, across = estimate.shape
    taps = kernels.shape[2]
    radius = (taps - 1) // 2
    keep = height // 2
    rows = min(height, -(-(keep + 2 * radius) // 16) * 16)
    parity = lax.axis_index("tile") % 2
    half = half_of(lax.axis_index("view"))
    near_pairs = [(i, i ^ 1) for i in range(tiles)]
    far_pairs = [(i, i + 1) for i in range(1, tiles - 1, 2)]
    far_pairs = far_pairs + [(b, a) for a, b in far_pairs]
    partner = [(i, i ^ 1) for i in range(views)]
    across_pairs = [(i, i ^ 3) for i in range(views)]

    shift = (height - rows) * half
    to_far = lax.dynamic_slice(estimate, (parity, shift, 0), (radius, rows, across))
    to_near = lax.dynamic_slice(estimate, (1 - parity, shift, 0), (radius, rows, across))
    to_partner = lax.dynamic_slice(measured[0], (0, (height - rows) * (1 - half), 0), (planes, rows, across))
    far = lax.ppermute(to_far, "tile", far_pairs)
    other_taps = lax.ppermute(kernels, "view", partner)
    near = lax.ppermute(to_near, "tile", near_pairs)
    swapped = lax.ppermute(to_partner, "view", partner)
    both = jnp.concatenate([kernels, other_taps], axis=0)
    weights = both / jnp.sum(both, axis=-1, keepdims=True)
    wide, tall, back = make_bands(0, kernels, other_taps, across, rows, keep)
    field, field_near, field_far = ratio_fields(
        weights, estimate, near, far, measured, swapped, wide, tall, back
    )
    rim_far = lax.ppermute(field_far, "tile", far_pairs)
    rim_near = lax.ppermute(field_near, "tile", near_pairs)
    mine = pair_correction(weights, field, rim_near, rim_far)
    other = lax.ppermute(mine, "view", across_pairs)
    sent = moment_rows(views, tiles, estimate, mine, labels, label_owner, label_index)
    got = lax.all_to_all(sent, "tile", split_axis=0, concat_axis=0, tiled=True)
    new_half = update(views, estimate, mine, other)
    new_other = lax.ppermute(new_half, "view", partner)
    table = segment_table(got)
    tables = [table] + [
        lax.ppermute(table, "view", [(i, i ^ step) for i in range(views)]) for step in (1, 2, 3)
    ]
    scale = label_index.shape[1] / (planes * height * across)
    new_estimate, moments = finish(scale, new_half, new_other, tables)
    return new_estimate, moments


def solution(mesh):
    placed = (
        P("tile", None, None),
        P("view", "tile", None, None),
        P("view", None, None),
        P("tile", None, None),
        P("tile", None, None),
        P("tile", None),
    )
    return jax.shard_map(
        on_device,
        mesh=mesh,
        in_specs=placed,
        out_specs=(P("tile", None, None), P(None, "tile")),
        check_vma=False,
    )
```

```python
import functools

import jax
import jax.numpy as jnp
from jax import lax
from jax.experimental import pallas as pl
from jax.experimental.pallas import tpu as pltpu
from jax.sharding import PartitionSpec as P

MOM = 10
ROWS = 8
NUC_DEV = 128
LANES = 128
F32 = jnp.float32
BF16 = jnp.bfloat16
ANY = pl.BlockSpec(memory_space=pl.ANY)
VMEM = pl.BlockSpec(memory_space=pltpu.VMEM)
LIMIT = 32 * 1024 * 1024


def half_of(view):
    return (view ^ (view >> 1)) & 1


def split(value):
    upper = value.astype(BF16)
    return upper, (value - upper.astype(F32)).astype(BF16)


def band(taps, shape, offset):
    rows = lax.broadcasted_iota(jnp.int32, shape, 0)
    cols = lax.broadcasted_iota(jnp.int32, shape, 1)
    place = cols - rows + offset
    result = jnp.zeros(shape, F32)
    for step, tap in enumerate(taps):
        result = jnp.where(place == step, tap, result)
    return result


def depth_terms(source, weights, first, last, planes, flipped):
    radius = (len(weights) - 1) // 2
    totals = {plane: None for plane in planes}
    for place in range(first, last):
        block = None
        for plane in planes:
            step = plane - place + radius if flipped else place - plane + radius
            if 0 <= step < len(weights):
                block = source(place) if block is None else block
                term = weights[step] * block
                totals[plane] = term if totals[plane] is None else totals[plane] + term
    return totals


def chunks(rows, across):
    return [(slice(row, row + 16), slice(lane, lane + LANES)) for row in range(0, rows, 16) for lane in range(0, across, LANES)]


def rims_out_kernel(estimate, to_far, to_near):
    planes, radius, rows = estimate.shape[0], to_far.shape[0], to_far.shape[1]
    odd = lax.axis_index("tile") % 2
    half = half_of(lax.axis_index("view"))
    start = pl.multiple_of((estimate.shape[1] - rows) * half, 8)
    to_far[...] = estimate[pl.ds(odd, radius), pl.ds(start, rows)]
    to_near[...] = estimate[pl.ds(1 - odd, radius), pl.ds(start, rows)]


def rims_out(estimate, radius, rows):
    shape = jax.ShapeDtypeStruct((radius, rows, estimate.shape[2]), F32)
    return pl.pallas_call(
        rims_out_kernel,
        out_shape=(shape, shape),
        in_specs=[VMEM],
        out_specs=(VMEM, VMEM),
        compiler_params=pltpu.CompilerParams(vmem_limit_bytes=LIMIT),
        name="rims_out",
    )(estimate)


def view_out_kernel(seen, measured, kernels, packed):
    planes, height = measured.shape[1], measured.shape[2]
    half = half_of(lax.axis_index("view"))
    start = pl.multiple_of((height - seen) * (1 - half), 8)
    for plane in range(planes):
        packed[plane * seen : (plane + 1) * seen] = measured[0, plane, pl.ds(start, seen)]
    packed[planes * seen :] = jnp.zeros((8, packed.shape[1]), F32)
    packed[planes * seen : planes * seen + kernels.shape[1], : kernels.shape[2]] = kernels[0]


def view_out(measured, kernels, seen):
    _, planes, _, across = measured.shape
    return pl.pallas_call(
        functools.partial(view_out_kernel, seen),
        out_shape=jax.ShapeDtypeStruct((planes * seen + 8, across), F32),
        in_specs=[VMEM, VMEM],
        out_specs=VMEM,
        compiler_params=pltpu.CompilerParams(vmem_limit_bytes=LIMIT),
        name="view_out",
    )(measured, kernels)


def prepare_kernel(packed, taps, source, estimate, wide, tall, back, part, spread):
    half = half_of(lax.axis_index("view"))
    across = wide.shape[-1]
    rows, keep, seen = part.shape[1], back.shape[0], tall.shape[0]
    planes = estimate.shape[0]
    radius = (taps - 1) // 2
    raw = source[source.shape[0] - 8 : source.shape[0] - 5, :taps] if packed else source[0]
    weights = raw / jnp.sum(raw, axis=-1, keepdims=True)
    deep, high, flat = [[weights[axis : axis + 1, t : t + 1] for t in range(taps)] for axis in range(3)]
    start = pl.multiple_of((2 * keep - rows) * half, 16)
    seen_start = (2 * keep - seen) * half
    upper, lower = split(band(flat[::-1], (across, across), radius))
    wide[0, 0] = upper
    wide[0, 1] = lower
    upper, lower = split(band(flat, (across, across), radius))
    wide[1, 0] = upper
    wide[1, 1] = lower
    upper, lower = split(band(high, (seen, rows), radius + start - seen_start))
    tall[...] = jnp.concatenate([upper, upper, lower], axis=1)
    upper, lower = split(band(high[::-1], (keep, rows), radius + seen_start - keep * half))
    back[...] = jnp.concatenate([upper, upper, lower], axis=1)
    factors = [jnp.broadcast_to(tap, (16, LANES)) for tap in deep]
    spread[...] = jnp.zeros_like(spread)
    for step in range(taps):
        spread[step : step + 1] = factors[step][:1]
    for row, lane in chunks(rows, across):
        where = pl.ds(pl.multiple_of(start + row.start, 16), 16)
        terms = depth_terms(
            lambda place: estimate[place, where, lane], factors, 0, planes, range(planes), False
        )
        for plane, block in terms.items():
            part[plane, row, lane] = block


def prepare(packed, taps, source, estimate, rows, seen, keep):
    planes, _, across = estimate.shape
    return pl.pallas_call(
        functools.partial(prepare_kernel, packed, taps),
        out_shape=(
            jax.ShapeDtypeStruct((2, 2, across, across), BF16),
            jax.ShapeDtypeStruct((seen, 3 * rows), BF16),
            jax.ShapeDtypeStruct((keep, 3 * rows), BF16),
            jax.ShapeDtypeStruct((planes, rows, across), F32),
            jax.ShapeDtypeStruct((-(-taps // 8) * 8, LANES), F32),
        ),
        in_specs=[VMEM, VMEM],
        out_specs=(VMEM,) * 5,
        compiler_params=pltpu.CompilerParams(vmem_limit_bytes=LIMIT),
        name="prepare",
    )(source, estimate)


def spread_factors(spread, taps):
    return [jnp.broadcast_to(spread[step : step + 1, :], (16, LANES)) for step in range(taps)]


def forward_kernel(
    wide_own, tall_own, back_own, part_own, spread_own,
    wide_other, tall_other, back_other, part_other, spread_other,
    near, far, measured, swapped,
    field, send_near, send_far,
    blur_hi, blur_lo, plane_hi, plane_lo,
):
    planes, radius = part_own.shape[0], near.shape[0]
    rows, across = near.shape[1], near.shape[2]
    keep, seen = back_own.shape[0], tall_own.shape[0]
    taps = 2 * radius + 1
    even = lax.axis_index("tile") % 2 == 0
    half = half_of(lax.axis_index("view"))
    seen_start = pl.multiple_of((2 * keep - seen) * half, 8)
    both = (
        (wide_own, tall_own, back_own, part_own, spread_own),
        (wide_other, tall_other, back_other, part_other, spread_other),
    )
    for which, (wide, tall, back, part, spread) in enumerate(both):
        factors = spread_factors(spread, taps)
        for row, lane in chunks(rows, across):

            def rim(place):
                if place < 0:
                    at = place + radius
                    return jnp.where(even, far[at, row, lane], near[at, row, lane])
                at = place - planes
                return jnp.where(even, near[at, row, lane], far[at, row, lane])

            below = depth_terms(rim, factors, -radius, 0, range(planes), False)
            above = depth_terms(rim, factors, planes, planes + radius, range(planes), False)
            for plane in range(planes):
                block = part[plane, row, lane]
                for term in (below[plane], above[plane]):
                    block = block if term is None else block + term
                upper, lower = split(block)
                at = slice(plane * rows + row.start, plane * rows + row.stop)
                blur_hi[which, at, lane] = upper
                blur_lo[which, at, lane] = lower
    for which, (wide, tall, back, part, spread) in enumerate(both):
        upper, lower = wide[0, 0], wide[0, 1]
        lines = jnp.dot(blur_hi[which], upper, preferred_element_type=F32)
        lines += jnp.dot(blur_lo[which], upper, preferred_element_type=F32)
        lines += jnp.dot(blur_hi[which], lower, preferred_element_type=F32)
        for plane in range(planes):
            hi, lo = split(lines[plane * rows : (plane + 1) * rows])
            forward = jnp.dot(
                tall[...], jnp.concatenate([hi, lo, hi], axis=0), preferred_element_type=F32
            )
            if which == 0:
                view = measured[0, plane, pl.ds(seen_start, seen), :]
            else:
                view = swapped[plane * seen : (plane + 1) * seen]
            ratio = view / forward
            if rows > seen:
                ratio = jnp.concatenate([ratio, jnp.zeros((rows - seen, across), F32)], axis=0)
            hi, lo = split(ratio)
            turned = jnp.dot(
                back[...], jnp.concatenate([hi, lo, hi], axis=0), preferred_element_type=F32
            )
            hi, lo = split(turned)
            plane_hi[which, plane * keep : (plane + 1) * keep] = hi
            plane_lo[which, plane * keep : (plane + 1) * keep] = lo
        upper, lower = wide[1, 0], wide[1, 1]
        lines = jnp.dot(plane_hi[which], upper, preferred_element_type=F32)
        lines += jnp.dot(plane_lo[which], upper, preferred_element_type=F32)
        lines += jnp.dot(plane_hi[which], lower, preferred_element_type=F32)
        field[which] = lines.reshape(planes, keep, across)
    for row, lane in chunks(keep, across):
        below, above = [], []
        for which in range(2):
            factors = spread_factors(both[which][4], taps)
            source = lambda place: field[which, place, row, lane]
            below.append(depth_terms(source, factors, 0, planes, range(-radius, 0), True))
            above.append(depth_terms(source, factors, 0, planes, range(planes, planes + radius), True))
        for at in range(radius):
            down = below[0][at - radius] + below[1][at - radius]
            up = above[0][at + planes] + above[1][at + planes]
            send_near[at, row, lane] = jnp.where(even, up, down)
            send_far[at, row, lane] = jnp.where(even, down, up)


def ratio_fields(own, others, near, far, measured, swapped):
    keep = own[2].shape[0]
    planes = own[3].shape[0]
    radius, rows, across = near.shape
    return pl.pallas_call(
        forward_kernel,
        out_shape=(
            jax.ShapeDtypeStruct((2, planes, keep, across), F32),
            jax.ShapeDtypeStruct((radius, keep, across), F32),
            jax.ShapeDtypeStruct((radius, keep, across), F32),
        ),
        in_specs=[VMEM] * 14,
        out_specs=(VMEM, VMEM, VMEM),
        scratch_shapes=[
            pltpu.VMEM((2, planes * rows, across), BF16),
            pltpu.VMEM((2, planes * rows, across), BF16),
            pltpu.VMEM((2, planes * keep, across), BF16),
            pltpu.VMEM((2, planes * keep, across), BF16),
        ],
        compiler_params=pltpu.CompilerParams(vmem_limit_bytes=LIMIT),
        name="ratio_fields",
    )(*own, *others, near, far, measured, swapped)


def own_kernel(taps, spread_own, spread_other, field, inner):
    planes, keep, across = inner.shape
    factors = [spread_factors(spread, taps) for spread in (spread_own, spread_other)]
    for row, lane in chunks(keep, across):
        parts = [
            depth_terms(
                lambda place: field[which, place, row, lane],
                factors[which], 0, planes, range(planes), True,
            )
            for which in range(2)
        ]
        for plane in range(planes):
            inner[plane, row, lane] = parts[0][plane] + parts[1][plane]


def own_planes(taps, spread_own, spread_other, field):
    return pl.pallas_call(
        functools.partial(own_kernel, taps),
        out_shape=jax.ShapeDtypeStruct(field.shape[1:], F32),
        in_specs=[VMEM] * 3,
        out_specs=VMEM,
        compiler_params=pltpu.CompilerParams(vmem_limit_bytes=LIMIT),
        name="own_planes",
    )(spread_own, spread_other, field)


def rims_kernel(inner, near, far, correction):
    planes, radius = inner.shape[0], near.shape[0]
    even = lax.axis_index("tile") % 2 == 0
    for plane in range(planes):
        total = inner[plane]
        if plane < radius:
            total += jnp.where(even, far[plane], near[plane])
        if plane >= planes - radius:
            at = plane - planes + radius
            total += jnp.where(even, near[at], far[at])
        correction[plane] = total


def add_rims(inner, near, far):
    return pl.pallas_call(
        rims_kernel,
        out_shape=jax.ShapeDtypeStruct(inner.shape, F32),
        in_specs=[VMEM] * 3,
        out_specs=VMEM,
        compiler_params=pltpu.CompilerParams(vmem_limit_bytes=LIMIT),
        name="add_rims",
    )(inner, near, far)


def update_kernel(views, estimate, mine, other, after, result):
    keep = mine.shape[1]
    half = half_of(lax.axis_index("view"))
    held = estimate[:, pl.ds(pl.multiple_of(keep * half, 8), keep)]
    result[...] = held * (mine[...] + other[...]) * (1.0 / views)


def update(views, estimate, mine, other, after):
    return pl.pallas_call(
        functools.partial(update_kernel, views),
        out_shape=jax.ShapeDtypeStruct(mine.shape, F32),
        in_specs=[VMEM, VMEM, VMEM, ANY],
        out_specs=VMEM,
        compiler_params=pltpu.CompilerParams(vmem_limit_bytes=LIMIT),
        name="update",
    )(estimate, mine, other, after)


def moments_kernel(
    views, depth_total, estimate, correction, labels, owner_row, owner_col, index_col,
    sent, held, sums,
):
    planes, keep, across = correction.shape
    height_total = estimate.shape[1]
    slots = owner_row.shape[1]
    half = half_of(lax.axis_index("view"))
    first = lax.axis_index("tile") * planes
    start = pl.multiple_of(keep * half, 8)
    held[...] = estimate[:, pl.ds(start, keep)] * correction[...] * (1.0 / views)
    group = 16
    columns = lax.broadcasted_iota(jnp.int32, (across, LANES), 1)
    spot = (lax.broadcasted_iota(jnp.int32, (across, LANES), 0).astype(F32) + 0.5) / across
    one, line, square = jnp.ones_like(spot), spot, spot * spot

    def placed(*pairs):
        result = jnp.zeros((across, LANES), F32)
        for lane, value in pairs:
            result = jnp.where(columns == lane, value, result)
        return result

    factors = jnp.concatenate(
        [
            placed((0, one), (3, line), (6, square)),
            placed((2, one), (9, line)),
            placed((5, one)),
            placed((1, one), (8, line)),
            placed((7, one)),
            placed((4, one)),
        ],
        axis=0,
    )
    base = lax.broadcasted_iota(jnp.int32, (8, across), 0)

    def one_group(number, carry):
        def one_slot(inner, carry):
            slot = number * group + inner
            parts = [jnp.zeros((8, across), F32) for _ in range(6)]
            for row in range(0, keep, 8):
                high = ((base + (row + start)).astype(F32) + 0.5) / height_total
                flat = [jnp.zeros((8, across), F32) for _ in range(3)]
                for plane in range(planes):
                    deep = ((first + plane).astype(F32) + 0.5) / depth_total
                    hit = labels[plane, pl.ds(pl.multiple_of(start + row, 8), 8)] == slot
                    value = jnp.where(hit, held[plane, row : row + 8], 0.0)
                    flat[0] = flat[0] + value
                    value = value * deep
                    flat[1] = flat[1] + value
                    flat[2] = flat[2] + value * deep
                scaled = flat[0] * high
                parts[0] = parts[0] + flat[0]
                parts[1] = parts[1] + scaled
                parts[2] = parts[2] + scaled * high
                parts[3] = parts[3] + flat[1]
                parts[4] = parts[4] + flat[1] * high
                parts[5] = parts[5] + flat[2]
            at = pl.multiple_of(inner * 8, 8)
            sums[pl.ds(at, 8), :] = jnp.concatenate(parts, axis=1)
            return carry

        lax.fori_loop(0, group, one_slot, 0)
        table = jnp.dot(
            sums[...], factors, precision=lax.Precision.HIGHEST, preferred_element_type=F32
        )
        table = jnp.sum(table.reshape(group, 8, LANES), axis=1)
        at = pl.multiple_of(number * group, group)
        ids = index_col[pl.ds(at, group), :].astype(F32)
        lanes = lax.broadcasted_iota(jnp.int32, (group, LANES), 1)
        table = jnp.where(lanes == MOM, ids, table)
        owner = owner_col[pl.ds(at, group), :]
        earlier = lax.broadcasted_iota(jnp.int32, (group, slots), 1) < (
            lax.broadcasted_iota(jnp.int32, (group, slots), 0) + number * group
        )
        same = (owner == owner_row[...]) & earlier
        rank = jnp.sum(same.astype(F32), axis=1, keepdims=True).astype(jnp.int32)
        place = owner * ROWS + rank
        spots = lax.broadcasted_iota(jnp.int32, (group, sent.shape[0]), 1)
        picked = (place == spots).astype(F32)
        sent[...] += lax.dot_general(
            picked, table, (((0,), (0,)), ((), ())),
            precision=lax.Precision.HIGHEST, preferred_element_type=F32,
        )
        return carry

    sent[...] = jnp.zeros_like(sent)
    lax.fori_loop(0, slots // group, one_group, 0)


def moment_rows(views, tiles, estimate, correction, labels, label_owner, label_index):
    slots = label_index.shape[1]
    planes, keep, across = correction.shape
    return pl.pallas_call(
        functools.partial(moments_kernel, views, tiles * planes),
        out_shape=jax.ShapeDtypeStruct((tiles * ROWS, LANES), F32),
        in_specs=[VMEM] * 6,
        out_specs=VMEM,
        scratch_shapes=[
            pltpu.VMEM(correction.shape, F32),
            pltpu.VMEM((16 * 8, 6 * across), F32),
        ],
        compiler_params=pltpu.CompilerParams(vmem_limit_bytes=LIMIT),
        name="moment_rows",
    )(
        estimate, correction, labels,
        label_owner.reshape(1, slots), label_owner.reshape(slots, 1), label_index.reshape(slots, 1),
    )


def segments_kernel(rows, table):
    values = rows[...]
    ids = values[:, MOM : MOM + 1].astype(jnp.int32)
    spots = lax.broadcasted_iota(jnp.int32, (values.shape[0], NUC_DEV), 1)
    picked = (ids == spots).astype(F32)
    full = lax.dot_general(
        values, picked, (((0,), (0,)), ((), ())),
        precision=lax.Precision.HIGHEST, preferred_element_type=F32,
    )
    table[...] = full[: table.shape[0]]


def segment_table(rows):
    return pl.pallas_call(
        segments_kernel,
        out_shape=jax.ShapeDtypeStruct((16, NUC_DEV), F32),
        in_specs=[VMEM],
        out_specs=VMEM,
        compiler_params=pltpu.CompilerParams(vmem_limit_bytes=LIMIT),
        name="segment_table",
    )(rows)


def finish_kernel(scale, mine, other, first, second, third, fourth, whole, moments, sems):
    keep = mine.shape[1]
    half = half_of(lax.axis_index("view"))
    copies = [
        pltpu.make_async_copy(
            mine, whole.at[:, pl.ds(pl.multiple_of(keep * half, 8), keep)], sems.at[0]
        ),
        pltpu.make_async_copy(
            other, whole.at[:, pl.ds(pl.multiple_of(keep * (1 - half), 8), keep)], sems.at[1]
        ),
    ]
    for copy in copies:
        copy.start()
    table = (first[...] + second[...]) + (third[...] + fourth[...])
    mass = table[0:1]
    lines = lax.broadcasted_iota(jnp.int32, table.shape, 0)
    result = jnp.where(lines == 0, table * scale, table / jnp.maximum(mass, 1.0))
    moments[...] = result[:MOM]
    for copy in copies:
        copy.wait()


def finish(scale, mine, other, tables):
    planes, keep, across = mine.shape
    return pl.pallas_call(
        functools.partial(finish_kernel, scale),
        out_shape=(
            jax.ShapeDtypeStruct((planes, 2 * keep, across), F32),
            jax.ShapeDtypeStruct((MOM, NUC_DEV), F32),
        ),
        in_specs=[ANY, ANY, VMEM, VMEM, VMEM, VMEM],
        out_specs=(ANY, VMEM),
        scratch_shapes=[pltpu.SemaphoreType.DMA((2,))],
        compiler_params=pltpu.CompilerParams(vmem_limit_bytes=LIMIT),
        name="finish",
    )(mine, other, *tables)


def on_device(estimate, measured, kernels, labels, label_owner, label_index):
    tiles, views = lax.axis_size("tile"), lax.axis_size("view")
    planes, height, across = estimate.shape
    taps = kernels.shape[2]
    radius = (taps - 1) // 2
    keep = height // 2
    seen = min(height, -(-(keep + radius) // 8) * 8)
    rows = min(height, -(-(keep + 2 * radius) // 16) * 16)
    near_pairs = [(i, i ^ 1) for i in range(tiles)]
    far_pairs = [(i, i + 1) for i in range(1, tiles - 1, 2)]
    far_pairs = far_pairs + [(b, a) for a, b in far_pairs]
    partner = [(i, i ^ 1) for i in range(views)]
    across_pairs = [(i, i ^ 3) for i in range(views)]

    to_far, to_near = rims_out(estimate, radius, rows)
    far = lax.ppermute(to_far, "tile", far_pairs)
    swapped = lax.ppermute(view_out(measured, kernels, seen), "view", partner)
    near = lax.ppermute(to_near, "tile", near_pairs)
    own = prepare(False, taps, kernels, estimate, rows, seen, keep)
    others = prepare(True, taps, swapped, estimate, rows, seen, keep)
    field, field_near, field_far = ratio_fields(own, others, near, far, measured, swapped)
    rim_far = lax.ppermute(field_far, "tile", far_pairs)
    rim_near = lax.ppermute(field_near, "tile", near_pairs)
    inner = own_planes(taps, own[4], others[4], field)
    mine = add_rims(inner, rim_near, rim_far)
    other = lax.ppermute(mine, "view", across_pairs)
    sent = moment_rows(views, tiles, estimate, mine, labels, label_owner, label_index)
    got = lax.all_to_all(sent, "tile", split_axis=0, concat_axis=0, tiled=True)
    new_half = update(views, estimate, mine, other, got)
    new_other = lax.ppermute(new_half, "view", partner)
    table = segment_table(got)
    tables = [table] + [
        lax.ppermute(table, "view", [(i, i ^ step) for i in range(views)]) for step in (1, 2, 3)
    ]
    scale = label_index.shape[1] / (planes * height * across)
    new_estimate, moments = finish(scale, new_half, new_other, tables)
    return new_estimate, moments


def solution(mesh):
    placed = (
        P("tile", None, None),
        P("view", "tile", None, None),
        P("view", None, None),
        P("tile", None, None),
        P("tile", None, None),
        P("tile", None),
    )
    return jax.shard_map(
        on_device,
        mesh=mesh,
        in_specs=placed,
        out_specs=(P("tile", None, None), P(None, "tile")),
        check_vma=False,
    )
```

```python
import functools

import jax
import jax.numpy as jnp
from jax import lax
from jax.experimental import pallas as pl
from jax.experimental.pallas import tpu as pltpu
from jax.sharding import PartitionSpec as P

MOM = 10
ROWS = 8
NUC_DEV = 128
LANES = 128
F32 = jnp.float32
BF16 = jnp.bfloat16
ANY = pl.BlockSpec(memory_space=pl.ANY)
VMEM = pl.BlockSpec(memory_space=pltpu.VMEM)
LIMIT = 32 * 1024 * 1024


def half_of(view):
    return (view ^ (view >> 1)) & 1


def split(value):
    upper = value.astype(BF16)
    return upper, (value - upper.astype(F32)).astype(BF16)


def band(taps, shape, offset):
    rows = lax.broadcasted_iota(jnp.int32, shape, 0)
    cols = lax.broadcasted_iota(jnp.int32, shape, 1)
    place = cols - rows + offset
    result = jnp.zeros(shape, F32)
    for step, tap in enumerate(taps):
        result = jnp.where(place == step, tap, result)
    return result


def depth_terms(source, weights, first, last, planes, flipped):
    radius = (len(weights) - 1) // 2
    totals = {plane: None for plane in planes}
    for place in range(first, last):
        block = None
        for plane in planes:
            step = plane - place + radius if flipped else place - plane + radius
            if 0 <= step < len(weights):
                block = source(place) if block is None else block
                term = weights[step] * block
                totals[plane] = term if totals[plane] is None else totals[plane] + term
    return totals


def chunks(rows, across):
    return [(slice(row, row + 16), slice(lane, lane + LANES)) for row in range(0, rows, 16) for lane in range(0, across, LANES)]


def rims_out_kernel(estimate, to_far, to_near):
    planes, radius, rows = estimate.shape[0], to_far.shape[0], to_far.shape[1]
    odd = lax.axis_index("tile") % 2
    half = half_of(lax.axis_index("view"))
    start = pl.multiple_of((estimate.shape[1] - rows) * half, 8)
    to_far[...] = estimate[pl.ds(odd, radius), pl.ds(start, rows)]
    to_near[...] = estimate[pl.ds(1 - odd, radius), pl.ds(start, rows)]


def rims_out(estimate, radius, rows):
    shape = jax.ShapeDtypeStruct((radius, rows, estimate.shape[2]), F32)
    return pl.pallas_call(
        rims_out_kernel,
        out_shape=(shape, shape),
        in_specs=[VMEM],
        out_specs=(VMEM, VMEM),
        compiler_params=pltpu.CompilerParams(vmem_limit_bytes=LIMIT),
        name="rims_out",
    )(estimate)


def view_out_kernel(seen, measured, kernels, packed):
    planes, height = measured.shape[1], measured.shape[2]
    half = half_of(lax.axis_index("view"))
    start = pl.multiple_of((height - seen) * (1 - half), 8)
    for plane in range(planes):
        packed[plane * seen : (plane + 1) * seen] = measured[0, plane, pl.ds(start, seen)]
    packed[planes * seen :] = jnp.zeros((8, packed.shape[1]), F32)
    packed[planes * seen : planes * seen + kernels.shape[1], : kernels.shape[2]] = kernels[0]


def view_out(measured, kernels, seen):
    _, planes, _, across = measured.shape
    return pl.pallas_call(
        functools.partial(view_out_kernel, seen),
        out_shape=jax.ShapeDtypeStruct((planes * seen + 8, across), F32),
        in_specs=[VMEM, VMEM],
        out_specs=VMEM,
        compiler_params=pltpu.CompilerParams(vmem_limit_bytes=LIMIT),
        name="view_out",
    )(measured, kernels)


def prepare_kernel(packed, taps, source, estimate, after, wide, tall, back, part, spread):
    half = half_of(lax.axis_index("view"))
    across = wide.shape[-1]
    rows, keep, seen = part.shape[1], back.shape[0], tall.shape[0]
    planes = estimate.shape[0]
    radius = (taps - 1) // 2
    raw = source[source.shape[0] - 8 : source.shape[0] - 5, :taps] if packed else source[0]
    weights = raw / jnp.sum(raw, axis=-1, keepdims=True)
    deep, high, flat = [[weights[axis : axis + 1, t : t + 1] for t in range(taps)] for axis in range(3)]
    start = pl.multiple_of((2 * keep - rows) * half, 16)
    seen_start = (2 * keep - seen) * half
    upper, lower = split(band(flat[::-1], (across, across), radius))
    wide[0, 0] = upper
    wide[0, 1] = lower
    upper, lower = split(band(flat, (across, across), radius))
    wide[1, 0] = upper
    wide[1, 1] = lower
    upper, lower = split(band(high, (seen, rows), radius + start - seen_start))
    tall[...] = jnp.concatenate([upper, upper, lower], axis=1)
    upper, lower = split(band(high[::-1], (keep, rows), radius + seen_start - keep * half))
    back[...] = jnp.concatenate([upper, upper, lower], axis=1)
    factors = [jnp.broadcast_to(tap, (16, LANES)) for tap in deep]
    spread[...] = jnp.zeros_like(spread)
    for step in range(taps):
        spread[step : step + 1] = factors[step][:1]
    for row, lane in chunks(rows, across):
        where = pl.ds(pl.multiple_of(start + row.start, 16), 16)
        terms = depth_terms(
            lambda place: estimate[place, where, lane], factors, 0, planes, range(planes), False
        )
        for plane, block in terms.items():
            part[plane, row, lane] = block


def prepare(packed, taps, source, estimate, after, rows, seen, keep):
    planes, _, across = estimate.shape
    return pl.pallas_call(
        functools.partial(prepare_kernel, packed, taps),
        out_shape=(
            jax.ShapeDtypeStruct((2, 2, across, across), BF16),
            jax.ShapeDtypeStruct((seen, 3 * rows), BF16),
            jax.ShapeDtypeStruct((keep, 3 * rows), BF16),
            jax.ShapeDtypeStruct((planes, rows, across), F32),
            jax.ShapeDtypeStruct((-(-taps // 8) * 8, LANES), F32),
        ),
        in_specs=[VMEM, VMEM, ANY],
        out_specs=(VMEM,) * 5,
        compiler_params=pltpu.CompilerParams(vmem_limit_bytes=LIMIT),
        name="prepare",
    )(source, estimate, after)


def spread_factors(spread, taps):
    return [jnp.broadcast_to(spread[step : step + 1, :], (16, LANES)) for step in range(taps)]


def view_kernel(
    first, wide, tall, back, part, spread, far, near, view, begun_near, begun_far,
    field, send_near, send_far,
    blur_hi, blur_lo, plane_hi, plane_lo,
):
    planes, radius = part.shape[0], near.shape[0]
    rows, across = near.shape[1], near.shape[2]
    keep, seen = back.shape[0], tall.shape[0]
    taps = 2 * radius + 1
    even = lax.axis_index("tile") % 2 == 0
    half = half_of(lax.axis_index("view"))
    seen_start = pl.multiple_of((2 * keep - seen) * half, 8)
    factors = spread_factors(spread, taps)
    for row, lane in chunks(rows, across):

        def rim(place):
            if place < 0:
                at = place + radius
                return jnp.where(even, far[at, row, lane], near[at, row, lane])
            at = place - planes
            return jnp.where(even, near[at, row, lane], far[at, row, lane])

        below = depth_terms(rim, factors, -radius, 0, range(planes), False)
        above = depth_terms(rim, factors, planes, planes + radius, range(planes), False)
        for plane in range(planes):
            block = part[plane, row, lane]
            for term in (below[plane], above[plane]):
                block = block if term is None else block + term
            upper, lower = split(block)
            at = slice(plane * rows + row.start, plane * rows + row.stop)
            blur_hi[at, lane] = upper
            blur_lo[at, lane] = lower
    upper, lower = wide[0, 0], wide[0, 1]
    lines = jnp.dot(blur_hi[...], upper, preferred_element_type=F32)
    lines += jnp.dot(blur_lo[...], upper, preferred_element_type=F32)
    lines += jnp.dot(blur_hi[...], lower, preferred_element_type=F32)
    for plane in range(planes):
        hi, lo = split(lines[plane * rows : (plane + 1) * rows])
        forward = jnp.dot(
            tall[...], jnp.concatenate([hi, lo, hi], axis=0), preferred_element_type=F32
        )
        if first:
            recorded = view[0, plane, pl.ds(seen_start, seen), :]
        else:
            recorded = view[plane * seen : (plane + 1) * seen]
        ratio = recorded / forward
        if rows > seen:
            ratio = jnp.concatenate([ratio, jnp.zeros((rows - seen, across), F32)], axis=0)
        hi, lo = split(ratio)
        turned = jnp.dot(
            back[...], jnp.concatenate([hi, lo, hi], axis=0), preferred_element_type=F32
        )
        hi, lo = split(turned)
        plane_hi[plane * keep : (plane + 1) * keep] = hi
        plane_lo[plane * keep : (plane + 1) * keep] = lo
    upper, lower = wide[1, 0], wide[1, 1]
    lines = jnp.dot(plane_hi[...], upper, preferred_element_type=F32)
    lines += jnp.dot(plane_lo[...], upper, preferred_element_type=F32)
    lines += jnp.dot(plane_hi[...], lower, preferred_element_type=F32)
    field[...] = lines.reshape(planes, keep, across)
    for row, lane in chunks(keep, across):
        source = lambda place: field[place, row, lane]
        below = depth_terms(source, factors, 0, planes, range(-radius, 0), True)
        above = depth_terms(source, factors, 0, planes, range(planes, planes + radius), True)
        for at in range(radius):
            down, up = below[at - radius], above[at + planes]
            to_near, to_far = jnp.where(even, up, down), jnp.where(even, down, up)
            if not first:
                to_near += begun_near[at, row, lane]
                to_far += begun_far[at, row, lane]
            send_near[at, row, lane] = to_near
            send_far[at, row, lane] = to_far


def view_field(first, prepared, near, far, view, begun):
    keep = prepared[2].shape[0]
    planes = prepared[3].shape[0]
    radius, rows, across = near.shape

    def body(*refs):
        if first:
            refs = refs[:8] + (None, None) + refs[8:]
        view_kernel(first, *refs)

    return pl.pallas_call(
        body,
        out_shape=(
            jax.ShapeDtypeStruct((planes, keep, across), F32),
            jax.ShapeDtypeStruct((radius, keep, across), F32),
            jax.ShapeDtypeStruct((radius, keep, across), F32),
        ),
        in_specs=[VMEM] * (8 + len(begun)),
        out_specs=(VMEM, VMEM, VMEM),
        scratch_shapes=[
            pltpu.VMEM((planes * rows, across), BF16),
            pltpu.VMEM((planes * rows, across), BF16),
            pltpu.VMEM((planes * keep, across), BF16),
            pltpu.VMEM((planes * keep, across), BF16),
        ],
        compiler_params=pltpu.CompilerParams(vmem_limit_bytes=LIMIT),
        name="view_first" if first else "view_second",
    )(*prepared, far, near, view, *begun)


def own_kernel(taps, spread_own, spread_other, field_own, field_other, inner):
    planes, keep, across = inner.shape
    factors = [spread_factors(spread, taps) for spread in (spread_own, spread_other)]
    for row, lane in chunks(keep, across):
        parts = [
            depth_terms(
                lambda place: field[place, row, lane], factors[which], 0, planes, range(planes), True
            )
            for which, field in enumerate((field_own, field_other))
        ]
        for plane in range(planes):
            inner[plane, row, lane] = parts[0][plane] + parts[1][plane]


def own_planes(taps, spread_own, spread_other, field_own, field_other):
    return pl.pallas_call(
        functools.partial(own_kernel, taps),
        out_shape=jax.ShapeDtypeStruct(field_own.shape, F32),
        in_specs=[VMEM] * 4,
        out_specs=VMEM,
        compiler_params=pltpu.CompilerParams(vmem_limit_bytes=LIMIT),
        name="own_planes",
    )(spread_own, spread_other, field_own, field_other)


def rims_kernel(inner, far, near, correction):
    planes, radius = inner.shape[0], near.shape[0]
    even = lax.axis_index("tile") % 2 == 0
    for plane in range(planes):
        total = inner[plane]
        if plane < radius:
            total += jnp.where(even, far[plane], near[plane])
        if plane >= planes - radius:
            at = plane - planes + radius
            total += jnp.where(even, near[at], far[at])
        correction[plane] = total


def add_rims(inner, near, far):
    return pl.pallas_call(
        rims_kernel,
        out_shape=jax.ShapeDtypeStruct(inner.shape, F32),
        in_specs=[VMEM] * 3,
        out_specs=VMEM,
        compiler_params=pltpu.CompilerParams(vmem_limit_bytes=LIMIT),
        name="add_rims",
    )(inner, far, near)


def table_rows(table):
    return jnp.concatenate([table[:8], table[8:]], axis=1)


def update_kernel(views, estimate, mine, other, table, result):
    planes, keep, across = mine.shape
    half = half_of(lax.axis_index("view"))
    start = pl.multiple_of(keep * half, 8)
    for plane in range(planes):
        held = estimate[plane, pl.ds(start, keep)]
        at = slice(plane * keep, (plane + 1) * keep)
        result[at] = held * (mine[plane] + other[plane]) * (1.0 / views)
    result[planes * keep :] = jnp.zeros((8, across), F32)
    result[planes * keep :, : 2 * LANES] = table_rows(table[...])


def update(views, estimate, mine, other, table):
    planes, keep, across = mine.shape
    return pl.pallas_call(
        functools.partial(update_kernel, views),
        out_shape=jax.ShapeDtypeStruct((planes * keep + 8, across), F32),
        in_specs=[VMEM] * 4,
        out_specs=VMEM,
        compiler_params=pltpu.CompilerParams(vmem_limit_bytes=LIMIT),
        name="update",
    )(estimate, mine, other, table)


def slots_kernel(owner_row, index_row, picked, base):
    count = picked.shape[0]
    slots = owner_row.shape[1]
    tiles = count // ROWS
    owner = owner_row[...]
    member = (lax.broadcasted_iota(jnp.int32, (tiles, slots), 0) == owner).astype(F32)
    upto = (
        lax.broadcasted_iota(jnp.int32, (slots, slots), 0)
        <= lax.broadcasted_iota(jnp.int32, (slots, slots), 1)
    ).astype(F32)
    running = jnp.dot(member, upto, preferred_element_type=F32)
    rank = jnp.sum(member * running, axis=0, keepdims=True).astype(jnp.int32) - 1
    place = owner * ROWS + rank
    chosen = lax.broadcasted_iota(jnp.int32, (count, slots), 0) == place
    picked[...] = chosen.astype(F32)
    ids = jnp.sum(jnp.where(chosen, index_row[...].astype(F32), 0.0), axis=1, keepdims=True)
    lanes = lax.broadcasted_iota(jnp.int32, (count, LANES), 1)
    base[...] = jnp.where(lanes == MOM, ids, 0.0)


def slot_places(tiles, label_owner, label_index):
    slots = label_index.shape[1]
    return pl.pallas_call(
        slots_kernel,
        out_shape=(
            jax.ShapeDtypeStruct((tiles * ROWS, slots), F32),
            jax.ShapeDtypeStruct((tiles * ROWS, LANES), F32),
        ),
        in_specs=[VMEM, VMEM],
        out_specs=(VMEM, VMEM),
        compiler_params=pltpu.CompilerParams(vmem_limit_bytes=LIMIT),
        name="slot_places",
    )(label_owner.reshape(1, slots), label_index)


def moments_kernel(
    views, depth_total, estimate, correction, labels, picked, base, sent, held, sums, table
):
    planes, keep, across = correction.shape
    height_total = estimate.shape[1]
    slots = picked.shape[1]
    half = half_of(lax.axis_index("view"))
    first = (lax.axis_index("tile") * planes).astype(F32) + 0.5
    start = pl.multiple_of(keep * half, 8)
    held[...] = estimate[:, pl.ds(start, keep)] * correction[...] * (1.0 / views)
    group = 16
    columns = lax.broadcasted_iota(jnp.int32, (across, LANES), 1)
    spot = (lax.broadcasted_iota(jnp.int32, (across, LANES), 0).astype(F32) + 0.5) / across
    one, line, square = jnp.ones_like(spot), spot, spot * spot

    def placed(*pairs):
        result = jnp.zeros((across, LANES), F32)
        for lane, value in pairs:
            result = jnp.where(columns == lane, value, result)
        return result

    factors = jnp.concatenate(
        [
            placed((0, one), (3, line), (6, square)),
            placed((2, one), (9, line)),
            placed((5, one)),
            placed((1, one), (8, line)),
            placed((7, one)),
            placed((4, one)),
        ],
        axis=0,
    )
    base_row = lax.broadcasted_iota(jnp.int32, (8, across), 0)

    def one_group(number, carry):
        def one_slot(inner, carry):
            slot = number * group + inner
            parts = [jnp.zeros((8, across), F32) for _ in range(6)]
            for row in range(0, keep, 8):
                high = ((base_row + (row + start)).astype(F32) + 0.5) / height_total
                flat, once, twice = [jnp.zeros((8, across), F32) for _ in range(3)]
                for plane in reversed(range(planes)):
                    hit = labels[plane, pl.ds(pl.multiple_of(start + row, 8), 8)] == slot
                    flat = flat + jnp.where(hit, held[plane, row : row + 8], 0.0)
                    if plane > 0:
                        once = once + flat
                        twice = twice + once
                square_sum = 2.0 * twice - once
                deep = (first * flat + once) * (1.0 / depth_total)
                deeper = (first * (first * flat + 2.0 * once) + square_sum) * (1.0 / depth_total**2)
                scaled = flat * high
                parts[0] = parts[0] + flat
                parts[1] = parts[1] + scaled
                parts[2] = parts[2] + scaled * high
                parts[3] = parts[3] + deep
                parts[4] = parts[4] + deep * high
                parts[5] = parts[5] + deeper
            at = pl.multiple_of(inner * 8, 8)
            sums[pl.ds(at, 8), :] = jnp.concatenate(parts, axis=1)
            return carry

        lax.fori_loop(0, group, one_slot, 0)
        lines = jnp.dot(
            sums[...], factors, precision=lax.Precision.HIGHEST, preferred_element_type=F32
        )
        at = pl.multiple_of(number * group, group)
        table[pl.ds(at, group), :] = jnp.sum(lines.reshape(group, 8, LANES), axis=1)
        return carry

    lax.fori_loop(0, slots // group, one_group, 0)
    sent[...] = base[...] + jnp.dot(
        picked[...], table[...], precision=lax.Precision.HIGHEST, preferred_element_type=F32
    )


def moment_rows(views, tiles, estimate, correction, labels, places):
    planes, keep, across = correction.shape
    slots = places[0].shape[1]
    return pl.pallas_call(
        functools.partial(moments_kernel, views, tiles * planes),
        out_shape=jax.ShapeDtypeStruct((tiles * ROWS, LANES), F32),
        in_specs=[VMEM] * 5,
        out_specs=VMEM,
        scratch_shapes=[
            pltpu.VMEM(correction.shape, F32),
            pltpu.VMEM((16 * 8, 6 * across), F32),
            pltpu.VMEM((slots, LANES), F32),
        ],
        compiler_params=pltpu.CompilerParams(vmem_limit_bytes=LIMIT),
        name="moment_rows",
    )(estimate, correction, labels, *places)


def segments_kernel(rows, table):
    values = rows[...]
    ids = values[:, MOM : MOM + 1].astype(jnp.int32)
    spots = lax.broadcasted_iota(jnp.int32, (values.shape[0], NUC_DEV), 1)
    picked = (ids == spots).astype(F32)
    full = lax.dot_general(
        values, picked, (((0,), (0,)), ((), ())),
        precision=lax.Precision.HIGHEST, preferred_element_type=F32,
    )
    table[...] = full[: table.shape[0]]


def segment_table(rows):
    return pl.pallas_call(
        segments_kernel,
        out_shape=jax.ShapeDtypeStruct((16, NUC_DEV), F32),
        in_specs=[VMEM],
        out_specs=VMEM,
        compiler_params=pltpu.CompilerParams(vmem_limit_bytes=LIMIT),
        name="segment_table",
    )(rows)


def own_half_kernel(keep, mine, whole, sems):
    planes = whole.shape[0]
    start = pl.multiple_of(keep * half_of(lax.axis_index("view")), 8)
    copies = [
        pltpu.make_async_copy(
            mine.at[pl.ds(plane * keep, keep)], whole.at[plane, pl.ds(start, keep)], sems.at[plane]
        )
        for plane in range(planes)
    ]
    for copy in copies:
        copy.start()
    for copy in copies:
        copy.wait()


def own_half(mine, planes, keep):
    return pl.pallas_call(
        functools.partial(own_half_kernel, keep),
        out_shape=jax.ShapeDtypeStruct((planes, 2 * keep, mine.shape[1]), F32),
        in_specs=[ANY],
        out_specs=ANY,
        scratch_shapes=[pltpu.SemaphoreType.DMA((planes,))],
        compiler_params=pltpu.CompilerParams(vmem_limit_bytes=LIMIT),
        name="own_half",
    )(mine)


def finish_kernel(scale, keep, begun, other, first, third, fourth, whole, moments, sems):
    planes = whole.shape[0]
    start = pl.multiple_of(keep * (1 - half_of(lax.axis_index("view"))), 8)
    copies = [
        pltpu.make_async_copy(
            other.at[pl.ds(plane * keep, keep)], whole.at[plane, pl.ds(start, keep)], sems.at[plane]
        )
        for plane in range(planes)
    ]
    for copy in copies:
        copy.start()
    rows = other[planes * keep :]
    second = jnp.concatenate([rows[:, :LANES], rows[:, LANES : 2 * LANES]], axis=0)
    table = (first[...] + second) + (third[...] + fourth[...])
    mass = table[0:1]
    lines = lax.broadcasted_iota(jnp.int32, table.shape, 0)
    result = jnp.where(lines == 0, table * scale, table / jnp.maximum(mass, 1.0))
    moments[...] = result[:MOM]
    for copy in copies:
        copy.wait()


def finish(scale, keep, begun, other, tables):
    planes = begun.shape[0]
    return pl.pallas_call(
        functools.partial(finish_kernel, scale, keep),
        out_shape=(
            jax.ShapeDtypeStruct(begun.shape, F32),
            jax.ShapeDtypeStruct((MOM, NUC_DEV), F32),
        ),
        in_specs=[ANY] + [VMEM] * 4,
        out_specs=(ANY, VMEM),
        input_output_aliases={0: 0},
        scratch_shapes=[pltpu.SemaphoreType.DMA((planes,))],
        compiler_params=pltpu.CompilerParams(vmem_limit_bytes=LIMIT),
        name="finish",
    )(begun, other, *tables)


def on_device(estimate, measured, kernels, labels, label_owner, label_index):
    tiles, views = lax.axis_size("tile"), lax.axis_size("view")
    planes, height, across = estimate.shape
    taps = kernels.shape[2]
    radius = (taps - 1) // 2
    keep = height // 2
    seen = min(height, -(-(keep + radius) // 8) * 8)
    rows = min(height, -(-(keep + 2 * radius) // 16) * 16)
    near_pairs = [(i, i ^ 1) for i in range(tiles)]
    far_pairs = [(i, i + 1) for i in range(1, tiles - 1, 2)]
    far_pairs = far_pairs + [(b, a) for a, b in far_pairs]
    partner = [(i, i ^ 1) for i in range(views)]
    across_pairs = [(i, i ^ 3) for i in range(views)]

    packed = view_out(measured, kernels, seen)
    swapped = lax.ppermute(packed, "view", partner)
    to_far, to_near = rims_out(estimate, radius, rows)
    far = lax.ppermute(to_far, "tile", far_pairs)
    near = lax.ppermute(to_near, "tile", near_pairs)
    own = prepare(False, taps, kernels, estimate, kernels, rows, seen, keep)
    field_own, *begun = view_field(True, own, near, far, measured, ())
    others = prepare(True, taps, swapped, estimate, begun[0], rows, seen, keep)
    field_other, sum_near, sum_far = view_field(False, others, near, far, swapped, begun)
    rim_far = lax.ppermute(sum_far, "tile", far_pairs)
    rim_near = lax.ppermute(sum_near, "tile", near_pairs)
    inner = own_planes(taps, own[4], others[4], field_own, field_other)
    mine = add_rims(inner, rim_near, rim_far)
    other = lax.ppermute(mine, "view", across_pairs)
    places = slot_places(tiles, label_owner, label_index)
    sent = moment_rows(views, tiles, estimate, mine, labels, places)
    got = lax.all_to_all(sent, "tile", split_axis=0, concat_axis=0, tiled=True)
    table = segment_table(got)
    tables = [table] + [
        lax.ppermute(table, "view", [(i, i ^ step) for i in range(views)]) for step in (2, 3)
    ]
    new_half = update(views, estimate, mine, other, table)
    new_other = lax.ppermute(new_half, "view", partner)
    scale = label_index.shape[1] / (planes * height * across)
    return finish(scale, keep, own_half(new_half, planes, keep), new_other, tables)


def solution(mesh):
    placed = (
        P("tile", None, None),
        P("view", "tile", None, None),
        P("view", None, None),
        P("tile", None, None),
        P("tile", None, None),
        P("tile", None),
    )
    return jax.shard_map(
        on_device,
        mesh=mesh,
        in_specs=placed,
        out_specs=(P("tile", None, None), P(None, "tile")),
        check_vma=False,
    )
```

```python
import functools

import jax
import jax.numpy as jnp
from jax import lax
from jax.experimental import pallas as pl
from jax.experimental.pallas import tpu as pltpu
from jax.sharding import PartitionSpec as P

MOM = 10
ROWS = 8
NUC_DEV = 128
LANES = 128
PARTS = 2
IDS = 24
F32 = jnp.float32
BF16 = jnp.bfloat16
ANY = pl.BlockSpec(memory_space=pl.ANY)
VMEM = pl.BlockSpec(memory_space=pltpu.VMEM)
LIMIT = 32 * 1024 * 1024


def half_of(view):
    return (view ^ (view >> 1)) & 1


def split(value):
    upper = value.astype(BF16)
    return upper, (value - upper.astype(F32)).astype(BF16)


def band(taps, shape, offset):
    rows = lax.broadcasted_iota(jnp.int32, shape, 0)
    cols = lax.broadcasted_iota(jnp.int32, shape, 1)
    place = cols - rows + offset
    result = jnp.zeros(shape, F32)
    for step, tap in enumerate(taps):
        result = jnp.where(place == step, tap, result)
    return result


def depth_terms(source, weights, first, last, planes, flipped):
    radius = (len(weights) - 1) // 2
    totals = {plane: None for plane in planes}
    for place in range(first, last):
        block = None
        for plane in planes:
            step = plane - place + radius if flipped else place - plane + radius
            if 0 <= step < len(weights):
                block = source(place) if block is None else block
                term = weights[step] * block
                totals[plane] = term if totals[plane] is None else totals[plane] + term
    return totals


def chunks(rows, across):
    return [(slice(row, row + 16), slice(lane, lane + LANES)) for row in range(0, rows, 16) for lane in range(0, across, LANES)]


def rims_out_kernel(estimate, to_far, to_near):
    planes, radius, rows = estimate.shape[0], to_far.shape[0], to_far.shape[1]
    odd = lax.axis_index("tile") % 2
    half = half_of(lax.axis_index("view"))
    start = pl.multiple_of((estimate.shape[1] - rows) * half, 8)
    to_far[...] = estimate[pl.ds(odd, radius), pl.ds(start, rows)]
    to_near[...] = estimate[pl.ds(1 - odd, radius), pl.ds(start, rows)]


def rims_out(estimate, radius, rows):
    shape = jax.ShapeDtypeStruct((radius, rows, estimate.shape[2]), F32)
    return pl.pallas_call(
        rims_out_kernel,
        out_shape=(shape, shape),
        in_specs=[VMEM],
        out_specs=(VMEM, VMEM),
        compiler_params=pltpu.CompilerParams(vmem_limit_bytes=LIMIT),
        name="rims_out",
    )(estimate)


def view_out_kernel(seen, measured, kernels, packed):
    planes, height = measured.shape[1], measured.shape[2]
    half = half_of(lax.axis_index("view"))
    start = pl.multiple_of((height - seen) * (1 - half), 8)
    for plane in range(planes):
        packed[plane * seen : (plane + 1) * seen] = measured[0, plane, pl.ds(start, seen)]
    packed[planes * seen :] = jnp.zeros((8, packed.shape[1]), F32)
    packed[planes * seen : planes * seen + kernels.shape[1], : kernels.shape[2]] = kernels[0]


def view_out(measured, kernels, seen):
    _, planes, _, across = measured.shape
    return pl.pallas_call(
        functools.partial(view_out_kernel, seen),
        out_shape=jax.ShapeDtypeStruct((planes * seen + 8, across), F32),
        in_specs=[VMEM, VMEM],
        out_specs=VMEM,
        compiler_params=pltpu.CompilerParams(vmem_limit_bytes=LIMIT),
        name="view_out",
    )(measured, kernels)


def prepare_kernel(packed, taps, source, estimate, after, wide, tall, back, part, spread):
    half = half_of(lax.axis_index("view"))
    across = wide.shape[-1]
    rows, keep, seen = part.shape[1], back.shape[0], tall.shape[0]
    planes = estimate.shape[0]
    radius = (taps - 1) // 2
    raw = source[source.shape[0] - 8 : source.shape[0] - 5, :taps] if packed else source[0]
    weights = raw / jnp.sum(raw, axis=-1, keepdims=True)
    deep, high, flat = [[weights[axis : axis + 1, t : t + 1] for t in range(taps)] for axis in range(3)]
    start = pl.multiple_of((2 * keep - rows) * half, 16)
    seen_start = (2 * keep - seen) * half
    near_diagonal = jnp.abs(
        lax.broadcasted_iota(jnp.int32, (across, across), 1)
        - lax.broadcasted_iota(jnp.int32, (across, across), 0)
    ) <= radius
    for turn, line in enumerate((flat[::-1], flat)):
        first_row = jnp.concatenate(
            line[radius:] + [jnp.zeros((1, across - taps), F32)] + line[:radius], axis=1
        )
        square = pltpu.roll(
            jnp.broadcast_to(first_row, (across, across)), 0, 1, stride=1, stride_axis=0
        )
        upper, lower = split(jnp.where(near_diagonal, square, 0.0))
        wide[turn, 0] = upper
        wide[turn, 1] = lower
    upper, lower = split(band(high, (seen, rows), radius + start - seen_start))
    tall[...] = jnp.concatenate([upper, upper, lower], axis=1)
    upper, lower = split(band(high[::-1], (keep, rows), radius + seen_start - keep * half))
    back[...] = jnp.concatenate([upper, upper, lower], axis=1)
    factors = [jnp.broadcast_to(tap, (16, LANES)) for tap in deep]
    spread[...] = jnp.zeros_like(spread)
    for step in range(taps):
        spread[step : step + 1] = factors[step][:1]
    for row, lane in chunks(rows, across):
        where = pl.ds(pl.multiple_of(start + row.start, 16), 16)
        terms = depth_terms(
            lambda place: estimate[place, where, lane], factors, 0, planes, range(planes), False
        )
        for plane, block in terms.items():
            part[plane, row, lane] = block


def prepare(packed, taps, source, estimate, after, rows, seen, keep):
    planes, _, across = estimate.shape
    return pl.pallas_call(
        functools.partial(prepare_kernel, packed, taps),
        out_shape=(
            jax.ShapeDtypeStruct((2, 2, across, across), BF16),
            jax.ShapeDtypeStruct((seen, 3 * rows), BF16),
            jax.ShapeDtypeStruct((keep, 3 * rows), BF16),
            jax.ShapeDtypeStruct((planes, rows, across), F32),
            jax.ShapeDtypeStruct((-(-taps // 8) * 8, LANES), F32),
        ),
        in_specs=[VMEM, VMEM, ANY],
        out_specs=(VMEM,) * 5,
        compiler_params=pltpu.CompilerParams(vmem_limit_bytes=LIMIT),
        name="prepare",
    )(source, estimate, after)


def spread_factors(spread, taps):
    return [jnp.broadcast_to(spread[step : step + 1, :], (16, LANES)) for step in range(taps)]


def view_kernel(first, *refs):
    wide, tall, back, part, spread, far, near, view = refs[:8]
    begun, refs = ((), refs[8:]) if first else (refs[8 : 8 + 2 * PARTS], refs[8 + 2 * PARTS :])
    field, *sends = refs[: 1 + 2 * PARTS]
    blur_hi, blur_lo, plane_hi, plane_lo = refs[1 + 2 * PARTS :]
    planes, radius = part.shape[0], near.shape[0]
    rows, across = near.shape[1], near.shape[2]
    keep, seen = back.shape[0], tall.shape[0]
    taps = 2 * radius + 1
    even = lax.axis_index("tile") % 2 == 0
    half = half_of(lax.axis_index("view"))
    seen_start = pl.multiple_of((2 * keep - seen) * half, 8)
    factors = spread_factors(spread, taps)
    for row, lane in chunks(rows, across):

        def rim(place):
            if place < 0:
                at = place + radius
                return jnp.where(even, far[at, row, lane], near[at, row, lane])
            at = place - planes
            return jnp.where(even, near[at, row, lane], far[at, row, lane])

        below = depth_terms(rim, factors, -radius, 0, range(planes), False)
        above = depth_terms(rim, factors, planes, planes + radius, range(planes), False)
        for plane in range(planes):
            block = part[plane, row, lane]
            for term in (below[plane], above[plane]):
                block = block if term is None else block + term
            upper, lower = split(block)
            at = slice(plane * rows + row.start, plane * rows + row.stop)
            blur_hi[at, lane] = upper
            blur_lo[at, lane] = lower
    upper, lower = wide[0, 0], wide[0, 1]
    lines = jnp.dot(blur_hi[...], upper, preferred_element_type=F32)
    lines += jnp.dot(blur_lo[...], upper, preferred_element_type=F32)
    lines += jnp.dot(blur_hi[...], lower, preferred_element_type=F32)
    forwards = []
    for plane in range(planes):
        hi, lo = split(lines[plane * rows : (plane + 1) * rows])
        forwards.append(
            jnp.dot(tall[...], jnp.concatenate([hi, lo, hi], axis=0), preferred_element_type=F32)
        )
    ratios = []
    for plane in range(planes):
        if first:
            recorded = view[0, plane, pl.ds(seen_start, seen), :]
        else:
            recorded = view[plane * seen : (plane + 1) * seen]
        ratio = recorded / forwards[plane]
        if rows > seen:
            ratio = jnp.concatenate([ratio, jnp.zeros((rows - seen, across), F32)], axis=0)
        ratios.append(split(ratio))
    turned = [
        jnp.dot(back[...], jnp.concatenate([hi, lo, hi], axis=0), preferred_element_type=F32)
        for hi, lo in ratios
    ]
    for plane in range(planes):
        hi, lo = split(turned[plane])
        plane_hi[plane * keep : (plane + 1) * keep] = hi
        plane_lo[plane * keep : (plane + 1) * keep] = lo
    upper, lower = wide[1, 0], wide[1, 1]
    lines = jnp.dot(plane_hi[...], upper, preferred_element_type=F32)
    lines += jnp.dot(plane_lo[...], upper, preferred_element_type=F32)
    lines += jnp.dot(plane_hi[...], lower, preferred_element_type=F32)
    field[...] = lines.reshape(planes, keep, across)
    for row, lane in chunks(keep, across):
        source = lambda place: field[place, row, lane]
        below = depth_terms(source, factors, 0, planes, range(-radius, 0), True)
        above = depth_terms(source, factors, 0, planes, range(planes, planes + radius), True)
        part_at, inside = divmod(row.start, keep // PARTS)
        inside = slice(inside, inside + 16)
        for at in range(radius):
            down, up = below[at - radius], above[at + planes]
            to_far, to_near = jnp.where(even, down, up), jnp.where(even, up, down)
            if not first:
                to_far += begun[2 * part_at][at, inside, lane]
                to_near += begun[2 * part_at + 1][at, inside, lane]
            sends[2 * part_at][at, inside, lane] = to_far
            sends[2 * part_at + 1][at, inside, lane] = to_near


def view_field(first, prepared, near, far, view, begun):
    keep = prepared[2].shape[0]
    planes = prepared[3].shape[0]
    radius, rows, across = near.shape

    send = jax.ShapeDtypeStruct((radius, keep // PARTS, across), F32)
    return pl.pallas_call(
        functools.partial(view_kernel, first),
        out_shape=(jax.ShapeDtypeStruct((planes, keep, across), F32),) + (send,) * (2 * PARTS),
        in_specs=[VMEM] * (8 + len(begun)),
        out_specs=(VMEM,) * (1 + 2 * PARTS),
        scratch_shapes=[
            pltpu.VMEM((planes * rows, across), BF16),
            pltpu.VMEM((planes * rows, across), BF16),
            pltpu.VMEM((planes * keep, across), BF16),
            pltpu.VMEM((planes * keep, across), BF16),
        ],
        compiler_params=pltpu.CompilerParams(vmem_limit_bytes=LIMIT),
        name="view_first" if first else "view_second",
    )(*prepared, far, near, view, *begun)


def own_kernel(taps, spread_own, spread_other, field_own, field_other, *inner):
    planes, keep, across = field_own.shape
    factors = [spread_factors(spread, taps) for spread in (spread_own, spread_other)]
    for row, lane in chunks(keep, across):
        parts = [
            depth_terms(
                lambda place: field[place, row, lane], factors[which], 0, planes, range(planes), True
            )
            for which, field in enumerate((field_own, field_other))
        ]
        part_at, inside = divmod(row.start, keep // PARTS)
        for plane in range(planes):
            inner[part_at][plane, inside : inside + 16, lane] = parts[0][plane] + parts[1][plane]


def own_planes(taps, spread_own, spread_other, field_own, field_other):
    planes, keep, across = field_own.shape
    return pl.pallas_call(
        functools.partial(own_kernel, taps),
        out_shape=(jax.ShapeDtypeStruct((planes, keep // PARTS, across), F32),) * PARTS,
        in_specs=[VMEM] * 4,
        out_specs=(VMEM,) * PARTS,
        compiler_params=pltpu.CompilerParams(vmem_limit_bytes=LIMIT),
        name="own_planes",
    )(spread_own, spread_other, field_own, field_other)


def rims_kernel(inner, far, near, *rest):
    correction = rest[-1]
    planes, radius = inner.shape[0], near.shape[0]
    even = lax.axis_index("tile") % 2 == 0
    for plane in range(planes):
        total = inner[plane]
        if plane < radius:
            total += jnp.where(even, far[plane], near[plane])
        if plane >= planes - radius:
            at = plane - planes + radius
            total += jnp.where(even, near[at], far[at])
        correction[plane] = total


def add_rims(inner, far, near, *after):
    return pl.pallas_call(
        rims_kernel,
        out_shape=jax.ShapeDtypeStruct(inner.shape, F32),
        in_specs=[VMEM] * 3 + [ANY] * len(after),
        out_specs=VMEM,
        compiler_params=pltpu.CompilerParams(vmem_limit_bytes=LIMIT),
        name="add_rims",
    )(inner, far, near, *after)


def table_rows(table):
    return jnp.concatenate([table[:8], table[8:]], axis=1)


def update_kernel(views, part, tabled, estimate, mine, other, *rest):
    planes, size, across = mine.shape
    half = half_of(lax.axis_index("view"))
    start = pl.multiple_of(size * (PARTS * half + part), 8)
    result = rest[-1]
    for plane in range(planes):
        held = estimate[plane, pl.ds(start, size)]
        at = slice(plane * size, (plane + 1) * size)
        result[at] = held * (mine[plane] + other[plane]) * (1.0 / views)
    if tabled:
        table = rest[0][...]
        result[planes * size :] = jnp.zeros((8, across), F32)
        result[planes * size :, : 2 * LANES] = jnp.concatenate([table[:8], table[8:]], axis=1)


def update(views, part, estimate, mine, other, table, after):
    planes, size, across = mine.shape
    return pl.pallas_call(
        functools.partial(update_kernel, views, part, len(table) > 0),
        out_shape=jax.ShapeDtypeStruct((planes * size + 8 * len(table), across), F32),
        in_specs=[VMEM] * (3 + len(table)) + [ANY] * len(after),
        out_specs=VMEM,
        compiler_params=pltpu.CompilerParams(vmem_limit_bytes=LIMIT),
        name="update",
    )(estimate, mine, other, *table, *after)


def slots_kernel(owner_row, index_row, picked, base):
    count = picked.shape[0]
    slots = owner_row.shape[1]
    tiles = count // ROWS
    owner = owner_row[...]
    member = (lax.broadcasted_iota(jnp.int32, (tiles, slots), 0) == owner).astype(F32)
    upto = (
        lax.broadcasted_iota(jnp.int32, (slots, slots), 0)
        <= lax.broadcasted_iota(jnp.int32, (slots, slots), 1)
    ).astype(F32)
    running = jnp.dot(member, upto, preferred_element_type=F32)
    rank = jnp.sum(member * running, axis=0, keepdims=True).astype(jnp.int32) - 1
    place = owner * ROWS + rank
    chosen = lax.broadcasted_iota(jnp.int32, (count, slots), 0) == place
    picked[...] = chosen.astype(F32)
    ids = jnp.sum(jnp.where(chosen, index_row[...].astype(F32), 0.0), axis=1, keepdims=True)
    lanes = lax.broadcasted_iota(jnp.int32, (count, LANES), 1)
    base[...] = jnp.where(lanes == IDS, ids, 0.0)


def slot_places(tiles, label_owner, label_index):
    slots = label_index.shape[1]
    return pl.pallas_call(
        slots_kernel,
        out_shape=(
            jax.ShapeDtypeStruct((tiles * ROWS, slots), F32),
            jax.ShapeDtypeStruct((tiles * ROWS, LANES), F32),
        ),
        in_specs=[VMEM, VMEM],
        out_specs=(VMEM, VMEM),
        compiler_params=pltpu.CompilerParams(vmem_limit_bytes=LIMIT),
        name="slot_places",
    )(label_owner.reshape(1, slots), label_index)


def moments_kernel(views, depth_total, estimate, labels, picked, base, *refs):
    corrections, (sent, held, sums, table) = refs[:PARTS], refs[PARTS:]
    planes, keep, across = held.shape
    size = keep // PARTS
    height_total = estimate.shape[1]
    slots = picked.shape[1]
    half = half_of(lax.axis_index("view"))
    first = (lax.axis_index("tile") * planes).astype(F32) + 0.5
    start = pl.multiple_of(keep * half, 8)
    for part, correction in enumerate(corrections):
        rows = pl.ds(pl.multiple_of(start + part * size, 8), size)
        held[:, part * size : (part + 1) * size] = (
            estimate[:, rows] * correction[...] * (1.0 / views)
        )
    group = 16
    spot = lax.broadcasted_iota(jnp.int32, (across, LANES), 0)
    lanes = lax.broadcasted_iota(jnp.int32, (across, LANES), 1)
    low = (spot * spot) & 255
    factors = jnp.where(lanes == 0, 1, jnp.where(lanes == 1, spot, 0))
    factors = jnp.where(lanes == 2, spot * spot - low, jnp.where(lanes == 3, low, factors))
    factors = factors.astype(F32).astype(BF16)
    base_row = lax.broadcasted_iota(jnp.int32, (8, across), 0)

    def one_group(number, carry):
        for pair in range(0, group, 2):
            slot = [number * group + pair, number * group + pair + 1]
            parts = [[None] * 6 for _ in slot]
            for row in range(0, keep, 8):
                high = ((base_row + (row + start)).astype(F32) + 0.5) * (1.0 / height_total)
                flat, once, twice = [[jnp.zeros((8, across), F32) for _ in slot] for _ in range(3)]
                for plane in reversed(range(planes)):
                    mark = labels[plane, pl.ds(pl.multiple_of(start + row, 8), 8)]
                    value = held[plane, row : row + 8]
                    for at in range(2):
                        flat[at] = flat[at] + jnp.where(mark == slot[at], value, 0.0)
                        if plane > 0:
                            once[at] = once[at] + flat[at]
                            twice[at] = twice[at] + once[at]
                for at in range(2):
                    square_sum = 2.0 * twice[at] - once[at]
                    line = first * flat[at]
                    deep = (line + once[at]) * (1.0 / depth_total)
                    deeper = (first * (line + 2.0 * once[at]) + square_sum) * (1.0 / depth_total**2)
                    scaled = flat[at] * high
                    terms = (flat[at], scaled, scaled * high, deep, deep * high, deeper)
                    parts[at] = [new if old is None else old + new for old, new in zip(parts[at], terms)]
            for at in range(2):
                for kind in range(6):
                    row = kind * group + pair + at
                    sums[row : row + 1, :] = jnp.sum(parts[at][kind], axis=0, keepdims=True)
        whole = sums[...]
        upper, rest = split(whole)
        rest = whole - upper.astype(F32)
        middle, lower = split(rest)
        lines = jnp.dot(
            jnp.concatenate([upper, middle, lower], axis=0), factors, preferred_element_type=F32
        )
        count = 6 * group
        lines = lines[:count] + lines[count : 2 * count] + lines[2 * count :]
        total = lines[:group]
        for kind in range(1, 6):
            total += pltpu.roll(lines[kind * group : (kind + 1) * group], 4 * kind, 1)
        table[pl.ds(pl.multiple_of(number * group, group), group), :] = total
        return carry

    lax.fori_loop(0, slots // group, one_group, 0)
    sent[...] = base[...] + jnp.dot(
        picked[...], table[...], precision=lax.Precision.HIGHEST, preferred_element_type=F32
    )


def moment_rows(views, tiles, estimate, corrections, labels, places):
    planes, size, across = corrections[0].shape
    slots = places[0].shape[1]
    return pl.pallas_call(
        functools.partial(moments_kernel, views, tiles * planes),
        out_shape=jax.ShapeDtypeStruct((tiles * ROWS, LANES), F32),
        in_specs=[VMEM] * (4 + PARTS),
        out_specs=VMEM,
        scratch_shapes=[
            pltpu.VMEM((planes, size * PARTS, across), F32),
            pltpu.VMEM((6 * 16, across), F32),
            pltpu.VMEM((slots, LANES), F32),
        ],
        compiler_params=pltpu.CompilerParams(vmem_limit_bytes=LIMIT),
        name="moment_rows",
    )(estimate, labels, *places, *corrections)


def segments_kernel(across, rows, table):
    values = rows[...]
    ids = values[:, IDS : IDS + 1].astype(jnp.int32)
    spots = lax.broadcasted_iota(jnp.int32, (values.shape[0], NUC_DEV), 1)
    picked = (ids == spots).astype(F32)
    full = lax.dot_general(
        values, picked, (((0,), (0,)), ((), ())),
        precision=lax.Precision.HIGHEST, preferred_element_type=F32,
    )
    mass, high, higher, deep, deep_high, deeper = [full[4 * kind : 4 * kind + 4] for kind in range(6)]
    flat = lambda sums: sums[0:1]
    line = lambda sums: (sums[1:2] + 0.5 * sums[0:1]) * (1.0 / across)
    square = lambda sums: (sums[2:3] + sums[3:4] + sums[1:2] + 0.25 * sums[0:1]) * (1.0 / across**2)
    table[...] = jnp.concatenate(
        [
            flat(mass), flat(deep), flat(high), line(mass),
            flat(deeper), flat(higher), square(mass),
            flat(deep_high), line(deep), line(high),
            jnp.zeros((table.shape[0] - MOM, NUC_DEV), F32),
        ],
        axis=0,
    )


def segment_table(across, rows):
    return pl.pallas_call(
        functools.partial(segments_kernel, across),
        out_shape=jax.ShapeDtypeStruct((16, NUC_DEV), F32),
        in_specs=[VMEM],
        out_specs=VMEM,
        compiler_params=pltpu.CompilerParams(vmem_limit_bytes=LIMIT),
        name="segment_table",
    )(rows)


def stores(source, whole, half, part, size, sems):
    start = pl.multiple_of(size * (PARTS * half + part), 8)
    copies = [
        pltpu.make_async_copy(
            source.at[pl.ds(plane * size, size)], whole.at[plane, pl.ds(start, size)], sems.at[plane]
        )
        for plane in range(whole.shape[0])
    ]
    for copy in copies:
        copy.start()
    return copies


def store_kernel(own, part, size, other, *refs):
    whole, token, sems = refs[-3:]
    half = half_of(lax.axis_index("view"))
    copies = stores(other, whole, half if own else 1 - half, part, size, sems)
    token[...] = jnp.zeros_like(token)
    for copy in copies:
        copy.wait()


def store_part(own, part, size, shape, other, begun):
    return pl.pallas_call(
        functools.partial(store_kernel, own, part, size),
        out_shape=(jax.ShapeDtypeStruct(shape, F32), jax.ShapeDtypeStruct((8, LANES), F32)),
        in_specs=[ANY] * (1 + len(begun)),
        out_specs=(ANY, VMEM),
        input_output_aliases={1: 0} if begun else {},
        scratch_shapes=[pltpu.SemaphoreType.DMA((shape[0],))],
        compiler_params=pltpu.CompilerParams(vmem_limit_bytes=LIMIT),
        name="store_part",
    )(other, *begun)


def finish_kernel(
    scale, size, begun, other, tabled, first, third, fourth, whole, moments, held, sems, sem
):
    planes = whole.shape[0]
    half = half_of(lax.axis_index("view"))
    copies = stores(other, whole, 1 - half, PARTS - 1, size, sems)
    rows = tabled[planes * size :]
    second = jnp.concatenate([rows[:, :LANES], rows[:, LANES : 2 * LANES]], axis=0)
    table = (first[...] + second) + (third[...] + fourth[...])
    lines = lax.broadcasted_iota(jnp.int32, table.shape, 0)
    result = jnp.where(lines == 0, table * scale, table / jnp.maximum(table[0:1], 1.0))
    held[...] = result[:MOM]
    last = pltpu.make_async_copy(held, moments, sem)
    last.start()
    for copy in copies:
        copy.wait()
    last.wait()


def finish(scale, size, begun, other, tabled, tables):
    return pl.pallas_call(
        functools.partial(finish_kernel, scale, size),
        out_shape=(
            jax.ShapeDtypeStruct(begun.shape, F32),
            jax.ShapeDtypeStruct((MOM, NUC_DEV), F32),
        ),
        in_specs=[ANY] + [VMEM] * 5,
        out_specs=(ANY, ANY),
        input_output_aliases={0: 0},
        scratch_shapes=[
            pltpu.VMEM((MOM, NUC_DEV), F32),
            pltpu.SemaphoreType.DMA((begun.shape[0],)),
            pltpu.SemaphoreType.DMA,
        ],
        compiler_params=pltpu.CompilerParams(vmem_limit_bytes=LIMIT),
        name="finish",
    )(begun, other, tabled, *tables)


def on_device(estimate, measured, kernels, labels, label_owner, label_index):
    tiles, views = lax.axis_size("tile"), lax.axis_size("view")
    planes, height, across = estimate.shape
    taps = kernels.shape[2]
    radius = (taps - 1) // 2
    keep = height // 2
    seen = min(height, -(-(keep + radius) // 8) * 8)
    rows = min(height, -(-(keep + 2 * radius) // 16) * 16)
    near_pairs = [(i, i ^ 1) for i in range(tiles)]
    far_pairs = [(i, i + 1) for i in range(1, tiles - 1, 2)]
    far_pairs = far_pairs + [(b, a) for a, b in far_pairs]
    partner = [(i, i ^ 1) for i in range(views)]
    across_pairs = [(i, i ^ 3) for i in range(views)]

    packed = view_out(measured, kernels, seen)
    swapped = lax.ppermute(packed, "view", partner)
    to_far, to_near = rims_out(estimate, radius, rows)
    far = lax.ppermute(to_far, "tile", far_pairs)
    near = lax.ppermute(to_near, "tile", near_pairs)
    places = slot_places(tiles, label_owner, label_index)
    own = prepare(False, taps, kernels, estimate, places[1], rows, seen, keep)
    field_own, *begun = view_field(True, own, near, far, measured, ())
    others = prepare(True, taps, swapped, estimate, begun[0], rows, seen, keep)
    field_other, *sends = view_field(False, others, near, far, swapped, begun)
    rims = [
        lax.ppermute(send, "tile", pairs) for send, pairs in zip(sends, (far_pairs, near_pairs) * PARTS)
    ]
    inner = own_planes(taps, own[4], others[4], field_own, field_other)
    mine = []
    for part in range(PARTS):
        mine.append(add_rims(inner[part], *rims[2 * part : 2 * part + 2], *mine[-1:]))
    other = [lax.ppermute(part, "view", across_pairs) for part in mine]
    sent = moment_rows(views, tiles, estimate, mine, labels, places)
    got = lax.all_to_all(sent, "tile", split_axis=0, concat_axis=0, tiled=True)
    table = segment_table(across, got)
    tables = [table] + [
        lax.ppermute(table, "view", [(i, i ^ step) for i in range(views)]) for step in (2, 3)
    ]
    size = keep // PARTS
    new_other, begun, token = [], [], []
    for part in range(PARTS):
        last = [table] if part == 0 else []
        new_mine = update(views, part, estimate, mine[part], other[part], last, token)
        new_other.append(lax.ppermute(new_mine, "view", partner))
        *begun, after = store_part(True, part, size, estimate.shape, new_mine, begun)
        token = [after]
    for part in range(PARTS - 1):
        *begun, _ = store_part(False, part, size, estimate.shape, new_other[part], begun)
    scale = label_index.shape[1] / (planes * height * across)
    return finish(scale, size, begun[0], new_other[-1], new_other[0], tables)


def solution(mesh):
    placed = (
        P("tile", None, None),
        P("view", "tile", None, None),
        P("view", None, None),
        P("tile", None, None),
        P("tile", None, None),
        P("tile", None),
    )
    return jax.shard_map(
        on_device,
        mesh=mesh,
        in_specs=placed,
        out_specs=(P("tile", None, None), P(None, "tile")),
        check_vma=False,
    )
```

```python
import functools

import jax
import jax.numpy as jnp
from jax import lax
from jax.experimental import pallas as pl
from jax.experimental.pallas import tpu as pltpu
from jax.sharding import PartitionSpec as P

MOM = 10
ROWS = 8
NUC_DEV = 128
LANES = 128
PARTS = 2
IDS = 24
F32 = jnp.float32
BF16 = jnp.bfloat16
ANY = pl.BlockSpec(memory_space=pl.ANY)
VMEM = pl.BlockSpec(memory_space=pltpu.VMEM)
LIMIT = 32 * 1024 * 1024


def half_of(view):
    return (view ^ (view >> 1)) & 1


def split(value):
    upper = value.astype(BF16)
    return upper, (value - upper.astype(F32)).astype(BF16)


def band(taps, shape, offset):
    rows = lax.broadcasted_iota(jnp.int32, shape, 0)
    cols = lax.broadcasted_iota(jnp.int32, shape, 1)
    place = cols - rows + offset
    result = jnp.zeros(shape, F32)
    for step, tap in enumerate(taps):
        result = jnp.where(place == step, tap, result)
    return result


def depth_terms(source, weights, first, last, planes, flipped):
    radius = (len(weights) - 1) // 2
    totals = {plane: None for plane in planes}
    for place in range(first, last):
        block = None
        for plane in planes:
            step = plane - place + radius if flipped else place - plane + radius
            if 0 <= step < len(weights):
                block = source(place) if block is None else block
                term = weights[step] * block
                totals[plane] = term if totals[plane] is None else totals[plane] + term
    return totals


def chunks(rows, across):
    return [(slice(row, row + 16), slice(lane, lane + LANES)) for row in range(0, rows, 16) for lane in range(0, across, LANES)]


def rims_out_kernel(estimate, to_far, to_near):
    planes, radius, rows = estimate.shape[0], to_far.shape[0], to_far.shape[1]
    odd = lax.axis_index("tile") % 2
    half = half_of(lax.axis_index("view"))
    start = pl.multiple_of((estimate.shape[1] - rows) * half, 8)
    to_far[...] = estimate[pl.ds(odd, radius), pl.ds(start, rows)]
    to_near[...] = estimate[pl.ds(1 - odd, radius), pl.ds(start, rows)]


def rims_out(estimate, radius, rows):
    shape = jax.ShapeDtypeStruct((radius, rows, estimate.shape[2]), F32)
    return pl.pallas_call(
        rims_out_kernel,
        out_shape=(shape, shape),
        in_specs=[VMEM],
        out_specs=(VMEM, VMEM),
        compiler_params=pltpu.CompilerParams(vmem_limit_bytes=LIMIT),
        name="rims_out",
    )(estimate)


def view_out_kernel(seen, measured, kernels, packed):
    planes, height = measured.shape[1], measured.shape[2]
    half = half_of(lax.axis_index("view"))
    start = pl.multiple_of((height - seen) * (1 - half), 8)
    for plane in range(planes):
        packed[plane * seen : (plane + 1) * seen] = measured[0, plane, pl.ds(start, seen)]
    packed[planes * seen :] = jnp.zeros((8, packed.shape[1]), F32)
    packed[planes * seen : planes * seen + kernels.shape[1], : kernels.shape[2]] = kernels[0]


def view_out(measured, kernels, seen):
    _, planes, _, across = measured.shape
    return pl.pallas_call(
        functools.partial(view_out_kernel, seen),
        out_shape=jax.ShapeDtypeStruct((planes * seen + 8, across), F32),
        in_specs=[VMEM, VMEM],
        out_specs=VMEM,
        compiler_params=pltpu.CompilerParams(vmem_limit_bytes=LIMIT),
        name="view_out",
    )(measured, kernels)


def prepare_kernel(packed, taps, source, estimate, after, wide, tall, back, part, spread):
    half = half_of(lax.axis_index("view"))
    across = wide.shape[-1]
    rows, keep, seen = part.shape[1], back.shape[0], tall.shape[0]
    planes = estimate.shape[0]
    radius = (taps - 1) // 2
    raw = source[source.shape[0] - 8 : source.shape[0] - 5, :taps] if packed else source[0]
    weights = raw / jnp.sum(raw, axis=-1, keepdims=True)
    deep, high, flat = [[weights[axis : axis + 1, t : t + 1] for t in range(taps)] for axis in range(3)]
    start = pl.multiple_of((2 * keep - rows) * half, 16)
    seen_start = (2 * keep - seen) * half
    near_diagonal = jnp.abs(
        lax.broadcasted_iota(jnp.int32, (across, across), 1)
        - lax.broadcasted_iota(jnp.int32, (across, across), 0)
    ) <= radius
    for turn, line in enumerate((flat[::-1], flat)):
        first_row = jnp.concatenate(
            line[radius:] + [jnp.zeros((1, across - taps), F32)] + line[:radius], axis=1
        )
        square = pltpu.roll(
            jnp.broadcast_to(first_row, (across, across)), 0, 1, stride=1, stride_axis=0
        )
        upper, lower = split(jnp.where(near_diagonal, square, 0.0))
        wide[turn, 0] = upper
        wide[turn, 1] = lower
    upper, lower = split(band(high, (seen, rows), radius + start - seen_start))
    tall[...] = jnp.concatenate([upper, upper, lower], axis=1)
    upper, lower = split(band(high[::-1], (keep, rows), radius + seen_start - keep * half))
    back[...] = jnp.concatenate([upper, upper, lower], axis=1)
    factors = [jnp.broadcast_to(tap, (16, LANES)) for tap in deep]
    spread[...] = jnp.zeros_like(spread)
    for step in range(taps):
        spread[step : step + 1] = factors[step][:1]
    for row, lane in chunks(rows, across):
        where = pl.ds(pl.multiple_of(start + row.start, 16), 16)
        terms = depth_terms(
            lambda place: estimate[place, where, lane], factors, 0, planes, range(planes), False
        )
        for plane, block in terms.items():
            part[plane, row, lane] = block


def prepare(packed, taps, source, estimate, after, rows, seen, keep):
    planes, _, across = estimate.shape
    return pl.pallas_call(
        functools.partial(prepare_kernel, packed, taps),
        out_shape=(
            jax.ShapeDtypeStruct((2, 2, across, across), BF16),
            jax.ShapeDtypeStruct((seen, 3 * rows), BF16),
            jax.ShapeDtypeStruct((keep, 3 * rows), BF16),
            jax.ShapeDtypeStruct((planes, rows, across), F32),
            jax.ShapeDtypeStruct((-(-taps // 8) * 8, LANES), F32),
        ),
        in_specs=[VMEM, VMEM, ANY],
        out_specs=(VMEM,) * 5,
        compiler_params=pltpu.CompilerParams(vmem_limit_bytes=LIMIT),
        name="prepare",
    )(source, estimate, after)


def spread_factors(spread, taps):
    return [jnp.broadcast_to(spread[step : step + 1, :], (16, LANES)) for step in range(taps)]


def view_kernel(first, *refs):
    wide, tall, back, part, spread, far, near, view = refs[:8]
    begun, refs = ((), refs[8:]) if first else (refs[8 : 8 + 2 * PARTS], refs[8 + 2 * PARTS :])
    field, *sends = refs[: 1 + 2 * PARTS]
    blur_hi, blur_lo, plane_hi, plane_lo = refs[1 + 2 * PARTS :]
    planes, radius = part.shape[0], near.shape[0]
    rows, across = near.shape[1], near.shape[2]
    keep, seen = back.shape[0], tall.shape[0]
    taps = 2 * radius + 1
    even = lax.axis_index("tile") % 2 == 0
    half = half_of(lax.axis_index("view"))
    seen_start = pl.multiple_of((2 * keep - seen) * half, 8)
    factors = spread_factors(spread, taps)
    for row, lane in chunks(rows, across):

        def rim(place):
            if place < 0:
                at = place + radius
                return jnp.where(even, far[at, row, lane], near[at, row, lane])
            at = place - planes
            return jnp.where(even, near[at, row, lane], far[at, row, lane])

        below = depth_terms(rim, factors, -radius, 0, range(planes), False)
        above = depth_terms(rim, factors, planes, planes + radius, range(planes), False)
        for plane in range(planes):
            block = part[plane, row, lane]
            for term in (below[plane], above[plane]):
                block = block if term is None else block + term
            upper, lower = split(block)
            at = slice(plane * rows + row.start, plane * rows + row.stop)
            blur_hi[at, lane] = upper
            blur_lo[at, lane] = lower
    upper, lower = wide[0, 0], wide[0, 1]
    lines = jnp.dot(blur_hi[...], upper, preferred_element_type=F32)
    lines += jnp.dot(blur_lo[...], upper, preferred_element_type=F32)
    lines += jnp.dot(blur_hi[...], lower, preferred_element_type=F32)
    forwards = []
    for plane in range(planes):
        hi, lo = split(lines[plane * rows : (plane + 1) * rows])
        forwards.append(
            jnp.dot(tall[...], jnp.concatenate([hi, lo, hi], axis=0), preferred_element_type=F32)
        )
    ratios = []
    for plane in range(planes):
        if first:
            recorded = view[0, plane, pl.ds(seen_start, seen), :]
        else:
            recorded = view[plane * seen : (plane + 1) * seen]
        ratio = recorded / forwards[plane]
        if rows > seen:
            ratio = jnp.concatenate([ratio, jnp.zeros((rows - seen, across), F32)], axis=0)
        ratios.append(split(ratio))
    turned = [
        jnp.dot(back[...], jnp.concatenate([hi, lo, hi], axis=0), preferred_element_type=F32)
        for hi, lo in ratios
    ]
    for plane in range(planes):
        hi, lo = split(turned[plane])
        plane_hi[plane * keep : (plane + 1) * keep] = hi
        plane_lo[plane * keep : (plane + 1) * keep] = lo
    upper, lower = wide[1, 0], wide[1, 1]
    lines = jnp.dot(plane_hi[...], upper, preferred_element_type=F32)
    lines += jnp.dot(plane_lo[...], upper, preferred_element_type=F32)
    lines += jnp.dot(plane_hi[...], lower, preferred_element_type=F32)
    field[...] = lines.reshape(planes, keep, across)
    for row, lane in chunks(keep, across):
        source = lambda place: field[place, row, lane]
        below = depth_terms(source, factors, 0, planes, range(-radius, 0), True)
        above = depth_terms(source, factors, 0, planes, range(planes, planes + radius), True)
        part_at, inside = divmod(row.start, keep // PARTS)
        inside = slice(inside, inside + 16)
        for at in range(radius):
            down, up = below[at - radius], above[at + planes]
            to_far, to_near = jnp.where(even, down, up), jnp.where(even, up, down)
            if not first:
                to_far += begun[2 * part_at][at, inside, lane]
                to_near += begun[2 * part_at + 1][at, inside, lane]
            sends[2 * part_at][at, inside, lane] = to_far
            sends[2 * part_at + 1][at, inside, lane] = to_near


def view_field(first, prepared, near, far, view, begun):
    keep = prepared[2].shape[0]
    planes = prepared[3].shape[0]
    radius, rows, across = near.shape

    send = jax.ShapeDtypeStruct((radius, keep // PARTS, across), F32)
    return pl.pallas_call(
        functools.partial(view_kernel, first),
        out_shape=(jax.ShapeDtypeStruct((planes, keep, across), F32),) + (send,) * (2 * PARTS),
        in_specs=[VMEM] * (8 + len(begun)),
        out_specs=(VMEM,) * (1 + 2 * PARTS),
        scratch_shapes=[
            pltpu.VMEM((planes * rows, across), BF16),
            pltpu.VMEM((planes * rows, across), BF16),
            pltpu.VMEM((planes * keep, across), BF16),
            pltpu.VMEM((planes * keep, across), BF16),
        ],
        compiler_params=pltpu.CompilerParams(vmem_limit_bytes=LIMIT),
        name="view_first" if first else "view_second",
    )(*prepared, far, near, view, *begun)


def own_kernel(taps, spread_own, spread_other, field_own, field_other, *inner):
    planes, keep, across = field_own.shape
    factors = [spread_factors(spread, taps) for spread in (spread_own, spread_other)]
    for row, lane in chunks(keep, across):
        parts = [
            depth_terms(
                lambda place: field[place, row, lane], factors[which], 0, planes, range(planes), True
            )
            for which, field in enumerate((field_own, field_other))
        ]
        part_at, inside = divmod(row.start, keep // PARTS)
        for plane in range(planes):
            inner[part_at][plane, inside : inside + 16, lane] = parts[0][plane] + parts[1][plane]


def own_planes(taps, spread_own, spread_other, field_own, field_other):
    planes, keep, across = field_own.shape
    return pl.pallas_call(
        functools.partial(own_kernel, taps),
        out_shape=(jax.ShapeDtypeStruct((planes, keep // PARTS, across), F32),) * PARTS,
        in_specs=[VMEM] * 4,
        out_specs=(VMEM,) * PARTS,
        compiler_params=pltpu.CompilerParams(vmem_limit_bytes=LIMIT),
        name="own_planes",
    )(spread_own, spread_other, field_own, field_other)


def rims_kernel(inner, far, near, *rest):
    correction = rest[-1]
    planes, radius = inner.shape[0], near.shape[0]
    even = lax.axis_index("tile") % 2 == 0
    for plane in range(planes):
        total = inner[plane]
        if plane < radius:
            total += jnp.where(even, far[plane], near[plane])
        if plane >= planes - radius:
            at = plane - planes + radius
            total += jnp.where(even, near[at], far[at])
        correction[plane] = total


def add_rims(inner, far, near, *after):
    return pl.pallas_call(
        rims_kernel,
        out_shape=jax.ShapeDtypeStruct(inner.shape, F32),
        in_specs=[VMEM] * 3 + [ANY] * len(after),
        out_specs=VMEM,
        compiler_params=pltpu.CompilerParams(vmem_limit_bytes=LIMIT),
        name="add_rims",
    )(inner, far, near, *after)


def table_rows(table):
    return jnp.concatenate([table[:8], table[8:]], axis=1)


def update_kernel(views, part, tabled, estimate, mine, other, *rest):
    planes, size, across = mine.shape
    half = half_of(lax.axis_index("view"))
    start = pl.multiple_of(size * (PARTS * half + part), 8)
    result = rest[-1]
    for plane in range(planes):
        held = estimate[plane, pl.ds(start, size)]
        at = slice(plane * size, (plane + 1) * size)
        result[at] = held * (mine[plane] + other[plane]) * (1.0 / views)
    if tabled:
        table = rest[0][...]
        result[planes * size :] = jnp.zeros((8, across), F32)
        result[planes * size :, : 2 * LANES] = jnp.concatenate([table[:8], table[8:]], axis=1)


def update(views, part, estimate, mine, other, table, after):
    planes, size, across = mine.shape
    return pl.pallas_call(
        functools.partial(update_kernel, views, part, len(table) > 0),
        out_shape=jax.ShapeDtypeStruct((planes * size + 8 * len(table), across), F32),
        in_specs=[VMEM] * (3 + len(table)) + [ANY] * len(after),
        out_specs=VMEM,
        compiler_params=pltpu.CompilerParams(vmem_limit_bytes=LIMIT),
        name="update",
    )(estimate, mine, other, *table, *after)


def slots_kernel(owner_row, index_row, picked, base):
    count = picked.shape[0]
    slots = owner_row.shape[1]
    tiles = count // ROWS
    owner = owner_row[...]
    member = (lax.broadcasted_iota(jnp.int32, (tiles, slots), 0) == owner).astype(F32)
    upto = (
        lax.broadcasted_iota(jnp.int32, (slots, slots), 0)
        <= lax.broadcasted_iota(jnp.int32, (slots, slots), 1)
    ).astype(F32)
    running = jnp.dot(member, upto, preferred_element_type=F32)
    rank = jnp.sum(member * running, axis=0, keepdims=True).astype(jnp.int32) - 1
    place = owner * ROWS + rank
    chosen = lax.broadcasted_iota(jnp.int32, (count, slots), 0) == place
    picked[...] = chosen.astype(F32)
    ids = jnp.sum(jnp.where(chosen, index_row[...].astype(F32), 0.0), axis=1, keepdims=True)
    lanes = lax.broadcasted_iota(jnp.int32, (count, LANES), 1)
    base[...] = jnp.where(lanes == IDS, ids, 0.0)


def slot_places(tiles, label_owner, label_index):
    slots = label_index.shape[1]
    return pl.pallas_call(
        slots_kernel,
        out_shape=(
            jax.ShapeDtypeStruct((tiles * ROWS, slots), F32),
            jax.ShapeDtypeStruct((tiles * ROWS, LANES), F32),
        ),
        in_specs=[VMEM, VMEM],
        out_specs=(VMEM, VMEM),
        compiler_params=pltpu.CompilerParams(vmem_limit_bytes=LIMIT),
        name="slot_places",
    )(label_owner.reshape(1, slots), label_index)


def moments_kernel(views, depth_total, part, estimate, labels, picked, base, correction, *refs):
    begun, (sent, held, sums, table) = refs[:-4], refs[-4:]
    planes, size, across = correction.shape
    height_total = estimate.shape[1]
    slots = picked.shape[1]
    half = half_of(lax.axis_index("view"))
    first = (lax.axis_index("tile") * planes).astype(F32) + 0.5
    start = pl.multiple_of(size * (PARTS * half + part), 8)
    held[...] = estimate[:, pl.ds(start, size)] * correction[...] * (1.0 / views)
    group = 16
    spot = lax.broadcasted_iota(jnp.int32, (across, LANES), 0)
    lanes = lax.broadcasted_iota(jnp.int32, (across, LANES), 1)
    low = (spot * spot) & 255
    factors = jnp.where(lanes == 0, 1, jnp.where(lanes == 1, spot, 0))
    factors = jnp.where(lanes == 2, spot * spot - low, jnp.where(lanes == 3, low, factors))
    factors = factors.astype(F32).astype(BF16)
    base_row = lax.broadcasted_iota(jnp.int32, (8, across), 0)

    def one_group(number, carry):
        for pair in range(0, group, 2):
            slot = [number * group + pair, number * group + pair + 1]
            parts = [[None] * 6 for _ in slot]
            for row in range(0, size, 8):
                high = ((base_row + (row + start)).astype(F32) + 0.5) * (1.0 / height_total)
                flat, once, twice = [[jnp.zeros((8, across), F32) for _ in slot] for _ in range(3)]
                for plane in reversed(range(planes)):
                    mark = labels[plane, pl.ds(pl.multiple_of(start + row, 8), 8)]
                    value = held[plane, row : row + 8]
                    for at in range(2):
                        flat[at] = flat[at] + jnp.where(mark == slot[at], value, 0.0)
                        if plane > 0:
                            once[at] = once[at] + flat[at]
                            twice[at] = twice[at] + once[at]
                for at in range(2):
                    square_sum = 2.0 * twice[at] - once[at]
                    line = first * flat[at]
                    deep = (line + once[at]) * (1.0 / depth_total)
                    deeper = (first * (line + 2.0 * once[at]) + square_sum) * (1.0 / depth_total**2)
                    scaled = flat[at] * high
                    terms = (flat[at], scaled, scaled * high, deep, deep * high, deeper)
                    parts[at] = [new if old is None else old + new for old, new in zip(parts[at], terms)]
            for at in range(2):
                for kind in range(6):
                    row = kind * group + pair + at
                    sums[row : row + 1, :] = jnp.sum(parts[at][kind], axis=0, keepdims=True)
        whole = sums[...]
        upper, rest = split(whole)
        rest = whole - upper.astype(F32)
        middle, lower = split(rest)
        lines = jnp.dot(
            jnp.concatenate([upper, middle, lower], axis=0), factors, preferred_element_type=F32
        )
        count = 6 * group
        lines = lines[:count] + lines[count : 2 * count] + lines[2 * count :]
        total = lines[:group]
        for kind in range(1, 6):
            total += pltpu.roll(lines[kind * group : (kind + 1) * group], 4 * kind, 1)
        rows = pl.ds(pl.multiple_of(number * group, group), group)
        target = table if part == PARTS - 1 else sent
        target[rows, :] = total + begun[0][rows, :] if begun else total
        return carry

    lax.fori_loop(0, slots // group, one_group, 0)
    if part < PARTS - 1:
        return
    sent[...] = base[...] + jnp.dot(
        picked[...], table[...], precision=lax.Precision.HIGHEST, preferred_element_type=F32
    )


def moment_rows(views, tiles, part, estimate, correction, labels, places, begun):
    planes, size, across = correction.shape
    slots = places[0].shape[1]
    count = tiles * ROWS if part == PARTS - 1 else slots
    return pl.pallas_call(
        functools.partial(moments_kernel, views, tiles * planes, part),
        out_shape=jax.ShapeDtypeStruct((count, LANES), F32),
        in_specs=[VMEM] * (5 + len(begun)),
        out_specs=VMEM,
        scratch_shapes=[
            pltpu.VMEM((planes, size, across), F32),
            pltpu.VMEM((6 * 16, across), F32),
            pltpu.VMEM((slots, LANES), F32),
        ],
        compiler_params=pltpu.CompilerParams(vmem_limit_bytes=LIMIT),
        name="moment_rows",
    )(estimate, labels, *places, correction, *begun)


def segments_kernel(across, rows, table):
    values = rows[...]
    ids = values[:, IDS : IDS + 1].astype(jnp.int32)
    spots = lax.broadcasted_iota(jnp.int32, (values.shape[0], NUC_DEV), 1)
    picked = (ids == spots).astype(F32)
    full = lax.dot_general(
        values, picked, (((0,), (0,)), ((), ())),
        precision=lax.Precision.HIGHEST, preferred_element_type=F32,
    )
    mass, high, higher, deep, deep_high, deeper = [full[4 * kind : 4 * kind + 4] for kind in range(6)]
    flat = lambda sums: sums[0:1]
    line = lambda sums: (sums[1:2] + 0.5 * sums[0:1]) * (1.0 / across)
    square = lambda sums: (sums[2:3] + sums[3:4] + sums[1:2] + 0.25 * sums[0:1]) * (1.0 / across**2)
    table[...] = jnp.concatenate(
        [
            flat(mass), flat(deep), flat(high), line(mass),
            flat(deeper), flat(higher), square(mass),
            flat(deep_high), line(deep), line(high),
            jnp.zeros((table.shape[0] - MOM, NUC_DEV), F32),
        ],
        axis=0,
    )


def segment_table(across, rows):
    return pl.pallas_call(
        functools.partial(segments_kernel, across),
        out_shape=jax.ShapeDtypeStruct((16, NUC_DEV), F32),
        in_specs=[VMEM],
        out_specs=VMEM,
        compiler_params=pltpu.CompilerParams(vmem_limit_bytes=LIMIT),
        name="segment_table",
    )(rows)


def stores(source, whole, half, part, size, sems):
    start = pl.multiple_of(size * (PARTS * half + part), 8)
    copies = [
        pltpu.make_async_copy(
            source.at[pl.ds(plane * size, size)], whole.at[plane, pl.ds(start, size)], sems.at[plane]
        )
        for plane in range(whole.shape[0])
    ]
    for copy in copies:
        copy.start()
    return copies


def token_kernel(source, token):
    token[...] = source[:8, :LANES]


def token_of(source):
    return pl.pallas_call(
        token_kernel,
        out_shape=jax.ShapeDtypeStruct((8, LANES), F32),
        in_specs=[VMEM],
        out_specs=VMEM,
        compiler_params=pltpu.CompilerParams(vmem_limit_bytes=LIMIT),
        name="token_of",
    )(source)


def begin_kernel(size, *refs):
    whole, sems = refs[-2:]
    half = half_of(lax.axis_index("view"))
    copies = []
    for part in range(PARTS):
        copies += stores(refs[part], whole, half, part, size, sems.at[part])
    for copy in copies:
        copy.wait()


def begin_result(size, shape, mine):
    return pl.pallas_call(
        functools.partial(begin_kernel, size),
        out_shape=jax.ShapeDtypeStruct(shape, F32),
        in_specs=[VMEM] * PARTS,
        out_specs=ANY,
        scratch_shapes=[pltpu.SemaphoreType.DMA((PARTS, shape[0]))],
        compiler_params=pltpu.CompilerParams(vmem_limit_bytes=LIMIT),
        name="begin_result",
    )(*mine)


def finish_kernel(scale, size, begun, *refs):
    others, (first, third, fourth, whole, moments, held, sems, sem) = refs[:PARTS], refs[PARTS:]
    planes = whole.shape[0]
    half = half_of(lax.axis_index("view"))
    copies = []
    for part in range(PARTS):
        copies += stores(others[part], whole, 1 - half, part, size, sems.at[part])
    rows = others[0][planes * size :]
    second = jnp.concatenate([rows[:, :LANES], rows[:, LANES : 2 * LANES]], axis=0)
    table = (first[...] + second) + (third[...] + fourth[...])
    lines = lax.broadcasted_iota(jnp.int32, table.shape, 0)
    result = jnp.where(lines == 0, table * scale, table / jnp.maximum(table[0:1], 1.0))
    held[...] = result[:MOM]
    last = pltpu.make_async_copy(held, moments, sem)
    last.start()
    for copy in copies:
        copy.wait()
    last.wait()


def finish(scale, size, begun, others, tables):
    return pl.pallas_call(
        functools.partial(finish_kernel, scale, size),
        out_shape=(
            jax.ShapeDtypeStruct(begun.shape, F32),
            jax.ShapeDtypeStruct((MOM, NUC_DEV), F32),
        ),
        in_specs=[ANY] + [VMEM] * (PARTS + 3),
        out_specs=(ANY, ANY),
        input_output_aliases={0: 0},
        scratch_shapes=[
            pltpu.VMEM((MOM, NUC_DEV), F32),
            pltpu.SemaphoreType.DMA((PARTS, begun.shape[0])),
            pltpu.SemaphoreType.DMA,
        ],
        compiler_params=pltpu.CompilerParams(vmem_limit_bytes=LIMIT),
        name="finish",
    )(begun, *others, *tables)


def on_device(estimate, measured, kernels, labels, label_owner, label_index):
    tiles, views = lax.axis_size("tile"), lax.axis_size("view")
    planes, height, across = estimate.shape
    taps = kernels.shape[2]
    radius = (taps - 1) // 2
    keep = height // 2
    seen = min(height, -(-(keep + radius) // 8) * 8)
    rows = min(height, -(-(keep + 2 * radius) // 16) * 16)
    near_pairs = [(i, i ^ 1) for i in range(tiles)]
    far_pairs = [(i, i + 1) for i in range(1, tiles - 1, 2)]
    far_pairs = far_pairs + [(b, a) for a, b in far_pairs]
    partner = [(i, i ^ 1) for i in range(views)]
    across_pairs = [(i, i ^ 3) for i in range(views)]

    packed = view_out(measured, kernels, seen)
    swapped = lax.ppermute(packed, "view", partner)
    to_far, to_near = rims_out(estimate, radius, rows)
    far = lax.ppermute(to_far, "tile", far_pairs)
    near = lax.ppermute(to_near, "tile", near_pairs)
    places = slot_places(tiles, label_owner, label_index)
    own = prepare(False, taps, kernels, estimate, places[1], rows, seen, keep)
    field_own, *begun = view_field(True, own, near, far, measured, ())
    others = prepare(True, taps, swapped, estimate, begun[0], rows, seen, keep)
    field_other, *sends = view_field(False, others, near, far, swapped, begun)
    rims = [
        lax.ppermute(send, "tile", pairs) for send, pairs in zip(sends, (far_pairs, near_pairs) * PARTS)
    ]
    inner = own_planes(taps, own[4], others[4], field_own, field_other)
    mine, other, sums = [], [], []
    for part in range(PARTS):
        mine.append(add_rims(inner[part], *rims[2 * part : 2 * part + 2], *sums))
        other.append(lax.ppermute(mine[part], "view", across_pairs))
        sums = [moment_rows(views, tiles, part, estimate, mine[part], labels, places, sums)]
    sent = sums[0]
    got = lax.all_to_all(sent, "tile", split_axis=0, concat_axis=0, tiled=True)
    table = segment_table(across, got)
    tables = [table] + [
        lax.ppermute(table, "view", [(i, i ^ step) for i in range(views)]) for step in (2, 3)
    ]
    size = keep // PARTS
    new_mine, new_other, token = [], [], []
    for part in range(PARTS):
        last = [table] if part == 0 else []
        new_mine.append(update(views, part, estimate, mine[part], other[part], last, token))
        new_other.append(lax.ppermute(new_mine[part], "view", partner))
        token = [token_of(new_mine[part])]
    scale = label_index.shape[1] / (planes * height * across)
    begun = begin_result(size, estimate.shape, new_mine)
    return finish(scale, size, begun, new_other, tables)


def solution(mesh):
    placed = (
        P("tile", None, None),
        P("view", "tile", None, None),
        P("view", None, None),
        P("tile", None, None),
        P("tile", None, None),
        P("tile", None),
    )
    return jax.shard_map(
        on_device,
        mesh=mesh,
        in_specs=placed,
        out_specs=(P("tile", None, None), P(None, "tile")),
        check_vma=False,
    )
```

```python
import functools

import jax
import jax.numpy as jnp
from jax import lax
from jax.experimental import pallas as pl
from jax.experimental.pallas import tpu as pltpu
from jax.sharding import PartitionSpec as P

MOM = 10
ROWS = 8
NUC_DEV = 128
LANES = 128
PARTS = 2
TAIL = 24
IDS = 24
F32 = jnp.float32
BF16 = jnp.bfloat16
ANY = pl.BlockSpec(memory_space=pl.ANY)
VMEM = pl.BlockSpec(memory_space=pltpu.VMEM)
LIMIT = 32 * 1024 * 1024


def half_of(view):
    return (view ^ (view >> 1)) & 1


def split(value):
    upper = value.astype(BF16)
    return upper, (value - upper.astype(F32)).astype(BF16)


def band(taps, shape, offset):
    rows = lax.broadcasted_iota(jnp.int32, shape, 0)
    cols = lax.broadcasted_iota(jnp.int32, shape, 1)
    place = cols - rows + offset
    result = jnp.zeros(shape, F32)
    for step, tap in enumerate(taps):
        result = jnp.where(place == step, tap, result)
    return result


def depth_terms(source, weights, first, last, planes, flipped):
    radius = (len(weights) - 1) // 2
    totals = {plane: None for plane in planes}
    for place in range(first, last):
        block = None
        for plane in planes:
            step = plane - place + radius if flipped else place - plane + radius
            if 0 <= step < len(weights):
                block = source(place) if block is None else block
                term = weights[step] * block
                totals[plane] = term if totals[plane] is None else totals[plane] + term
    return totals


def chunks(rows, across):
    return [(slice(row, row + 16), slice(lane, lane + LANES)) for row in range(0, rows, 16) for lane in range(0, across, LANES)]


def rims_out_kernel(estimate, to_far, to_near):
    planes, radius, rows = estimate.shape[0], to_far.shape[0], to_far.shape[1]
    odd = lax.axis_index("tile") % 2
    half = half_of(lax.axis_index("view"))
    start = pl.multiple_of((estimate.shape[1] - rows) * half, 8)
    to_far[...] = estimate[pl.ds(odd, radius), pl.ds(start, rows)]
    to_near[...] = estimate[pl.ds(1 - odd, radius), pl.ds(start, rows)]


def rims_out(estimate, radius, rows):
    shape = jax.ShapeDtypeStruct((radius, rows, estimate.shape[2]), F32)
    return pl.pallas_call(
        rims_out_kernel,
        out_shape=(shape, shape),
        in_specs=[VMEM],
        out_specs=(VMEM, VMEM),
        compiler_params=pltpu.CompilerParams(vmem_limit_bytes=LIMIT),
        name="rims_out",
    )(estimate)


def view_out_kernel(seen, measured, kernels, packed):
    planes, height = measured.shape[1], measured.shape[2]
    half = half_of(lax.axis_index("view"))
    start = pl.multiple_of((height - seen) * (1 - half), 8)
    for plane in range(planes):
        packed[plane * seen : (plane + 1) * seen] = measured[0, plane, pl.ds(start, seen)]
    packed[planes * seen :] = jnp.zeros((TAIL, packed.shape[1]), F32)
    packed[planes * seen : planes * seen + kernels.shape[1], : kernels.shape[2]] = kernels[0]


def view_out(measured, kernels, seen):
    _, planes, _, across = measured.shape
    return pl.pallas_call(
        functools.partial(view_out_kernel, seen),
        out_shape=jax.ShapeDtypeStruct((planes * seen + TAIL, across), F32),
        in_specs=[VMEM, VMEM],
        out_specs=VMEM,
        compiler_params=pltpu.CompilerParams(vmem_limit_bytes=LIMIT),
        name="view_out",
    )(measured, kernels)


def prepare_kernel(packed, taps, source, estimate, after, wide, tall, back, part, spread):
    half = half_of(lax.axis_index("view"))
    across = wide.shape[-1]
    rows, keep, seen = part.shape[1], back.shape[0], tall.shape[0]
    planes = estimate.shape[0]
    radius = (taps - 1) // 2
    at = source.shape[0] - TAIL
    raw = source[at : at + 3, :taps] if packed else source[0]
    weights = raw / jnp.sum(raw, axis=-1, keepdims=True)
    deep, high, flat = [[weights[axis : axis + 1, t : t + 1] for t in range(taps)] for axis in range(3)]
    start = pl.multiple_of((2 * keep - rows) * half, 16)
    seen_start = (2 * keep - seen) * half
    near_diagonal = jnp.abs(
        lax.broadcasted_iota(jnp.int32, (across, across), 1)
        - lax.broadcasted_iota(jnp.int32, (across, across), 0)
    ) <= radius
    for turn, line in enumerate((flat[::-1], flat)):
        first_row = jnp.concatenate(
            line[radius:] + [jnp.zeros((1, across - taps), F32)] + line[:radius], axis=1
        )
        square = pltpu.roll(
            jnp.broadcast_to(first_row, (across, across)), 0, 1, stride=1, stride_axis=0
        )
        upper, lower = split(jnp.where(near_diagonal, square, 0.0))
        wide[turn, 0] = upper
        wide[turn, 1] = lower
    upper, lower = split(band(high, (seen, rows), radius + start - seen_start))
    tall[...] = jnp.concatenate([upper, upper, lower], axis=1)
    upper, lower = split(band(high[::-1], (keep, rows), radius + seen_start - keep * half))
    back[...] = jnp.concatenate([upper, upper, lower], axis=1)
    factors = [jnp.broadcast_to(tap, (16, LANES)) for tap in deep]
    spread[...] = jnp.zeros_like(spread)
    for step in range(taps):
        spread[step : step + 1] = factors[step][:1]
    for row, lane in chunks(rows, across):
        where = pl.ds(pl.multiple_of(start + row.start, 16), 16)
        terms = depth_terms(
            lambda place: estimate[place, where, lane], factors, 0, planes, range(planes), False
        )
        for plane, block in terms.items():
            part[plane, row, lane] = block


def prepare(packed, taps, source, estimate, after, rows, seen, keep):
    planes, _, across = estimate.shape
    return pl.pallas_call(
        functools.partial(prepare_kernel, packed, taps),
        out_shape=(
            jax.ShapeDtypeStruct((2, 2, across, across), BF16),
            jax.ShapeDtypeStruct((seen, 3 * rows), BF16),
            jax.ShapeDtypeStruct((keep, 3 * rows), BF16),
            jax.ShapeDtypeStruct((planes, rows, across), F32),
            jax.ShapeDtypeStruct((-(-taps // 8) * 8, LANES), F32),
        ),
        in_specs=[VMEM, VMEM, ANY],
        out_specs=(VMEM,) * 5,
        compiler_params=pltpu.CompilerParams(vmem_limit_bytes=LIMIT),
        name="prepare",
    )(source, estimate, after)


def spread_factors(spread, taps):
    return [jnp.broadcast_to(spread[step : step + 1, :], (16, LANES)) for step in range(taps)]


def fields_kernel(*refs):
    sets, (far, near, measured, swapped), refs = (refs[:5], refs[5:10]), refs[10:14], refs[14:]
    fields, sends, (blur_hi, blur_lo, plane_hi, plane_lo) = refs[:2], refs[2:-4], refs[-4:]
    planes = sets[0][3].shape[0]
    radius, rows, across = near.shape
    keep, seen = sets[0][2].shape[0], sets[0][1].shape[0]
    taps = 2 * radius + 1
    even = lax.axis_index("tile") % 2 == 0
    half = half_of(lax.axis_index("view"))
    seen_start = pl.multiple_of((2 * keep - seen) * half, 8)
    factors = [spread_factors(spread, taps) for _, _, _, _, spread in sets]
    for which, (_, _, _, part, _) in enumerate(sets):
        for row, lane in chunks(rows, across):

            def rim(place):
                if place < 0:
                    at = place + radius
                    return jnp.where(even, far[at, row, lane], near[at, row, lane])
                at = place - planes
                return jnp.where(even, near[at, row, lane], far[at, row, lane])

            below = depth_terms(rim, factors[which], -radius, 0, range(planes), False)
            above = depth_terms(rim, factors[which], planes, planes + radius, range(planes), False)
            for plane in range(planes):
                block = part[plane, row, lane]
                for term in (below[plane], above[plane]):
                    block = block if term is None else block + term
                upper, lower = split(block)
                at = slice(plane * rows + row.start, plane * rows + row.stop)
                blur_hi[which, at, lane] = upper
                blur_lo[which, at, lane] = lower
    lines = []
    for which, (wide, _, _, _, _) in enumerate(sets):
        upper, lower = wide[0, 0], wide[0, 1]
        lines.append(
            jnp.dot(blur_hi[which], upper, preferred_element_type=F32)
            + jnp.dot(blur_lo[which], upper, preferred_element_type=F32)
            + jnp.dot(blur_hi[which], lower, preferred_element_type=F32)
        )
    both = [(which, plane) for which in range(2) for plane in range(planes)]
    forwards = {}
    for which, plane in both:
        hi, lo = split(lines[which][plane * rows : (plane + 1) * rows])
        forwards[which, plane] = jnp.dot(
            sets[which][1][...], jnp.concatenate([hi, lo, hi], axis=0), preferred_element_type=F32
        )
    ratios = {}
    for which, plane in both:
        if which == 0:
            recorded = measured[0, plane, pl.ds(seen_start, seen), :]
        else:
            recorded = swapped[plane * seen : (plane + 1) * seen]
        ratio = recorded / forwards[which, plane]
        if rows > seen:
            ratio = jnp.concatenate([ratio, jnp.zeros((rows - seen, across), F32)], axis=0)
        ratios[which, plane] = split(ratio)
    turned = {}
    for which, plane in both:
        hi, lo = ratios[which, plane]
        turned[which, plane] = jnp.dot(
            sets[which][2][...], jnp.concatenate([hi, lo, hi], axis=0), preferred_element_type=F32
        )
    for which, plane in both:
        hi, lo = split(turned[which, plane])
        plane_hi[which, plane * keep : (plane + 1) * keep] = hi
        plane_lo[which, plane * keep : (plane + 1) * keep] = lo
    for which, (wide, _, _, _, _) in enumerate(sets):
        upper, lower = wide[1, 0], wide[1, 1]
        result = (
            jnp.dot(plane_hi[which], upper, preferred_element_type=F32)
            + jnp.dot(plane_lo[which], upper, preferred_element_type=F32)
            + jnp.dot(plane_hi[which], lower, preferred_element_type=F32)
        )
        fields[which][...] = result.reshape(planes, keep, across)
    for row, lane in chunks(keep, across):
        below, above = [], []
        for which in range(2):
            source = lambda place: fields[which][place, row, lane]
            outer = range(planes, planes + radius)
            below.append(depth_terms(source, factors[which], 0, planes, range(-radius, 0), True))
            above.append(depth_terms(source, factors[which], 0, planes, outer, True))
        part_at, inside = divmod(row.start, keep // PARTS)
        inside = slice(inside, inside + 16)
        for at in range(radius):
            down = below[0][at - radius] + below[1][at - radius]
            up = above[0][at + planes] + above[1][at + planes]
            sends[2 * part_at][at, inside, lane] = jnp.where(even, down, up)
            sends[2 * part_at + 1][at, inside, lane] = jnp.where(even, up, down)


def ratio_fields(own, others, far, near, measured, swapped):
    keep, planes = own[2].shape[0], own[3].shape[0]
    radius, rows, across = near.shape
    field = jax.ShapeDtypeStruct((planes, keep, across), F32)
    send = jax.ShapeDtypeStruct((radius, keep // PARTS, across), F32)
    return pl.pallas_call(
        fields_kernel,
        out_shape=(field,) * 2 + (send,) * (2 * PARTS),
        in_specs=[VMEM] * 14,
        out_specs=(VMEM,) * (2 + 2 * PARTS),
        scratch_shapes=[
            pltpu.VMEM((2, planes * rows, across), BF16),
            pltpu.VMEM((2, planes * rows, across), BF16),
            pltpu.VMEM((2, planes * keep, across), BF16),
            pltpu.VMEM((2, planes * keep, across), BF16),
        ],
        compiler_params=pltpu.CompilerParams(vmem_limit_bytes=LIMIT),
        name="ratio_fields",
    )(*own, *others, far, near, measured, swapped)


def own_kernel(taps, spread_own, spread_other, field_own, field_other, *inner):
    planes, keep, across = field_own.shape
    factors = [spread_factors(spread, taps) for spread in (spread_own, spread_other)]
    for row, lane in chunks(keep, across):
        parts = [
            depth_terms(
                lambda place: field[place, row, lane], factors[which], 0, planes, range(planes), True
            )
            for which, field in enumerate((field_own, field_other))
        ]
        part_at, inside = divmod(row.start, keep // PARTS)
        for plane in range(planes):
            inner[part_at][plane, inside : inside + 16, lane] = parts[0][plane] + parts[1][plane]


def own_planes(taps, spread_own, spread_other, field_own, field_other):
    planes, keep, across = field_own.shape
    return pl.pallas_call(
        functools.partial(own_kernel, taps),
        out_shape=(jax.ShapeDtypeStruct((planes, keep // PARTS, across), F32),) * PARTS,
        in_specs=[VMEM] * 4,
        out_specs=(VMEM,) * PARTS,
        compiler_params=pltpu.CompilerParams(vmem_limit_bytes=LIMIT),
        name="own_planes",
    )(spread_own, spread_other, field_own, field_other)


def rims_kernel(inner, far, near, *rest):
    correction = rest[-1]
    planes, radius = inner.shape[0], near.shape[0]
    even = lax.axis_index("tile") % 2 == 0
    for plane in range(planes):
        total = inner[plane]
        if plane < radius:
            total += jnp.where(even, far[plane], near[plane])
        if plane >= planes - radius:
            at = plane - planes + radius
            total += jnp.where(even, near[at], far[at])
        correction[plane] = total


def add_rims(inner, far, near, *after):
    return pl.pallas_call(
        rims_kernel,
        out_shape=jax.ShapeDtypeStruct(inner.shape, F32),
        in_specs=[VMEM] * 3 + [ANY] * len(after),
        out_specs=VMEM,
        compiler_params=pltpu.CompilerParams(vmem_limit_bytes=LIMIT),
        name="add_rims",
    )(inner, far, near, *after)


def table_rows(table):
    return jnp.concatenate([table[:8], table[8:]], axis=1)


def update_kernel(views, part, tabled, estimate, mine, other, *rest):
    planes, size, across = mine.shape
    half = half_of(lax.axis_index("view"))
    start = pl.multiple_of(size * (PARTS * half + part), 8)
    result = rest[-1]
    for plane in range(planes):
        held = estimate[plane, pl.ds(start, size)]
        at = slice(plane * size, (plane + 1) * size)
        result[at] = held * (mine[plane] + other[plane]) * (1.0 / views)
    if tabled:
        table = rest[0][...]
        result[planes * size :] = jnp.zeros((8, across), F32)
        result[planes * size :, : 2 * LANES] = jnp.concatenate([table[:8], table[8:]], axis=1)


def update(views, part, estimate, mine, other, table, after):
    planes, size, across = mine.shape
    return pl.pallas_call(
        functools.partial(update_kernel, views, part, len(table) > 0),
        out_shape=jax.ShapeDtypeStruct((planes * size + 8 * len(table), across), F32),
        in_specs=[VMEM] * (3 + len(table)) + [ANY] * len(after),
        out_specs=VMEM,
        compiler_params=pltpu.CompilerParams(vmem_limit_bytes=LIMIT),
        name="update",
    )(estimate, mine, other, *table, *after)


def slots_kernel(owner_row, index_row, picked, base):
    count = picked.shape[0]
    slots = owner_row.shape[1]
    tiles = count // ROWS
    owner = owner_row[...]
    member = (lax.broadcasted_iota(jnp.int32, (tiles, slots), 0) == owner).astype(F32)
    upto = (
        lax.broadcasted_iota(jnp.int32, (slots, slots), 0)
        <= lax.broadcasted_iota(jnp.int32, (slots, slots), 1)
    ).astype(F32)
    running = jnp.dot(member, upto, preferred_element_type=F32)
    rank = jnp.sum(member * running, axis=0, keepdims=True).astype(jnp.int32) - 1
    place = owner * ROWS + rank
    chosen = lax.broadcasted_iota(jnp.int32, (count, slots), 0) == place
    picked[...] = chosen.astype(F32)
    ids = jnp.sum(jnp.where(chosen, index_row[...].astype(F32), 0.0), axis=1, keepdims=True)
    lanes = lax.broadcasted_iota(jnp.int32, (count, LANES), 1)
    base[...] = jnp.where(lanes == IDS, ids, 0.0)


def slot_places(tiles, label_owner, label_index):
    slots = label_index.shape[1]
    return pl.pallas_call(
        slots_kernel,
        out_shape=(
            jax.ShapeDtypeStruct((tiles * ROWS, slots), F32),
            jax.ShapeDtypeStruct((tiles * ROWS, LANES), F32),
        ),
        in_specs=[VMEM, VMEM],
        out_specs=(VMEM, VMEM),
        compiler_params=pltpu.CompilerParams(vmem_limit_bytes=LIMIT),
        name="slot_places",
    )(label_owner.reshape(1, slots), label_index)


def moments_kernel(views, depth_total, part, estimate, labels, picked, base, correction, *refs):
    begun, (sent, held, sums, table) = refs[:-4], refs[-4:]
    planes, size, across = correction.shape
    height_total = estimate.shape[1]
    slots = picked.shape[1]
    half = half_of(lax.axis_index("view"))
    first = (lax.axis_index("tile") * planes).astype(F32) + 0.5
    start = pl.multiple_of(size * (PARTS * half + part), 8)
    held[...] = estimate[:, pl.ds(start, size)] * correction[...] * (1.0 / views)
    group = 16
    spot = lax.broadcasted_iota(jnp.int32, (across, LANES), 0)
    lanes = lax.broadcasted_iota(jnp.int32, (across, LANES), 1)
    low = (spot * spot) & 255
    factors = jnp.where(lanes == 0, 1, jnp.where(lanes == 1, spot, 0))
    factors = jnp.where(lanes == 2, spot * spot - low, jnp.where(lanes == 3, low, factors))
    factors = factors.astype(F32).astype(BF16)
    base_row = lax.broadcasted_iota(jnp.int32, (8, across), 0)

    def one_group(number, carry):
        for pair in range(0, group, 2):
            slot = [number * group + pair, number * group + pair + 1]
            parts = [[None] * 6 for _ in slot]
            for row in range(0, size, 8):
                high = ((base_row + (row + start)).astype(F32) + 0.5) * (1.0 / height_total)
                flat, once, twice = [[jnp.zeros((8, across), F32) for _ in slot] for _ in range(3)]
                for plane in reversed(range(planes)):
                    mark = labels[plane, pl.ds(pl.multiple_of(start + row, 8), 8)]
                    value = held[plane, row : row + 8]
                    for at in range(2):
                        flat[at] = flat[at] + jnp.where(mark == slot[at], value, 0.0)
                        if plane > 0:
                            once[at] = once[at] + flat[at]
                            twice[at] = twice[at] + once[at]
                for at in range(2):
                    square_sum = 2.0 * twice[at] - once[at]
                    line = first * flat[at]
                    deep = (line + once[at]) * (1.0 / depth_total)
                    deeper = (first * (line + 2.0 * once[at]) + square_sum) * (1.0 / depth_total**2)
                    scaled = flat[at] * high
                    terms = (flat[at], scaled, scaled * high, deep, deep * high, deeper)
                    parts[at] = [new if old is None else old + new for old, new in zip(parts[at], terms)]
            for at in range(2):
                for kind in range(6):
                    row = kind * group + pair + at
                    sums[row : row + 1, :] = jnp.sum(parts[at][kind], axis=0, keepdims=True)
        whole = sums[...]
        upper, rest = split(whole)
        rest = whole - upper.astype(F32)
        middle, lower = split(rest)
        lines = jnp.dot(
            jnp.concatenate([upper, middle, lower], axis=0), factors, preferred_element_type=F32
        )
        count = 6 * group
        lines = lines[:count] + lines[count : 2 * count] + lines[2 * count :]
        total = lines[:group]
        for kind in range(1, 6):
            total += pltpu.roll(lines[kind * group : (kind + 1) * group], 4 * kind, 1)
        rows = pl.ds(pl.multiple_of(number * group, group), group)
        target = table if part == PARTS - 1 else sent
        target[rows, :] = total + begun[0][rows, :] if begun else total
        return carry

    lax.fori_loop(0, slots // group, one_group, 0)
    if part < PARTS - 1:
        return
    sent[...] = base[...] + jnp.dot(
        picked[...], table[...], precision=lax.Precision.HIGHEST, preferred_element_type=F32
    )


def moment_rows(views, tiles, part, estimate, correction, labels, places, begun):
    planes, size, across = correction.shape
    slots = places[0].shape[1]
    count = tiles * ROWS if part == PARTS - 1 else slots
    return pl.pallas_call(
        functools.partial(moments_kernel, views, tiles * planes, part),
        out_shape=jax.ShapeDtypeStruct((count, LANES), F32),
        in_specs=[VMEM] * (5 + len(begun)),
        out_specs=VMEM,
        scratch_shapes=[
            pltpu.VMEM((planes, size, across), F32),
            pltpu.VMEM((6 * 16, across), F32),
            pltpu.VMEM((slots, LANES), F32),
        ],
        compiler_params=pltpu.CompilerParams(vmem_limit_bytes=LIMIT),
        name="moment_rows",
    )(estimate, labels, *places, correction, *begun)


def segments_kernel(across, rows, table):
    values = rows[...]
    ids = values[:, IDS : IDS + 1].astype(jnp.int32)
    spots = lax.broadcasted_iota(jnp.int32, (values.shape[0], NUC_DEV), 1)
    picked = (ids == spots).astype(F32)
    full = lax.dot_general(
        values, picked, (((0,), (0,)), ((), ())),
        precision=lax.Precision.HIGHEST, preferred_element_type=F32,
    )
    mass, high, higher, deep, deep_high, deeper = [full[4 * kind : 4 * kind + 4] for kind in range(6)]
    flat = lambda sums: sums[0:1]
    line = lambda sums: (sums[1:2] + 0.5 * sums[0:1]) * (1.0 / across)
    square = lambda sums: (sums[2:3] + sums[3:4] + sums[1:2] + 0.25 * sums[0:1]) * (1.0 / across**2)
    table[...] = jnp.concatenate(
        [
            flat(mass), flat(deep), flat(high), line(mass),
            flat(deeper), flat(higher), square(mass),
            flat(deep_high), line(deep), line(high),
            jnp.zeros((table.shape[0] - MOM, NUC_DEV), F32),
        ],
        axis=0,
    )


def segment_table(across, rows):
    return pl.pallas_call(
        functools.partial(segments_kernel, across),
        out_shape=jax.ShapeDtypeStruct((16, NUC_DEV), F32),
        in_specs=[VMEM],
        out_specs=VMEM,
        compiler_params=pltpu.CompilerParams(vmem_limit_bytes=LIMIT),
        name="segment_table",
    )(rows)


def stores(source, whole, half, part, size, sems):
    start = pl.multiple_of(size * (PARTS * half + part), 8)
    copies = [
        pltpu.make_async_copy(
            source.at[pl.ds(plane * size, size)], whole.at[plane, pl.ds(start, size)], sems.at[plane]
        )
        for plane in range(whole.shape[0])
    ]
    for copy in copies:
        copy.start()
    return copies


def token_kernel(source, token):
    token[...] = source[:8, :LANES]


def token_of(source):
    return pl.pallas_call(
        token_kernel,
        out_shape=jax.ShapeDtypeStruct((8, LANES), F32),
        in_specs=[VMEM],
        out_specs=VMEM,
        compiler_params=pltpu.CompilerParams(vmem_limit_bytes=LIMIT),
        name="token_of",
    )(source)


def begin_kernel(size, *refs):
    whole, sems = refs[-2:]
    half = half_of(lax.axis_index("view"))
    copies = []
    for part in range(PARTS):
        copies += stores(refs[part], whole, half, part, size, sems.at[part])
    for copy in copies:
        copy.wait()


def begin_result(size, shape, mine):
    return pl.pallas_call(
        functools.partial(begin_kernel, size),
        out_shape=jax.ShapeDtypeStruct(shape, F32),
        in_specs=[VMEM] * PARTS,
        out_specs=ANY,
        scratch_shapes=[pltpu.SemaphoreType.DMA((PARTS, shape[0]))],
        compiler_params=pltpu.CompilerParams(vmem_limit_bytes=LIMIT),
        name="begin_result",
    )(*mine)


def finish_kernel(scale, size, begun, *refs):
    others, (first, third, fourth, whole, moments, held, sems, sem) = refs[:PARTS], refs[PARTS:]
    planes = whole.shape[0]
    half = half_of(lax.axis_index("view"))
    copies = []
    for part in range(PARTS):
        copies += stores(others[part], whole, 1 - half, part, size, sems.at[part])
    rows = others[0][planes * size :]
    second = jnp.concatenate([rows[:, :LANES], rows[:, LANES : 2 * LANES]], axis=0)
    table = (first[...] + second) + (third[...] + fourth[...])
    lines = lax.broadcasted_iota(jnp.int32, table.shape, 0)
    result = jnp.where(lines == 0, table * scale, table / jnp.maximum(table[0:1], 1.0))
    held[...] = result[:MOM]
    last = pltpu.make_async_copy(held, moments, sem)
    last.start()
    for copy in copies:
        copy.wait()
    last.wait()


def finish(scale, size, begun, others, tables):
    return pl.pallas_call(
        functools.partial(finish_kernel, scale, size),
        out_shape=(
            jax.ShapeDtypeStruct(begun.shape, F32),
            jax.ShapeDtypeStruct((MOM, NUC_DEV), F32),
        ),
        in_specs=[ANY] + [VMEM] * (PARTS + 3),
        out_specs=(ANY, ANY),
        input_output_aliases={0: 0},
        scratch_shapes=[
            pltpu.VMEM((MOM, NUC_DEV), F32),
            pltpu.SemaphoreType.DMA((PARTS, begun.shape[0])),
            pltpu.SemaphoreType.DMA,
        ],
        compiler_params=pltpu.CompilerParams(vmem_limit_bytes=LIMIT),
        name="finish",
    )(begun, *others, *tables)


def on_device(estimate, measured, kernels, labels, label_owner, label_index):
    tiles, views = lax.axis_size("tile"), lax.axis_size("view")
    planes, height, across = estimate.shape
    taps = kernels.shape[2]
    radius = (taps - 1) // 2
    keep = height // 2
    seen = min(height, -(-(keep + radius) // 8) * 8)
    rows = min(height, -(-(keep + 2 * radius) // 16) * 16)
    near_pairs = [(i, i ^ 1) for i in range(tiles)]
    far_pairs = [(i, i + 1) for i in range(1, tiles - 1, 2)]
    far_pairs = far_pairs + [(b, a) for a, b in far_pairs]
    partner = [(i, i ^ 1) for i in range(views)]
    across_pairs = [(i, i ^ 3) for i in range(views)]

    packed = view_out(measured, kernels, seen)
    swapped = lax.ppermute(packed, "view", partner)
    to_far, to_near = rims_out(estimate, radius, rows)
    far = lax.ppermute(to_far, "tile", far_pairs)
    near = lax.ppermute(to_near, "tile", near_pairs)
    places = slot_places(tiles, label_owner, label_index)
    own = prepare(False, taps, kernels, estimate, places[1], rows, seen, keep)
    others = prepare(True, taps, swapped, estimate, kernels, rows, seen, keep)
    field_own, field_other, *sends = ratio_fields(own, others, far, near, measured, swapped)
    rims = [
        lax.ppermute(send, "tile", pairs) for send, pairs in zip(sends, (far_pairs, near_pairs) * PARTS)
    ]
    inner = own_planes(taps, own[4], others[4], field_own, field_other)
    mine, other, sums = [], [], []
    for part in range(PARTS):
        mine.append(add_rims(inner[part], *rims[2 * part : 2 * part + 2], *sums))
        other.append(lax.ppermute(mine[part], "view", across_pairs))
        sums = [moment_rows(views, tiles, part, estimate, mine[part], labels, places, sums)]
    sent = sums[0]
    got = lax.all_to_all(sent, "tile", split_axis=0, concat_axis=0, tiled=True)
    table = segment_table(across, got)
    tables = [table] + [
        lax.ppermute(table, "view", [(i, i ^ step) for i in range(views)]) for step in (2, 3)
    ]
    size = keep // PARTS
    new_mine, new_other, token = [], [], []
    for part in range(PARTS):
        last = [table] if part == 0 else []
        new_mine.append(update(views, part, estimate, mine[part], other[part], last, token))
        new_other.append(lax.ppermute(new_mine[part], "view", partner))
        token = [token_of(new_mine[part])]
    scale = label_index.shape[1] / (planes * height * across)
    begun = begin_result(size, estimate.shape, new_mine)
    return finish(scale, size, begun, new_other, tables)


def solution(mesh):
    placed = (
        P("tile", None, None),
        P("view", "tile", None, None),
        P("view", None, None),
        P("tile", None, None),
        P("tile", None, None),
        P("tile", None),
    )
    return jax.shard_map(
        on_device,
        mesh=mesh,
        in_specs=placed,
        out_specs=(P("tile", None, None), P(None, "tile")),
        check_vma=False,
    )
```

```python
import functools

import jax
import jax.numpy as jnp
from jax import lax
from jax.experimental import pallas as pl
from jax.experimental.pallas import tpu as pltpu
from jax.sharding import PartitionSpec as P

MOM = 10
ROWS = 8
NUC_DEV = 128
LANES = 128
PARTS = 2
TAIL = 24
IDS = 24
F32 = jnp.float32
BF16 = jnp.bfloat16
ANY = pl.BlockSpec(memory_space=pl.ANY)
VMEM = pl.BlockSpec(memory_space=pltpu.VMEM)
LIMIT = 32 * 1024 * 1024


def half_of(view):
    return (view ^ (view >> 1)) & 1


def split(value):
    upper = value.astype(BF16)
    return upper, (value - upper.astype(F32)).astype(BF16)


def band(taps, shape, offset):
    rows = lax.broadcasted_iota(jnp.int32, shape, 0)
    cols = lax.broadcasted_iota(jnp.int32, shape, 1)
    place = cols - rows + offset
    result = jnp.zeros(shape, F32)
    for step, tap in enumerate(taps):
        result = jnp.where(place == step, tap, result)
    return result


def depth_terms(source, weights, first, last, planes, flipped):
    radius = (len(weights) - 1) // 2
    totals = {plane: None for plane in planes}
    for place in range(first, last):
        block = None
        for plane in planes:
            step = plane - place + radius if flipped else place - plane + radius
            if 0 <= step < len(weights):
                block = source(place) if block is None else block
                term = weights[step] * block
                totals[plane] = term if totals[plane] is None else totals[plane] + term
    return totals


def chunks(rows, across):
    return [(slice(row, row + 16), slice(lane, lane + LANES)) for row in range(0, rows, 16) for lane in range(0, across, LANES)]


def rims_out_kernel(estimate, to_far, to_near):
    planes, radius, rows = estimate.shape[0], to_far.shape[0], to_far.shape[1]
    odd = lax.axis_index("tile") % 2
    half = half_of(lax.axis_index("view"))
    start = pl.multiple_of((estimate.shape[1] - rows) * half, 8)
    to_far[...] = estimate[pl.ds(odd, radius), pl.ds(start, rows)]
    to_near[...] = estimate[pl.ds(1 - odd, radius), pl.ds(start, rows)]


def rims_out(estimate, radius, rows):
    shape = jax.ShapeDtypeStruct((radius, rows, estimate.shape[2]), F32)
    return pl.pallas_call(
        rims_out_kernel,
        out_shape=(shape, shape),
        in_specs=[VMEM],
        out_specs=(VMEM, VMEM),
        compiler_params=pltpu.CompilerParams(vmem_limit_bytes=LIMIT),
        name="rims_out",
    )(estimate)


def view_out_kernel(seen, measured, taps, packed):
    planes, height = measured.shape[1], measured.shape[2]
    half = half_of(lax.axis_index("view"))
    start = pl.multiple_of((height - seen) * (1 - half), 8)
    for plane in range(planes):
        packed[plane * seen : (plane + 1) * seen] = measured[0, plane, pl.ds(start, seen)]
    packed[planes * seen :] = jnp.zeros((TAIL, packed.shape[1]), F32)
    for axis in range(taps.shape[0]):
        at = planes * seen + axis
        packed[at : at + 1, : taps.shape[2]] = taps[axis]


def view_out(measured, kernels, seen):
    _, planes, _, across = measured.shape
    return pl.pallas_call(
        functools.partial(view_out_kernel, seen),
        out_shape=jax.ShapeDtypeStruct((planes * seen + TAIL, across), F32),
        in_specs=[VMEM, VMEM],
        out_specs=VMEM,
        compiler_params=pltpu.CompilerParams(vmem_limit_bytes=LIMIT),
        name="view_out",
    )(measured, kernels)


def prepare_kernel(packed, taps, source, estimate, after, wide, tall, back, part, spread):
    half = half_of(lax.axis_index("view"))
    across = wide.shape[-1]
    rows, keep, seen = part.shape[1], back.shape[0], tall.shape[0]
    planes = estimate.shape[0]
    radius = (taps - 1) // 2
    at = source.shape[0] - TAIL
    if packed:
        raw = source[at : at + 3, :taps]
    else:
        raw = jnp.concatenate([source[axis] for axis in range(source.shape[0])], axis=0)
    weights = raw / jnp.sum(raw, axis=-1, keepdims=True)
    deep, high, flat = [[weights[axis : axis + 1, t : t + 1] for t in range(taps)] for axis in range(3)]
    start = pl.multiple_of((2 * keep - rows) * half, 16)
    seen_start = (2 * keep - seen) * half
    near_diagonal = jnp.abs(
        lax.broadcasted_iota(jnp.int32, (across, across), 1)
        - lax.broadcasted_iota(jnp.int32, (across, across), 0)
    ) <= radius
    for turn, line in enumerate((flat[::-1], flat)):
        first_row = jnp.concatenate(
            line[radius:] + [jnp.zeros((1, across - taps), F32)] + line[:radius], axis=1
        )
        square = pltpu.roll(
            jnp.broadcast_to(first_row, (across, across)), 0, 1, stride=1, stride_axis=0
        )
        upper, lower = split(jnp.where(near_diagonal, square, 0.0))
        wide[turn, 0] = upper
        wide[turn, 1] = lower
    upper, lower = split(band(high, (seen, rows), radius + start - seen_start))
    tall[...] = jnp.concatenate([upper, upper, lower], axis=1)
    upper, lower = split(band(high[::-1], (keep, rows), radius + seen_start - keep * half))
    back[...] = jnp.concatenate([upper, upper, lower], axis=1)
    factors = [jnp.broadcast_to(tap, (16, LANES)) for tap in deep]
    spread[...] = jnp.zeros_like(spread)
    for step in range(taps):
        spread[step : step + 1] = factors[step][:1]
    for row, lane in chunks(rows, across):
        where = pl.ds(pl.multiple_of(start + row.start, 16), 16)
        terms = depth_terms(
            lambda place: estimate[place, where, lane], factors, 0, planes, range(planes), False
        )
        for plane, block in terms.items():
            part[plane, row, lane] = block


def prepare(packed, taps, source, estimate, after, rows, seen, keep):
    planes, _, across = estimate.shape
    return pl.pallas_call(
        functools.partial(prepare_kernel, packed, taps),
        out_shape=(
            jax.ShapeDtypeStruct((2, 2, across, across), BF16),
            jax.ShapeDtypeStruct((seen, 3 * rows), BF16),
            jax.ShapeDtypeStruct((keep, 3 * rows), BF16),
            jax.ShapeDtypeStruct((planes, rows, across), F32),
            jax.ShapeDtypeStruct((-(-taps // 8) * 8, LANES), F32),
        ),
        in_specs=[VMEM, VMEM, ANY],
        out_specs=(VMEM,) * 5,
        compiler_params=pltpu.CompilerParams(vmem_limit_bytes=LIMIT),
        name="prepare",
    )(source, estimate, after)


def spread_factors(spread, taps):
    return [jnp.broadcast_to(spread[step : step + 1, :], (16, LANES)) for step in range(taps)]


def fields_kernel(*refs):
    sets, (far, near, measured, swapped), refs = (refs[:5], refs[5:10]), refs[10:14], refs[14:]
    fields, sends, (blur_hi, blur_lo, plane_hi, plane_lo) = refs[:2], refs[2:-4], refs[-4:]
    planes = sets[0][3].shape[0]
    radius, rows, across = near.shape
    keep, seen = sets[0][2].shape[0], sets[0][1].shape[0]
    taps = 2 * radius + 1
    even = lax.axis_index("tile") % 2 == 0
    half = half_of(lax.axis_index("view"))
    seen_start = pl.multiple_of((2 * keep - seen) * half, 8)
    factors = [spread_factors(spread, taps) for _, _, _, _, spread in sets]
    for which, (_, _, _, part, _) in enumerate(sets):
        for row, lane in chunks(rows, across):

            def rim(place):
                if place < 0:
                    at = place + radius
                    return jnp.where(even, far[at, row, lane], near[at, row, lane])
                at = place - planes
                return jnp.where(even, near[at, row, lane], far[at, row, lane])

            below = depth_terms(rim, factors[which], -radius, 0, range(planes), False)
            above = depth_terms(rim, factors[which], planes, planes + radius, range(planes), False)
            for plane in range(planes):
                block = part[plane, row, lane]
                for term in (below[plane], above[plane]):
                    block = block if term is None else block + term
                upper, lower = split(block)
                at = slice(plane * rows + row.start, plane * rows + row.stop)
                blur_hi[which, at, lane] = upper
                blur_lo[which, at, lane] = lower
    lines = []
    for which, (wide, _, _, _, _) in enumerate(sets):
        upper, lower = wide[0, 0], wide[0, 1]
        lines.append(
            jnp.dot(blur_hi[which], upper, preferred_element_type=F32)
            + jnp.dot(blur_lo[which], upper, preferred_element_type=F32)
            + jnp.dot(blur_hi[which], lower, preferred_element_type=F32)
        )
    both = [(which, plane) for which in range(2) for plane in range(planes)]
    forwards = {}
    for which, plane in both:
        hi, lo = split(lines[which][plane * rows : (plane + 1) * rows])
        forwards[which, plane] = jnp.dot(
            sets[which][1][...], jnp.concatenate([hi, lo, hi], axis=0), preferred_element_type=F32
        )
    ratios = {}
    for which, plane in both:
        if which == 0:
            recorded = measured[0, plane, pl.ds(seen_start, seen), :]
        else:
            recorded = swapped[plane * seen : (plane + 1) * seen]
        ratio = recorded / forwards[which, plane]
        if rows > seen:
            ratio = jnp.concatenate([ratio, jnp.zeros((rows - seen, across), F32)], axis=0)
        ratios[which, plane] = split(ratio)
    turned = {}
    for which, plane in both:
        hi, lo = ratios[which, plane]
        turned[which, plane] = jnp.dot(
            sets[which][2][...], jnp.concatenate([hi, lo, hi], axis=0), preferred_element_type=F32
        )
    for which, plane in both:
        hi, lo = split(turned[which, plane])
        plane_hi[which, plane * keep : (plane + 1) * keep] = hi
        plane_lo[which, plane * keep : (plane + 1) * keep] = lo
    for which, (wide, _, _, _, _) in enumerate(sets):
        upper, lower = wide[1, 0], wide[1, 1]
        result = (
            jnp.dot(plane_hi[which], upper, preferred_element_type=F32)
            + jnp.dot(plane_lo[which], upper, preferred_element_type=F32)
            + jnp.dot(plane_hi[which], lower, preferred_element_type=F32)
        )
        fields[which][...] = result.reshape(planes, keep, across)
    for row, lane in chunks(keep, across):
        below, above = [], []
        for which in range(2):
            source = lambda place: fields[which][place, row, lane]
            outer = range(planes, planes + radius)
            below.append(depth_terms(source, factors[which], 0, planes, range(-radius, 0), True))
            above.append(depth_terms(source, factors[which], 0, planes, outer, True))
        part_at, inside = divmod(row.start, keep // PARTS)
        inside = slice(inside, inside + 16)
        for at in range(radius):
            down = below[0][at - radius] + below[1][at - radius]
            up = above[0][at + planes] + above[1][at + planes]
            sends[2 * part_at][at, inside, lane] = jnp.where(even, down, up)
            sends[2 * part_at + 1][at, inside, lane] = jnp.where(even, up, down)


def ratio_fields(own, others, far, near, measured, swapped):
    keep, planes = own[2].shape[0], own[3].shape[0]
    radius, rows, across = near.shape
    field = jax.ShapeDtypeStruct((planes, keep, across), F32)
    send = jax.ShapeDtypeStruct((radius, keep // PARTS, across), F32)
    return pl.pallas_call(
        fields_kernel,
        out_shape=(field,) * 2 + (send,) * (2 * PARTS),
        in_specs=[VMEM] * 14,
        out_specs=(VMEM,) * (2 + 2 * PARTS),
        scratch_shapes=[
            pltpu.VMEM((2, planes * rows, across), BF16),
            pltpu.VMEM((2, planes * rows, across), BF16),
            pltpu.VMEM((2, planes * keep, across), BF16),
            pltpu.VMEM((2, planes * keep, across), BF16),
        ],
        compiler_params=pltpu.CompilerParams(vmem_limit_bytes=LIMIT),
        name="ratio_fields",
    )(*own, *others, far, near, measured, swapped)


def own_kernel(taps, spread_own, spread_other, field_own, field_other, *inner):
    planes, keep, across = field_own.shape
    factors = [spread_factors(spread, taps) for spread in (spread_own, spread_other)]
    for row, lane in chunks(keep, across):
        parts = [
            depth_terms(
                lambda place: field[place, row, lane], factors[which], 0, planes, range(planes), True
            )
            for which, field in enumerate((field_own, field_other))
        ]
        part_at, inside = divmod(row.start, keep // PARTS)
        for plane in range(planes):
            inner[part_at][plane, inside : inside + 16, lane] = parts[0][plane] + parts[1][plane]


def own_planes(taps, spread_own, spread_other, field_own, field_other):
    planes, keep, across = field_own.shape
    return pl.pallas_call(
        functools.partial(own_kernel, taps),
        out_shape=(jax.ShapeDtypeStruct((planes, keep // PARTS, across), F32),) * PARTS,
        in_specs=[VMEM] * 4,
        out_specs=(VMEM,) * PARTS,
        compiler_params=pltpu.CompilerParams(vmem_limit_bytes=LIMIT),
        name="own_planes",
    )(spread_own, spread_other, field_own, field_other)


def rims_kernel(inner, far, near, *rest):
    correction = rest[-1]
    planes, radius = inner.shape[0], near.shape[0]
    even = lax.axis_index("tile") % 2 == 0
    for plane in range(planes):
        total = inner[plane]
        if plane < radius:
            total += jnp.where(even, far[plane], near[plane])
        if plane >= planes - radius:
            at = plane - planes + radius
            total += jnp.where(even, near[at], far[at])
        correction[plane] = total


def add_rims(inner, far, near, *after):
    return pl.pallas_call(
        rims_kernel,
        out_shape=jax.ShapeDtypeStruct(inner.shape, F32),
        in_specs=[VMEM] * 3 + [ANY] * len(after),
        out_specs=VMEM,
        compiler_params=pltpu.CompilerParams(vmem_limit_bytes=LIMIT),
        name="add_rims",
    )(inner, far, near, *after)


def table_rows(table):
    return jnp.concatenate([table[:8], table[8:]], axis=1)


def update_kernel(views, part, tabled, estimate, mine, other, *rest):
    planes, size, across = mine.shape
    half = half_of(lax.axis_index("view"))
    start = pl.multiple_of(size * (PARTS * half + part), 8)
    result = rest[-1]
    for plane in range(planes):
        held = estimate[plane, pl.ds(start, size)]
        at = slice(plane * size, (plane + 1) * size)
        result[at] = held * (mine[plane] + other[plane]) * (1.0 / views)
    rows = result.shape[0] - planes * size
    result[planes * size :] = jnp.zeros((rows, across), F32)
    if tabled:
        table = rest[0][...]
        result[planes * size :, : 2 * LANES] = jnp.concatenate([table[:8], table[8:]], axis=1)


def update(views, part, estimate, mine, other, table, after):
    planes, size, across = mine.shape
    return pl.pallas_call(
        functools.partial(update_kernel, views, part, len(table) > 0),
        out_shape=jax.ShapeDtypeStruct((planes * size + 8 * (PARTS - part), across), F32),
        in_specs=[VMEM] * (3 + len(table)) + [ANY] * len(after),
        out_specs=VMEM,
        compiler_params=pltpu.CompilerParams(vmem_limit_bytes=LIMIT),
        name="update",
    )(estimate, mine, other, *table, *after)


def slots_kernel(owner_row, index_row, picked, base):
    count = picked.shape[0]
    slots = owner_row.shape[1]
    tiles = count // ROWS
    owner = owner_row[...]
    member = (lax.broadcasted_iota(jnp.int32, (tiles, slots), 0) == owner).astype(F32)
    upto = (
        lax.broadcasted_iota(jnp.int32, (slots, slots), 0)
        <= lax.broadcasted_iota(jnp.int32, (slots, slots), 1)
    ).astype(F32)
    running = jnp.dot(member, upto, preferred_element_type=F32)
    rank = jnp.sum(member * running, axis=0, keepdims=True).astype(jnp.int32) - 1
    place = owner * ROWS + rank
    chosen = lax.broadcasted_iota(jnp.int32, (count, slots), 0) == place
    picked[...] = chosen.astype(F32)
    ids = jnp.sum(jnp.where(chosen, index_row[...].astype(F32), 0.0), axis=1, keepdims=True)
    lanes = lax.broadcasted_iota(jnp.int32, (count, LANES), 1)
    base[...] = jnp.where(lanes == IDS, ids, 0.0)


def slot_places(tiles, label_owner, label_index):
    slots = label_index.shape[1]
    return pl.pallas_call(
        slots_kernel,
        out_shape=(
            jax.ShapeDtypeStruct((tiles * ROWS, slots), F32),
            jax.ShapeDtypeStruct((tiles * ROWS, LANES), F32),
        ),
        in_specs=[VMEM, VMEM],
        out_specs=(VMEM, VMEM),
        compiler_params=pltpu.CompilerParams(vmem_limit_bytes=LIMIT),
        name="slot_places",
    )(label_owner.reshape(1, slots), label_index)


def moments_kernel(views, depth_total, part, estimate, labels, picked, base, correction, *refs):
    begun, (sent, held, sums, table) = refs[:-4], refs[-4:]
    planes, size, across = correction.shape
    height_total = estimate.shape[1]
    slots = picked.shape[1]
    half = half_of(lax.axis_index("view"))
    first = (lax.axis_index("tile") * planes).astype(F32) + 0.5
    start = pl.multiple_of(size * (PARTS * half + part), 8)
    held[...] = estimate[:, pl.ds(start, size)] * correction[...] * (1.0 / views)
    group = 16
    spot = lax.broadcasted_iota(jnp.int32, (across, LANES), 0)
    lanes = lax.broadcasted_iota(jnp.int32, (across, LANES), 1)
    low = (spot * spot) & 255
    factors = jnp.where(lanes == 0, 1, jnp.where(lanes == 1, spot, 0))
    factors = jnp.where(lanes == 2, spot * spot - low, jnp.where(lanes == 3, low, factors))
    factors = factors.astype(F32).astype(BF16)
    base_row = lax.broadcasted_iota(jnp.int32, (8, across), 0)

    def one_group(number, carry):
        for pair in range(0, group, 2):
            slot = [number * group + pair, number * group + pair + 1]
            parts = [[None] * 6 for _ in slot]
            for row in range(0, size, 8):
                high = ((base_row + (row + start)).astype(F32) + 0.5) * (1.0 / height_total)
                flat, once, twice = [[jnp.zeros((8, across), F32) for _ in slot] for _ in range(3)]
                for plane in reversed(range(planes)):
                    mark = labels[plane, pl.ds(pl.multiple_of(start + row, 8), 8)]
                    value = held[plane, row : row + 8]
                    for at in range(2):
                        flat[at] = flat[at] + jnp.where(mark == slot[at], value, 0.0)
                        if plane > 0:
                            once[at] = once[at] + flat[at]
                            twice[at] = twice[at] + once[at]
                for at in range(2):
                    square_sum = 2.0 * twice[at] - once[at]
                    line = first * flat[at]
                    deep = (line + once[at]) * (1.0 / depth_total)
                    deeper = (first * (line + 2.0 * once[at]) + square_sum) * (1.0 / depth_total**2)
                    scaled = flat[at] * high
                    terms = (flat[at], scaled, scaled * high, deep, deep * high, deeper)
                    parts[at] = [new if old is None else old + new for old, new in zip(parts[at], terms)]
            for at in range(2):
                for kind in range(6):
                    row = kind * group + pair + at
                    sums[row : row + 1, :] = jnp.sum(parts[at][kind], axis=0, keepdims=True)
        whole = sums[...]
        upper, rest = split(whole)
        rest = whole - upper.astype(F32)
        middle, lower = split(rest)
        lines = jnp.dot(
            jnp.concatenate([upper, middle, lower], axis=0), factors, preferred_element_type=F32
        )
        count = 6 * group
        lines = lines[:count] + lines[count : 2 * count] + lines[2 * count :]
        total = lines[:group]
        for kind in range(1, 6):
            total += pltpu.roll(lines[kind * group : (kind + 1) * group], 4 * kind, 1)
        rows = pl.ds(pl.multiple_of(number * group, group), group)
        target = table if part == PARTS - 1 else sent
        target[rows, :] = total + begun[0][rows, :] if begun else total
        return carry

    lax.fori_loop(0, slots // group, one_group, 0)
    if part < PARTS - 1:
        return
    sent[...] = base[...] + jnp.dot(
        picked[...], table[...], precision=lax.Precision.HIGHEST, preferred_element_type=F32
    )


def moment_rows(views, tiles, part, estimate, correction, labels, places, begun):
    planes, size, across = correction.shape
    slots = places[0].shape[1]
    count = tiles * ROWS if part == PARTS - 1 else slots
    return pl.pallas_call(
        functools.partial(moments_kernel, views, tiles * planes, part),
        out_shape=jax.ShapeDtypeStruct((count, LANES), F32),
        in_specs=[VMEM] * (5 + len(begun)),
        out_specs=VMEM,
        scratch_shapes=[
            pltpu.VMEM((planes, size, across), F32),
            pltpu.VMEM((6 * 16, across), F32),
            pltpu.VMEM((slots, LANES), F32),
        ],
        compiler_params=pltpu.CompilerParams(vmem_limit_bytes=LIMIT),
        name="moment_rows",
    )(estimate, labels, *places, correction, *begun)


def segments_kernel(across, rows, table):
    values = rows[...]
    ids = values[:, IDS : IDS + 1].astype(jnp.int32)
    spots = lax.broadcasted_iota(jnp.int32, (values.shape[0], NUC_DEV), 1)
    picked = (ids == spots).astype(F32)
    full = lax.dot_general(
        values, picked, (((0,), (0,)), ((), ())),
        precision=lax.Precision.HIGHEST, preferred_element_type=F32,
    )
    mass, high, higher, deep, deep_high, deeper = [full[4 * kind : 4 * kind + 4] for kind in range(6)]
    flat = lambda sums: sums[0:1]
    line = lambda sums: (sums[1:2] + 0.5 * sums[0:1]) * (1.0 / across)
    square = lambda sums: (sums[2:3] + sums[3:4] + sums[1:2] + 0.25 * sums[0:1]) * (1.0 / across**2)
    table[...] = jnp.concatenate(
        [
            flat(mass), flat(deep), flat(high), line(mass),
            flat(deeper), flat(higher), square(mass),
            flat(deep_high), line(deep), line(high),
            jnp.zeros((table.shape[0] - MOM, NUC_DEV), F32),
        ],
        axis=0,
    )


def segment_table(across, rows):
    return pl.pallas_call(
        functools.partial(segments_kernel, across),
        out_shape=jax.ShapeDtypeStruct((16, NUC_DEV), F32),
        in_specs=[VMEM],
        out_specs=VMEM,
        compiler_params=pltpu.CompilerParams(vmem_limit_bytes=LIMIT),
        name="segment_table",
    )(rows)


def stores(source, whole, half, part, size, sems):
    start = pl.multiple_of(size * (PARTS * half + part), 8)
    copies = [
        pltpu.make_async_copy(
            source.at[pl.ds(plane * size, size)], whole.at[plane, pl.ds(start, size)], sems.at[plane]
        )
        for plane in range(whole.shape[0])
    ]
    for copy in copies:
        copy.start()
    return copies


def token_kernel(source, token):
    token[...] = source[:8, :LANES]


def token_of(source):
    return pl.pallas_call(
        token_kernel,
        out_shape=jax.ShapeDtypeStruct((8, LANES), F32),
        in_specs=[VMEM],
        out_specs=VMEM,
        compiler_params=pltpu.CompilerParams(vmem_limit_bytes=LIMIT),
        name="token_of",
    )(source)


def begin_kernel(size, *refs):
    whole, sems = refs[-2:]
    half = half_of(lax.axis_index("view"))
    copies = []
    for part in range(PARTS):
        copies += stores(refs[part], whole, half, part, size, sems.at[part])
    for copy in copies:
        copy.wait()


def begin_result(size, shape, mine):
    return pl.pallas_call(
        functools.partial(begin_kernel, size),
        out_shape=jax.ShapeDtypeStruct(shape, F32),
        in_specs=[VMEM] * PARTS,
        out_specs=ANY,
        scratch_shapes=[pltpu.SemaphoreType.DMA((PARTS, shape[0]))],
        compiler_params=pltpu.CompilerParams(vmem_limit_bytes=LIMIT),
        name="begin_result",
    )(*mine)


def finish_kernel(scale, size, begun, *refs):
    others, (first, third, fourth, whole, moments, held, sems, sem) = refs[:PARTS], refs[PARTS:]
    planes = whole.shape[0]
    half = half_of(lax.axis_index("view"))
    copies = []
    for part in range(PARTS):
        copies += stores(others[part], whole, 1 - half, part, size, sems.at[part])
    rows = others[-1][planes * size :]
    second = jnp.concatenate([rows[:, :LANES], rows[:, LANES : 2 * LANES]], axis=0)
    table = (first[...] + second) + (third[...] + fourth[...])
    lines = lax.broadcasted_iota(jnp.int32, table.shape, 0)
    result = jnp.where(lines == 0, table * scale, table / jnp.maximum(table[0:1], 1.0))
    held[...] = result[:MOM]
    last = pltpu.make_async_copy(held, moments, sem)
    last.start()
    for copy in copies:
        copy.wait()
    last.wait()


def finish(scale, size, begun, others, tables):
    return pl.pallas_call(
        functools.partial(finish_kernel, scale, size),
        out_shape=(
            jax.ShapeDtypeStruct(begun.shape, F32),
            jax.ShapeDtypeStruct((MOM, NUC_DEV), F32),
        ),
        in_specs=[ANY] + [VMEM] * (PARTS + 3),
        out_specs=(ANY, ANY),
        input_output_aliases={0: 0},
        scratch_shapes=[
            pltpu.VMEM((MOM, NUC_DEV), F32),
            pltpu.SemaphoreType.DMA((PARTS, begun.shape[0])),
            pltpu.SemaphoreType.DMA,
        ],
        compiler_params=pltpu.CompilerParams(vmem_limit_bytes=LIMIT),
        name="finish",
    )(begun, *others, *tables)


def on_device(estimate, measured, kernels, labels, label_owner, label_index):
    tiles, views = lax.axis_size("tile"), lax.axis_size("view")
    planes, height, across = estimate.shape
    taps = kernels.shape[2]
    radius = (taps - 1) // 2
    keep = height // 2
    seen = min(height, -(-(keep + radius) // 8) * 8)
    rows = min(height, -(-(keep + 2 * radius) // 16) * 16)
    near_pairs = [(i, i ^ 1) for i in range(tiles)]
    far_pairs = [(i, i + 1) for i in range(1, tiles - 1, 2)]
    far_pairs = far_pairs + [(b, a) for a, b in far_pairs]
    partner = [(i, i ^ 1) for i in range(views)]
    across_pairs = [(i, i ^ 3) for i in range(views)]

    lines = jnp.transpose(kernels, (1, 0, 2))
    packed = view_out(measured, lines, seen)
    swapped = lax.ppermute(packed, "view", partner)
    to_far, to_near = rims_out(estimate, radius, rows)
    far = lax.ppermute(to_far, "tile", far_pairs)
    near = lax.ppermute(to_near, "tile", near_pairs)
    places = slot_places(tiles, label_owner, label_index)
    own = prepare(False, taps, lines, estimate, places[1], rows, seen, keep)
    others = prepare(True, taps, swapped, estimate, lines, rows, seen, keep)
    field_own, field_other, *sends = ratio_fields(own, others, far, near, measured, swapped)
    rims = [
        lax.ppermute(send, "tile", pairs) for send, pairs in zip(sends, (far_pairs, near_pairs) * PARTS)
    ]
    inner = own_planes(taps, own[4], others[4], field_own, field_other)
    mine, other, sums = [], [], []
    for part in range(PARTS):
        mine.append(add_rims(inner[part], *rims[2 * part : 2 * part + 2], *sums))
        other.append(lax.ppermute(mine[part], "view", across_pairs))
        sums = [moment_rows(views, tiles, part, estimate, mine[part], labels, places, sums)]
    sent = sums[0]
    got = lax.all_to_all(sent, "tile", split_axis=0, concat_axis=0, tiled=True)
    table = segment_table(across, got)
    tables = [table] + [
        lax.ppermute(table, "view", [(i, i ^ step) for i in range(views)]) for step in (2, 3)
    ]
    size = keep // PARTS
    new_mine, new_other, token = [], [], []
    for part in range(PARTS):
        last = [table] if part == PARTS - 1 else []
        new_mine.append(update(views, part, estimate, mine[part], other[part], last, token))
        new_other.append(lax.ppermute(new_mine[part], "view", partner))
        token = [token_of(new_mine[part])]
    scale = label_index.shape[1] / (planes * height * across)
    begun = begin_result(size, estimate.shape, new_mine)
    return finish(scale, size, begun, new_other, tables)


def solution(mesh):
    placed = (
        P("tile", None, None),
        P("view", "tile", None, None),
        P("view", None, None),
        P("tile", None, None),
        P("tile", None, None),
        P("tile", None),
    )
    return jax.shard_map(
        on_device,
        mesh=mesh,
        in_specs=placed,
        out_specs=(P("tile", None, None), P(None, "tile")),
        check_vma=False,
    )
```

```python
import functools

import jax
import jax.numpy as jnp
from jax import lax
from jax.experimental import pallas as pl
from jax.experimental.pallas import tpu as pltpu
from jax.sharding import PartitionSpec as P

MOM = 10
ROWS = 8
NUC_DEV = 128
LANES = 128
PARTS = 2
TAIL = 8
IDS = 24
F32 = jnp.float32
BF16 = jnp.bfloat16
ANY = pl.BlockSpec(memory_space=pl.ANY)
VMEM = pl.BlockSpec(memory_space=pltpu.VMEM)
LIMIT = 32 * 1024 * 1024


def half_of(view):
    return (view ^ (view >> 1)) & 1


def split(value):
    upper = value.astype(BF16)
    return upper, (value - upper.astype(F32)).astype(BF16)


def band(taps, shape, offset):
    rows = lax.broadcasted_iota(jnp.int32, shape, 0)
    cols = lax.broadcasted_iota(jnp.int32, shape, 1)
    place = cols - rows + offset
    result = jnp.zeros(shape, F32)
    for step, tap in enumerate(taps):
        result = jnp.where(place == step, tap, result)
    return result


def depth_terms(source, weights, first, last, planes, flipped):
    radius = (len(weights) - 1) // 2
    totals = {plane: None for plane in planes}
    for place in range(first, last):
        block = None
        for plane in planes:
            step = plane - place + radius if flipped else place - plane + radius
            if 0 <= step < len(weights):
                block = source(place) if block is None else block
                term = weights[step] * block
                totals[plane] = term if totals[plane] is None else totals[plane] + term
    return totals


def chunks(rows, across):
    return [(slice(row, row + 16), slice(lane, lane + LANES)) for row in range(0, rows, 16) for lane in range(0, across, LANES)]


def rims_out_kernel(estimate, to_far, to_near):
    planes, radius, rows = estimate.shape[0], to_far.shape[0], to_far.shape[1]
    odd = lax.axis_index("tile") % 2
    half = half_of(lax.axis_index("view"))
    start = pl.multiple_of((estimate.shape[1] - rows) * half, 8)
    to_far[...] = estimate[pl.ds(odd, radius), pl.ds(start, rows)]
    to_near[...] = estimate[pl.ds(1 - odd, radius), pl.ds(start, rows)]


def rims_out(estimate, radius, rows):
    shape = jax.ShapeDtypeStruct((radius, rows, estimate.shape[2]), F32)
    return pl.pallas_call(
        rims_out_kernel,
        out_shape=(shape, shape),
        in_specs=[VMEM],
        out_specs=(VMEM, VMEM),
        compiler_params=pltpu.CompilerParams(vmem_limit_bytes=LIMIT),
        name="rims_out",
    )(estimate)


def view_out_kernel(seen, measured, taps, packed):
    planes, height = measured.shape[1], measured.shape[2]
    half = half_of(lax.axis_index("view"))
    start = pl.multiple_of((height - seen) * (1 - half), 8)
    for plane in range(planes):
        packed[plane * seen : (plane + 1) * seen] = measured[0, plane, pl.ds(start, seen)]
    packed[planes * seen :] = jnp.zeros((TAIL, packed.shape[1]), F32)
    for axis in range(taps.shape[0]):
        at = planes * seen + axis
        packed[at : at + 1, : taps.shape[2]] = taps[axis]


def view_out(measured, kernels, seen):
    _, planes, _, across = measured.shape
    return pl.pallas_call(
        functools.partial(view_out_kernel, seen),
        out_shape=jax.ShapeDtypeStruct((planes * seen + TAIL, across), F32),
        in_specs=[VMEM, VMEM],
        out_specs=VMEM,
        compiler_params=pltpu.CompilerParams(vmem_limit_bytes=LIMIT),
        name="view_out",
    )(measured, kernels)


def prepare_kernel(packed, taps, source, estimate, after, wide, tall, back, part, spread):
    half = half_of(lax.axis_index("view"))
    across = wide.shape[-1]
    rows, keep, seen = part.shape[1], back.shape[0], tall.shape[0]
    planes = estimate.shape[0]
    radius = (taps - 1) // 2
    at = source.shape[0] - TAIL
    if packed:
        raw = source[at : at + 3, :taps]
    else:
        raw = jnp.concatenate([source[axis] for axis in range(source.shape[0])], axis=0)
    weights = raw / jnp.sum(raw, axis=-1, keepdims=True)
    deep, high, flat = [[weights[axis : axis + 1, t : t + 1] for t in range(taps)] for axis in range(3)]
    start = pl.multiple_of((2 * keep - rows) * half, 16)
    seen_start = (2 * keep - seen) * half
    near_diagonal = jnp.abs(
        lax.broadcasted_iota(jnp.int32, (across, across), 1)
        - lax.broadcasted_iota(jnp.int32, (across, across), 0)
    ) <= radius
    for turn, line in enumerate((flat[::-1], flat)):
        first_row = jnp.concatenate(
            line[radius:] + [jnp.zeros((1, across - taps), F32)] + line[:radius], axis=1
        )
        square = pltpu.roll(
            jnp.broadcast_to(first_row, (across, across)), 0, 1, stride=1, stride_axis=0
        )
        upper, lower = split(jnp.where(near_diagonal, square, 0.0))
        wide[turn, 0] = upper
        wide[turn, 1] = lower
    upper, lower = split(band(high, (seen, rows), radius + start - seen_start))
    tall[...] = jnp.concatenate([upper, upper, lower], axis=1)
    upper, lower = split(band(high[::-1], (keep, rows), radius + seen_start - keep * half))
    back[...] = jnp.concatenate([upper, upper, lower], axis=1)
    factors = [jnp.broadcast_to(tap, (16, LANES)) for tap in deep]
    spread[...] = jnp.zeros_like(spread)
    for step in range(taps):
        spread[step : step + 1] = factors[step][:1]
    for row, lane in chunks(rows, across):
        where = pl.ds(pl.multiple_of(start + row.start, 16), 16)
        terms = depth_terms(
            lambda place: estimate[place, where, lane], factors, 0, planes, range(planes), False
        )
        for plane, block in terms.items():
            part[plane, row, lane] = block


def prepare(packed, taps, source, estimate, after, rows, seen, keep):
    planes, _, across = estimate.shape
    return pl.pallas_call(
        functools.partial(prepare_kernel, packed, taps),
        out_shape=(
            jax.ShapeDtypeStruct((2, 2, across, across), BF16),
            jax.ShapeDtypeStruct((seen, 3 * rows), BF16),
            jax.ShapeDtypeStruct((keep, 3 * rows), BF16),
            jax.ShapeDtypeStruct((planes, rows, across), F32),
            jax.ShapeDtypeStruct((-(-taps // 8) * 8, LANES), F32),
        ),
        in_specs=[VMEM, VMEM, ANY],
        out_specs=(VMEM,) * 5,
        compiler_params=pltpu.CompilerParams(vmem_limit_bytes=LIMIT),
        name="prepare",
    )(source, estimate, after)


def spread_factors(spread, taps):
    return [jnp.broadcast_to(spread[step : step + 1, :], (16, LANES)) for step in range(taps)]


def fields_kernel(*refs):
    sets, (far, near, measured, swapped), refs = (refs[:5], refs[5:10]), refs[10:14], refs[14:]
    fields, sends, (blur_hi, blur_lo, plane_hi, plane_lo) = refs[:2], refs[2:-4], refs[-4:]
    planes = sets[0][3].shape[0]
    radius, rows, across = near.shape
    keep, seen = sets[0][2].shape[0], sets[0][1].shape[0]
    taps = 2 * radius + 1
    even = lax.axis_index("tile") % 2 == 0
    half = half_of(lax.axis_index("view"))
    seen_start = pl.multiple_of((2 * keep - seen) * half, 8)
    factors = [spread_factors(spread, taps) for _, _, _, _, spread in sets]
    for which, (_, _, _, part, _) in enumerate(sets):
        for row, lane in chunks(rows, across):

            def rim(place):
                if place < 0:
                    at = place + radius
                    return jnp.where(even, far[at, row, lane], near[at, row, lane])
                at = place - planes
                return jnp.where(even, near[at, row, lane], far[at, row, lane])

            below = depth_terms(rim, factors[which], -radius, 0, range(planes), False)
            above = depth_terms(rim, factors[which], planes, planes + radius, range(planes), False)
            for plane in range(planes):
                block = part[plane, row, lane]
                for term in (below[plane], above[plane]):
                    block = block if term is None else block + term
                upper, lower = split(block)
                at = slice(plane * rows + row.start, plane * rows + row.stop)
                blur_hi[which, at, lane] = upper
                blur_lo[which, at, lane] = lower
    lines = []
    for which, (wide, _, _, _, _) in enumerate(sets):
        upper, lower = wide[0, 0], wide[0, 1]
        lines.append(
            jnp.dot(blur_hi[which], upper, preferred_element_type=F32)
            + jnp.dot(blur_lo[which], upper, preferred_element_type=F32)
            + jnp.dot(blur_hi[which], lower, preferred_element_type=F32)
        )
    both = [(which, plane) for which in range(2) for plane in range(planes)]
    forwards = {}
    for which, plane in both:
        hi, lo = split(lines[which][plane * rows : (plane + 1) * rows])
        forwards[which, plane] = jnp.dot(
            sets[which][1][...], jnp.concatenate([hi, lo, hi], axis=0), preferred_element_type=F32
        )
    ratios = {}
    for which, plane in both:
        if which == 0:
            recorded = measured[0, plane, pl.ds(seen_start, seen), :]
        else:
            recorded = swapped[plane * seen : (plane + 1) * seen]
        ratio = recorded / forwards[which, plane]
        if rows > seen:
            ratio = jnp.concatenate([ratio, jnp.zeros((rows - seen, across), F32)], axis=0)
        ratios[which, plane] = split(ratio)
    turned = {}
    for which, plane in both:
        hi, lo = ratios[which, plane]
        turned[which, plane] = jnp.dot(
            sets[which][2][...], jnp.concatenate([hi, lo, hi], axis=0), preferred_element_type=F32
        )
    for which, plane in both:
        hi, lo = split(turned[which, plane])
        plane_hi[which, plane * keep : (plane + 1) * keep] = hi
        plane_lo[which, plane * keep : (plane + 1) * keep] = lo
    for which, (wide, _, _, _, _) in enumerate(sets):
        upper, lower = wide[1, 0], wide[1, 1]
        result = (
            jnp.dot(plane_hi[which], upper, preferred_element_type=F32)
            + jnp.dot(plane_lo[which], upper, preferred_element_type=F32)
            + jnp.dot(plane_hi[which], lower, preferred_element_type=F32)
        )
        fields[which][...] = result.reshape(planes, keep, across)
    for row, lane in chunks(keep, across):
        below, above = [], []
        for which in range(2):
            source = lambda place: fields[which][place, row, lane]
            outer = range(planes, planes + radius)
            below.append(depth_terms(source, factors[which], 0, planes, range(-radius, 0), True))
            above.append(depth_terms(source, factors[which], 0, planes, outer, True))
        part_at, inside = divmod(row.start, keep // PARTS)
        inside = slice(inside, inside + 16)
        for at in range(radius):
            down = below[0][at - radius] + below[1][at - radius]
            up = above[0][at + planes] + above[1][at + planes]
            sends[2 * part_at][at, inside, lane] = jnp.where(even, down, up)
            sends[2 * part_at + 1][at, inside, lane] = jnp.where(even, up, down)


def ratio_fields(own, others, far, near, measured, swapped):
    keep, planes = own[2].shape[0], own[3].shape[0]
    radius, rows, across = near.shape
    field = jax.ShapeDtypeStruct((planes, keep, across), F32)
    send = jax.ShapeDtypeStruct((radius, keep // PARTS, across), F32)
    return pl.pallas_call(
        fields_kernel,
        out_shape=(field,) * 2 + (send,) * (2 * PARTS),
        in_specs=[VMEM] * 14,
        out_specs=(VMEM,) * (2 + 2 * PARTS),
        scratch_shapes=[
            pltpu.VMEM((2, planes * rows, across), BF16),
            pltpu.VMEM((2, planes * rows, across), BF16),
            pltpu.VMEM((2, planes * keep, across), BF16),
            pltpu.VMEM((2, planes * keep, across), BF16),
        ],
        compiler_params=pltpu.CompilerParams(vmem_limit_bytes=LIMIT),
        name="ratio_fields",
    )(*own, *others, far, near, measured, swapped)


def own_kernel(taps, spread_own, spread_other, field_own, field_other, *inner):
    planes, keep, across = field_own.shape
    factors = [spread_factors(spread, taps) for spread in (spread_own, spread_other)]
    for row, lane in chunks(keep, across):
        parts = [
            depth_terms(
                lambda place: field[place, row, lane], factors[which], 0, planes, range(planes), True
            )
            for which, field in enumerate((field_own, field_other))
        ]
        part_at, inside = divmod(row.start, keep // PARTS)
        for plane in range(planes):
            inner[part_at][plane, inside : inside + 16, lane] = parts[0][plane] + parts[1][plane]


def own_planes(taps, spread_own, spread_other, field_own, field_other):
    planes, keep, across = field_own.shape
    return pl.pallas_call(
        functools.partial(own_kernel, taps),
        out_shape=(jax.ShapeDtypeStruct((planes, keep // PARTS, across), F32),) * PARTS,
        in_specs=[VMEM] * 4,
        out_specs=(VMEM,) * PARTS,
        compiler_params=pltpu.CompilerParams(vmem_limit_bytes=LIMIT),
        name="own_planes",
    )(spread_own, spread_other, field_own, field_other)


def rims_kernel(inner, far, near, *rest):
    correction = rest[-1]
    planes, radius = inner.shape[0], near.shape[0]
    even = lax.axis_index("tile") % 2 == 0
    for plane in range(planes):
        total = inner[plane]
        if plane < radius:
            total += jnp.where(even, far[plane], near[plane])
        if plane >= planes - radius:
            at = plane - planes + radius
            total += jnp.where(even, near[at], far[at])
        correction[plane] = total


def add_rims(inner, far, near, *after):
    return pl.pallas_call(
        rims_kernel,
        out_shape=jax.ShapeDtypeStruct(inner.shape, F32),
        in_specs=[VMEM] * 3 + [ANY] * len(after),
        out_specs=VMEM,
        compiler_params=pltpu.CompilerParams(vmem_limit_bytes=LIMIT),
        name="add_rims",
    )(inner, far, near, *after)


def table_rows(table):
    return jnp.concatenate([table[:8], table[8:]], axis=1)


def update_kernel(views, keep, part, low, tabled, estimate, mine, other, *rest):
    planes, whole, across = mine.shape
    result = rest[-1]
    size = low[1] - low[0]
    half = half_of(lax.axis_index("view"))
    start = pl.multiple_of(keep * half + whole * part + low[0], 8)
    for plane in range(planes):
        held = estimate[plane, pl.ds(start, size)]
        at = slice(plane * size, (plane + 1) * size)
        rows = slice(low[0], low[1])
        result[at] = held * (mine[plane, rows] + other[plane, rows]) * (1.0 / views)
    result[planes * size :] = jnp.zeros((result.shape[0] - planes * size, across), F32)
    if tabled:
        table = rest[0][...]
        result[planes * size :, : 2 * LANES] = jnp.concatenate([table[:8], table[8:]], axis=1)


def update(views, keep, part, low, spare, estimate, mine, other, table, after):
    planes, _, across = mine.shape
    return pl.pallas_call(
        functools.partial(update_kernel, views, keep, part, low, len(table) > 0),
        out_shape=jax.ShapeDtypeStruct((planes * (low[1] - low[0]) + spare, across), F32),
        in_specs=[VMEM] * (3 + len(table)) + [ANY] * len(after),
        out_specs=VMEM,
        compiler_params=pltpu.CompilerParams(vmem_limit_bytes=LIMIT),
        name="update",
    )(estimate, mine, other, *table, *after)


def slots_kernel(owner_row, index_row, picked, base):
    count = picked.shape[0]
    slots = owner_row.shape[1]
    tiles = count // ROWS
    owner = owner_row[...]
    member = (lax.broadcasted_iota(jnp.int32, (tiles, slots), 0) == owner).astype(F32)
    upto = (
        lax.broadcasted_iota(jnp.int32, (slots, slots), 0)
        <= lax.broadcasted_iota(jnp.int32, (slots, slots), 1)
    ).astype(F32)
    running = jnp.dot(member, upto, preferred_element_type=F32)
    rank = jnp.sum(member * running, axis=0, keepdims=True).astype(jnp.int32) - 1
    place = owner * ROWS + rank
    chosen = lax.broadcasted_iota(jnp.int32, (count, slots), 0) == place
    picked[...] = chosen.astype(F32)
    ids = jnp.sum(jnp.where(chosen, index_row[...].astype(F32), 0.0), axis=1, keepdims=True)
    lanes = lax.broadcasted_iota(jnp.int32, (count, LANES), 1)
    base[...] = jnp.where(lanes == IDS, ids, 0.0)


def slot_places(tiles, label_owner, label_index):
    slots = label_index.shape[1]
    return pl.pallas_call(
        slots_kernel,
        out_shape=(
            jax.ShapeDtypeStruct((tiles * ROWS, slots), F32),
            jax.ShapeDtypeStruct((tiles * ROWS, LANES), F32),
        ),
        in_specs=[VMEM, VMEM],
        out_specs=(VMEM, VMEM),
        compiler_params=pltpu.CompilerParams(vmem_limit_bytes=LIMIT),
        name="slot_places",
    )(label_owner.reshape(1, slots), label_index)


def merge_rows(blocks):
    rows = lax.broadcasted_iota(jnp.int32, blocks[0].shape, 0)
    step = 4
    while step:
        low = (rows & step) == 0
        half = len(blocks) // 2
        merged = []
        for one, two in zip(blocks[:half], blocks[half:]):
            kept = jnp.where(low, one, two)
            turned = jnp.where(low, two, one)
            moved = pltpu.roll(turned, step, 0)
            if step < 4:
                moved = jnp.where(low, pltpu.roll(turned, 8 - step, 0), moved)
            merged.append(kept + moved)
        blocks = merged
        step //= 2
    return blocks[0]


def moments_kernel(views, depth_total, part, estimate, labels, picked, base, correction, *refs):
    begun, (sent, held, sums, table) = refs[:-4], refs[-4:]
    planes, size, across = correction.shape
    height_total = estimate.shape[1]
    slots = picked.shape[1]
    half = half_of(lax.axis_index("view"))
    first = (lax.axis_index("tile") * planes).astype(F32) + 0.5
    start = pl.multiple_of(size * (PARTS * half + part), 8)
    held[...] = estimate[:, pl.ds(start, size)] * correction[...] * (1.0 / views)
    group = 16
    spot = lax.broadcasted_iota(jnp.int32, (across, LANES), 0)
    lanes = lax.broadcasted_iota(jnp.int32, (across, LANES), 1)
    low = (spot * spot) & 255
    factors = jnp.where(lanes == 0, 1, jnp.where(lanes == 1, spot, 0))
    factors = jnp.where(lanes == 2, spot * spot - low, jnp.where(lanes == 3, low, factors))
    factors = factors.astype(F32).astype(BF16)
    base_row = lax.broadcasted_iota(jnp.int32, (8, across), 0)

    def one_group(number, carry):
        held_parts = []
        for pair in range(0, group, 2):
            slot = [number * group + pair, number * group + pair + 1]
            parts = [[None] * 6 for _ in slot]
            for row in range(0, size, 8):
                high = ((base_row + (row + start)).astype(F32) + 0.5) * (1.0 / height_total)
                flat, once, twice = [[jnp.zeros((8, across), F32) for _ in slot] for _ in range(3)]
                for plane in reversed(range(planes)):
                    mark = labels[plane, pl.ds(pl.multiple_of(start + row, 8), 8)]
                    value = held[plane, row : row + 8]
                    for at in range(2):
                        flat[at] = flat[at] + jnp.where(mark == slot[at], value, 0.0)
                        if plane > 0:
                            once[at] = once[at] + flat[at]
                            twice[at] = twice[at] + once[at]
                for at in range(2):
                    scaled = flat[at] * high
                    terms = (flat[at], scaled, scaled * high, once[at], once[at] * high, twice[at])
                    parts[at] = [new if old is None else old + new for old, new in zip(parts[at], terms)]
            held_parts += parts
            if len(held_parts) == 8:
                for kind in range(6):
                    row = kind * group + pair + 2 - 8
                    sums[row : row + 8, :] = merge_rows([parts[kind] for parts in held_parts])
                held_parts = []
        whole = sums[...]
        upper, rest = split(whole)
        rest = whole - upper.astype(F32)
        middle, lower = split(rest)
        lines = jnp.dot(
            jnp.concatenate([upper, middle, lower], axis=0), factors, preferred_element_type=F32
        )
        count = 6 * group
        lines = lines[:count] + lines[count : 2 * count] + lines[2 * count :]
        flat, high_flat, square_flat, once, high_once, twice = [
            lines[kind * group : (kind + 1) * group] for kind in range(6)
        ]
        deep = (first * flat + once) * (1.0 / depth_total)
        deep_high = (first * high_flat + high_once) * (1.0 / depth_total)
        deeper = first * (first * flat + 2.0 * once) + (2.0 * twice - once)
        deeper = deeper * (1.0 / depth_total**2)
        total = flat
        for kind, sums_of in enumerate((high_flat, square_flat, deep, deep_high, deeper), 1):
            total += pltpu.roll(sums_of, 4 * kind, 1)
        rows = pl.ds(pl.multiple_of(number * group, group), group)
        target = table if part == PARTS - 1 else sent
        target[rows, :] = total + begun[0][rows, :] if begun else total
        return carry

    lax.fori_loop(0, slots // group, one_group, 0)
    if part < PARTS - 1:
        return
    sent[...] = base[...] + jnp.dot(
        picked[...], table[...], precision=lax.Precision.HIGHEST, preferred_element_type=F32
    )


def moment_rows(views, tiles, part, estimate, correction, labels, places, begun):
    planes, size, across = correction.shape
    slots = places[0].shape[1]
    count = tiles * ROWS if part == PARTS - 1 else slots
    return pl.pallas_call(
        functools.partial(moments_kernel, views, tiles * planes, part),
        out_shape=jax.ShapeDtypeStruct((count, LANES), F32),
        in_specs=[VMEM] * (5 + len(begun)),
        out_specs=VMEM,
        scratch_shapes=[
            pltpu.VMEM((planes, size, across), F32),
            pltpu.VMEM((6 * 16, across), F32),
            pltpu.VMEM((slots, LANES), F32),
        ],
        compiler_params=pltpu.CompilerParams(vmem_limit_bytes=LIMIT),
        name="moment_rows",
    )(estimate, labels, *places, correction, *begun)


def segments_kernel(across, rows, after, table):
    values = rows[...]
    ids = values[:, IDS : IDS + 1].astype(jnp.int32)
    spots = lax.broadcasted_iota(jnp.int32, (values.shape[0], NUC_DEV), 1)
    picked = (ids == spots).astype(F32)
    full = lax.dot_general(
        values, picked, (((0,), (0,)), ((), ())),
        precision=lax.Precision.HIGHEST, preferred_element_type=F32,
    )
    mass, high, higher, deep, deep_high, deeper = [full[4 * kind : 4 * kind + 4] for kind in range(6)]
    flat = lambda sums: sums[0:1]
    line = lambda sums: (sums[1:2] + 0.5 * sums[0:1]) * (1.0 / across)
    square = lambda sums: (sums[2:3] + sums[3:4] + sums[1:2] + 0.25 * sums[0:1]) * (1.0 / across**2)
    table[...] = jnp.concatenate(
        [
            flat(mass), flat(deep), flat(high), line(mass),
            flat(deeper), flat(higher), square(mass),
            flat(deep_high), line(deep), line(high),
            jnp.zeros((table.shape[0] - MOM, NUC_DEV), F32),
        ],
        axis=0,
    )


def segment_table(across, rows, after):
    return pl.pallas_call(
        functools.partial(segments_kernel, across),
        out_shape=jax.ShapeDtypeStruct((16, NUC_DEV), F32),
        in_specs=[VMEM, ANY],
        out_specs=VMEM,
        compiler_params=pltpu.CompilerParams(vmem_limit_bytes=LIMIT),
        name="segment_table",
    )(rows, after)


def stores(pieces, sources, whole, half, sems):
    keep = whole.shape[1] // 2
    copies = []
    for number, ((first, size), source) in enumerate(zip(pieces, sources)):
        start = pl.multiple_of(keep * half + first, 8)
        for plane in range(whole.shape[0]):
            copies.append(
                pltpu.make_async_copy(
                    source.at[pl.ds(plane * size, size)],
                    whole.at[plane, pl.ds(start, size)],
                    sems.at[number, plane],
                )
            )
    for copy in copies:
        copy.start()
    return copies


def token_kernel(source, token):
    token[...] = source[:8, :LANES]


def token_of(source):
    return pl.pallas_call(
        token_kernel,
        out_shape=jax.ShapeDtypeStruct((8, LANES), F32),
        in_specs=[VMEM],
        out_specs=VMEM,
        compiler_params=pltpu.CompilerParams(vmem_limit_bytes=LIMIT),
        name="token_of",
    )(source)


def begin_kernel(pieces, *refs):
    sources, (whole, sems) = refs[:-2], refs[-2:]
    for copy in stores(pieces, sources, whole, half_of(lax.axis_index("view")), sems):
        copy.wait()


def begin_result(pieces, shape, mine):
    return pl.pallas_call(
        functools.partial(begin_kernel, pieces),
        out_shape=jax.ShapeDtypeStruct(shape, F32),
        in_specs=[VMEM] * len(mine),
        out_specs=ANY,
        scratch_shapes=[pltpu.SemaphoreType.DMA((len(pieces), shape[0]))],
        compiler_params=pltpu.CompilerParams(vmem_limit_bytes=LIMIT),
        name="begin_result",
    )(*mine)


def finish_kernel(scale, pieces, begun, *refs):
    others, tables = refs[: len(pieces)], refs[len(pieces) : -5]
    whole, moments, held, sems, sem = refs[-5:]
    copies = stores(pieces, others, whole, 1 - half_of(lax.axis_index("view")), sems)
    rows = others[-1][whole.shape[0] * pieces[-1][1] :]
    table = jnp.concatenate([rows[:, :LANES], rows[:, LANES : 2 * LANES]], axis=0)
    for other in tables:
        table += other[...]
    lines = lax.broadcasted_iota(jnp.int32, table.shape, 0)
    result = jnp.where(lines == 0, table * scale, table / jnp.maximum(table[0:1], 1.0))
    held[...] = result[:MOM]
    last = pltpu.make_async_copy(held, moments, sem)
    last.start()
    for copy in copies:
        copy.wait()
    last.wait()


def finish(scale, pieces, begun, others, tables):
    return pl.pallas_call(
        functools.partial(finish_kernel, scale, pieces),
        out_shape=(
            jax.ShapeDtypeStruct(begun.shape, F32),
            jax.ShapeDtypeStruct((MOM, NUC_DEV), F32),
        ),
        in_specs=[ANY] + [VMEM] * (len(others) + len(tables)),
        out_specs=(ANY, ANY),
        input_output_aliases={0: 0},
        scratch_shapes=[
            pltpu.VMEM((MOM, NUC_DEV), F32),
            pltpu.SemaphoreType.DMA((len(pieces), begun.shape[0])),
            pltpu.SemaphoreType.DMA,
        ],
        compiler_params=pltpu.CompilerParams(vmem_limit_bytes=LIMIT),
        name="finish",
    )(begun, *others, *tables)


def on_device(estimate, measured, kernels, labels, label_owner, label_index):
    tiles, views = lax.axis_size("tile"), lax.axis_size("view")
    planes, height, across = estimate.shape
    taps = kernels.shape[2]
    radius = (taps - 1) // 2
    keep = height // 2
    seen = min(height, -(-(keep + radius) // 8) * 8)
    rows = min(height, -(-(keep + 2 * radius) // 16) * 16)
    near_pairs = [(i, i ^ 1) for i in range(tiles)]
    far_pairs = [(i, i + 1) for i in range(1, tiles - 1, 2)]
    far_pairs = far_pairs + [(b, a) for a, b in far_pairs]
    partner = [(i, i ^ 1) for i in range(views)]
    across_pairs = [(i, i ^ 3) for i in range(views)]

    lines = jnp.transpose(kernels, (1, 0, 2))
    packed = view_out(measured, lines, seen)
    swapped = lax.ppermute(packed, "view", partner)
    to_far, to_near = rims_out(estimate, radius, rows)
    far = lax.ppermute(to_far, "tile", far_pairs)
    near = lax.ppermute(to_near, "tile", near_pairs)
    places = slot_places(tiles, label_owner, label_index)
    own = prepare(False, taps, lines, estimate, places[1], rows, seen, keep)
    others = prepare(True, taps, swapped, estimate, lines, rows, seen, keep)
    field_own, field_other, *sends = ratio_fields(own, others, far, near, measured, swapped)
    rims = [
        lax.ppermute(send, "tile", pairs) for send, pairs in zip(sends, (far_pairs, near_pairs) * PARTS)
    ]
    inner = own_planes(taps, own[4], others[4], field_own, field_other)
    mine, other, sums = [], [], []
    for part in range(PARTS):
        mine.append(add_rims(inner[part], *rims[2 * part : 2 * part + 2], *sums))
        other.append(lax.ppermute(mine[part], "view", across_pairs))
        sums = [moment_rows(views, tiles, part, estimate, mine[part], labels, places, sums)]
    sent = sums[0]
    got = lax.all_to_all(sent, "tile", split_axis=0, concat_axis=0, tiled=True)
    size = keep // PARTS
    cuts = [(part, (0, size), 8 * (PARTS + 1 - part)) for part in range(PARTS - 1)]
    cuts += [(PARTS - 1, (0, size // 2), 16), (PARTS - 1, (size // 2, size), 8)]
    pieces = [(part * size + low, high - low) for part, (low, high), _ in cuts]
    new_mine, new_other, token, table = [], [], [sent], []
    for number, (part, low, spare) in enumerate(cuts):
        if number == len(cuts) - 1:
            table = [segment_table(across, got, token[0])]
        piece = update(views, keep, part, low, spare, estimate, mine[part], other[part], table, token)
        new_mine.append(piece)
        new_other.append(lax.ppermute(piece, "view", partner))
        token = [token_of(piece)]
    tables = table + [
        lax.ppermute(table[0], "view", [(i, i ^ step) for i in range(views)]) for step in (2, 3)
    ]
    scale = label_index.shape[1] / (planes * height * across)
    begun = begin_result(pieces, estimate.shape, new_mine)
    return finish(scale, pieces, begun, new_other, tables)


def solution(mesh):
    placed = (
        P("tile", None, None),
        P("view", "tile", None, None),
        P("view", None, None),
        P("tile", None, None),
        P("tile", None, None),
        P("tile", None),
    )
    return jax.shard_map(
        on_device,
        mesh=mesh,
        in_specs=placed,
        out_specs=(P("tile", None, None), P(None, "tile")),
        check_vma=False,
    )
```

```python
import functools

import jax
import jax.numpy as jnp
from jax import lax
from jax.experimental import pallas as pl
from jax.experimental.pallas import tpu as pltpu
from jax.sharding import PartitionSpec as P

MOM = 10
ROWS = 8
NUC_DEV = 128
LANES = 128
PARTS = 2
TAIL = 8
IDS = 24
F32 = jnp.float32
BF16 = jnp.bfloat16
ANY = pl.BlockSpec(memory_space=pl.ANY)
VMEM = pl.BlockSpec(memory_space=pltpu.VMEM)
LIMIT = 32 * 1024 * 1024


def half_of(view):
    return (view ^ (view >> 1)) & 1


def split(value):
    upper = value.astype(BF16)
    return upper, (value - upper.astype(F32)).astype(BF16)


def band(taps, shape, offset):
    rows = lax.broadcasted_iota(jnp.int32, shape, 0)
    cols = lax.broadcasted_iota(jnp.int32, shape, 1)
    place = cols - rows + offset
    result = jnp.zeros(shape, F32)
    for step, tap in enumerate(taps):
        result = jnp.where(place == step, tap, result)
    return result


def depth_terms(source, weights, first, last, planes, flipped):
    radius = (len(weights) - 1) // 2
    totals = {plane: None for plane in planes}
    for place in range(first, last):
        block = None
        for plane in planes:
            step = plane - place + radius if flipped else place - plane + radius
            if 0 <= step < len(weights):
                block = source(place) if block is None else block
                term = weights[step] * block
                totals[plane] = term if totals[plane] is None else totals[plane] + term
    return totals


def chunks(rows, across):
    return [(slice(row, row + 16), slice(lane, lane + LANES)) for row in range(0, rows, 16) for lane in range(0, across, LANES)]


def rims_out_kernel(estimate, to_far, to_near):
    planes, radius, rows = estimate.shape[0], to_far.shape[0], to_far.shape[1]
    odd = lax.axis_index("tile") % 2
    half = half_of(lax.axis_index("view"))
    start = pl.multiple_of((estimate.shape[1] - rows) * half, 8)
    to_far[...] = estimate[pl.ds(odd, radius), pl.ds(start, rows)]
    to_near[...] = estimate[pl.ds(1 - odd, radius), pl.ds(start, rows)]


def rims_out(estimate, radius, rows):
    shape = jax.ShapeDtypeStruct((radius, rows, estimate.shape[2]), F32)
    return pl.pallas_call(
        rims_out_kernel,
        out_shape=(shape, shape),
        in_specs=[VMEM],
        out_specs=(VMEM, VMEM),
        compiler_params=pltpu.CompilerParams(vmem_limit_bytes=LIMIT),
        name="rims_out",
    )(estimate)


def view_out_kernel(seen, measured, taps, packed):
    planes, height = measured.shape[1], measured.shape[2]
    half = half_of(lax.axis_index("view"))
    start = pl.multiple_of((height - seen) * (1 - half), 8)
    for plane in range(planes):
        packed[plane * seen : (plane + 1) * seen] = measured[0, plane, pl.ds(start, seen)]
    packed[planes * seen :] = jnp.zeros((TAIL, packed.shape[1]), F32)
    for axis in range(taps.shape[0]):
        at = planes * seen + axis
        packed[at : at + 1, : taps.shape[2]] = taps[axis]


def view_out(measured, kernels, seen):
    _, planes, _, across = measured.shape
    return pl.pallas_call(
        functools.partial(view_out_kernel, seen),
        out_shape=jax.ShapeDtypeStruct((planes * seen + TAIL, across), F32),
        in_specs=[VMEM, VMEM],
        out_specs=VMEM,
        compiler_params=pltpu.CompilerParams(vmem_limit_bytes=LIMIT),
        name="view_out",
    )(measured, kernels)


def prepare_kernel(packed, taps, source, estimate, after, wide, tall, back, part, spread):
    half = half_of(lax.axis_index("view"))
    across = wide.shape[-1]
    rows, keep, seen = part.shape[1], back.shape[0], tall.shape[0]
    planes = estimate.shape[0]
    radius = (taps - 1) // 2
    at = source.shape[0] - TAIL
    if packed:
        raw = source[at : at + 3, :taps]
    else:
        raw = jnp.concatenate([source[axis] for axis in range(source.shape[0])], axis=0)
    weights = raw / jnp.sum(raw, axis=-1, keepdims=True)
    deep, high, flat = [[weights[axis : axis + 1, t : t + 1] for t in range(taps)] for axis in range(3)]
    start = pl.multiple_of((2 * keep - rows) * half, 16)
    seen_start = (2 * keep - seen) * half
    near_diagonal = jnp.abs(
        lax.broadcasted_iota(jnp.int32, (across, across), 1)
        - lax.broadcasted_iota(jnp.int32, (across, across), 0)
    ) <= radius
    for turn, line in enumerate((flat[::-1], flat)):
        first_row = jnp.concatenate(
            line[radius:] + [jnp.zeros((1, across - taps), F32)] + line[:radius], axis=1
        )
        square = pltpu.roll(
            jnp.broadcast_to(first_row, (across, across)), 0, 1, stride=1, stride_axis=0
        )
        upper, lower = split(jnp.where(near_diagonal, square, 0.0))
        wide[turn, 0] = upper
        wide[turn, 1] = lower
    upper, lower = split(band(high, (seen, rows), radius + start - seen_start))
    tall[...] = jnp.concatenate([upper, upper, lower], axis=1)
    upper, lower = split(band(high[::-1], (keep, rows), radius + seen_start - keep * half))
    back[...] = jnp.concatenate([upper, upper, lower], axis=1)
    factors = [jnp.broadcast_to(tap, (16, LANES)) for tap in deep]
    spread[...] = jnp.zeros_like(spread)
    for step in range(taps):
        spread[step : step + 1] = factors[step][:1]
    for row, lane in chunks(rows, across):
        where = pl.ds(pl.multiple_of(start + row.start, 16), 16)
        terms = depth_terms(
            lambda place: estimate[place, where, lane], factors, 0, planes, range(planes), False
        )
        for plane, block in terms.items():
            part[plane, row, lane] = block


def prepare(packed, taps, source, estimate, after, rows, seen, keep):
    planes, _, across = estimate.shape
    return pl.pallas_call(
        functools.partial(prepare_kernel, packed, taps),
        out_shape=(
            jax.ShapeDtypeStruct((2, 2, across, across), BF16),
            jax.ShapeDtypeStruct((seen, 3 * rows), BF16),
            jax.ShapeDtypeStruct((keep, 3 * rows), BF16),
            jax.ShapeDtypeStruct((planes, rows, across), F32),
            jax.ShapeDtypeStruct((-(-taps // 8) * 8, LANES), F32),
        ),
        in_specs=[VMEM, VMEM, ANY],
        out_specs=(VMEM,) * 5,
        compiler_params=pltpu.CompilerParams(vmem_limit_bytes=LIMIT),
        name="prepare",
    )(source, estimate, after)


def spread_factors(spread, taps):
    return [jnp.broadcast_to(spread[step : step + 1, :], (16, LANES)) for step in range(taps)]


def fields_kernel(*refs):
    sets, (far, near, measured, swapped), refs = (refs[:5], refs[5:10]), refs[10:14], refs[14:]
    fields, sends, (blur_hi, blur_lo, plane_hi, plane_lo) = refs[:2], refs[2:-4], refs[-4:]
    planes = sets[0][3].shape[0]
    radius, rows, across = near.shape
    keep, seen = sets[0][2].shape[0], sets[0][1].shape[0]
    taps = 2 * radius + 1
    even = lax.axis_index("tile") % 2 == 0
    half = half_of(lax.axis_index("view"))
    seen_start = pl.multiple_of((2 * keep - seen) * half, 8)
    factors = [spread_factors(spread, taps) for _, _, _, _, spread in sets]
    for which, (_, _, _, part, _) in enumerate(sets):
        for row, lane in chunks(rows, across):

            def rim(place):
                if place < 0:
                    at = place + radius
                    return jnp.where(even, far[at, row, lane], near[at, row, lane])
                at = place - planes
                return jnp.where(even, near[at, row, lane], far[at, row, lane])

            below = depth_terms(rim, factors[which], -radius, 0, range(planes), False)
            above = depth_terms(rim, factors[which], planes, planes + radius, range(planes), False)
            for plane in range(planes):
                block = part[plane, row, lane]
                for term in (below[plane], above[plane]):
                    block = block if term is None else block + term
                upper, lower = split(block)
                at = slice(plane * rows + row.start, plane * rows + row.stop)
                blur_hi[which, at, lane] = upper
                blur_lo[which, at, lane] = lower
    lines = []
    for which, (wide, _, _, _, _) in enumerate(sets):
        upper, lower = wide[0, 0], wide[0, 1]
        lines.append(
            jnp.dot(blur_hi[which], upper, preferred_element_type=F32)
            + jnp.dot(blur_lo[which], upper, preferred_element_type=F32)
            + jnp.dot(blur_hi[which], lower, preferred_element_type=F32)
        )
    both = [(which, plane) for which in range(2) for plane in range(planes)]
    forwards = {}
    for which, plane in both:
        hi, lo = split(lines[which][plane * rows : (plane + 1) * rows])
        forwards[which, plane] = jnp.dot(
            sets[which][1][...], jnp.concatenate([hi, lo, hi], axis=0), preferred_element_type=F32
        )
    ratios = {}
    for which, plane in both:
        if which == 0:
            recorded = measured[0, plane, pl.ds(seen_start, seen), :]
        else:
            recorded = swapped[plane * seen : (plane + 1) * seen]
        ratio = recorded / forwards[which, plane]
        if rows > seen:
            ratio = jnp.concatenate([ratio, jnp.zeros((rows - seen, across), F32)], axis=0)
        ratios[which, plane] = split(ratio)
    turned = {}
    for which, plane in both:
        hi, lo = ratios[which, plane]
        turned[which, plane] = jnp.dot(
            sets[which][2][...], jnp.concatenate([hi, lo, hi], axis=0), preferred_element_type=F32
        )
    for which, plane in both:
        hi, lo = split(turned[which, plane])
        plane_hi[which, plane * keep : (plane + 1) * keep] = hi
        plane_lo[which, plane * keep : (plane + 1) * keep] = lo
    for which, (wide, _, _, _, _) in enumerate(sets):
        upper, lower = wide[1, 0], wide[1, 1]
        result = (
            jnp.dot(plane_hi[which], upper, preferred_element_type=F32)
            + jnp.dot(plane_lo[which], upper, preferred_element_type=F32)
            + jnp.dot(plane_hi[which], lower, preferred_element_type=F32)
        )
        fields[which][...] = result.reshape(planes, keep, across)
    for row, lane in chunks(keep, across):
        below, above = [], []
        for which in range(2):
            source = lambda place: fields[which][place, row, lane]
            outer = range(planes, planes + radius)
            below.append(depth_terms(source, factors[which], 0, planes, range(-radius, 0), True))
            above.append(depth_terms(source, factors[which], 0, planes, outer, True))
        part_at, inside = divmod(row.start, keep // PARTS)
        inside = slice(inside, inside + 16)
        for at in range(radius):
            down = below[0][at - radius] + below[1][at - radius]
            up = above[0][at + planes] + above[1][at + planes]
            sends[2 * part_at][at, inside, lane] = jnp.where(even, down, up)
            sends[2 * part_at + 1][at, inside, lane] = jnp.where(even, up, down)


def ratio_fields(own, others, far, near, measured, swapped):
    keep, planes = own[2].shape[0], own[3].shape[0]
    radius, rows, across = near.shape
    field = jax.ShapeDtypeStruct((planes, keep, across), F32)
    send = jax.ShapeDtypeStruct((radius, keep // PARTS, across), F32)
    return pl.pallas_call(
        fields_kernel,
        out_shape=(field,) * 2 + (send,) * (2 * PARTS),
        in_specs=[VMEM] * 14,
        out_specs=(VMEM,) * (2 + 2 * PARTS),
        scratch_shapes=[
            pltpu.VMEM((2, planes * rows, across), BF16),
            pltpu.VMEM((2, planes * rows, across), BF16),
            pltpu.VMEM((2, planes * keep, across), BF16),
            pltpu.VMEM((2, planes * keep, across), BF16),
        ],
        compiler_params=pltpu.CompilerParams(vmem_limit_bytes=LIMIT),
        name="ratio_fields",
    )(*own, *others, far, near, measured, swapped)


def own_kernel(taps, spread_own, spread_other, field_own, field_other, *inner):
    planes, keep, across = field_own.shape
    factors = [spread_factors(spread, taps) for spread in (spread_own, spread_other)]
    for row, lane in chunks(keep, across):
        parts = [
            depth_terms(
                lambda place: field[place, row, lane], factors[which], 0, planes, range(planes), True
            )
            for which, field in enumerate((field_own, field_other))
        ]
        part_at, inside = divmod(row.start, keep // PARTS)
        for plane in range(planes):
            inner[part_at][plane, inside : inside + 16, lane] = parts[0][plane] + parts[1][plane]


def own_planes(taps, spread_own, spread_other, field_own, field_other):
    planes, keep, across = field_own.shape
    return pl.pallas_call(
        functools.partial(own_kernel, taps),
        out_shape=(jax.ShapeDtypeStruct((planes, keep // PARTS, across), F32),) * PARTS,
        in_specs=[VMEM] * 4,
        out_specs=(VMEM,) * PARTS,
        compiler_params=pltpu.CompilerParams(vmem_limit_bytes=LIMIT),
        name="own_planes",
    )(spread_own, spread_other, field_own, field_other)


def rims_kernel(inner, far, near, *rest):
    correction = rest[-1]
    planes, radius = inner.shape[0], near.shape[0]
    even = lax.axis_index("tile") % 2 == 0
    for plane in range(planes):
        total = inner[plane]
        if plane < radius:
            total += jnp.where(even, far[plane], near[plane])
        if plane >= planes - radius:
            at = plane - planes + radius
            total += jnp.where(even, near[at], far[at])
        correction[plane] = total


def add_rims(inner, far, near, *after):
    return pl.pallas_call(
        rims_kernel,
        out_shape=jax.ShapeDtypeStruct(inner.shape, F32),
        in_specs=[VMEM] * 3 + [ANY] * len(after),
        out_specs=VMEM,
        compiler_params=pltpu.CompilerParams(vmem_limit_bytes=LIMIT),
        name="add_rims",
    )(inner, far, near, *after)


def table_rows(table):
    return jnp.concatenate([table[:8], table[8:]], axis=1)


def update_kernel(views, part, estimate, mine, other, *rest):
    planes, size, across = mine.shape
    result = rest[-1]
    half = half_of(lax.axis_index("view"))
    start = pl.multiple_of(size * (PARTS * half + part), 8)
    for plane in range(planes):
        held = estimate[plane, pl.ds(start, size)]
        at = slice(plane * size, (plane + 1) * size)
        result[at] = held * (mine[plane] + other[plane]) * (1.0 / views)
    spare = result.shape[0] - planes * size
    if spare:
        result[planes * size :] = jnp.zeros((spare, across), F32)


def update(views, part, estimate, mine, other, after):
    planes, size, across = mine.shape
    spare = 8 * (PARTS - 1 - part)
    return pl.pallas_call(
        functools.partial(update_kernel, views, part),
        out_shape=jax.ShapeDtypeStruct((planes * size + spare, across), F32),
        in_specs=[VMEM] * 3 + [ANY] * len(after),
        out_specs=VMEM,
        compiler_params=pltpu.CompilerParams(vmem_limit_bytes=LIMIT),
        name="update",
    )(estimate, mine, other, *after)


def slots_kernel(views, owner_row, index_row, picked, base):
    count = picked.shape[0]
    slots = owner_row.shape[1]
    tiles = count // (views * ROWS)
    owner = owner_row[...]
    member = (lax.broadcasted_iota(jnp.int32, (tiles, slots), 0) == owner).astype(F32)
    upto = (
        lax.broadcasted_iota(jnp.int32, (slots, slots), 0)
        <= lax.broadcasted_iota(jnp.int32, (slots, slots), 1)
    ).astype(F32)
    running = jnp.dot(member, upto, preferred_element_type=F32)
    rank = jnp.sum(member * running, axis=0, keepdims=True).astype(jnp.int32) - 1
    line = lax.broadcasted_iota(jnp.int32, (count, slots), 0)
    spot = (line // (views * ROWS)) * ROWS + line % ROWS
    chosen = spot == owner * ROWS + rank
    picked[...] = chosen.astype(F32)
    ids = jnp.sum(jnp.where(chosen, index_row[...].astype(F32), 0.0), axis=1, keepdims=True)
    lanes = lax.broadcasted_iota(jnp.int32, (count, LANES), 1)
    base[...] = jnp.where(lanes == IDS, ids, 0.0)


def slot_places(tiles, views, label_owner, label_index):
    slots = label_index.shape[1]
    count = tiles * views * ROWS
    return pl.pallas_call(
        functools.partial(slots_kernel, views),
        out_shape=(
            jax.ShapeDtypeStruct((count, slots), F32),
            jax.ShapeDtypeStruct((count, LANES), F32),
        ),
        in_specs=[VMEM, VMEM],
        out_specs=(VMEM, VMEM),
        compiler_params=pltpu.CompilerParams(vmem_limit_bytes=LIMIT),
        name="slot_places",
    )(label_owner.reshape(1, slots), label_index)


def merge_rows(blocks):
    rows = lax.broadcasted_iota(jnp.int32, blocks[0].shape, 0)
    step = 4
    while step:
        low = (rows & step) == 0
        half = len(blocks) // 2
        merged = []
        for one, two in zip(blocks[:half], blocks[half:]):
            kept = jnp.where(low, one, two)
            turned = jnp.where(low, two, one)
            moved = pltpu.roll(turned, step, 0)
            if step < 4:
                moved = jnp.where(low, pltpu.roll(turned, 8 - step, 0), moved)
            merged.append(kept + moved)
        blocks = merged
        step //= 2
    return blocks[0]


def moments_kernel(views, depth_total, part, estimate, labels, picked, base, correction, *refs):
    begun, (sent, held, sums, table) = refs[:-4], refs[-4:]
    planes, size, across = correction.shape
    height_total = estimate.shape[1]
    slots = picked.shape[1]
    half = half_of(lax.axis_index("view"))
    first = (lax.axis_index("tile") * planes).astype(F32) + 0.5
    start = pl.multiple_of(size * (PARTS * half + part), 8)
    held[...] = estimate[:, pl.ds(start, size)] * correction[...] * (1.0 / views)
    group = 16
    spot = lax.broadcasted_iota(jnp.int32, (across, LANES), 0)
    lanes = lax.broadcasted_iota(jnp.int32, (across, LANES), 1)
    low = (spot * spot) & 255
    factors = jnp.where(lanes == 0, 1, jnp.where(lanes == 1, spot, 0))
    factors = jnp.where(lanes == 2, spot * spot - low, jnp.where(lanes == 3, low, factors))
    factors = factors.astype(F32).astype(BF16)
    base_row = lax.broadcasted_iota(jnp.int32, (8, across), 0)

    def one_group(number, carry):
        held_parts = []
        for pair in range(0, group, 2):
            slot = [number * group + pair, number * group + pair + 1]
            parts = [[None] * 6 for _ in slot]
            for row in range(0, size, 8):
                high = ((base_row + (row + start)).astype(F32) + 0.5) * (1.0 / height_total)
                flat, once, twice = [[jnp.zeros((8, across), F32) for _ in slot] for _ in range(3)]
                for plane in reversed(range(planes)):
                    mark = labels[plane, pl.ds(pl.multiple_of(start + row, 8), 8)]
                    value = held[plane, row : row + 8]
                    for at in range(2):
                        flat[at] = flat[at] + jnp.where(mark == slot[at], value, 0.0)
                        if plane > 0:
                            once[at] = once[at] + flat[at]
                            twice[at] = twice[at] + once[at]
                for at in range(2):
                    scaled = flat[at] * high
                    terms = (flat[at], scaled, scaled * high, once[at], once[at] * high, twice[at])
                    parts[at] = [new if old is None else old + new for old, new in zip(parts[at], terms)]
            held_parts += parts
            if len(held_parts) == 8:
                for kind in range(6):
                    row = kind * group + pair + 2 - 8
                    sums[row : row + 8, :] = merge_rows([parts[kind] for parts in held_parts])
                held_parts = []
        whole = sums[...]
        upper, rest = split(whole)
        rest = whole - upper.astype(F32)
        middle, lower = split(rest)
        lines = jnp.dot(
            jnp.concatenate([upper, middle, lower], axis=0), factors, preferred_element_type=F32
        )
        count = 6 * group
        lines = lines[:count] + lines[count : 2 * count] + lines[2 * count :]
        flat, high_flat, square_flat, once, high_once, twice = [
            lines[kind * group : (kind + 1) * group] for kind in range(6)
        ]
        deep = (first * flat + once) * (1.0 / depth_total)
        deep_high = (first * high_flat + high_once) * (1.0 / depth_total)
        deeper = first * (first * flat + 2.0 * once) + (2.0 * twice - once)
        deeper = deeper * (1.0 / depth_total**2)
        total = flat
        for kind, sums_of in enumerate((high_flat, square_flat, deep, deep_high, deeper), 1):
            total += pltpu.roll(sums_of, 4 * kind, 1)
        rows = pl.ds(pl.multiple_of(number * group, group), group)
        target = table if part == PARTS - 1 else sent
        target[rows, :] = total + begun[0][rows, :] if begun else total
        return carry

    lax.fori_loop(0, slots // group, one_group, 0)
    if part < PARTS - 1:
        return
    sent[...] = base[...] + jnp.dot(
        picked[...], table[...], precision=lax.Precision.HIGHEST, preferred_element_type=F32
    )


def moment_rows(views, tiles, part, estimate, correction, labels, places, begun):
    planes, size, across = correction.shape
    slots = places[0].shape[1]
    count = places[0].shape[0] if part == PARTS - 1 else slots
    return pl.pallas_call(
        functools.partial(moments_kernel, views, tiles * planes, part),
        out_shape=jax.ShapeDtypeStruct((count, LANES), F32),
        in_specs=[VMEM] * (5 + len(begun)),
        out_specs=VMEM,
        scratch_shapes=[
            pltpu.VMEM((planes, size, across), F32),
            pltpu.VMEM((6 * 16, across), F32),
            pltpu.VMEM((slots, LANES), F32),
        ],
        compiler_params=pltpu.CompilerParams(vmem_limit_bytes=LIMIT),
        name="moment_rows",
    )(estimate, labels, *places, correction, *begun)


def segments_kernel(across, scale, rows, moments):
    values = rows[...]
    ids = values[:, IDS : IDS + 1].astype(jnp.int32)
    spots = lax.broadcasted_iota(jnp.int32, (values.shape[0], NUC_DEV), 1)
    picked = (ids == spots).astype(F32)
    full = lax.dot_general(
        values, picked, (((0,), (0,)), ((), ())),
        precision=lax.Precision.HIGHEST, preferred_element_type=F32,
    )
    mass, high, higher, deep, deep_high, deeper = [full[4 * kind : 4 * kind + 4] for kind in range(6)]
    flat = lambda sums: sums[0:1]
    line = lambda sums: (sums[1:2] + 0.5 * sums[0:1]) * (1.0 / across)
    square = lambda sums: (sums[2:3] + sums[3:4] + sums[1:2] + 0.25 * sums[0:1]) * (1.0 / across**2)
    whole = flat(mass)
    sums = jnp.concatenate(
        [
            flat(deep), flat(high), line(mass),
            flat(deeper), flat(higher), square(mass),
            flat(deep_high), line(deep), line(high),
        ],
        axis=0,
    )
    moments[...] = jnp.concatenate([whole * scale, sums / jnp.maximum(whole, 1.0)], axis=0)


def nucleus_table(across, scale, rows):
    return pl.pallas_call(
        functools.partial(segments_kernel, across, scale),
        out_shape=jax.ShapeDtypeStruct((MOM, NUC_DEV), F32),
        in_specs=[VMEM],
        out_specs=VMEM,
        compiler_params=pltpu.CompilerParams(vmem_limit_bytes=LIMIT),
        name="nucleus_table",
    )(rows)


def stores(pieces, sources, whole, half, sems):
    keep = whole.shape[1] // 2
    copies = []
    for number, ((first, size), source) in enumerate(zip(pieces, sources)):
        start = pl.multiple_of(keep * half + first, 8)
        for plane in range(whole.shape[0]):
            copies.append(
                pltpu.make_async_copy(
                    source.at[pl.ds(plane * size, size)],
                    whole.at[plane, pl.ds(start, size)],
                    sems.at[number, plane],
                )
            )
    for copy in copies:
        copy.start()
    return copies


def token_kernel(source, token):
    token[...] = source[:8, :LANES]


def token_of(source):
    return pl.pallas_call(
        token_kernel,
        out_shape=jax.ShapeDtypeStruct((8, LANES), F32),
        in_specs=[VMEM],
        out_specs=VMEM,
        compiler_params=pltpu.CompilerParams(vmem_limit_bytes=LIMIT),
        name="token_of",
    )(source)


def begin_kernel(pieces, *refs):
    sources, (whole, sems) = refs[:-2], refs[-2:]
    for copy in stores(pieces, sources, whole, half_of(lax.axis_index("view")), sems):
        copy.wait()


def begin_result(pieces, shape, mine):
    return pl.pallas_call(
        functools.partial(begin_kernel, pieces),
        out_shape=jax.ShapeDtypeStruct(shape, F32),
        in_specs=[VMEM] * len(mine),
        out_specs=ANY,
        scratch_shapes=[pltpu.SemaphoreType.DMA((len(pieces), shape[0]))],
        compiler_params=pltpu.CompilerParams(vmem_limit_bytes=LIMIT),
        name="begin_result",
    )(*mine)


def finish_kernel(pieces, begun, *refs):
    others, (whole, sems) = refs[:-2], refs[-2:]
    for copy in stores(pieces, others, whole, 1 - half_of(lax.axis_index("view")), sems):
        copy.wait()


def finish(pieces, begun, others):
    return pl.pallas_call(
        functools.partial(finish_kernel, pieces),
        out_shape=jax.ShapeDtypeStruct(begun.shape, F32),
        in_specs=[ANY] + [VMEM] * len(others),
        out_specs=ANY,
        input_output_aliases={0: 0},
        scratch_shapes=[pltpu.SemaphoreType.DMA((len(pieces), begun.shape[0]))],
        compiler_params=pltpu.CompilerParams(vmem_limit_bytes=LIMIT),
        name="finish",
    )(begun, *others)


def on_device(estimate, measured, kernels, labels, label_owner, label_index):
    tiles, views = lax.axis_size("tile"), lax.axis_size("view")
    planes, height, across = estimate.shape
    taps = kernels.shape[2]
    radius = (taps - 1) // 2
    keep = height // 2
    seen = min(height, -(-(keep + radius) // 8) * 8)
    rows = min(height, -(-(keep + 2 * radius) // 16) * 16)
    near_pairs = [(i, i ^ 1) for i in range(tiles)]
    far_pairs = [(i, i + 1) for i in range(1, tiles - 1, 2)]
    far_pairs = far_pairs + [(b, a) for a, b in far_pairs]
    partner = [(i, i ^ 1) for i in range(views)]
    across_pairs = [(i, i ^ 3) for i in range(views)]

    lines = jnp.transpose(kernels, (1, 0, 2))
    packed = view_out(measured, lines, seen)
    swapped = lax.ppermute(packed, "view", partner)
    to_far, to_near = rims_out(estimate, radius, rows)
    far = lax.ppermute(to_far, "tile", far_pairs)
    near = lax.ppermute(to_near, "tile", near_pairs)
    places = slot_places(tiles, views, label_owner, label_index)
    own = prepare(False, taps, lines, estimate, places[1], rows, seen, keep)
    others = prepare(True, taps, swapped, estimate, lines, rows, seen, keep)
    field_own, field_other, *sends = ratio_fields(own, others, far, near, measured, swapped)
    rims = [
        lax.ppermute(send, "tile", pairs) for send, pairs in zip(sends, (far_pairs, near_pairs) * PARTS)
    ]
    inner = own_planes(taps, own[4], others[4], field_own, field_other)
    mine, other, sums = [], [], []
    for part in range(PARTS):
        mine.append(add_rims(inner[part], *rims[2 * part : 2 * part + 2], *sums))
        other.append(lax.ppermute(mine[part], "view", across_pairs))
        sums = [moment_rows(views, tiles, part, estimate, mine[part], labels, places, sums)]
    sent = sums[0]
    got = lax.all_to_all(sent, ("tile", "view"), split_axis=0, concat_axis=0, tiled=True)
    size = keep // PARTS
    pieces = [(part * size, size) for part in range(PARTS)]
    new_mine, new_other, token = [], [], [sent]
    for part in range(PARTS):
        new_mine.append(update(views, part, estimate, mine[part], other[part], token))
        new_other.append(lax.ppermute(new_mine[part], "view", partner))
        token = [token_of(new_mine[part])]
    scale = label_index.shape[1] / (planes * height * across)
    moments = nucleus_table(across, scale, got)
    begun = begin_result(pieces, estimate.shape, new_mine)
    return finish(pieces, begun, new_other), moments


def solution(mesh):
    placed = (
        P("tile", None, None),
        P("view", "tile", None, None),
        P("view", None, None),
        P("tile", None, None),
        P("tile", None, None),
        P("tile", None),
    )
    return jax.shard_map(
        on_device,
        mesh=mesh,
        in_specs=placed,
        out_specs=(P("tile", None, None), P(None, "tile")),
        check_vma=False,
    )
```

```python
import functools

import jax
import jax.numpy as jnp
from jax import lax
from jax.experimental import pallas as pl
from jax.experimental.pallas import tpu as pltpu
from jax.sharding import PartitionSpec as P

MOM = 10
CAP = 5
WIDTH = 25
NUC_DEV = 128
LANES = 128
PARTS = 2
TAIL = 8
IDS = 24
F32 = jnp.float32
BF16 = jnp.bfloat16
ANY = pl.BlockSpec(memory_space=pl.ANY)
VMEM = pl.BlockSpec(memory_space=pltpu.VMEM)
LIMIT = 32 * 1024 * 1024


def half_of(view):
    return (view ^ (view >> 1)) & 1


def split(value):
    upper = value.astype(BF16)
    return upper, (value - upper.astype(F32)).astype(BF16)


def band(taps, shape, offset):
    rows = lax.broadcasted_iota(jnp.int32, shape, 0)
    cols = lax.broadcasted_iota(jnp.int32, shape, 1)
    place = cols - rows + offset
    result = jnp.zeros(shape, F32)
    for step, tap in enumerate(taps):
        result = jnp.where(place == step, tap, result)
    return result


def depth_terms(source, weights, first, last, planes, flipped):
    radius = (len(weights) - 1) // 2
    totals = {plane: None for plane in planes}
    for place in range(first, last):
        block = None
        for plane in planes:
            step = plane - place + radius if flipped else place - plane + radius
            if 0 <= step < len(weights):
                block = source(place) if block is None else block
                term = weights[step] * block
                totals[plane] = term if totals[plane] is None else totals[plane] + term
    return totals


def chunks(rows, across):
    return [(slice(row, row + 16), slice(lane, lane + LANES)) for row in range(0, rows, 16) for lane in range(0, across, LANES)]


def rims_out_kernel(estimate, to_far, to_near):
    planes, radius, rows = estimate.shape[0], to_far.shape[0], to_far.shape[1]
    odd = lax.axis_index("tile") % 2
    half = half_of(lax.axis_index("view"))
    start = pl.multiple_of((estimate.shape[1] - rows) * half, 8)
    to_far[...] = estimate[pl.ds(odd, radius), pl.ds(start, rows)]
    to_near[...] = estimate[pl.ds(1 - odd, radius), pl.ds(start, rows)]


def rims_out(estimate, radius, rows):
    shape = jax.ShapeDtypeStruct((radius, rows, estimate.shape[2]), F32)
    return pl.pallas_call(
        rims_out_kernel,
        out_shape=(shape, shape),
        in_specs=[VMEM],
        out_specs=(VMEM, VMEM),
        compiler_params=pltpu.CompilerParams(vmem_limit_bytes=LIMIT),
        name="rims_out",
    )(estimate)


def view_out_kernel(seen, measured, taps, packed):
    planes, height = measured.shape[1], measured.shape[2]
    half = half_of(lax.axis_index("view"))
    start = pl.multiple_of((height - seen) * (1 - half), 8)
    for plane in range(planes):
        packed[plane * seen : (plane + 1) * seen] = measured[0, plane, pl.ds(start, seen)]
    packed[planes * seen :] = jnp.zeros((TAIL, packed.shape[1]), F32)
    for axis in range(taps.shape[0]):
        at = planes * seen + axis
        packed[at : at + 1, : taps.shape[2]] = taps[axis]


def view_out(measured, kernels, seen):
    _, planes, _, across = measured.shape
    return pl.pallas_call(
        functools.partial(view_out_kernel, seen),
        out_shape=jax.ShapeDtypeStruct((planes * seen + TAIL, across), F32),
        in_specs=[VMEM, VMEM],
        out_specs=VMEM,
        compiler_params=pltpu.CompilerParams(vmem_limit_bytes=LIMIT),
        name="view_out",
    )(measured, kernels)


def prepare_kernel(packed, taps, source, estimate, after, wide, tall, back, part, spread):
    half = half_of(lax.axis_index("view"))
    across = wide.shape[-1]
    rows, keep, seen = part.shape[1], back.shape[0], tall.shape[0]
    planes = estimate.shape[0]
    radius = (taps - 1) // 2
    at = source.shape[0] - TAIL
    if packed:
        raw = source[at : at + 3, :taps]
    else:
        raw = jnp.concatenate([source[axis] for axis in range(source.shape[0])], axis=0)
    weights = raw / jnp.sum(raw, axis=-1, keepdims=True)
    deep, high, flat = [[weights[axis : axis + 1, t : t + 1] for t in range(taps)] for axis in range(3)]
    start = pl.multiple_of((2 * keep - rows) * half, 16)
    seen_start = (2 * keep - seen) * half
    near_diagonal = jnp.abs(
        lax.broadcasted_iota(jnp.int32, (across, across), 1)
        - lax.broadcasted_iota(jnp.int32, (across, across), 0)
    ) <= radius
    for turn, line in enumerate((flat[::-1], flat)):
        first_row = jnp.concatenate(
            line[radius:] + [jnp.zeros((1, across - taps), F32)] + line[:radius], axis=1
        )
        square = pltpu.roll(
            jnp.broadcast_to(first_row, (across, across)), 0, 1, stride=1, stride_axis=0
        )
        upper, lower = split(jnp.where(near_diagonal, square, 0.0))
        wide[turn, 0] = upper
        wide[turn, 1] = lower
    upper, lower = split(band(high, (seen, rows), radius + start - seen_start))
    tall[...] = jnp.concatenate([upper, upper, lower], axis=1)
    upper, lower = split(band(high[::-1], (keep, rows), radius + seen_start - keep * half))
    back[...] = jnp.concatenate([upper, upper, lower], axis=1)
    factors = [jnp.broadcast_to(tap, (16, LANES)) for tap in deep]
    spread[...] = jnp.zeros_like(spread)
    for step in range(taps):
        spread[step : step + 1] = factors[step][:1]
    for row, lane in chunks(rows, across):
        where = pl.ds(pl.multiple_of(start + row.start, 16), 16)
        terms = depth_terms(
            lambda place: estimate[place, where, lane], factors, 0, planes, range(planes), False
        )
        for plane, block in terms.items():
            part[plane, row, lane] = block


def prepare(packed, taps, source, estimate, after, rows, seen, keep):
    planes, _, across = estimate.shape
    return pl.pallas_call(
        functools.partial(prepare_kernel, packed, taps),
        out_shape=(
            jax.ShapeDtypeStruct((2, 2, across, across), BF16),
            jax.ShapeDtypeStruct((seen, 3 * rows), BF16),
            jax.ShapeDtypeStruct((keep, 3 * rows), BF16),
            jax.ShapeDtypeStruct((planes, rows, across), F32),
            jax.ShapeDtypeStruct((-(-taps // 8) * 8, LANES), F32),
        ),
        in_specs=[VMEM, VMEM, ANY],
        out_specs=(VMEM,) * 5,
        compiler_params=pltpu.CompilerParams(vmem_limit_bytes=LIMIT),
        name="prepare",
    )(source, estimate, after)


def spread_factors(spread, taps):
    return [jnp.broadcast_to(spread[step : step + 1, :], (16, LANES)) for step in range(taps)]


def fields_kernel(*refs):
    sets, (far, near, measured, swapped), refs = (refs[:5], refs[5:10]), refs[10:14], refs[14:]
    fields, sends, (blur_hi, blur_lo, plane_hi, plane_lo) = refs[:2], refs[2:-4], refs[-4:]
    planes = sets[0][3].shape[0]
    radius, rows, across = near.shape
    keep, seen = sets[0][2].shape[0], sets[0][1].shape[0]
    taps = 2 * radius + 1
    even = lax.axis_index("tile") % 2 == 0
    half = half_of(lax.axis_index("view"))
    seen_start = pl.multiple_of((2 * keep - seen) * half, 8)
    factors = [spread_factors(spread, taps) for _, _, _, _, spread in sets]
    for which, (_, _, _, part, _) in enumerate(sets):
        for row, lane in chunks(rows, across):

            def rim(place):
                if place < 0:
                    at = place + radius
                    return jnp.where(even, far[at, row, lane], near[at, row, lane])
                at = place - planes
                return jnp.where(even, near[at, row, lane], far[at, row, lane])

            below = depth_terms(rim, factors[which], -radius, 0, range(planes), False)
            above = depth_terms(rim, factors[which], planes, planes + radius, range(planes), False)
            for plane in range(planes):
                block = part[plane, row, lane]
                for term in (below[plane], above[plane]):
                    block = block if term is None else block + term
                upper, lower = split(block)
                at = slice(plane * rows + row.start, plane * rows + row.stop)
                blur_hi[which, at, lane] = upper
                blur_lo[which, at, lane] = lower
    lines = []
    for which, (wide, _, _, _, _) in enumerate(sets):
        upper, lower = wide[0, 0], wide[0, 1]
        lines.append(
            jnp.dot(blur_hi[which], upper, preferred_element_type=F32)
            + jnp.dot(blur_lo[which], upper, preferred_element_type=F32)
            + jnp.dot(blur_hi[which], lower, preferred_element_type=F32)
        )
    both = [(which, plane) for which in range(2) for plane in range(planes)]
    forwards = {}
    for which, plane in both:
        hi, lo = split(lines[which][plane * rows : (plane + 1) * rows])
        forwards[which, plane] = jnp.dot(
            sets[which][1][...], jnp.concatenate([hi, lo, hi], axis=0), preferred_element_type=F32
        )
    ratios = {}
    for which, plane in both:
        if which == 0:
            recorded = measured[0, plane, pl.ds(seen_start, seen), :]
        else:
            recorded = swapped[plane * seen : (plane + 1) * seen]
        ratio = recorded / forwards[which, plane]
        if rows > seen:
            ratio = jnp.concatenate([ratio, jnp.zeros((rows - seen, across), F32)], axis=0)
        ratios[which, plane] = split(ratio)
    turned = {}
    for which, plane in both:
        hi, lo = ratios[which, plane]
        turned[which, plane] = jnp.dot(
            sets[which][2][...], jnp.concatenate([hi, lo, hi], axis=0), preferred_element_type=F32
        )
    for which, plane in both:
        hi, lo = split(turned[which, plane])
        plane_hi[which, plane * keep : (plane + 1) * keep] = hi
        plane_lo[which, plane * keep : (plane + 1) * keep] = lo
    for which, (wide, _, _, _, _) in enumerate(sets):
        upper, lower = wide[1, 0], wide[1, 1]
        result = (
            jnp.dot(plane_hi[which], upper, preferred_element_type=F32)
            + jnp.dot(plane_lo[which], upper, preferred_element_type=F32)
            + jnp.dot(plane_hi[which], lower, preferred_element_type=F32)
        )
        fields[which][...] = result.reshape(planes, keep, across)
    for row, lane in chunks(keep, across):
        below, above = [], []
        for which in range(2):
            source = lambda place: fields[which][place, row, lane]
            outer = range(planes, planes + radius)
            below.append(depth_terms(source, factors[which], 0, planes, range(-radius, 0), True))
            above.append(depth_terms(source, factors[which], 0, planes, outer, True))
        part_at, inside = divmod(row.start, keep // PARTS)
        inside = slice(inside, inside + 16)
        for at in range(radius):
            down = below[0][at - radius] + below[1][at - radius]
            up = above[0][at + planes] + above[1][at + planes]
            sends[2 * part_at][at, inside, lane] = jnp.where(even, down, up)
            sends[2 * part_at + 1][at, inside, lane] = jnp.where(even, up, down)


def ratio_fields(own, others, far, near, measured, swapped):
    keep, planes = own[2].shape[0], own[3].shape[0]
    radius, rows, across = near.shape
    field = jax.ShapeDtypeStruct((planes, keep, across), F32)
    send = jax.ShapeDtypeStruct((radius, keep // PARTS, across), F32)
    return pl.pallas_call(
        fields_kernel,
        out_shape=(field,) * 2 + (send,) * (2 * PARTS),
        in_specs=[VMEM] * 14,
        out_specs=(VMEM,) * (2 + 2 * PARTS),
        scratch_shapes=[
            pltpu.VMEM((2, planes * rows, across), BF16),
            pltpu.VMEM((2, planes * rows, across), BF16),
            pltpu.VMEM((2, planes * keep, across), BF16),
            pltpu.VMEM((2, planes * keep, across), BF16),
        ],
        compiler_params=pltpu.CompilerParams(vmem_limit_bytes=LIMIT),
        name="ratio_fields",
    )(*own, *others, far, near, measured, swapped)


def own_kernel(taps, spread_own, spread_other, field_own, field_other, *inner):
    planes, keep, across = field_own.shape
    factors = [spread_factors(spread, taps) for spread in (spread_own, spread_other)]
    for row, lane in chunks(keep, across):
        parts = [
            depth_terms(
                lambda place: field[place, row, lane], factors[which], 0, planes, range(planes), True
            )
            for which, field in enumerate((field_own, field_other))
        ]
        part_at, inside = divmod(row.start, keep // PARTS)
        for plane in range(planes):
            inner[part_at][plane, inside : inside + 16, lane] = parts[0][plane] + parts[1][plane]


def own_planes(taps, spread_own, spread_other, field_own, field_other):
    planes, keep, across = field_own.shape
    return pl.pallas_call(
        functools.partial(own_kernel, taps),
        out_shape=(jax.ShapeDtypeStruct((planes, keep // PARTS, across), F32),) * PARTS,
        in_specs=[VMEM] * 4,
        out_specs=(VMEM,) * PARTS,
        compiler_params=pltpu.CompilerParams(vmem_limit_bytes=LIMIT),
        name="own_planes",
    )(spread_own, spread_other, field_own, field_other)


def rims_kernel(inner, far, near, *rest):
    correction = rest[-1]
    planes, radius = inner.shape[0], near.shape[0]
    even = lax.axis_index("tile") % 2 == 0
    for plane in range(planes):
        total = inner[plane]
        if plane < radius:
            total += jnp.where(even, far[plane], near[plane])
        if plane >= planes - radius:
            at = plane - planes + radius
            total += jnp.where(even, near[at], far[at])
        correction[plane] = total


def add_rims(inner, far, near, *after):
    return pl.pallas_call(
        rims_kernel,
        out_shape=jax.ShapeDtypeStruct(inner.shape, F32),
        in_specs=[VMEM] * 3 + [ANY] * len(after),
        out_specs=VMEM,
        compiler_params=pltpu.CompilerParams(vmem_limit_bytes=LIMIT),
        name="add_rims",
    )(inner, far, near, *after)


def table_rows(table):
    return jnp.concatenate([table[:8], table[8:]], axis=1)


def update_kernel(views, part, estimate, mine, other, *rest):
    planes, size, across = mine.shape
    result = rest[-1]
    half = half_of(lax.axis_index("view"))
    start = pl.multiple_of(size * (PARTS * half + part), 8)
    for plane in range(planes):
        held = estimate[plane, pl.ds(start, size)]
        at = slice(plane * size, (plane + 1) * size)
        result[at] = held * (mine[plane] + other[plane]) * (1.0 / views)
    spare = result.shape[0] - planes * size
    if spare:
        result[planes * size :] = jnp.zeros((spare, across), F32)


def update(views, part, estimate, mine, other, after):
    planes, size, across = mine.shape
    spare = 8 * (PARTS - 1 - part)
    return pl.pallas_call(
        functools.partial(update_kernel, views, part),
        out_shape=jax.ShapeDtypeStruct((planes * size + spare, across), F32),
        in_specs=[VMEM] * 3 + [ANY] * len(after),
        out_specs=VMEM,
        compiler_params=pltpu.CompilerParams(vmem_limit_bytes=LIMIT),
        name="update",
    )(estimate, mine, other, *after)


def slots_kernel(views, owner_row, index_row, picked, base):
    count = base.shape[0]
    slots = owner_row.shape[1]
    owner = owner_row[...]
    member = (lax.broadcasted_iota(jnp.int32, (count // views, slots), 0) == owner).astype(F32)
    upto = (
        lax.broadcasted_iota(jnp.int32, (slots, slots), 0)
        <= lax.broadcasted_iota(jnp.int32, (slots, slots), 1)
    ).astype(F32)
    running = jnp.dot(member, upto, preferred_element_type=F32)
    rank = jnp.sum(member * running, axis=0, keepdims=True).astype(jnp.int32) - 1
    named = lax.broadcasted_iota(jnp.int32, (count, slots), 0) // views == owner
    index = index_row[...].astype(F32)
    lanes = lax.broadcasted_iota(jnp.int32, (count, LANES), 1)
    result = jnp.zeros((count, LANES), F32)
    for place in range(CAP):
        chosen = named & (rank == place)
        picked[place * count : (place + 1) * count] = chosen.astype(F32)
        ids = jnp.sum(jnp.where(chosen, index, 0.0), axis=1, keepdims=True)
        result = jnp.where(lanes == place * WIDTH + IDS, ids, result)
    base[...] = result


def slot_places(tiles, views, label_owner, label_index):
    slots = label_index.shape[1]
    count = tiles * views
    return pl.pallas_call(
        functools.partial(slots_kernel, views),
        out_shape=(
            jax.ShapeDtypeStruct((CAP * count, slots), F32),
            jax.ShapeDtypeStruct((count, LANES), F32),
        ),
        in_specs=[VMEM, VMEM],
        out_specs=(VMEM, VMEM),
        compiler_params=pltpu.CompilerParams(vmem_limit_bytes=LIMIT),
        name="slot_places",
    )(label_owner.reshape(1, slots), label_index)


def merge_rows(blocks):
    rows = lax.broadcasted_iota(jnp.int32, blocks[0].shape, 0)
    step = 4
    while step:
        low = (rows & step) == 0
        half = len(blocks) // 2
        merged = []
        for one, two in zip(blocks[:half], blocks[half:]):
            kept = jnp.where(low, one, two)
            turned = jnp.where(low, two, one)
            moved = pltpu.roll(turned, step, 0)
            if step < 4:
                moved = jnp.where(low, pltpu.roll(turned, 8 - step, 0), moved)
            merged.append(kept + moved)
        blocks = merged
        step //= 2
    return blocks[0]


def moments_kernel(views, depth_total, part, estimate, labels, picked, base, correction, *refs):
    begun, (sent, held, sums, table) = refs[:-4], refs[-4:]
    planes, size, across = correction.shape
    height_total = estimate.shape[1]
    slots = picked.shape[1]
    half = half_of(lax.axis_index("view"))
    first = (lax.axis_index("tile") * planes).astype(F32) + 0.5
    start = pl.multiple_of(size * (PARTS * half + part), 8)
    held[...] = estimate[:, pl.ds(start, size)] * correction[...] * (1.0 / views)
    group = 16
    spot = lax.broadcasted_iota(jnp.int32, (across, LANES), 0)
    lanes = lax.broadcasted_iota(jnp.int32, (across, LANES), 1)
    low = (spot * spot) & 255
    factors = jnp.where(lanes == 0, 1, jnp.where(lanes == 1, spot, 0))
    factors = jnp.where(lanes == 2, spot * spot - low, jnp.where(lanes == 3, low, factors))
    factors = factors.astype(F32).astype(BF16)
    base_row = lax.broadcasted_iota(jnp.int32, (8, across), 0)

    def one_group(number, carry):
        held_parts = []
        for pair in range(0, group, 2):
            slot = [number * group + pair, number * group + pair + 1]
            parts = [[None] * 6 for _ in slot]
            for row in range(0, size, 8):
                high = ((base_row + (row + start)).astype(F32) + 0.5) * (1.0 / height_total)
                flat, once, twice = [[jnp.zeros((8, across), F32) for _ in slot] for _ in range(3)]
                for plane in reversed(range(planes)):
                    mark = labels[plane, pl.ds(pl.multiple_of(start + row, 8), 8)]
                    value = held[plane, row : row + 8]
                    for at in range(2):
                        flat[at] = flat[at] + jnp.where(mark == slot[at], value, 0.0)
                        if plane > 0:
                            once[at] = once[at] + flat[at]
                            twice[at] = twice[at] + once[at]
                for at in range(2):
                    scaled = flat[at] * high
                    terms = (flat[at], scaled, scaled * high, once[at], once[at] * high, twice[at])
                    parts[at] = [new if old is None else old + new for old, new in zip(parts[at], terms)]
            held_parts += parts
            if len(held_parts) == 8:
                for kind in range(6):
                    row = kind * group + pair + 2 - 8
                    sums[row : row + 8, :] = merge_rows([parts[kind] for parts in held_parts])
                held_parts = []
        whole = sums[...]
        upper, rest = split(whole)
        rest = whole - upper.astype(F32)
        middle, lower = split(rest)
        lines = jnp.dot(
            jnp.concatenate([upper, middle, lower], axis=0), factors, preferred_element_type=F32
        )
        count = 6 * group
        lines = lines[:count] + lines[count : 2 * count] + lines[2 * count :]
        flat, high_flat, square_flat, once, high_once, twice = [
            lines[kind * group : (kind + 1) * group] for kind in range(6)
        ]
        deep = (first * flat + once) * (1.0 / depth_total)
        deep_high = (first * high_flat + high_once) * (1.0 / depth_total)
        deeper = first * (first * flat + 2.0 * once) + (2.0 * twice - once)
        deeper = deeper * (1.0 / depth_total**2)
        total = flat
        for kind, sums_of in enumerate((high_flat, square_flat, deep, deep_high, deeper), 1):
            total += pltpu.roll(sums_of, 4 * kind, 1)
        rows = pl.ds(pl.multiple_of(number * group, group), group)
        target = table if part == PARTS - 1 else sent
        target[rows, :] = total + begun[0][rows, :] if begun else total
        return carry

    lax.fori_loop(0, slots // group, one_group, 0)
    if part < PARTS - 1:
        return
    rows = jnp.dot(
        picked[...], table[...], precision=lax.Precision.HIGHEST, preferred_element_type=F32
    )
    total = base[...]
    count = total.shape[0]
    for place in range(CAP):
        total += pltpu.roll(rows[place * count : (place + 1) * count], place * WIDTH, 1)
    sent[...] = total


def moment_rows(views, tiles, part, estimate, correction, labels, places, begun):
    planes, size, across = correction.shape
    slots = places[0].shape[1]
    count = places[1].shape[0] if part == PARTS - 1 else slots
    return pl.pallas_call(
        functools.partial(moments_kernel, views, tiles * planes, part),
        out_shape=jax.ShapeDtypeStruct((count, LANES), F32),
        in_specs=[VMEM] * (5 + len(begun)),
        out_specs=VMEM,
        scratch_shapes=[
            pltpu.VMEM((planes, size, across), F32),
            pltpu.VMEM((6 * 16, across), F32),
            pltpu.VMEM((slots, LANES), F32),
        ],
        compiler_params=pltpu.CompilerParams(vmem_limit_bytes=LIMIT),
        name="moment_rows",
    )(estimate, labels, *places, correction, *begun)


def segments_kernel(across, scale, rows, moments):
    whole = rows[...]
    parts = [whole] + [pltpu.roll(whole, LANES - place * WIDTH, 1) for place in range(1, CAP)]
    values = jnp.concatenate(parts, axis=0)
    ids = values[:, IDS : IDS + 1].astype(jnp.int32)
    spots = lax.broadcasted_iota(jnp.int32, (values.shape[0], NUC_DEV), 1)
    picked = (ids == spots).astype(F32)
    full = lax.dot_general(
        values, picked, (((0,), (0,)), ((), ())),
        precision=lax.Precision.HIGHEST, preferred_element_type=F32,
    )
    mass, high, higher, deep, deep_high, deeper = [full[4 * kind : 4 * kind + 4] for kind in range(6)]
    flat = lambda sums: sums[0:1]
    line = lambda sums: (sums[1:2] + 0.5 * sums[0:1]) * (1.0 / across)
    square = lambda sums: (sums[2:3] + sums[3:4] + sums[1:2] + 0.25 * sums[0:1]) * (1.0 / across**2)
    total = flat(mass)
    sums = jnp.concatenate(
        [
            flat(deep), flat(high), line(mass),
            flat(deeper), flat(higher), square(mass),
            flat(deep_high), line(deep), line(high),
        ],
        axis=0,
    )
    moments[...] = jnp.concatenate([total * scale, sums / jnp.maximum(total, 1.0)], axis=0)


def nucleus_table(across, scale, rows):
    return pl.pallas_call(
        functools.partial(segments_kernel, across, scale),
        out_shape=jax.ShapeDtypeStruct((MOM, NUC_DEV), F32),
        in_specs=[VMEM],
        out_specs=VMEM,
        compiler_params=pltpu.CompilerParams(vmem_limit_bytes=LIMIT),
        cost_estimate=pl.CostEstimate(flops=10_000_000_000, bytes_accessed=20_000_000, transcendentals=0),
        name="nucleus_table",
    )(rows)


def stores(pieces, sources, whole, half, sems):
    keep = whole.shape[1] // 2
    copies = []
    for number, ((first, size), source) in enumerate(zip(pieces, sources)):
        start = pl.multiple_of(keep * half + first, 8)
        for plane in range(whole.shape[0]):
            copies.append(
                pltpu.make_async_copy(
                    source.at[pl.ds(plane * size, size)],
                    whole.at[plane, pl.ds(start, size)],
                    sems.at[number, plane],
                )
            )
    for copy in copies:
        copy.start()
    return copies


def token_kernel(source, token):
    token[...] = source[:8, :LANES]


def token_of(source):
    return pl.pallas_call(
        token_kernel,
        out_shape=jax.ShapeDtypeStruct((8, LANES), F32),
        in_specs=[VMEM],
        out_specs=VMEM,
        compiler_params=pltpu.CompilerParams(vmem_limit_bytes=LIMIT),
        name="token_of",
    )(source)


def begin_kernel(pieces, *refs):
    sources, (whole, sems) = refs[:-2], refs[-2:]
    for copy in stores(pieces, sources, whole, half_of(lax.axis_index("view")), sems):
        copy.wait()


def begin_result(pieces, shape, mine):
    return pl.pallas_call(
        functools.partial(begin_kernel, pieces),
        out_shape=jax.ShapeDtypeStruct(shape, F32),
        in_specs=[VMEM] * len(mine),
        out_specs=ANY,
        scratch_shapes=[pltpu.SemaphoreType.DMA((len(pieces), shape[0]))],
        compiler_params=pltpu.CompilerParams(vmem_limit_bytes=LIMIT),
        name="begin_result",
    )(*mine)


def finish_kernel(pieces, begun, *refs):
    others, (whole, sems) = refs[:-2], refs[-2:]
    for copy in stores(pieces, others, whole, 1 - half_of(lax.axis_index("view")), sems):
        copy.wait()


def finish(pieces, begun, others):
    return pl.pallas_call(
        functools.partial(finish_kernel, pieces),
        out_shape=jax.ShapeDtypeStruct(begun.shape, F32),
        in_specs=[ANY] + [VMEM] * len(others),
        out_specs=ANY,
        input_output_aliases={0: 0},
        scratch_shapes=[pltpu.SemaphoreType.DMA((len(pieces), begun.shape[0]))],
        compiler_params=pltpu.CompilerParams(vmem_limit_bytes=LIMIT),
        name="finish",
    )(begun, *others)


def on_device(estimate, measured, kernels, labels, label_owner, label_index):
    tiles, views = lax.axis_size("tile"), lax.axis_size("view")
    planes, height, across = estimate.shape
    taps = kernels.shape[2]
    radius = (taps - 1) // 2
    keep = height // 2
    seen = min(height, -(-(keep + radius) // 8) * 8)
    rows = min(height, -(-(keep + 2 * radius) // 16) * 16)
    near_pairs = [(i, i ^ 1) for i in range(tiles)]
    far_pairs = [(i, i + 1) for i in range(1, tiles - 1, 2)]
    far_pairs = far_pairs + [(b, a) for a, b in far_pairs]
    partner = [(i, i ^ 1) for i in range(views)]
    across_pairs = [(i, i ^ 3) for i in range(views)]

    lines = jnp.transpose(kernels, (1, 0, 2))
    packed = view_out(measured, lines, seen)
    swapped = lax.ppermute(packed, "view", partner)
    to_far, to_near = rims_out(estimate, radius, rows)
    far = lax.ppermute(to_far, "tile", far_pairs)
    near = lax.ppermute(to_near, "tile", near_pairs)
    places = slot_places(tiles, views, label_owner, label_index)
    own = prepare(False, taps, lines, estimate, places[1], rows, seen, keep)
    others = prepare(True, taps, swapped, estimate, lines, rows, seen, keep)
    field_own, field_other, *sends = ratio_fields(own, others, far, near, measured, swapped)
    rims = [
        lax.ppermute(send, "tile", pairs) for send, pairs in zip(sends, (far_pairs, near_pairs) * PARTS)
    ]
    inner = own_planes(taps, own[4], others[4], field_own, field_other)
    mine, other, sums = [], [], []
    for part in range(PARTS):
        mine.append(add_rims(inner[part], *rims[2 * part : 2 * part + 2], *sums))
        other.append(lax.ppermute(mine[part], "view", across_pairs))
        sums = [moment_rows(views, tiles, part, estimate, mine[part], labels, places, sums)]
    sent = sums[0]
    got = lax.all_to_all(sent, ("tile", "view"), split_axis=0, concat_axis=0, tiled=True)
    size = keep // PARTS
    pieces = [(part * size, size) for part in range(PARTS)]
    new_mine, new_other, token = [], [], [sent]
    for part in range(PARTS):
        new_mine.append(update(views, part, estimate, mine[part], other[part], token))
        new_other.append(lax.ppermute(new_mine[part], "view", partner))
        token = [token_of(new_mine[part])]
    scale = label_index.shape[1] / (planes * height * across)
    moments = nucleus_table(across, scale, got)
    begun = begin_result(pieces, estimate.shape, new_mine)
    return finish(pieces, begun, new_other), moments


def solution(mesh):
    placed = (
        P("tile", None, None),
        P("view", "tile", None, None),
        P("view", None, None),
        P("tile", None, None),
        P("tile", None, None),
        P("tile", None),
    )
    return jax.shard_map(
        on_device,
        mesh=mesh,
        in_specs=placed,
        out_specs=(P("tile", None, None), P(None, "tile")),
        check_vma=False,
    )
```

```python
import functools

import jax
import jax.numpy as jnp
from jax import lax
from jax.experimental import pallas as pl
from jax.experimental.pallas import tpu as pltpu
from jax.sharding import PartitionSpec as P

MOM = 10
CAP = 5
WIDTH = 25
NUC_DEV = 128
LANES = 128
PARTS = 2
TAIL = 8
IDS = 24
F32 = jnp.float32
BF16 = jnp.bfloat16
ANY = pl.BlockSpec(memory_space=pl.ANY)
VMEM = pl.BlockSpec(memory_space=pltpu.VMEM)
LIMIT = 32 * 1024 * 1024


def half_of(view):
    return (view ^ (view >> 1)) & 1


def split(value):
    upper = value.astype(BF16)
    return upper, (value - upper.astype(F32)).astype(BF16)


def band(taps, shape, offset):
    rows = lax.broadcasted_iota(jnp.int32, shape, 0)
    cols = lax.broadcasted_iota(jnp.int32, shape, 1)
    place = cols - rows + offset
    result = jnp.zeros(shape, F32)
    for step, tap in enumerate(taps):
        result = jnp.where(place == step, tap, result)
    return result


def depth_terms(source, weights, first, last, planes, flipped):
    radius = (len(weights) - 1) // 2
    totals = {plane: None for plane in planes}
    for place in range(first, last):
        block = None
        for plane in planes:
            step = plane - place + radius if flipped else place - plane + radius
            if 0 <= step < len(weights):
                block = source(place) if block is None else block
                term = weights[step] * block
                totals[plane] = term if totals[plane] is None else totals[plane] + term
    return totals


def chunks(rows, across):
    return [(slice(row, row + 16), slice(lane, lane + LANES)) for row in range(0, rows, 16) for lane in range(0, across, LANES)]


def rims_out_kernel(estimate, to_far, to_near):
    planes, radius, rows = estimate.shape[0], to_far.shape[0], to_far.shape[1]
    odd = lax.axis_index("tile") % 2
    half = half_of(lax.axis_index("view"))
    start = pl.multiple_of((estimate.shape[1] - rows) * half, 8)
    to_far[...] = estimate[pl.ds(odd, radius), pl.ds(start, rows)]
    to_near[...] = estimate[pl.ds(1 - odd, radius), pl.ds(start, rows)]


def rims_out(estimate, radius, rows):
    shape = jax.ShapeDtypeStruct((radius, rows, estimate.shape[2]), F32)
    return pl.pallas_call(
        rims_out_kernel,
        out_shape=(shape, shape),
        in_specs=[VMEM],
        out_specs=(VMEM, VMEM),
        compiler_params=pltpu.CompilerParams(vmem_limit_bytes=LIMIT),
        name="rims_out",
    )(estimate)


def view_out_kernel(seen, measured, taps, packed):
    planes, height = measured.shape[1], measured.shape[2]
    half = half_of(lax.axis_index("view"))
    start = pl.multiple_of((height - seen) * (1 - half), 8)
    for plane in range(planes):
        packed[plane * seen : (plane + 1) * seen] = measured[0, plane, pl.ds(start, seen)]
    packed[planes * seen :] = jnp.zeros((TAIL, packed.shape[1]), F32)
    for axis in range(taps.shape[0]):
        at = planes * seen + axis
        packed[at : at + 1, : taps.shape[2]] = taps[axis]


def view_out(measured, kernels, seen):
    _, planes, _, across = measured.shape
    return pl.pallas_call(
        functools.partial(view_out_kernel, seen),
        out_shape=jax.ShapeDtypeStruct((planes * seen + TAIL, across), F32),
        in_specs=[VMEM, VMEM],
        out_specs=VMEM,
        compiler_params=pltpu.CompilerParams(vmem_limit_bytes=LIMIT),
        name="view_out",
    )(measured, kernels)


def prepare_kernel(packed, taps, source, estimate, after, wide, tall, back, part, spread):
    half = half_of(lax.axis_index("view"))
    across = wide.shape[-1]
    rows, keep, seen = part.shape[1], back.shape[0], tall.shape[0]
    planes = estimate.shape[0]
    radius = (taps - 1) // 2
    at = source.shape[0] - TAIL
    if packed:
        raw = source[at : at + 3, :taps]
    else:
        raw = jnp.concatenate([source[axis] for axis in range(source.shape[0])], axis=0)
    weights = raw / jnp.sum(raw, axis=-1, keepdims=True)
    deep, high, flat = [[weights[axis : axis + 1, t : t + 1] for t in range(taps)] for axis in range(3)]
    start = pl.multiple_of((2 * keep - rows) * half, 16)
    seen_start = (2 * keep - seen) * half
    near_diagonal = jnp.abs(
        lax.broadcasted_iota(jnp.int32, (across, across), 1)
        - lax.broadcasted_iota(jnp.int32, (across, across), 0)
    ) <= radius
    for turn, line in enumerate((flat[::-1], flat)):
        first_row = jnp.concatenate(
            line[radius:] + [jnp.zeros((1, across - taps), F32)] + line[:radius], axis=1
        )
        square = pltpu.roll(
            jnp.broadcast_to(first_row, (across, across)), 0, 1, stride=1, stride_axis=0
        )
        upper, lower = split(jnp.where(near_diagonal, square, 0.0))
        wide[turn, 0] = upper
        wide[turn, 1] = lower
    upper, lower = split(band(high, (seen, rows), radius + start - seen_start))
    tall[...] = jnp.concatenate([upper, upper, lower], axis=1)
    upper, lower = split(band(high[::-1], (keep, rows), radius + seen_start - keep * half))
    back[...] = jnp.concatenate([upper, upper, lower], axis=1)
    factors = [jnp.broadcast_to(tap, (16, LANES)) for tap in deep]
    spread[...] = jnp.zeros_like(spread)
    for step in range(taps):
        spread[step : step + 1] = factors[step][:1]
    for row, lane in chunks(rows, across):
        where = pl.ds(pl.multiple_of(start + row.start, 16), 16)
        terms = depth_terms(
            lambda place: estimate[place, where, lane], factors, 0, planes, range(planes), False
        )
        for plane, block in terms.items():
            part[plane, row, lane] = block


def prepare(packed, taps, source, estimate, after, rows, seen, keep):
    planes, _, across = estimate.shape
    return pl.pallas_call(
        functools.partial(prepare_kernel, packed, taps),
        out_shape=(
            jax.ShapeDtypeStruct((2, 2, across, across), BF16),
            jax.ShapeDtypeStruct((seen, 3 * rows), BF16),
            jax.ShapeDtypeStruct((keep, 3 * rows), BF16),
            jax.ShapeDtypeStruct((planes, rows, across), F32),
            jax.ShapeDtypeStruct((-(-taps // 8) * 8, LANES), F32),
        ),
        in_specs=[VMEM, VMEM, ANY],
        out_specs=(VMEM,) * 5,
        compiler_params=pltpu.CompilerParams(vmem_limit_bytes=LIMIT),
        name="prepare",
    )(source, estimate, after)


def spread_factors(spread, taps):
    return [jnp.broadcast_to(spread[step : step + 1, :], (16, LANES)) for step in range(taps)]


def fields_kernel(*refs):
    sets, (far, near, measured, swapped), refs = (refs[:5], refs[5:10]), refs[10:14], refs[15:]
    fields, sends, (blur_hi, blur_lo, plane_hi, plane_lo) = refs[:2], refs[2:-4], refs[-4:]
    planes = sets[0][3].shape[0]
    radius, rows, across = near.shape
    keep, seen = sets[0][2].shape[0], sets[0][1].shape[0]
    taps = 2 * radius + 1
    even = lax.axis_index("tile") % 2 == 0
    half = half_of(lax.axis_index("view"))
    seen_start = pl.multiple_of((2 * keep - seen) * half, 8)
    factors = [spread_factors(spread, taps) for _, _, _, _, spread in sets]
    for which, (_, _, _, part, _) in enumerate(sets):
        for row, lane in chunks(rows, across):

            def rim(place):
                if place < 0:
                    at = place + radius
                    return jnp.where(even, far[at, row, lane], near[at, row, lane])
                at = place - planes
                return jnp.where(even, near[at, row, lane], far[at, row, lane])

            below = depth_terms(rim, factors[which], -radius, 0, range(planes), False)
            above = depth_terms(rim, factors[which], planes, planes + radius, range(planes), False)
            for plane in range(planes):
                block = part[plane, row, lane]
                for term in (below[plane], above[plane]):
                    block = block if term is None else block + term
                upper, lower = split(block)
                at = slice(plane * rows + row.start, plane * rows + row.stop)
                blur_hi[which, at, lane] = upper
                blur_lo[which, at, lane] = lower
    lines = []
    for which, (wide, _, _, _, _) in enumerate(sets):
        upper, lower = wide[0, 0], wide[0, 1]
        lines.append(
            jnp.dot(blur_hi[which], upper, preferred_element_type=F32)
            + jnp.dot(blur_lo[which], upper, preferred_element_type=F32)
            + jnp.dot(blur_hi[which], lower, preferred_element_type=F32)
        )
    both = [(which, plane) for which in range(2) for plane in range(planes)]
    forwards = {}
    for which, plane in both:
        hi, lo = split(lines[which][plane * rows : (plane + 1) * rows])
        forwards[which, plane] = jnp.dot(
            sets[which][1][...], jnp.concatenate([hi, lo, hi], axis=0), preferred_element_type=F32
        )
    ratios = {}
    for which, plane in both:
        if which == 0:
            recorded = measured[0, plane, pl.ds(seen_start, seen), :]
        else:
            recorded = swapped[plane * seen : (plane + 1) * seen]
        ratio = recorded / forwards[which, plane]
        if rows > seen:
            ratio = jnp.concatenate([ratio, jnp.zeros((rows - seen, across), F32)], axis=0)
        ratios[which, plane] = split(ratio)
    turned = {}
    for which, plane in both:
        hi, lo = ratios[which, plane]
        turned[which, plane] = jnp.dot(
            sets[which][2][...], jnp.concatenate([hi, lo, hi], axis=0), preferred_element_type=F32
        )
    for which, plane in both:
        hi, lo = split(turned[which, plane])
        plane_hi[which, plane * keep : (plane + 1) * keep] = hi
        plane_lo[which, plane * keep : (plane + 1) * keep] = lo
    for which, (wide, _, _, _, _) in enumerate(sets):
        upper, lower = wide[1, 0], wide[1, 1]
        result = (
            jnp.dot(plane_hi[which], upper, preferred_element_type=F32)
            + jnp.dot(plane_lo[which], upper, preferred_element_type=F32)
            + jnp.dot(plane_hi[which], lower, preferred_element_type=F32)
        )
        fields[which][...] = result.reshape(planes, keep, across)
    for row, lane in chunks(keep, across):
        below, above = [], []
        for which in range(2):
            source = lambda place: fields[which][place, row, lane]
            outer = range(planes, planes + radius)
            below.append(depth_terms(source, factors[which], 0, planes, range(-radius, 0), True))
            above.append(depth_terms(source, factors[which], 0, planes, outer, True))
        part_at, inside = divmod(row.start, keep // PARTS)
        inside = slice(inside, inside + 16)
        for at in range(radius):
            down = below[0][at - radius] + below[1][at - radius]
            up = above[0][at + planes] + above[1][at + planes]
            sends[2 * part_at][at, inside, lane] = jnp.where(even, down, up)
            sends[2 * part_at + 1][at, inside, lane] = jnp.where(even, up, down)


def ratio_fields(own, others, far, near, measured, swapped, after):
    keep, planes = own[2].shape[0], own[3].shape[0]
    radius, rows, across = near.shape
    field = jax.ShapeDtypeStruct((planes, keep, across), F32)
    send = jax.ShapeDtypeStruct((radius, keep // PARTS, across), F32)
    return pl.pallas_call(
        fields_kernel,
        out_shape=(field,) * 2 + (send,) * (2 * PARTS),
        in_specs=[VMEM] * 14 + [ANY],
        out_specs=(VMEM,) * (2 + 2 * PARTS),
        scratch_shapes=[
            pltpu.VMEM((2, planes * rows, across), BF16),
            pltpu.VMEM((2, planes * rows, across), BF16),
            pltpu.VMEM((2, planes * keep, across), BF16),
            pltpu.VMEM((2, planes * keep, across), BF16),
        ],
        compiler_params=pltpu.CompilerParams(vmem_limit_bytes=LIMIT),
        name="ratio_fields",
    )(*own, *others, far, near, measured, swapped, after)


def own_kernel(taps, spread_own, spread_other, field_own, field_other, *inner):
    planes, keep, across = field_own.shape
    factors = [spread_factors(spread, taps) for spread in (spread_own, spread_other)]
    for row, lane in chunks(keep, across):
        parts = [
            depth_terms(
                lambda place: field[place, row, lane], factors[which], 0, planes, range(planes), True
            )
            for which, field in enumerate((field_own, field_other))
        ]
        part_at, inside = divmod(row.start, keep // PARTS)
        for plane in range(planes):
            inner[part_at][plane, inside : inside + 16, lane] = parts[0][plane] + parts[1][plane]


def own_planes(taps, spread_own, spread_other, field_own, field_other):
    planes, keep, across = field_own.shape
    return pl.pallas_call(
        functools.partial(own_kernel, taps),
        out_shape=(jax.ShapeDtypeStruct((planes, keep // PARTS, across), F32),) * PARTS,
        in_specs=[VMEM] * 4,
        out_specs=(VMEM,) * PARTS,
        compiler_params=pltpu.CompilerParams(vmem_limit_bytes=LIMIT),
        name="own_planes",
    )(spread_own, spread_other, field_own, field_other)


def rims_kernel(inner, far, near, *rest):
    correction = rest[-1]
    planes, radius = inner.shape[0], near.shape[0]
    even = lax.axis_index("tile") % 2 == 0
    for plane in range(planes):
        total = inner[plane]
        if plane < radius:
            total += jnp.where(even, far[plane], near[plane])
        if plane >= planes - radius:
            at = plane - planes + radius
            total += jnp.where(even, near[at], far[at])
        correction[plane] = total


def add_rims(inner, far, near, *after):
    return pl.pallas_call(
        rims_kernel,
        out_shape=jax.ShapeDtypeStruct(inner.shape, F32),
        in_specs=[VMEM] * 3 + [ANY] * len(after),
        out_specs=VMEM,
        compiler_params=pltpu.CompilerParams(vmem_limit_bytes=LIMIT),
        name="add_rims",
    )(inner, far, near, *after)


def table_rows(table):
    return jnp.concatenate([table[:8], table[8:]], axis=1)


def update_kernel(views, part, estimate, mine, other, *rest):
    planes, size, across = mine.shape
    result = rest[-1]
    half = half_of(lax.axis_index("view"))
    start = pl.multiple_of(size * (PARTS * half + part), 8)
    for plane in range(planes):
        held = estimate[plane, pl.ds(start, size)]
        at = slice(plane * size, (plane + 1) * size)
        result[at] = held * (mine[plane] + other[plane]) * (1.0 / views)
    spare = result.shape[0] - planes * size
    if spare:
        result[planes * size :] = jnp.zeros((spare, across), F32)


def update(views, part, estimate, mine, other, after):
    planes, size, across = mine.shape
    spare = 8 * (PARTS - 1 - part)
    return pl.pallas_call(
        functools.partial(update_kernel, views, part),
        out_shape=jax.ShapeDtypeStruct((planes * size + spare, across), F32),
        in_specs=[VMEM] * 3 + [ANY] * len(after),
        out_specs=VMEM,
        compiler_params=pltpu.CompilerParams(vmem_limit_bytes=LIMIT),
        name="update",
    )(estimate, mine, other, *after)


def slots_kernel(views, owner_row, index_row, picked, base):
    count = base.shape[0]
    slots = owner_row.shape[1]
    owner = owner_row[...]
    member = (lax.broadcasted_iota(jnp.int32, (count // views, slots), 0) == owner).astype(F32)
    upto = (
        lax.broadcasted_iota(jnp.int32, (slots, slots), 0)
        <= lax.broadcasted_iota(jnp.int32, (slots, slots), 1)
    ).astype(F32)
    running = jnp.dot(member, upto, preferred_element_type=F32)
    rank = jnp.sum(member * running, axis=0, keepdims=True).astype(jnp.int32) - 1
    named = lax.broadcasted_iota(jnp.int32, (count, slots), 0) // views == owner
    index = index_row[...].astype(F32)
    lanes = lax.broadcasted_iota(jnp.int32, (count, LANES), 1)
    result = jnp.zeros((count, LANES), F32)
    for place in range(CAP):
        chosen = named & (rank == place)
        picked[place * count : (place + 1) * count] = chosen.astype(F32)
        ids = jnp.sum(jnp.where(chosen, index, 0.0), axis=1, keepdims=True)
        result = jnp.where(lanes == place * WIDTH + IDS, ids, result)
    base[...] = result


def slot_places(tiles, views, label_owner, label_index):
    slots = label_index.shape[1]
    count = tiles * views
    return pl.pallas_call(
        functools.partial(slots_kernel, views),
        out_shape=(
            jax.ShapeDtypeStruct((CAP * count, slots), F32),
            jax.ShapeDtypeStruct((count, LANES), F32),
        ),
        in_specs=[VMEM, VMEM],
        out_specs=(VMEM, VMEM),
        compiler_params=pltpu.CompilerParams(vmem_limit_bytes=LIMIT),
        name="slot_places",
    )(label_owner.reshape(1, slots), label_index)


def merge_rows(blocks):
    rows = lax.broadcasted_iota(jnp.int32, blocks[0].shape, 0)
    step = 4
    while step:
        low = (rows & step) == 0
        half = len(blocks) // 2
        merged = []
        for one, two in zip(blocks[:half], blocks[half:]):
            kept = jnp.where(low, one, two)
            turned = jnp.where(low, two, one)
            moved = pltpu.roll(turned, step, 0)
            if step < 4:
                moved = jnp.where(low, pltpu.roll(turned, 8 - step, 0), moved)
            merged.append(kept + moved)
        blocks = merged
        step //= 2
    return blocks[0]


def moments_kernel(views, depth_total, part, estimate, labels, picked, base, correction, *refs):
    begun, (sent, held, sums, table) = refs[:-4], refs[-4:]
    planes, size, across = correction.shape
    height_total = estimate.shape[1]
    slots = picked.shape[1]
    half = half_of(lax.axis_index("view"))
    first = (lax.axis_index("tile") * planes).astype(F32) + 0.5
    start = pl.multiple_of(size * (PARTS * half + part), 8)
    held[...] = estimate[:, pl.ds(start, size)] * correction[...] * (1.0 / views)
    group = 16
    spot = lax.broadcasted_iota(jnp.int32, (across, LANES), 0)
    lanes = lax.broadcasted_iota(jnp.int32, (across, LANES), 1)
    low = (spot * spot) & 255
    factors = jnp.where(lanes == 0, 1, jnp.where(lanes == 1, spot, 0))
    factors = jnp.where(lanes == 2, spot * spot - low, jnp.where(lanes == 3, low, factors))
    factors = factors.astype(F32).astype(BF16)
    base_row = lax.broadcasted_iota(jnp.int32, (8, across), 0)

    def one_group(number, carry):
        held_parts = []
        for pair in range(0, group, 2):
            slot = [number * group + pair, number * group + pair + 1]
            parts = [[None] * 6 for _ in slot]
            for row in range(0, size, 8):
                high = ((base_row + (row + start)).astype(F32) + 0.5) * (1.0 / height_total)
                flat, once, twice = [[jnp.zeros((8, across), F32) for _ in slot] for _ in range(3)]
                for plane in reversed(range(planes)):
                    mark = labels[plane, pl.ds(pl.multiple_of(start + row, 8), 8)]
                    value = held[plane, row : row + 8]
                    for at in range(2):
                        flat[at] = flat[at] + jnp.where(mark == slot[at], value, 0.0)
                        if plane > 0:
                            once[at] = once[at] + flat[at]
                            twice[at] = twice[at] + once[at]
                for at in range(2):
                    scaled = flat[at] * high
                    terms = (flat[at], scaled, scaled * high, once[at], once[at] * high, twice[at])
                    parts[at] = [new if old is None else old + new for old, new in zip(parts[at], terms)]
            held_parts += parts
            if len(held_parts) == 8:
                for kind in range(6):
                    row = kind * group + pair + 2 - 8
                    sums[row : row + 8, :] = merge_rows([parts[kind] for parts in held_parts])
                held_parts = []
        whole = sums[...]
        upper, rest = split(whole)
        rest = whole - upper.astype(F32)
        middle, lower = split(rest)
        lines = jnp.dot(
            jnp.concatenate([upper, middle, lower], axis=0), factors, preferred_element_type=F32
        )
        count = 6 * group
        lines = lines[:count] + lines[count : 2 * count] + lines[2 * count :]
        flat, high_flat, square_flat, once, high_once, twice = [
            lines[kind * group : (kind + 1) * group] for kind in range(6)
        ]
        deep = (first * flat + once) * (1.0 / depth_total)
        deep_high = (first * high_flat + high_once) * (1.0 / depth_total)
        deeper = first * (first * flat + 2.0 * once) + (2.0 * twice - once)
        deeper = deeper * (1.0 / depth_total**2)
        total = flat
        for kind, sums_of in enumerate((high_flat, square_flat, deep, deep_high, deeper), 1):
            total += pltpu.roll(sums_of, 4 * kind, 1)
        rows = pl.ds(pl.multiple_of(number * group, group), group)
        target = table if part == PARTS - 1 else sent
        target[rows, :] = total + begun[0][rows, :] if begun else total
        return carry

    lax.fori_loop(0, slots // group, one_group, 0)
    if part < PARTS - 1:
        return
    rows = jnp.dot(
        picked[...], table[...], precision=lax.Precision.HIGHEST, preferred_element_type=F32
    )
    total = base[...]
    count = total.shape[0]
    for place in range(CAP):
        total += pltpu.roll(rows[place * count : (place + 1) * count], place * WIDTH, 1)
    sent[...] = total


def moment_rows(views, tiles, part, estimate, correction, labels, places, begun):
    planes, size, across = correction.shape
    slots = places[0].shape[1]
    count = places[1].shape[0] if part == PARTS - 1 else slots
    return pl.pallas_call(
        functools.partial(moments_kernel, views, tiles * planes, part),
        out_shape=jax.ShapeDtypeStruct((count, LANES), F32),
        in_specs=[VMEM] * (5 + len(begun)),
        out_specs=VMEM,
        scratch_shapes=[
            pltpu.VMEM((planes, size, across), F32),
            pltpu.VMEM((6 * 16, across), F32),
            pltpu.VMEM((slots, LANES), F32),
        ],
        compiler_params=pltpu.CompilerParams(vmem_limit_bytes=LIMIT),
        name="moment_rows",
    )(estimate, labels, *places, correction, *begun)


def segments_kernel(across, scale, rows, moments):
    whole = rows[...]
    parts = [whole] + [pltpu.roll(whole, LANES - place * WIDTH, 1) for place in range(1, CAP)]
    values = jnp.concatenate(parts, axis=0)
    ids = values[:, IDS : IDS + 1].astype(jnp.int32)
    spots = lax.broadcasted_iota(jnp.int32, (values.shape[0], NUC_DEV), 1)
    picked = (ids == spots).astype(F32)
    full = lax.dot_general(
        values, picked, (((0,), (0,)), ((), ())),
        precision=lax.Precision.HIGHEST, preferred_element_type=F32,
    )
    mass, high, higher, deep, deep_high, deeper = [full[4 * kind : 4 * kind + 4] for kind in range(6)]
    flat = lambda sums: sums[0:1]
    line = lambda sums: (sums[1:2] + 0.5 * sums[0:1]) * (1.0 / across)
    square = lambda sums: (sums[2:3] + sums[3:4] + sums[1:2] + 0.25 * sums[0:1]) * (1.0 / across**2)
    total = flat(mass)
    sums = jnp.concatenate(
        [
            flat(deep), flat(high), line(mass),
            flat(deeper), flat(higher), square(mass),
            flat(deep_high), line(deep), line(high),
        ],
        axis=0,
    )
    moments[...] = jnp.concatenate([total * scale, sums / jnp.maximum(total, 1.0)], axis=0)


def nucleus_table(across, scale, rows):
    return pl.pallas_call(
        functools.partial(segments_kernel, across, scale),
        out_shape=jax.ShapeDtypeStruct((MOM, NUC_DEV), F32),
        in_specs=[VMEM],
        out_specs=VMEM,
        compiler_params=pltpu.CompilerParams(vmem_limit_bytes=LIMIT),
        cost_estimate=pl.CostEstimate(flops=10_000_000_000, bytes_accessed=20_000_000, transcendentals=0),
        name="nucleus_table",
    )(rows)


def stores(pieces, sources, whole, half, sems):
    keep = whole.shape[1] // 2
    copies = []
    for number, ((first, size), source) in enumerate(zip(pieces, sources)):
        start = pl.multiple_of(keep * half + first, 8)
        for plane in range(whole.shape[0]):
            copies.append(
                pltpu.make_async_copy(
                    source.at[pl.ds(plane * size, size)],
                    whole.at[plane, pl.ds(start, size)],
                    sems.at[number, plane],
                )
            )
    for copy in copies:
        copy.start()
    return copies


def token_kernel(source, *rest):
    token = rest[-1]
    token[...] = source[:8, :LANES]


def token_of(source, after=(), flops=0):
    return pl.pallas_call(
        token_kernel,
        out_shape=jax.ShapeDtypeStruct((8, LANES), F32),
        in_specs=[VMEM] + [ANY] * len(after),
        out_specs=VMEM,
        compiler_params=pltpu.CompilerParams(vmem_limit_bytes=LIMIT),
        cost_estimate=pl.CostEstimate(flops=flops, bytes_accessed=flops // 500, transcendentals=0),
        name="token_of",
    )(source, *after)


def begin_kernel(pieces, *refs):
    sources, (whole, sems) = refs[:-2], refs[-2:]
    for copy in stores(pieces, sources, whole, half_of(lax.axis_index("view")), sems):
        copy.wait()


def begin_result(pieces, shape, mine):
    return pl.pallas_call(
        functools.partial(begin_kernel, pieces),
        out_shape=jax.ShapeDtypeStruct(shape, F32),
        in_specs=[VMEM] * len(mine),
        out_specs=ANY,
        scratch_shapes=[pltpu.SemaphoreType.DMA((len(pieces), shape[0]))],
        compiler_params=pltpu.CompilerParams(vmem_limit_bytes=LIMIT),
        name="begin_result",
    )(*mine)


def finish_kernel(pieces, begun, *refs):
    others, (whole, sems) = refs[:-2], refs[-2:]
    for copy in stores(pieces, others, whole, 1 - half_of(lax.axis_index("view")), sems):
        copy.wait()


def finish(pieces, begun, others):
    return pl.pallas_call(
        functools.partial(finish_kernel, pieces),
        out_shape=jax.ShapeDtypeStruct(begun.shape, F32),
        in_specs=[ANY] + [VMEM] * len(others),
        out_specs=ANY,
        input_output_aliases={0: 0},
        scratch_shapes=[pltpu.SemaphoreType.DMA((len(pieces), begun.shape[0]))],
        compiler_params=pltpu.CompilerParams(vmem_limit_bytes=LIMIT),
        name="finish",
    )(begun, *others)


def on_device(estimate, measured, kernels, labels, label_owner, label_index):
    tiles, views = lax.axis_size("tile"), lax.axis_size("view")
    planes, height, across = estimate.shape
    taps = kernels.shape[2]
    radius = (taps - 1) // 2
    keep = height // 2
    seen = min(height, -(-(keep + radius) // 8) * 8)
    rows = min(height, -(-(keep + 2 * radius) // 16) * 16)
    near_pairs = [(i, i ^ 1) for i in range(tiles)]
    far_pairs = [(i, i + 1) for i in range(1, tiles - 1, 2)]
    far_pairs = far_pairs + [(b, a) for a, b in far_pairs]
    partner = [(i, i ^ 1) for i in range(views)]
    across_pairs = [(i, i ^ 3) for i in range(views)]

    lines = jnp.transpose(kernels, (1, 0, 2))
    packed = view_out(measured, lines, seen)
    swapped = lax.ppermute(packed, "view", partner)
    to_far, to_near = rims_out(estimate, radius, rows)
    far = lax.ppermute(to_far, "tile", far_pairs)
    near = lax.ppermute(to_near, "tile", near_pairs)
    places = slot_places(tiles, views, label_owner, label_index)
    own = prepare(False, taps, lines, estimate, places[1], rows, seen, keep)
    others = prepare(True, taps, swapped, estimate, lines, rows, seen, keep)
    came = token_of(far.reshape(radius * rows, across), (others[4],), 8_000_000_000)
    field_own, field_other, *sends = ratio_fields(
        own, others, far, near, measured, swapped, came
    )
    rims = [
        lax.ppermute(send, "tile", pairs) for send, pairs in zip(sends, (far_pairs, near_pairs) * PARTS)
    ]
    inner = own_planes(taps, own[4], others[4], field_own, field_other)
    mine, other, sums = [], [], []
    for part in range(PARTS):
        mine.append(add_rims(inner[part], *rims[2 * part : 2 * part + 2], *sums))
        other.append(lax.ppermute(mine[part], "view", across_pairs))
        sums = [moment_rows(views, tiles, part, estimate, mine[part], labels, places, sums)]
    sent = sums[0]
    got = lax.all_to_all(sent, ("tile", "view"), split_axis=0, concat_axis=0, tiled=True)
    size = keep // PARTS
    pieces = [(part * size, size) for part in range(PARTS)]
    new_mine, new_other, token = [], [], [sent]
    for part in range(PARTS):
        new_mine.append(update(views, part, estimate, mine[part], other[part], token))
        new_other.append(lax.ppermute(new_mine[part], "view", partner))
        token = [token_of(new_mine[part])]
    scale = label_index.shape[1] / (planes * height * across)
    moments = nucleus_table(across, scale, got)
    begun = begin_result(pieces, estimate.shape, new_mine)
    return finish(pieces, begun, new_other), moments


def solution(mesh):
    placed = (
        P("tile", None, None),
        P("view", "tile", None, None),
        P("view", None, None),
        P("tile", None, None),
        P("tile", None, None),
        P("tile", None),
    )
    return jax.shard_map(
        on_device,
        mesh=mesh,
        in_specs=placed,
        out_specs=(P("tile", None, None), P(None, "tile")),
        check_vma=False,
    )
```

```python
import functools

import jax
import jax.numpy as jnp
from jax import lax
from jax.experimental import pallas as pl
from jax.experimental.pallas import tpu as pltpu
from jax.sharding import PartitionSpec as P

MOM = 10
CAP = 5
WIDTH = 25
NUC_DEV = 128
LANES = 128
PARTS = 2
TAIL = 24
IDS = 24
F32 = jnp.float32
BF16 = jnp.bfloat16
ANY = pl.BlockSpec(memory_space=pl.ANY)
VMEM = pl.BlockSpec(memory_space=pltpu.VMEM)
LIMIT = 32 * 1024 * 1024


def half_of(view):
    return (view ^ (view >> 1)) & 1


def split(value):
    upper = value.astype(BF16)
    return upper, (value - upper.astype(F32)).astype(BF16)


def band(taps, shape, offset):
    rows = lax.broadcasted_iota(jnp.int32, shape, 0)
    cols = lax.broadcasted_iota(jnp.int32, shape, 1)
    place = cols - rows + offset
    result = jnp.zeros(shape, F32)
    for step, tap in enumerate(taps):
        result = jnp.where(place == step, tap, result)
    return result


def depth_terms(source, weights, first, last, planes, flipped):
    radius = (len(weights) - 1) // 2
    totals = {plane: None for plane in planes}
    for place in range(first, last):
        block = None
        for plane in planes:
            step = plane - place + radius if flipped else place - plane + radius
            if 0 <= step < len(weights):
                block = source(place) if block is None else block
                term = weights[step] * block
                totals[plane] = term if totals[plane] is None else totals[plane] + term
    return totals


def chunks(rows, across):
    return [(slice(row, row + 16), slice(lane, lane + LANES)) for row in range(0, rows, 16) for lane in range(0, across, LANES)]


def rims_out_kernel(estimate, after, to_far, to_near):
    planes, radius, rows = estimate.shape[0], to_far.shape[0], to_far.shape[1]
    odd = lax.axis_index("tile") % 2
    half = half_of(lax.axis_index("view"))
    start = pl.multiple_of((estimate.shape[1] - rows) * half, 8)
    to_far[...] = estimate[pl.ds(odd, radius), pl.ds(start, rows)]
    to_near[...] = estimate[pl.ds(1 - odd, radius), pl.ds(start, rows)]


def rims_out(estimate, after, radius, rows):
    shape = jax.ShapeDtypeStruct((radius, rows, estimate.shape[2]), F32)
    return pl.pallas_call(
        rims_out_kernel,
        out_shape=(shape, shape),
        in_specs=[VMEM, ANY],
        out_specs=(VMEM, VMEM),
        compiler_params=pltpu.CompilerParams(vmem_limit_bytes=LIMIT),
        name="rims_out",
    )(estimate, after)


def blank_kernel(rows):
    rows[...] = jnp.zeros_like(rows)


def blank_rows(across):
    return pl.pallas_call(
        blank_kernel,
        out_shape=jax.ShapeDtypeStruct((TAIL, across), F32),
        out_specs=VMEM,
        compiler_params=pltpu.CompilerParams(vmem_limit_bytes=LIMIT),
        cost_estimate=pl.CostEstimate(flops=8_000_000_000, bytes_accessed=16_000_000, transcendentals=0),
        name="blank_rows",
    )()


def view_out_kernel(seen, measured, taps, blank, packed):
    planes, height = measured.shape[1], measured.shape[2]
    half = half_of(lax.axis_index("view"))
    start = pl.multiple_of((height - seen) * (1 - half), 8)
    for plane in range(planes):
        packed[plane * seen : (plane + 1) * seen] = measured[0, plane, pl.ds(start, seen)]
    packed[planes * seen :] = blank[...]
    for axis in range(taps.shape[0]):
        at = planes * seen + axis
        packed[at : at + 1, : taps.shape[2]] = taps[axis]


def view_out(measured, lines, blank, seen):
    _, planes, _, across = measured.shape
    return pl.pallas_call(
        functools.partial(view_out_kernel, seen),
        out_shape=jax.ShapeDtypeStruct((planes * seen + TAIL, across), F32),
        in_specs=[VMEM] * 3,
        out_specs=VMEM,
        compiler_params=pltpu.CompilerParams(vmem_limit_bytes=LIMIT),
        name="view_out",
    )(measured, lines, blank)


def prepare_kernel(packed, taps, source, estimate, after, wide, tall, back, part, spread):
    half = half_of(lax.axis_index("view"))
    across = wide.shape[-1]
    rows, keep, seen = part.shape[1], back.shape[0], tall.shape[0]
    planes = estimate.shape[0]
    radius = (taps - 1) // 2
    at = source.shape[0] - TAIL
    if packed:
        raw = source[at : at + 3, :taps]
    else:
        raw = jnp.concatenate([source[axis] for axis in range(source.shape[0])], axis=0)
    weights = raw / jnp.sum(raw, axis=-1, keepdims=True)
    deep, high, flat = [[weights[axis : axis + 1, t : t + 1] for t in range(taps)] for axis in range(3)]
    start = pl.multiple_of((2 * keep - rows) * half, 16)
    seen_start = (2 * keep - seen) * half
    near_diagonal = jnp.abs(
        lax.broadcasted_iota(jnp.int32, (across, across), 1)
        - lax.broadcasted_iota(jnp.int32, (across, across), 0)
    ) <= radius
    for turn, line in enumerate((flat[::-1], flat)):
        first_row = jnp.concatenate(
            line[radius:] + [jnp.zeros((1, across - taps), F32)] + line[:radius], axis=1
        )
        square = pltpu.roll(
            jnp.broadcast_to(first_row, (across, across)), 0, 1, stride=1, stride_axis=0
        )
        upper, lower = split(jnp.where(near_diagonal, square, 0.0))
        wide[turn, 0] = upper
        wide[turn, 1] = lower
    upper, lower = split(band(high, (seen, rows), radius + start - seen_start))
    tall[...] = jnp.concatenate([upper, upper, lower], axis=1)
    upper, lower = split(band(high[::-1], (keep, rows), radius + seen_start - keep * half))
    back[...] = jnp.concatenate([upper, upper, lower], axis=1)
    factors = [jnp.broadcast_to(tap, (16, LANES)) for tap in deep]
    spread[...] = jnp.zeros_like(spread)
    for step in range(taps):
        spread[step : step + 1] = factors[step][:1]
    for row, lane in chunks(rows, across):
        where = pl.ds(pl.multiple_of(start + row.start, 16), 16)
        terms = depth_terms(
            lambda place: estimate[place, where, lane], factors, 0, planes, range(planes), False
        )
        for plane, block in terms.items():
            part[plane, row, lane] = block


def prepare(packed, taps, source, estimate, after, rows, seen, keep):
    planes, _, across = estimate.shape
    return pl.pallas_call(
        functools.partial(prepare_kernel, packed, taps),
        out_shape=(
            jax.ShapeDtypeStruct((2, 2, across, across), BF16),
            jax.ShapeDtypeStruct((seen, 3 * rows), BF16),
            jax.ShapeDtypeStruct((keep, 3 * rows), BF16),
            jax.ShapeDtypeStruct((planes, rows, across), F32),
            jax.ShapeDtypeStruct((-(-taps // 8) * 8, LANES), F32),
        ),
        in_specs=[VMEM, VMEM, ANY],
        out_specs=(VMEM,) * 5,
        compiler_params=pltpu.CompilerParams(vmem_limit_bytes=LIMIT),
        name="prepare",
    )(source, estimate, after)


def spread_factors(spread, taps):
    return [jnp.broadcast_to(spread[step : step + 1, :], (16, LANES)) for step in range(taps)]


def fields_kernel(*refs):
    sets, (far, near, measured, swapped), refs = (refs[:5], refs[5:10]), refs[10:14], refs[15:]
    fields, sends, (blur_hi, blur_lo, plane_hi, plane_lo) = refs[:2], refs[2:-4], refs[-4:]
    planes = sets[0][3].shape[0]
    radius, rows, across = near.shape
    keep, seen = sets[0][2].shape[0], sets[0][1].shape[0]
    taps = 2 * radius + 1
    even = lax.axis_index("tile") % 2 == 0
    half = half_of(lax.axis_index("view"))
    seen_start = pl.multiple_of((2 * keep - seen) * half, 8)
    factors = [spread_factors(spread, taps) for _, _, _, _, spread in sets]
    for which, (_, _, _, part, _) in enumerate(sets):
        for row, lane in chunks(rows, across):

            def rim(place):
                if place < 0:
                    at = place + radius
                    return jnp.where(even, far[at, row, lane], near[at, row, lane])
                at = place - planes
                return jnp.where(even, near[at, row, lane], far[at, row, lane])

            below = depth_terms(rim, factors[which], -radius, 0, range(planes), False)
            above = depth_terms(rim, factors[which], planes, planes + radius, range(planes), False)
            for plane in range(planes):
                block = part[plane, row, lane]
                for term in (below[plane], above[plane]):
                    block = block if term is None else block + term
                upper, lower = split(block)
                at = slice(plane * rows + row.start, plane * rows + row.stop)
                blur_hi[which, at, lane] = upper
                blur_lo[which, at, lane] = lower
    lines = []
    for which, (wide, _, _, _, _) in enumerate(sets):
        upper, lower = wide[0, 0], wide[0, 1]
        lines.append(
            jnp.dot(blur_hi[which], upper, preferred_element_type=F32)
            + jnp.dot(blur_lo[which], upper, preferred_element_type=F32)
            + jnp.dot(blur_hi[which], lower, preferred_element_type=F32)
        )
    both = [(which, plane) for which in range(2) for plane in range(planes)]
    forwards = {}
    for which, plane in both:
        hi, lo = split(lines[which][plane * rows : (plane + 1) * rows])
        forwards[which, plane] = jnp.dot(
            sets[which][1][...], jnp.concatenate([hi, lo, hi], axis=0), preferred_element_type=F32
        )
    ratios = {}
    for which, plane in both:
        if which == 0:
            recorded = measured[0, plane, pl.ds(seen_start, seen), :]
        else:
            recorded = swapped[plane * seen : (plane + 1) * seen]
        ratio = recorded / forwards[which, plane]
        if rows > seen:
            ratio = jnp.concatenate([ratio, jnp.zeros((rows - seen, across), F32)], axis=0)
        ratios[which, plane] = split(ratio)
    turned = {}
    for which, plane in both:
        hi, lo = ratios[which, plane]
        turned[which, plane] = jnp.dot(
            sets[which][2][...], jnp.concatenate([hi, lo, hi], axis=0), preferred_element_type=F32
        )
    for which, plane in both:
        hi, lo = split(turned[which, plane])
        plane_hi[which, plane * keep : (plane + 1) * keep] = hi
        plane_lo[which, plane * keep : (plane + 1) * keep] = lo
    for which, (wide, _, _, _, _) in enumerate(sets):
        upper, lower = wide[1, 0], wide[1, 1]
        result = (
            jnp.dot(plane_hi[which], upper, preferred_element_type=F32)
            + jnp.dot(plane_lo[which], upper, preferred_element_type=F32)
            + jnp.dot(plane_hi[which], lower, preferred_element_type=F32)
        )
        fields[which][...] = result.reshape(planes, keep, across)
    for row, lane in chunks(keep, across):
        below, above = [], []
        for which in range(2):
            source = lambda place: fields[which][place, row, lane]
            outer = range(planes, planes + radius)
            below.append(depth_terms(source, factors[which], 0, planes, range(-radius, 0), True))
            above.append(depth_terms(source, factors[which], 0, planes, outer, True))
        part_at, inside = divmod(row.start, keep // PARTS)
        inside = slice(inside, inside + 16)
        for at in range(radius):
            down = below[0][at - radius] + below[1][at - radius]
            up = above[0][at + planes] + above[1][at + planes]
            sends[2 * part_at][at, inside, lane] = jnp.where(even, down, up)
            sends[2 * part_at + 1][at, inside, lane] = jnp.where(even, up, down)


def ratio_fields(own, others, far, near, measured, swapped, after):
    keep, planes = own[2].shape[0], own[3].shape[0]
    radius, rows, across = near.shape
    field = jax.ShapeDtypeStruct((planes, keep, across), F32)
    send = jax.ShapeDtypeStruct((radius, keep // PARTS, across), F32)
    return pl.pallas_call(
        fields_kernel,
        out_shape=(field,) * 2 + (send,) * (2 * PARTS),
        in_specs=[VMEM] * 14 + [ANY],
        out_specs=(VMEM,) * (2 + 2 * PARTS),
        scratch_shapes=[
            pltpu.VMEM((2, planes * rows, across), BF16),
            pltpu.VMEM((2, planes * rows, across), BF16),
            pltpu.VMEM((2, planes * keep, across), BF16),
            pltpu.VMEM((2, planes * keep, across), BF16),
        ],
        compiler_params=pltpu.CompilerParams(vmem_limit_bytes=LIMIT),
        name="ratio_fields",
    )(*own, *others, far, near, measured, swapped, after)


def own_kernel(taps, spread_own, spread_other, field_own, field_other, *inner):
    planes, keep, across = field_own.shape
    factors = [spread_factors(spread, taps) for spread in (spread_own, spread_other)]
    for row, lane in chunks(keep, across):
        parts = [
            depth_terms(
                lambda place: field[place, row, lane], factors[which], 0, planes, range(planes), True
            )
            for which, field in enumerate((field_own, field_other))
        ]
        part_at, inside = divmod(row.start, keep // PARTS)
        for plane in range(planes):
            inner[part_at][plane, inside : inside + 16, lane] = parts[0][plane] + parts[1][plane]


def own_planes(taps, spread_own, spread_other, field_own, field_other):
    planes, keep, across = field_own.shape
    return pl.pallas_call(
        functools.partial(own_kernel, taps),
        out_shape=(jax.ShapeDtypeStruct((planes, keep // PARTS, across), F32),) * PARTS,
        in_specs=[VMEM] * 4,
        out_specs=(VMEM,) * PARTS,
        compiler_params=pltpu.CompilerParams(vmem_limit_bytes=LIMIT),
        name="own_planes",
    )(spread_own, spread_other, field_own, field_other)


def rims_kernel(inner, far, near, *rest):
    correction = rest[-1]
    planes, radius = inner.shape[0], near.shape[0]
    even = lax.axis_index("tile") % 2 == 0
    for plane in range(planes):
        total = inner[plane]
        if plane < radius:
            total += jnp.where(even, far[plane], near[plane])
        if plane >= planes - radius:
            at = plane - planes + radius
            total += jnp.where(even, near[at], far[at])
        correction[plane] = total


def add_rims(inner, far, near, *after):
    return pl.pallas_call(
        rims_kernel,
        out_shape=jax.ShapeDtypeStruct(inner.shape, F32),
        in_specs=[VMEM] * 3 + [ANY] * len(after),
        out_specs=VMEM,
        compiler_params=pltpu.CompilerParams(vmem_limit_bytes=LIMIT),
        name="add_rims",
    )(inner, far, near, *after)


def table_rows(table):
    return jnp.concatenate([table[:8], table[8:]], axis=1)


def update_kernel(views, part, estimate, mine, other, *rest):
    planes, size, across = mine.shape
    result = rest[-1]
    half = half_of(lax.axis_index("view"))
    start = pl.multiple_of(size * (PARTS * half + part), 8)
    for plane in range(planes):
        held = estimate[plane, pl.ds(start, size)]
        at = slice(plane * size, (plane + 1) * size)
        result[at] = held * (mine[plane] + other[plane]) * (1.0 / views)
    spare = result.shape[0] - planes * size
    if spare:
        result[planes * size :] = jnp.zeros((spare, across), F32)


def update(views, part, estimate, mine, other, after):
    planes, size, across = mine.shape
    spare = 8 * (PARTS - 1 - part)
    return pl.pallas_call(
        functools.partial(update_kernel, views, part),
        out_shape=jax.ShapeDtypeStruct((planes * size + spare, across), F32),
        in_specs=[VMEM] * 3 + [ANY] * len(after),
        out_specs=VMEM,
        compiler_params=pltpu.CompilerParams(vmem_limit_bytes=LIMIT),
        name="update",
    )(estimate, mine, other, *after)


def slots_kernel(views, owner_row, index_row, picked, base):
    count = base.shape[0]
    slots = owner_row.shape[1]
    owner = owner_row[...]
    member = (lax.broadcasted_iota(jnp.int32, (count // views, slots), 0) == owner).astype(F32)
    upto = (
        lax.broadcasted_iota(jnp.int32, (slots, slots), 0)
        <= lax.broadcasted_iota(jnp.int32, (slots, slots), 1)
    ).astype(F32)
    running = jnp.dot(member, upto, preferred_element_type=F32)
    rank = jnp.sum(member * running, axis=0, keepdims=True).astype(jnp.int32) - 1
    named = lax.broadcasted_iota(jnp.int32, (count, slots), 0) // views == owner
    index = index_row[...].astype(F32)
    lanes = lax.broadcasted_iota(jnp.int32, (count, LANES), 1)
    result = jnp.zeros((count, LANES), F32)
    for place in range(CAP):
        chosen = named & (rank == place)
        picked[place * count : (place + 1) * count] = chosen.astype(F32)
        ids = jnp.sum(jnp.where(chosen, index, 0.0), axis=1, keepdims=True)
        result = jnp.where(lanes == place * WIDTH + IDS, ids, result)
    base[...] = result


def slot_places(tiles, views, label_owner, label_index):
    slots = label_index.shape[1]
    count = tiles * views
    return pl.pallas_call(
        functools.partial(slots_kernel, views),
        out_shape=(
            jax.ShapeDtypeStruct((CAP * count, slots), F32),
            jax.ShapeDtypeStruct((count, LANES), F32),
        ),
        in_specs=[VMEM, VMEM],
        out_specs=(VMEM, VMEM),
        compiler_params=pltpu.CompilerParams(vmem_limit_bytes=LIMIT),
        name="slot_places",
    )(label_owner.reshape(1, slots), label_index)


def merge_rows(blocks):
    rows = lax.broadcasted_iota(jnp.int32, blocks[0].shape, 0)
    step = 4
    while step:
        low = (rows & step) == 0
        half = len(blocks) // 2
        merged = []
        for one, two in zip(blocks[:half], blocks[half:]):
            kept = jnp.where(low, one, two)
            turned = jnp.where(low, two, one)
            moved = pltpu.roll(turned, step, 0)
            if step < 4:
                moved = jnp.where(low, pltpu.roll(turned, 8 - step, 0), moved)
            merged.append(kept + moved)
        blocks = merged
        step //= 2
    return blocks[0]


def moments_kernel(views, depth_total, part, estimate, labels, picked, base, correction, *refs):
    begun, (sent, held, sums, table) = refs[:-4], refs[-4:]
    planes, size, across = correction.shape
    height_total = estimate.shape[1]
    slots = picked.shape[1]
    half = half_of(lax.axis_index("view"))
    first = (lax.axis_index("tile") * planes).astype(F32) + 0.5
    start = pl.multiple_of(size * (PARTS * half + part), 8)
    held[...] = estimate[:, pl.ds(start, size)] * correction[...] * (1.0 / views)
    group = 16
    spot = lax.broadcasted_iota(jnp.int32, (across, LANES), 0)
    lanes = lax.broadcasted_iota(jnp.int32, (across, LANES), 1)
    low = (spot * spot) & 255
    factors = jnp.where(lanes == 0, 1, jnp.where(lanes == 1, spot, 0))
    factors = jnp.where(lanes == 2, spot * spot - low, jnp.where(lanes == 3, low, factors))
    factors = factors.astype(F32).astype(BF16)
    base_row = lax.broadcasted_iota(jnp.int32, (8, across), 0)

    def one_group(number, carry):
        held_parts = []
        for pair in range(0, group, 2):
            slot = [number * group + pair, number * group + pair + 1]
            parts = [[None] * 6 for _ in slot]
            for row in range(0, size, 8):
                high = ((base_row + (row + start)).astype(F32) + 0.5) * (1.0 / height_total)
                flat, once, twice = [[jnp.zeros((8, across), F32) for _ in slot] for _ in range(3)]
                for plane in reversed(range(planes)):
                    mark = labels[plane, pl.ds(pl.multiple_of(start + row, 8), 8)]
                    value = held[plane, row : row + 8]
                    for at in range(2):
                        flat[at] = flat[at] + jnp.where(mark == slot[at], value, 0.0)
                        if plane > 0:
                            once[at] = once[at] + flat[at]
                            twice[at] = twice[at] + once[at]
                for at in range(2):
                    scaled = flat[at] * high
                    terms = (flat[at], scaled, scaled * high, once[at], once[at] * high, twice[at])
                    parts[at] = [new if old is None else old + new for old, new in zip(parts[at], terms)]
            held_parts += parts
            if len(held_parts) == 8:
                for kind in range(6):
                    row = kind * group + pair + 2 - 8
                    sums[row : row + 8, :] = merge_rows([parts[kind] for parts in held_parts])
                held_parts = []
        whole = sums[...]
        upper, rest = split(whole)
        rest = whole - upper.astype(F32)
        middle, lower = split(rest)
        lines = jnp.dot(
            jnp.concatenate([upper, middle, lower], axis=0), factors, preferred_element_type=F32
        )
        count = 6 * group
        lines = lines[:count] + lines[count : 2 * count] + lines[2 * count :]
        flat, high_flat, square_flat, once, high_once, twice = [
            lines[kind * group : (kind + 1) * group] for kind in range(6)
        ]
        deep = (first * flat + once) * (1.0 / depth_total)
        deep_high = (first * high_flat + high_once) * (1.0 / depth_total)
        deeper = first * (first * flat + 2.0 * once) + (2.0 * twice - once)
        deeper = deeper * (1.0 / depth_total**2)
        total = flat
        for kind, sums_of in enumerate((high_flat, square_flat, deep, deep_high, deeper), 1):
            total += pltpu.roll(sums_of, 4 * kind, 1)
        rows = pl.ds(pl.multiple_of(number * group, group), group)
        target = table if part == PARTS - 1 else sent
        target[rows, :] = total + begun[0][rows, :] if begun else total
        return carry

    lax.fori_loop(0, slots // group, one_group, 0)
    if part < PARTS - 1:
        return
    rows = jnp.dot(
        picked[...], table[...], precision=lax.Precision.HIGHEST, preferred_element_type=F32
    )
    total = base[...]
    count = total.shape[0]
    for place in range(CAP):
        total += pltpu.roll(rows[place * count : (place + 1) * count], place * WIDTH, 1)
    sent[...] = total


def moment_rows(views, tiles, part, estimate, correction, labels, places, begun):
    planes, size, across = correction.shape
    slots = places[0].shape[1]
    count = places[1].shape[0] if part == PARTS - 1 else slots
    return pl.pallas_call(
        functools.partial(moments_kernel, views, tiles * planes, part),
        out_shape=jax.ShapeDtypeStruct((count, LANES), F32),
        in_specs=[VMEM] * (5 + len(begun)),
        out_specs=VMEM,
        scratch_shapes=[
            pltpu.VMEM((planes, size, across), F32),
            pltpu.VMEM((6 * 16, across), F32),
            pltpu.VMEM((slots, LANES), F32),
        ],
        compiler_params=pltpu.CompilerParams(vmem_limit_bytes=LIMIT),
        name="moment_rows",
    )(estimate, labels, *places, correction, *begun)


def segments_kernel(across, scale, rows, moments):
    whole = rows[...]
    parts = [whole] + [pltpu.roll(whole, LANES - place * WIDTH, 1) for place in range(1, CAP)]
    values = jnp.concatenate(parts, axis=0)
    ids = values[:, IDS : IDS + 1].astype(jnp.int32)
    spots = lax.broadcasted_iota(jnp.int32, (values.shape[0], NUC_DEV), 1)
    picked = (ids == spots).astype(F32)
    full = lax.dot_general(
        values, picked, (((0,), (0,)), ((), ())),
        precision=lax.Precision.HIGHEST, preferred_element_type=F32,
    )
    mass, high, higher, deep, deep_high, deeper = [full[4 * kind : 4 * kind + 4] for kind in range(6)]
    flat = lambda sums: sums[0:1]
    line = lambda sums: (sums[1:2] + 0.5 * sums[0:1]) * (1.0 / across)
    square = lambda sums: (sums[2:3] + sums[3:4] + sums[1:2] + 0.25 * sums[0:1]) * (1.0 / across**2)
    total = flat(mass)
    sums = jnp.concatenate(
        [
            flat(deep), flat(high), line(mass),
            flat(deeper), flat(higher), square(mass),
            flat(deep_high), line(deep), line(high),
        ],
        axis=0,
    )
    moments[...] = jnp.concatenate([total * scale, sums / jnp.maximum(total, 1.0)], axis=0)


def nucleus_table(across, scale, rows):
    return pl.pallas_call(
        functools.partial(segments_kernel, across, scale),
        out_shape=jax.ShapeDtypeStruct((MOM, NUC_DEV), F32),
        in_specs=[VMEM],
        out_specs=VMEM,
        compiler_params=pltpu.CompilerParams(vmem_limit_bytes=LIMIT),
        cost_estimate=pl.CostEstimate(flops=10_000_000_000, bytes_accessed=20_000_000, transcendentals=0),
        name="nucleus_table",
    )(rows)


def stores(pieces, sources, whole, half, sems):
    keep = whole.shape[1] // 2
    copies = []
    for number, ((first, size), source) in enumerate(zip(pieces, sources)):
        start = pl.multiple_of(keep * half + first, 8)
        for plane in range(whole.shape[0]):
            copies.append(
                pltpu.make_async_copy(
                    source.at[pl.ds(plane * size, size)],
                    whole.at[plane, pl.ds(start, size)],
                    sems.at[number, plane],
                )
            )
    for copy in copies:
        copy.start()
    return copies


def token_kernel(source, *rest):
    token = rest[-1]
    token[...] = source[:8, :LANES]


def token_of(source, after=(), flops=0):
    return pl.pallas_call(
        token_kernel,
        out_shape=jax.ShapeDtypeStruct((8, LANES), F32),
        in_specs=[VMEM] + [ANY] * len(after),
        out_specs=VMEM,
        compiler_params=pltpu.CompilerParams(vmem_limit_bytes=LIMIT),
        cost_estimate=pl.CostEstimate(flops=flops, bytes_accessed=flops // 500, transcendentals=0),
        name="token_of",
    )(source, *after)


def begin_kernel(pieces, *refs):
    sources, (whole, sems) = refs[:-2], refs[-2:]
    for copy in stores(pieces, sources, whole, half_of(lax.axis_index("view")), sems):
        copy.wait()


def begin_result(pieces, shape, mine):
    return pl.pallas_call(
        functools.partial(begin_kernel, pieces),
        out_shape=jax.ShapeDtypeStruct(shape, F32),
        in_specs=[VMEM] * len(mine),
        out_specs=ANY,
        scratch_shapes=[pltpu.SemaphoreType.DMA((len(pieces), shape[0]))],
        compiler_params=pltpu.CompilerParams(vmem_limit_bytes=LIMIT),
        name="begin_result",
    )(*mine)


def finish_kernel(pieces, begun, *refs):
    others, (whole, sems) = refs[:-2], refs[-2:]
    for copy in stores(pieces, others, whole, 1 - half_of(lax.axis_index("view")), sems):
        copy.wait()


def finish(pieces, begun, others):
    return pl.pallas_call(
        functools.partial(finish_kernel, pieces),
        out_shape=jax.ShapeDtypeStruct(begun.shape, F32),
        in_specs=[ANY] + [VMEM] * len(others),
        out_specs=ANY,
        input_output_aliases={0: 0},
        scratch_shapes=[pltpu.SemaphoreType.DMA((len(pieces), begun.shape[0]))],
        compiler_params=pltpu.CompilerParams(vmem_limit_bytes=LIMIT),
        name="finish",
    )(begun, *others)


def on_device(estimate, measured, kernels, labels, label_owner, label_index):
    tiles, views = lax.axis_size("tile"), lax.axis_size("view")
    planes, height, across = estimate.shape
    taps = kernels.shape[2]
    radius = (taps - 1) // 2
    keep = height // 2
    seen = min(height, -(-(keep + radius) // 8) * 8)
    rows = min(height, -(-(keep + 2 * radius) // 16) * 16)
    near_pairs = [(i, i ^ 1) for i in range(tiles)]
    far_pairs = [(i, i + 1) for i in range(1, tiles - 1, 2)]
    far_pairs = far_pairs + [(b, a) for a, b in far_pairs]
    partner = [(i, i ^ 1) for i in range(views)]
    across_pairs = [(i, i ^ 3) for i in range(views)]

    lines = jnp.transpose(kernels, (1, 0, 2))
    blank = blank_rows(across)
    packed = view_out(measured, lines, blank, seen)
    swapped = lax.ppermute(packed, "view", partner)
    to_far, to_near = rims_out(estimate, blank, radius, rows)
    far = lax.ppermute(to_far, "tile", far_pairs)
    near = lax.ppermute(to_near, "tile", near_pairs)
    places = slot_places(tiles, views, label_owner, label_index)
    own = prepare(False, taps, lines, estimate, places[1], rows, seen, keep)
    others = prepare(True, taps, swapped, estimate, lines, rows, seen, keep)
    came = token_of(far.reshape(radius * rows, across), (others[4],), 0)
    field_own, field_other, *sends = ratio_fields(
        own, others, far, near, measured, swapped, came
    )
    rims = [
        lax.ppermute(send, "tile", pairs) for send, pairs in zip(sends, (far_pairs, near_pairs) * PARTS)
    ]
    inner = own_planes(taps, own[4], others[4], field_own, field_other)
    mine, other, sums = [], [], []
    for part in range(PARTS):
        mine.append(add_rims(inner[part], *rims[2 * part : 2 * part + 2], *sums))
        other.append(lax.ppermute(mine[part], "view", across_pairs))
        sums = [moment_rows(views, tiles, part, estimate, mine[part], labels, places, sums)]
    sent = sums[0]
    got = lax.all_to_all(sent, ("tile", "view"), split_axis=0, concat_axis=0, tiled=True)
    size = keep // PARTS
    pieces = [(part * size, size) for part in range(PARTS)]
    new_mine, new_other, token = [], [], [sent]
    for part in range(PARTS):
        new_mine.append(update(views, part, estimate, mine[part], other[part], token))
        new_other.append(lax.ppermute(new_mine[part], "view", partner))
        token = [token_of(new_mine[part])]
    scale = label_index.shape[1] / (planes * height * across)
    moments = nucleus_table(across, scale, got)
    begun = begin_result(pieces, estimate.shape, new_mine)
    return finish(pieces, begun, new_other), moments


def solution(mesh):
    placed = (
        P("tile", None, None),
        P("view", "tile", None, None),
        P("view", None, None),
        P("tile", None, None),
        P("tile", None, None),
        P("tile", None),
    )
    return jax.shard_map(
        on_device,
        mesh=mesh,
        in_specs=placed,
        out_specs=(P("tile", None, None), P(None, "tile")),
        check_vma=False,
    )
```

```python
import functools

import jax
import jax.numpy as jnp
from jax import lax
from jax.experimental import pallas as pl
from jax.experimental.pallas import tpu as pltpu
from jax.sharding import PartitionSpec as P

MOM = 10
CAP = 5
WIDTH = 25
NUC_DEV = 128
LANES = 128
PARTS = 2
TAIL = 24
IDS = 24
F32 = jnp.float32
BF16 = jnp.bfloat16
ANY = pl.BlockSpec(memory_space=pl.ANY)
VMEM = pl.BlockSpec(memory_space=pltpu.VMEM)
LIMIT = 32 * 1024 * 1024


def half_of(view):
    return (view ^ (view >> 1)) & 1


def split(value):
    upper = value.astype(BF16)
    return upper, (value - upper.astype(F32)).astype(BF16)


def band(taps, shape, offset):
    rows = lax.broadcasted_iota(jnp.int32, shape, 0)
    cols = lax.broadcasted_iota(jnp.int32, shape, 1)
    place = cols - rows + offset
    result = jnp.zeros(shape, F32)
    for step, tap in enumerate(taps):
        result = jnp.where(place == step, tap, result)
    return result


def depth_terms(source, weights, first, last, planes, flipped):
    radius = (len(weights) - 1) // 2
    totals = {plane: None for plane in planes}
    for place in range(first, last):
        block = None
        for plane in planes:
            step = plane - place + radius if flipped else place - plane + radius
            if 0 <= step < len(weights):
                block = source(place) if block is None else block
                term = weights[step] * block
                totals[plane] = term if totals[plane] is None else totals[plane] + term
    return totals


def chunks(rows, across):
    return [(slice(row, row + 16), slice(lane, lane + LANES)) for row in range(0, rows, 16) for lane in range(0, across, LANES)]


def rims_out_kernel(estimate, after, to_far, to_near):
    planes, radius, rows = estimate.shape[0], to_far.shape[0], to_far.shape[1]
    odd = lax.axis_index("tile") % 2
    half = half_of(lax.axis_index("view"))
    start = pl.multiple_of((estimate.shape[1] - rows) * half, 8)
    to_far[...] = estimate[pl.ds(odd, radius), pl.ds(start, rows)]
    to_near[...] = estimate[pl.ds(1 - odd, radius), pl.ds(start, rows)]


def rims_out(estimate, after, radius, rows):
    shape = jax.ShapeDtypeStruct((radius, rows, estimate.shape[2]), F32)
    return pl.pallas_call(
        rims_out_kernel,
        out_shape=(shape, shape),
        in_specs=[VMEM, ANY],
        out_specs=(VMEM, VMEM),
        compiler_params=pltpu.CompilerParams(vmem_limit_bytes=LIMIT),
        name="rims_out",
    )(estimate, after)


def blank_kernel(rows):
    rows[...] = jnp.zeros_like(rows)


def blank_rows(across):
    return pl.pallas_call(
        blank_kernel,
        out_shape=jax.ShapeDtypeStruct((TAIL, across), F32),
        out_specs=VMEM,
        compiler_params=pltpu.CompilerParams(vmem_limit_bytes=LIMIT),
        cost_estimate=pl.CostEstimate(flops=8_000_000_000, bytes_accessed=16_000_000, transcendentals=0),
        name="blank_rows",
    )()


def view_out_kernel(seen, measured, taps, blank, packed):
    planes, height = measured.shape[1], measured.shape[2]
    half = half_of(lax.axis_index("view"))
    start = pl.multiple_of((height - seen) * (1 - half), 8)
    for plane in range(planes):
        packed[plane * seen : (plane + 1) * seen] = measured[0, plane, pl.ds(start, seen)]
    packed[planes * seen :] = blank[...]
    for axis in range(taps.shape[0]):
        at = planes * seen + axis
        packed[at : at + 1, : taps.shape[2]] = taps[axis]


def view_out(measured, lines, blank, seen):
    _, planes, _, across = measured.shape
    return pl.pallas_call(
        functools.partial(view_out_kernel, seen),
        out_shape=jax.ShapeDtypeStruct((planes * seen + TAIL, across), F32),
        in_specs=[VMEM] * 3,
        out_specs=VMEM,
        compiler_params=pltpu.CompilerParams(vmem_limit_bytes=LIMIT),
        name="view_out",
    )(measured, lines, blank)


def prepare_kernel(packed, taps, source, estimate, after, wide, tall, back, part, spread):
    half = half_of(lax.axis_index("view"))
    across = wide.shape[-1]
    rows, keep, seen = part.shape[1], back.shape[0], tall.shape[0]
    planes = estimate.shape[0]
    radius = (taps - 1) // 2
    at = source.shape[0] - TAIL
    if packed:
        raw = source[at : at + 3, :taps]
    else:
        raw = jnp.concatenate([source[axis] for axis in range(source.shape[0])], axis=0)
    weights = raw / jnp.sum(raw, axis=-1, keepdims=True)
    deep, high, flat = [[weights[axis : axis + 1, t : t + 1] for t in range(taps)] for axis in range(3)]
    start = pl.multiple_of((2 * keep - rows) * half, 16)
    seen_start = (2 * keep - seen) * half
    near_diagonal = jnp.abs(
        lax.broadcasted_iota(jnp.int32, (across, across), 1)
        - lax.broadcasted_iota(jnp.int32, (across, across), 0)
    ) <= radius
    for turn, line in enumerate((flat[::-1], flat)):
        first_row = jnp.concatenate(
            line[radius:] + [jnp.zeros((1, across - taps), F32)] + line[:radius], axis=1
        )
        square = pltpu.roll(
            jnp.broadcast_to(first_row, (across, across)), 0, 1, stride=1, stride_axis=0
        )
        upper, lower = split(jnp.where(near_diagonal, square, 0.0))
        wide[turn, 0] = upper
        wide[turn, 1] = lower
    upper, lower = split(band(high, (seen, rows), radius + start - seen_start))
    tall[...] = jnp.concatenate([upper, upper, lower], axis=1)
    upper, lower = split(band(high[::-1], (keep, rows), radius + seen_start - keep * half))
    back[...] = jnp.concatenate([upper, upper, lower], axis=1)
    factors = [jnp.broadcast_to(tap, (16, LANES)) for tap in deep]
    spread[...] = jnp.zeros_like(spread)
    for step in range(taps):
        spread[step : step + 1] = factors[step][:1]
    for row, lane in chunks(rows, across):
        where = pl.ds(pl.multiple_of(start + row.start, 16), 16)
        terms = depth_terms(
            lambda place: estimate[place, where, lane], factors, 0, planes, range(planes), False
        )
        for plane, block in terms.items():
            part[plane, row, lane] = block


def prepare(packed, taps, source, estimate, after, rows, seen, keep):
    planes, _, across = estimate.shape
    return pl.pallas_call(
        functools.partial(prepare_kernel, packed, taps),
        out_shape=(
            jax.ShapeDtypeStruct((2, 2, across, across), BF16),
            jax.ShapeDtypeStruct((seen, 3 * rows), BF16),
            jax.ShapeDtypeStruct((keep, 3 * rows), BF16),
            jax.ShapeDtypeStruct((planes, rows, across), F32),
            jax.ShapeDtypeStruct((-(-taps // 8) * 8, LANES), F32),
        ),
        in_specs=[VMEM, VMEM, ANY],
        out_specs=(VMEM,) * 5,
        compiler_params=pltpu.CompilerParams(vmem_limit_bytes=LIMIT),
        name="prepare",
    )(source, estimate, after)


def spread_factors(spread, taps):
    return [jnp.broadcast_to(spread[step : step + 1, :], (16, LANES)) for step in range(taps)]


def fields_kernel(*refs):
    sets, (far, near, measured, swapped), refs = (refs[:5], refs[5:10]), refs[10:14], refs[15:]
    fields, sends, (blur_hi, blur_lo, plane_hi, plane_lo) = refs[:2], refs[2:-4], refs[-4:]
    planes = sets[0][3].shape[0]
    radius, rows, across = near.shape
    keep, seen = sets[0][2].shape[0], sets[0][1].shape[0]
    taps = 2 * radius + 1
    even = lax.axis_index("tile") % 2 == 0
    half = half_of(lax.axis_index("view"))
    seen_start = pl.multiple_of((2 * keep - seen) * half, 8)
    factors = [spread_factors(spread, taps) for _, _, _, _, spread in sets]
    for which, (_, _, _, part, _) in enumerate(sets):
        for row, lane in chunks(rows, across):

            def rim(place):
                if place < 0:
                    at = place + radius
                    return jnp.where(even, far[at, row, lane], near[at, row, lane])
                at = place - planes
                return jnp.where(even, near[at, row, lane], far[at, row, lane])

            below = depth_terms(rim, factors[which], -radius, 0, range(planes), False)
            above = depth_terms(rim, factors[which], planes, planes + radius, range(planes), False)
            for plane in range(planes):
                block = part[plane, row, lane]
                for term in (below[plane], above[plane]):
                    block = block if term is None else block + term
                upper, lower = split(block)
                at = slice(plane * rows + row.start, plane * rows + row.stop)
                blur_hi[which, at, lane] = upper
                blur_lo[which, at, lane] = lower
    lines = []
    for which, (wide, _, _, _, _) in enumerate(sets):
        upper, lower = wide[0, 0], wide[0, 1]
        lines.append(
            jnp.dot(blur_hi[which], upper, preferred_element_type=F32)
            + jnp.dot(blur_lo[which], upper, preferred_element_type=F32)
            + jnp.dot(blur_hi[which], lower, preferred_element_type=F32)
        )
    both = [(which, plane) for which in range(2) for plane in range(planes)]
    forwards = {}
    for which, plane in both:
        hi, lo = split(lines[which][plane * rows : (plane + 1) * rows])
        forwards[which, plane] = jnp.dot(
            sets[which][1][...], jnp.concatenate([hi, lo, hi], axis=0), preferred_element_type=F32
        )
    ratios = {}
    for which, plane in both:
        if which == 0:
            recorded = measured[0, plane, pl.ds(seen_start, seen), :]
        else:
            recorded = swapped[plane * seen : (plane + 1) * seen]
        ratio = recorded / forwards[which, plane]
        if rows > seen:
            ratio = jnp.concatenate([ratio, jnp.zeros((rows - seen, across), F32)], axis=0)
        ratios[which, plane] = split(ratio)
    turned = {}
    for which, plane in both:
        hi, lo = ratios[which, plane]
        turned[which, plane] = jnp.dot(
            sets[which][2][...], jnp.concatenate([hi, lo, hi], axis=0), preferred_element_type=F32
        )
    for which, plane in both:
        hi, lo = split(turned[which, plane])
        plane_hi[which, plane * keep : (plane + 1) * keep] = hi
        plane_lo[which, plane * keep : (plane + 1) * keep] = lo
    for which, (wide, _, _, _, _) in enumerate(sets):
        upper, lower = wide[1, 0], wide[1, 1]
        result = (
            jnp.dot(plane_hi[which], upper, preferred_element_type=F32)
            + jnp.dot(plane_lo[which], upper, preferred_element_type=F32)
            + jnp.dot(plane_hi[which], lower, preferred_element_type=F32)
        )
        fields[which][...] = result.reshape(planes, keep, across)
    for row, lane in chunks(keep, across):
        below, above = [], []
        for which in range(2):
            source = lambda place: fields[which][place, row, lane]
            outer = range(planes, planes + radius)
            below.append(depth_terms(source, factors[which], 0, planes, range(-radius, 0), True))
            above.append(depth_terms(source, factors[which], 0, planes, outer, True))
        part_at, inside = divmod(row.start, keep // PARTS)
        inside = slice(inside, inside + 16)
        for at in range(radius):
            down = below[0][at - radius] + below[1][at - radius]
            up = above[0][at + planes] + above[1][at + planes]
            sends[2 * part_at][at, inside, lane] = jnp.where(even, down, up)
            sends[2 * part_at + 1][at, inside, lane] = jnp.where(even, up, down)


def ratio_fields(own, others, far, near, measured, swapped, after):
    keep, planes = own[2].shape[0], own[3].shape[0]
    radius, rows, across = near.shape
    field = jax.ShapeDtypeStruct((planes, keep, across), F32)
    send = jax.ShapeDtypeStruct((radius, keep // PARTS, across), F32)
    return pl.pallas_call(
        fields_kernel,
        out_shape=(field,) * 2 + (send,) * (2 * PARTS),
        in_specs=[VMEM] * 14 + [ANY],
        out_specs=(VMEM,) * (2 + 2 * PARTS),
        scratch_shapes=[
            pltpu.VMEM((2, planes * rows, across), BF16),
            pltpu.VMEM((2, planes * rows, across), BF16),
            pltpu.VMEM((2, planes * keep, across), BF16),
            pltpu.VMEM((2, planes * keep, across), BF16),
        ],
        compiler_params=pltpu.CompilerParams(vmem_limit_bytes=LIMIT),
        name="ratio_fields",
    )(*own, *others, far, near, measured, swapped, after)


def own_kernel(taps, spread_own, spread_other, field_own, field_other, *inner):
    planes, keep, across = field_own.shape
    factors = [spread_factors(spread, taps) for spread in (spread_own, spread_other)]
    for row, lane in chunks(keep, across):
        parts = [
            depth_terms(
                lambda place: field[place, row, lane], factors[which], 0, planes, range(planes), True
            )
            for which, field in enumerate((field_own, field_other))
        ]
        part_at, inside = divmod(row.start, keep // PARTS)
        for plane in range(planes):
            inner[part_at][plane, inside : inside + 16, lane] = parts[0][plane] + parts[1][plane]


def own_planes(taps, spread_own, spread_other, field_own, field_other):
    planes, keep, across = field_own.shape
    return pl.pallas_call(
        functools.partial(own_kernel, taps),
        out_shape=(jax.ShapeDtypeStruct((planes, keep // PARTS, across), F32),) * PARTS,
        in_specs=[VMEM] * 4,
        out_specs=(VMEM,) * PARTS,
        compiler_params=pltpu.CompilerParams(vmem_limit_bytes=LIMIT),
        name="own_planes",
    )(spread_own, spread_other, field_own, field_other)


def rims_kernel(inner, far, near, *rest):
    correction = rest[-1]
    planes, radius = inner.shape[0], near.shape[0]
    even = lax.axis_index("tile") % 2 == 0
    for plane in range(planes):
        total = inner[plane]
        if plane < radius:
            total += jnp.where(even, far[plane], near[plane])
        if plane >= planes - radius:
            at = plane - planes + radius
            total += jnp.where(even, near[at], far[at])
        correction[plane] = total


def add_rims(inner, far, near, *after):
    return pl.pallas_call(
        rims_kernel,
        out_shape=jax.ShapeDtypeStruct(inner.shape, F32),
        in_specs=[VMEM] * 3 + [ANY] * len(after),
        out_specs=VMEM,
        compiler_params=pltpu.CompilerParams(vmem_limit_bytes=LIMIT),
        name="add_rims",
    )(inner, far, near, *after)


def table_rows(table):
    return jnp.concatenate([table[:8], table[8:]], axis=1)


def update_kernel(views, part, estimate, mine, other, *rest):
    planes, size, across = mine.shape
    result = rest[-1]
    half = half_of(lax.axis_index("view"))
    start = pl.multiple_of(size * (PARTS * half + part), 8)
    held = estimate[:, pl.ds(start, size)]
    result[:planes] = held * (mine[...] + other[...]) * (1.0 / views)
    if result.shape[0] > planes:
        result[planes:] = jnp.zeros((result.shape[0] - planes, size, across), F32)


def update(views, part, estimate, mine, other, after):
    planes, size, across = mine.shape
    count = planes + PARTS - 1 - part
    return pl.pallas_call(
        functools.partial(update_kernel, views, part),
        out_shape=jax.ShapeDtypeStruct((count, size, across), F32),
        in_specs=[VMEM] * 3 + [ANY] * len(after),
        out_specs=VMEM,
        compiler_params=pltpu.CompilerParams(vmem_limit_bytes=LIMIT),
        name="update",
    )(estimate, mine, other, *after)


def slots_kernel(views, owner_row, index_row, picked, base):
    count = base.shape[0]
    slots = owner_row.shape[1]
    owner = owner_row[...]
    member = (lax.broadcasted_iota(jnp.int32, (count // views, slots), 0) == owner).astype(F32)
    upto = (
        lax.broadcasted_iota(jnp.int32, (slots, slots), 0)
        <= lax.broadcasted_iota(jnp.int32, (slots, slots), 1)
    ).astype(F32)
    running = jnp.dot(member, upto, preferred_element_type=F32)
    rank = jnp.sum(member * running, axis=0, keepdims=True).astype(jnp.int32) - 1
    named = lax.broadcasted_iota(jnp.int32, (count, slots), 0) // views == owner
    index = index_row[...].astype(F32)
    lanes = lax.broadcasted_iota(jnp.int32, (count, LANES), 1)
    result = jnp.zeros((count, LANES), F32)
    for place in range(CAP):
        chosen = named & (rank == place)
        picked[place * count : (place + 1) * count] = chosen.astype(F32)
        ids = jnp.sum(jnp.where(chosen, index, 0.0), axis=1, keepdims=True)
        result = jnp.where(lanes == place * WIDTH + IDS, ids, result)
    base[...] = result


def slot_places(tiles, views, label_owner, label_index):
    slots = label_index.shape[1]
    count = tiles * views
    return pl.pallas_call(
        functools.partial(slots_kernel, views),
        out_shape=(
            jax.ShapeDtypeStruct((CAP * count, slots), F32),
            jax.ShapeDtypeStruct((count, LANES), F32),
        ),
        in_specs=[VMEM, VMEM],
        out_specs=(VMEM, VMEM),
        compiler_params=pltpu.CompilerParams(vmem_limit_bytes=LIMIT),
        name="slot_places",
    )(label_owner.reshape(1, slots), label_index)


def merge_rows(blocks):
    rows = lax.broadcasted_iota(jnp.int32, blocks[0].shape, 0)
    step = 4
    while step:
        low = (rows & step) == 0
        half = len(blocks) // 2
        merged = []
        for one, two in zip(blocks[:half], blocks[half:]):
            kept = jnp.where(low, one, two)
            turned = jnp.where(low, two, one)
            moved = pltpu.roll(turned, step, 0)
            if step < 4:
                moved = jnp.where(low, pltpu.roll(turned, 8 - step, 0), moved)
            merged.append(kept + moved)
        blocks = merged
        step //= 2
    return blocks[0]


def moments_kernel(views, depth_total, part, estimate, labels, picked, base, correction, *refs):
    begun, (sent, held, sums, table) = refs[:-4], refs[-4:]
    planes, size, across = correction.shape
    height_total = estimate.shape[1]
    slots = picked.shape[1]
    half = half_of(lax.axis_index("view"))
    first = (lax.axis_index("tile") * planes).astype(F32) + 0.5
    start = pl.multiple_of(size * (PARTS * half + part), 8)
    held[...] = estimate[:, pl.ds(start, size)] * correction[...] * (1.0 / views)
    group = 16
    spot = lax.broadcasted_iota(jnp.int32, (across, LANES), 0)
    lanes = lax.broadcasted_iota(jnp.int32, (across, LANES), 1)
    low = (spot * spot) & 255
    factors = jnp.where(lanes == 0, 1, jnp.where(lanes == 1, spot, 0))
    factors = jnp.where(lanes == 2, spot * spot - low, jnp.where(lanes == 3, low, factors))
    factors = factors.astype(F32).astype(BF16)
    base_row = lax.broadcasted_iota(jnp.int32, (8, across), 0)

    def one_group(number, carry):
        held_parts = []
        for pair in range(0, group, 2):
            slot = [number * group + pair, number * group + pair + 1]
            parts = [[None] * 6 for _ in slot]
            for row in range(0, size, 8):
                high = ((base_row + (row + start)).astype(F32) + 0.5) * (1.0 / height_total)
                flat, once, twice = [[jnp.zeros((8, across), F32) for _ in slot] for _ in range(3)]
                for plane in reversed(range(planes)):
                    mark = labels[plane, pl.ds(pl.multiple_of(start + row, 8), 8)]
                    value = held[plane, row : row + 8]
                    for at in range(2):
                        flat[at] = flat[at] + jnp.where(mark == slot[at], value, 0.0)
                        if plane > 0:
                            once[at] = once[at] + flat[at]
                            twice[at] = twice[at] + once[at]
                for at in range(2):
                    scaled = flat[at] * high
                    terms = (flat[at], scaled, scaled * high, once[at], once[at] * high, twice[at])
                    parts[at] = [new if old is None else old + new for old, new in zip(parts[at], terms)]
            held_parts += parts
            if len(held_parts) == 8:
                for kind in range(6):
                    row = kind * group + pair + 2 - 8
                    sums[row : row + 8, :] = merge_rows([parts[kind] for parts in held_parts])
                held_parts = []
        whole = sums[...]
        upper, rest = split(whole)
        rest = whole - upper.astype(F32)
        middle, lower = split(rest)
        lines = jnp.dot(
            jnp.concatenate([upper, middle, lower], axis=0), factors, preferred_element_type=F32
        )
        count = 6 * group
        lines = lines[:count] + lines[count : 2 * count] + lines[2 * count :]
        flat, high_flat, square_flat, once, high_once, twice = [
            lines[kind * group : (kind + 1) * group] for kind in range(6)
        ]
        deep = (first * flat + once) * (1.0 / depth_total)
        deep_high = (first * high_flat + high_once) * (1.0 / depth_total)
        deeper = first * (first * flat + 2.0 * once) + (2.0 * twice - once)
        deeper = deeper * (1.0 / depth_total**2)
        total = flat
        for kind, sums_of in enumerate((high_flat, square_flat, deep, deep_high, deeper), 1):
            total += pltpu.roll(sums_of, 4 * kind, 1)
        rows = pl.ds(pl.multiple_of(number * group, group), group)
        target = table if part == PARTS - 1 else sent
        target[rows, :] = total + begun[0][rows, :] if begun else total
        return carry

    lax.fori_loop(0, slots // group, one_group, 0)
    if part < PARTS - 1:
        return
    rows = jnp.dot(
        picked[...], table[...], precision=lax.Precision.HIGHEST, preferred_element_type=F32
    )
    total = base[...]
    count = total.shape[0]
    for place in range(CAP):
        total += pltpu.roll(rows[place * count : (place + 1) * count], place * WIDTH, 1)
    sent[...] = total


def moment_rows(views, tiles, part, estimate, correction, labels, places, begun):
    planes, size, across = correction.shape
    slots = places[0].shape[1]
    count = places[1].shape[0] if part == PARTS - 1 else slots
    return pl.pallas_call(
        functools.partial(moments_kernel, views, tiles * planes, part),
        out_shape=jax.ShapeDtypeStruct((count, LANES), F32),
        in_specs=[VMEM] * (5 + len(begun)),
        out_specs=VMEM,
        scratch_shapes=[
            pltpu.VMEM((planes, size, across), F32),
            pltpu.VMEM((6 * 16, across), F32),
            pltpu.VMEM((slots, LANES), F32),
        ],
        compiler_params=pltpu.CompilerParams(vmem_limit_bytes=LIMIT),
        name="moment_rows",
    )(estimate, labels, *places, correction, *begun)


def segments_kernel(across, scale, rows, moments):
    whole = rows[...]
    parts = [whole] + [pltpu.roll(whole, LANES - place * WIDTH, 1) for place in range(1, CAP)]
    values = jnp.concatenate(parts, axis=0)
    ids = values[:, IDS : IDS + 1].astype(jnp.int32)
    spots = lax.broadcasted_iota(jnp.int32, (values.shape[0], NUC_DEV), 1)
    picked = (ids == spots).astype(F32)
    full = lax.dot_general(
        values, picked, (((0,), (0,)), ((), ())),
        precision=lax.Precision.HIGHEST, preferred_element_type=F32,
    )
    mass, high, higher, deep, deep_high, deeper = [full[4 * kind : 4 * kind + 4] for kind in range(6)]
    flat = lambda sums: sums[0:1]
    line = lambda sums: (sums[1:2] + 0.5 * sums[0:1]) * (1.0 / across)
    square = lambda sums: (sums[2:3] + sums[3:4] + sums[1:2] + 0.25 * sums[0:1]) * (1.0 / across**2)
    total = flat(mass)
    sums = jnp.concatenate(
        [
            flat(deep), flat(high), line(mass),
            flat(deeper), flat(higher), square(mass),
            flat(deep_high), line(deep), line(high),
        ],
        axis=0,
    )
    moments[...] = jnp.concatenate([total * scale, sums / jnp.maximum(total, 1.0)], axis=0)


def nucleus_table(across, scale, rows):
    return pl.pallas_call(
        functools.partial(segments_kernel, across, scale),
        out_shape=jax.ShapeDtypeStruct((MOM, NUC_DEV), F32),
        in_specs=[VMEM],
        out_specs=VMEM,
        compiler_params=pltpu.CompilerParams(vmem_limit_bytes=LIMIT),
        cost_estimate=pl.CostEstimate(flops=10_000_000_000, bytes_accessed=20_000_000, transcendentals=0),
        name="nucleus_table",
    )(rows)


def store_of(source, whole, half, part, sem):
    planes, size = whole.shape[0], source.shape[1]
    start = pl.multiple_of(size * (PARTS * half + part), 8)
    return pltpu.make_async_copy(
        source.at[pl.ds(0, planes)], whole.at[:, pl.ds(start, size)], sem
    )


def token_kernel(source, *rest):
    token = rest[-1]
    token[...] = source[0, :8, :LANES]


def token_of(source, after=()):
    return pl.pallas_call(
        token_kernel,
        out_shape=jax.ShapeDtypeStruct((8, LANES), F32),
        in_specs=[VMEM] + [ANY] * len(after),
        out_specs=VMEM,
        compiler_params=pltpu.CompilerParams(vmem_limit_bytes=LIMIT),
        name="token_of",
    )(source, *after)


def begin_kernel(*refs):
    sources, (whole, sems) = refs[:-2], refs[-2:]
    half = half_of(lax.axis_index("view"))
    copies = [
        store_of(source, whole, half, part, sems.at[part]) for part, source in enumerate(sources)
    ]
    for copy in copies:
        copy.start()
    for copy in copies:
        copy.wait()


def begin_result(shape, mine):
    return pl.pallas_call(
        begin_kernel,
        out_shape=jax.ShapeDtypeStruct(shape, F32),
        in_specs=[VMEM] * len(mine),
        out_specs=ANY,
        scratch_shapes=[pltpu.SemaphoreType.DMA((len(mine),))],
        compiler_params=pltpu.CompilerParams(vmem_limit_bytes=LIMIT),
        name="begin_result",
    )(*mine)


def store_kernel(part, begun, other, whole, sem):
    copy = store_of(other, whole, 1 - half_of(lax.axis_index("view")), part, sem)
    copy.start()
    copy.wait()


def store_part(part, begun, other):
    return pl.pallas_call(
        functools.partial(store_kernel, part),
        out_shape=jax.ShapeDtypeStruct(begun.shape, F32),
        in_specs=[ANY, VMEM],
        out_specs=ANY,
        input_output_aliases={0: 0},
        scratch_shapes=[pltpu.SemaphoreType.DMA],
        compiler_params=pltpu.CompilerParams(vmem_limit_bytes=LIMIT),
        name="store_part",
    )(begun, other)


def on_device(estimate, measured, kernels, labels, label_owner, label_index):
    tiles, views = lax.axis_size("tile"), lax.axis_size("view")
    planes, height, across = estimate.shape
    taps = kernels.shape[2]
    radius = (taps - 1) // 2
    keep = height // 2
    seen = min(height, -(-(keep + radius) // 8) * 8)
    rows = min(height, -(-(keep + 2 * radius) // 16) * 16)
    near_pairs = [(i, i ^ 1) for i in range(tiles)]
    far_pairs = [(i, i + 1) for i in range(1, tiles - 1, 2)]
    far_pairs = far_pairs + [(b, a) for a, b in far_pairs]
    partner = [(i, i ^ 1) for i in range(views)]
    across_pairs = [(i, i ^ 3) for i in range(views)]

    lines = jnp.transpose(kernels, (1, 0, 2))
    blank = blank_rows(across)
    packed = view_out(measured, lines, blank, seen)
    swapped = lax.ppermute(packed, "view", partner)
    to_far, to_near = rims_out(estimate, blank, radius, rows)
    far = lax.ppermute(to_far, "tile", far_pairs)
    near = lax.ppermute(to_near, "tile", near_pairs)
    places = slot_places(tiles, views, label_owner, label_index)
    own = prepare(False, taps, lines, estimate, places[1], rows, seen, keep)
    others = prepare(True, taps, swapped, estimate, lines, rows, seen, keep)
    came = token_of(far, (others[4],))
    field_own, field_other, *sends = ratio_fields(
        own, others, far, near, measured, swapped, came
    )
    rims = [
        lax.ppermute(send, "tile", pairs) for send, pairs in zip(sends, (far_pairs, near_pairs) * PARTS)
    ]
    inner = own_planes(taps, own[4], others[4], field_own, field_other)
    mine, other, sums = [], [], []
    for part in range(PARTS):
        mine.append(add_rims(inner[part], *rims[2 * part : 2 * part + 2], *sums))
        other.append(lax.ppermute(mine[part], "view", across_pairs))
        sums = [moment_rows(views, tiles, part, estimate, mine[part], labels, places, sums)]
    sent = sums[0]
    got = lax.all_to_all(sent, ("tile", "view"), split_axis=0, concat_axis=0, tiled=True)
    new_mine, new_other, token = [], [], [sent]
    for part in range(PARTS):
        new_mine.append(update(views, part, estimate, mine[part], other[part], token))
        new_other.append(lax.ppermute(new_mine[part], "view", partner))
        token = [token_of(new_mine[part])]
    scale = label_index.shape[1] / (planes * height * across)
    moments = nucleus_table(across, scale, got)
    whole = begin_result(estimate.shape, new_mine)
    for part in range(PARTS):
        whole = store_part(part, whole, new_other[part])
    return whole, moments


def solution(mesh):
    placed = (
        P("tile", None, None),
        P("view", "tile", None, None),
        P("view", None, None),
        P("tile", None, None),
        P("tile", None, None),
        P("tile", None),
    )
    return jax.shard_map(
        on_device,
        mesh=mesh,
        in_specs=placed,
        out_specs=(P("tile", None, None), P(None, "tile")),
        check_vma=False,
    )
```

```python
import functools

import jax
import jax.numpy as jnp
from jax import lax
from jax.experimental import pallas as pl
from jax.experimental.pallas import tpu as pltpu
from jax.sharding import PartitionSpec as P

MOM = 10
CAP = 5
WIDTH = 25
NUC_DEV = 128
LANES = 128
PARTS = 2
TAIL = 24
IDS = 24
F32 = jnp.float32
BF16 = jnp.bfloat16
ANY = pl.BlockSpec(memory_space=pl.ANY)
VMEM = pl.BlockSpec(memory_space=pltpu.VMEM)
LIMIT = 32 * 1024 * 1024


def told(billions):
    return pl.CostEstimate(
        flops=billions * 10**9, bytes_accessed=2 * billions * 10**6, transcendentals=0
    )


def half_of(view):
    return (view ^ (view >> 1)) & 1


def split(value):
    upper = value.astype(BF16)
    return upper, (value - upper.astype(F32)).astype(BF16)


def band(taps, shape, offset):
    rows = lax.broadcasted_iota(jnp.int32, shape, 0)
    cols = lax.broadcasted_iota(jnp.int32, shape, 1)
    place = cols - rows + offset
    result = jnp.zeros(shape, F32)
    for step, tap in enumerate(taps):
        result = jnp.where(place == step, tap, result)
    return result


def depth_terms(source, weights, first, last, planes, flipped):
    radius = (len(weights) - 1) // 2
    totals = {plane: None for plane in planes}
    for place in range(first, last):
        block = None
        for plane in planes:
            step = plane - place + radius if flipped else place - plane + radius
            if 0 <= step < len(weights):
                block = source(place) if block is None else block
                term = weights[step] * block
                totals[plane] = term if totals[plane] is None else totals[plane] + term
    return totals


def chunks(rows, across):
    return [(slice(row, row + 16), slice(lane, lane + LANES)) for row in range(0, rows, 16) for lane in range(0, across, LANES)]


def rims_out_kernel(estimate, after, to_far, to_near):
    planes, radius, rows = estimate.shape[0], to_far.shape[0], to_far.shape[1]
    odd = lax.axis_index("tile") % 2
    half = half_of(lax.axis_index("view"))
    start = pl.multiple_of((estimate.shape[1] - rows) * half, 8)
    to_far[...] = estimate[pl.ds(odd, radius), pl.ds(start, rows)]
    to_near[...] = estimate[pl.ds(1 - odd, radius), pl.ds(start, rows)]


def rims_out(estimate, after, radius, rows):
    shape = jax.ShapeDtypeStruct((radius, rows, estimate.shape[2]), F32)
    return pl.pallas_call(
        rims_out_kernel,
        out_shape=(shape, shape),
        in_specs=[VMEM, ANY],
        out_specs=(VMEM, VMEM),
        compiler_params=pltpu.CompilerParams(vmem_limit_bytes=LIMIT),
        name="rims_out",
    )(estimate, after)


def blank_kernel(rows):
    rows[...] = jnp.zeros_like(rows)


def blank_rows(across):
    return pl.pallas_call(
        blank_kernel,
        out_shape=jax.ShapeDtypeStruct((TAIL, across), F32),
        out_specs=VMEM,
        compiler_params=pltpu.CompilerParams(vmem_limit_bytes=LIMIT),
        cost_estimate=told(8),
        name="blank_rows",
    )()


def view_out_kernel(seen, measured, taps, blank, packed):
    planes, height = measured.shape[1], measured.shape[2]
    half = half_of(lax.axis_index("view"))
    start = pl.multiple_of((height - seen) * (1 - half), 8)
    for plane in range(planes):
        packed[plane * seen : (plane + 1) * seen] = measured[0, plane, pl.ds(start, seen)]
    packed[planes * seen :] = blank[...]
    for axis in range(taps.shape[0]):
        at = planes * seen + axis
        packed[at : at + 1, : taps.shape[2]] = taps[axis]


def view_out(measured, lines, blank, seen):
    _, planes, _, across = measured.shape
    return pl.pallas_call(
        functools.partial(view_out_kernel, seen),
        out_shape=jax.ShapeDtypeStruct((planes * seen + TAIL, across), F32),
        in_specs=[VMEM] * 3,
        out_specs=VMEM,
        compiler_params=pltpu.CompilerParams(vmem_limit_bytes=LIMIT),
        name="view_out",
    )(measured, lines, blank)


def prepare_kernel(packed, taps, source, estimate, after, wide, tall, back, part, spread):
    half = half_of(lax.axis_index("view"))
    across = wide.shape[-1]
    rows, keep, seen = part.shape[1], back.shape[0], tall.shape[0]
    planes = estimate.shape[0]
    radius = (taps - 1) // 2
    at = source.shape[0] - TAIL
    if packed:
        raw = source[at : at + 3, :taps]
    else:
        raw = jnp.concatenate([source[axis] for axis in range(source.shape[0])], axis=0)
    weights = raw / jnp.sum(raw, axis=-1, keepdims=True)
    deep, high, flat = [[weights[axis : axis + 1, t : t + 1] for t in range(taps)] for axis in range(3)]
    start = pl.multiple_of((2 * keep - rows) * half, 16)
    seen_start = (2 * keep - seen) * half
    near_diagonal = jnp.abs(
        lax.broadcasted_iota(jnp.int32, (across, across), 1)
        - lax.broadcasted_iota(jnp.int32, (across, across), 0)
    ) <= radius
    for turn, line in enumerate((flat[::-1], flat)):
        first_row = jnp.concatenate(
            line[radius:] + [jnp.zeros((1, across - taps), F32)] + line[:radius], axis=1
        )
        square = pltpu.roll(
            jnp.broadcast_to(first_row, (across, across)), 0, 1, stride=1, stride_axis=0
        )
        upper, lower = split(jnp.where(near_diagonal, square, 0.0))
        wide[turn, 0] = upper
        wide[turn, 1] = lower
    upper, lower = split(band(high, (seen, rows), radius + start - seen_start))
    tall[...] = jnp.concatenate([upper, upper, lower], axis=1)
    upper, lower = split(band(high[::-1], (keep, rows), radius + seen_start - keep * half))
    back[...] = jnp.concatenate([upper, upper, lower], axis=1)
    factors = [jnp.broadcast_to(tap, (16, LANES)) for tap in deep]
    spread[...] = jnp.zeros_like(spread)
    for step in range(taps):
        spread[step : step + 1] = factors[step][:1]
    for row, lane in chunks(rows, across):
        where = pl.ds(pl.multiple_of(start + row.start, 16), 16)
        terms = depth_terms(
            lambda place: estimate[place, where, lane], factors, 0, planes, range(planes), False
        )
        for plane, block in terms.items():
            part[plane, row, lane] = block


def prepare(packed, taps, source, estimate, after, rows, seen, keep):
    planes, _, across = estimate.shape
    return pl.pallas_call(
        functools.partial(prepare_kernel, packed, taps),
        out_shape=(
            jax.ShapeDtypeStruct((2, 2, across, across), BF16),
            jax.ShapeDtypeStruct((seen, 3 * rows), BF16),
            jax.ShapeDtypeStruct((keep, 3 * rows), BF16),
            jax.ShapeDtypeStruct((planes, rows, across), F32),
            jax.ShapeDtypeStruct((-(-taps // 8) * 8, LANES), F32),
        ),
        in_specs=[VMEM, VMEM, ANY],
        out_specs=(VMEM,) * 5,
        compiler_params=pltpu.CompilerParams(vmem_limit_bytes=LIMIT),
        name="prepare",
    )(source, estimate, after)


def spread_factors(spread, taps):
    return [jnp.broadcast_to(spread[step : step + 1, :], (16, LANES)) for step in range(taps)]


def view_kernel(first, *refs):
    wide, tall, back, part, spread, far, near, view = refs[:8]
    begun = () if first else refs[9 : 9 + 2 * PARTS]
    refs = refs[9 + len(begun) :]
    field, *sends = refs[: 1 + 2 * PARTS]
    blur_hi, blur_lo, plane_hi, plane_lo = refs[1 + 2 * PARTS :]
    planes = part.shape[0]
    radius, rows, across = near.shape
    keep, seen = back.shape[0], tall.shape[0]
    taps = 2 * radius + 1
    even = lax.axis_index("tile") % 2 == 0
    half = half_of(lax.axis_index("view"))
    seen_start = pl.multiple_of((2 * keep - seen) * half, 8)
    factors = spread_factors(spread, taps)
    for row, lane in chunks(rows, across):

        def rim(place):
            if place < 0:
                at = place + radius
                return jnp.where(even, far[at, row, lane], near[at, row, lane])
            at = place - planes
            return jnp.where(even, near[at, row, lane], far[at, row, lane])

        below = depth_terms(rim, factors, -radius, 0, range(planes), False)
        above = depth_terms(rim, factors, planes, planes + radius, range(planes), False)
        for plane in range(planes):
            block = part[plane, row, lane]
            for term in (below[plane], above[plane]):
                block = block if term is None else block + term
            upper, lower = split(block)
            at = slice(plane * rows + row.start, plane * rows + row.stop)
            blur_hi[at, lane] = upper
            blur_lo[at, lane] = lower
    upper, lower = wide[0, 0], wide[0, 1]
    lines = (
        jnp.dot(blur_hi[...], upper, preferred_element_type=F32)
        + jnp.dot(blur_lo[...], upper, preferred_element_type=F32)
        + jnp.dot(blur_hi[...], lower, preferred_element_type=F32)
    )
    forwards = []
    for plane in range(planes):
        hi, lo = split(lines[plane * rows : (plane + 1) * rows])
        forwards.append(
            jnp.dot(tall[...], jnp.concatenate([hi, lo, hi], axis=0), preferred_element_type=F32)
        )
    ratios = []
    for plane in range(planes):
        if first:
            recorded = view[0, plane, pl.ds(seen_start, seen), :]
        else:
            recorded = view[plane * seen : (plane + 1) * seen]
        ratio = recorded / forwards[plane]
        if rows > seen:
            ratio = jnp.concatenate([ratio, jnp.zeros((rows - seen, across), F32)], axis=0)
        ratios.append(split(ratio))
    turned = [
        jnp.dot(back[...], jnp.concatenate([hi, lo, hi], axis=0), preferred_element_type=F32)
        for hi, lo in ratios
    ]
    for plane in range(planes):
        hi, lo = split(turned[plane])
        plane_hi[plane * keep : (plane + 1) * keep] = hi
        plane_lo[plane * keep : (plane + 1) * keep] = lo
    upper, lower = wide[1, 0], wide[1, 1]
    result = (
        jnp.dot(plane_hi[...], upper, preferred_element_type=F32)
        + jnp.dot(plane_lo[...], upper, preferred_element_type=F32)
        + jnp.dot(plane_hi[...], lower, preferred_element_type=F32)
    )
    field[...] = result.reshape(planes, keep, across)
    for row, lane in chunks(keep, across):
        source = lambda place: field[place, row, lane]
        below = depth_terms(source, factors, 0, planes, range(-radius, 0), True)
        above = depth_terms(source, factors, 0, planes, range(planes, planes + radius), True)
        part_at, inside = divmod(row.start, keep // PARTS)
        inside = slice(inside, inside + 16)
        for at in range(radius):
            down, up = below[at - radius], above[at + planes]
            to_far, to_near = jnp.where(even, down, up), jnp.where(even, up, down)
            if begun:
                to_far += begun[2 * part_at][at, inside, lane]
                to_near += begun[2 * part_at + 1][at, inside, lane]
            sends[2 * part_at][at, inside, lane] = to_far
            sends[2 * part_at + 1][at, inside, lane] = to_near


def view_field(first, prepared, far, near, view, after, begun):
    keep, planes = prepared[2].shape[0], prepared[3].shape[0]
    radius, rows, across = near.shape
    send = jax.ShapeDtypeStruct((radius, keep // PARTS, across), F32)
    return pl.pallas_call(
        functools.partial(view_kernel, first),
        out_shape=(jax.ShapeDtypeStruct((planes, keep, across), F32),) + (send,) * (2 * PARTS),
        in_specs=[VMEM] * 8 + [ANY] + [VMEM] * len(begun),
        out_specs=(VMEM,) * (1 + 2 * PARTS),
        scratch_shapes=[
            pltpu.VMEM((planes * rows, across), BF16),
            pltpu.VMEM((planes * rows, across), BF16),
            pltpu.VMEM((planes * keep, across), BF16),
            pltpu.VMEM((planes * keep, across), BF16),
        ],
        compiler_params=pltpu.CompilerParams(vmem_limit_bytes=LIMIT),
        name="own_view" if first else "other_view",
    )(*prepared, far, near, view, after, *begun)


def own_kernel(taps, spread_own, spread_other, field_own, field_other, *inner):
    planes, keep, across = field_own.shape
    factors = [spread_factors(spread, taps) for spread in (spread_own, spread_other)]
    for row, lane in chunks(keep, across):
        parts = [
            depth_terms(
                lambda place: field[place, row, lane], factors[which], 0, planes, range(planes), True
            )
            for which, field in enumerate((field_own, field_other))
        ]
        part_at, inside = divmod(row.start, keep // PARTS)
        for plane in range(planes):
            inner[part_at][plane, inside : inside + 16, lane] = parts[0][plane] + parts[1][plane]


def own_planes(taps, spread_own, spread_other, field_own, field_other):
    planes, keep, across = field_own.shape
    return pl.pallas_call(
        functools.partial(own_kernel, taps),
        out_shape=(jax.ShapeDtypeStruct((planes, keep // PARTS, across), F32),) * PARTS,
        in_specs=[VMEM] * 4,
        out_specs=(VMEM,) * PARTS,
        compiler_params=pltpu.CompilerParams(vmem_limit_bytes=LIMIT),
        name="own_planes",
    )(spread_own, spread_other, field_own, field_other)


def rims_kernel(inner, far, near, *rest):
    correction = rest[-1]
    planes, radius = inner.shape[0], near.shape[0]
    even = lax.axis_index("tile") % 2 == 0
    for plane in range(planes):
        total = inner[plane]
        if plane < radius:
            total += jnp.where(even, far[plane], near[plane])
        if plane >= planes - radius:
            at = plane - planes + radius
            total += jnp.where(even, near[at], far[at])
        correction[plane] = total


def add_rims(inner, far, near, *after):
    return pl.pallas_call(
        rims_kernel,
        out_shape=jax.ShapeDtypeStruct(inner.shape, F32),
        in_specs=[VMEM] * 3 + [ANY] * len(after),
        out_specs=VMEM,
        compiler_params=pltpu.CompilerParams(vmem_limit_bytes=LIMIT),
        name="add_rims",
    )(inner, far, near, *after)


def table_rows(table):
    return jnp.concatenate([table[:8], table[8:]], axis=1)


def update_kernel(views, part, estimate, mine, other, *rest):
    planes, size, across = mine.shape
    result = rest[-1]
    half = half_of(lax.axis_index("view"))
    start = pl.multiple_of(size * (PARTS * half + part), 8)
    held = estimate[:, pl.ds(start, size)]
    result[:planes] = held * (mine[...] + other[...]) * (1.0 / views)
    if result.shape[0] > planes:
        result[planes:] = jnp.zeros((result.shape[0] - planes, size, across), F32)


def update(views, part, estimate, mine, other, after):
    planes, size, across = mine.shape
    count = planes + PARTS - 1 - part
    return pl.pallas_call(
        functools.partial(update_kernel, views, part),
        out_shape=jax.ShapeDtypeStruct((count, size, across), F32),
        in_specs=[VMEM] * 3 + [ANY] * len(after),
        out_specs=VMEM,
        compiler_params=pltpu.CompilerParams(vmem_limit_bytes=LIMIT),
        name="update",
    )(estimate, mine, other, *after)


def slots_kernel(views, owner_row, index_row, picked, base):
    count = base.shape[0]
    slots = owner_row.shape[1]
    owner = owner_row[...]
    member = (lax.broadcasted_iota(jnp.int32, (count // views, slots), 0) == owner).astype(F32)
    upto = (
        lax.broadcasted_iota(jnp.int32, (slots, slots), 0)
        <= lax.broadcasted_iota(jnp.int32, (slots, slots), 1)
    ).astype(F32)
    running = jnp.dot(member, upto, preferred_element_type=F32)
    rank = jnp.sum(member * running, axis=0, keepdims=True).astype(jnp.int32) - 1
    named = lax.broadcasted_iota(jnp.int32, (count, slots), 0) // views == owner
    index = index_row[...].astype(F32)
    lanes = lax.broadcasted_iota(jnp.int32, (count, LANES), 1)
    result = jnp.zeros((count, LANES), F32)
    for place in range(CAP):
        chosen = named & (rank == place)
        picked[place * count : (place + 1) * count] = chosen.astype(F32)
        ids = jnp.sum(jnp.where(chosen, index, 0.0), axis=1, keepdims=True)
        result = jnp.where(lanes == place * WIDTH + IDS, ids, result)
    base[...] = result


def slot_places(tiles, views, label_owner, label_index):
    slots = label_index.shape[1]
    count = tiles * views
    return pl.pallas_call(
        functools.partial(slots_kernel, views),
        out_shape=(
            jax.ShapeDtypeStruct((CAP * count, slots), F32),
            jax.ShapeDtypeStruct((count, LANES), F32),
        ),
        in_specs=[VMEM, VMEM],
        out_specs=(VMEM, VMEM),
        compiler_params=pltpu.CompilerParams(vmem_limit_bytes=LIMIT),
        name="slot_places",
    )(label_owner.reshape(1, slots), label_index)


def merge_rows(blocks):
    rows = lax.broadcasted_iota(jnp.int32, blocks[0].shape, 0)
    step = 4
    while step:
        low = (rows & step) == 0
        half = len(blocks) // 2
        merged = []
        for one, two in zip(blocks[:half], blocks[half:]):
            kept = jnp.where(low, one, two)
            turned = jnp.where(low, two, one)
            moved = pltpu.roll(turned, step, 0)
            if step < 4:
                moved = jnp.where(low, pltpu.roll(turned, 8 - step, 0), moved)
            merged.append(kept + moved)
        blocks = merged
        step //= 2
    return blocks[0]


def moments_kernel(views, depth_total, part, estimate, labels, picked, base, correction, *refs):
    begun, (sent, held, sums, table) = refs[:-4], refs[-4:]
    planes, size, across = correction.shape
    height_total = estimate.shape[1]
    slots = picked.shape[1]
    half = half_of(lax.axis_index("view"))
    first = (lax.axis_index("tile") * planes).astype(F32) + 0.5
    start = pl.multiple_of(size * (PARTS * half + part), 8)
    held[...] = estimate[:, pl.ds(start, size)] * correction[...] * (1.0 / views)
    group = 16
    spot = lax.broadcasted_iota(jnp.int32, (across, LANES), 0)
    lanes = lax.broadcasted_iota(jnp.int32, (across, LANES), 1)
    low = (spot * spot) & 255
    factors = jnp.where(lanes == 0, 1, jnp.where(lanes == 1, spot, 0))
    factors = jnp.where(lanes == 2, spot * spot - low, jnp.where(lanes == 3, low, factors))
    factors = factors.astype(F32).astype(BF16)
    base_row = lax.broadcasted_iota(jnp.int32, (8, across), 0)

    def one_group(number, carry):
        held_parts = []
        for pair in range(0, group, 2):
            slot = [number * group + pair, number * group + pair + 1]
            parts = [[None] * 6 for _ in slot]
            for row in range(0, size, 8):
                high = ((base_row + (row + start)).astype(F32) + 0.5) * (1.0 / height_total)
                flat, once, twice = [[jnp.zeros((8, across), F32) for _ in slot] for _ in range(3)]
                for plane in reversed(range(planes)):
                    mark = labels[plane, pl.ds(pl.multiple_of(start + row, 8), 8)]
                    value = held[plane, row : row + 8]
                    for at in range(2):
                        flat[at] = flat[at] + jnp.where(mark == slot[at], value, 0.0)
                        if plane > 0:
                            once[at] = once[at] + flat[at]
                            twice[at] = twice[at] + once[at]
                for at in range(2):
                    scaled = flat[at] * high
                    terms = (flat[at], scaled, scaled * high, once[at], once[at] * high, twice[at])
                    parts[at] = [new if old is None else old + new for old, new in zip(parts[at], terms)]
            held_parts += parts
            if len(held_parts) == 8:
                for kind in range(6):
                    row = kind * group + pair + 2 - 8
                    sums[row : row + 8, :] = merge_rows([parts[kind] for parts in held_parts])
                held_parts = []
        whole = sums[...]
        upper, rest = split(whole)
        rest = whole - upper.astype(F32)
        middle, lower = split(rest)
        lines = jnp.dot(
            jnp.concatenate([upper, middle, lower], axis=0), factors, preferred_element_type=F32
        )
        count = 6 * group
        lines = lines[:count] + lines[count : 2 * count] + lines[2 * count :]
        flat, high_flat, square_flat, once, high_once, twice = [
            lines[kind * group : (kind + 1) * group] for kind in range(6)
        ]
        deep = (first * flat + once) * (1.0 / depth_total)
        deep_high = (first * high_flat + high_once) * (1.0 / depth_total)
        deeper = first * (first * flat + 2.0 * once) + (2.0 * twice - once)
        deeper = deeper * (1.0 / depth_total**2)
        total = flat
        for kind, sums_of in enumerate((high_flat, square_flat, deep, deep_high, deeper), 1):
            total += pltpu.roll(sums_of, 4 * kind, 1)
        rows = pl.ds(pl.multiple_of(number * group, group), group)
        target = table if part == PARTS - 1 else sent
        target[rows, :] = total + begun[0][rows, :] if begun else total
        return carry

    lax.fori_loop(0, slots // group, one_group, 0)
    if part < PARTS - 1:
        return
    rows = jnp.dot(
        picked[...], table[...], precision=lax.Precision.HIGHEST, preferred_element_type=F32
    )
    total = base[...]
    count = total.shape[0]
    for place in range(CAP):
        total += pltpu.roll(rows[place * count : (place + 1) * count], place * WIDTH, 1)
    sent[...] = total


def moment_rows(views, tiles, part, estimate, correction, labels, places, begun):
    planes, size, across = correction.shape
    slots = places[0].shape[1]
    count = places[1].shape[0] if part == PARTS - 1 else slots
    return pl.pallas_call(
        functools.partial(moments_kernel, views, tiles * planes, part),
        out_shape=jax.ShapeDtypeStruct((count, LANES), F32),
        in_specs=[VMEM] * (5 + len(begun)),
        out_specs=VMEM,
        scratch_shapes=[
            pltpu.VMEM((planes, size, across), F32),
            pltpu.VMEM((6 * 16, across), F32),
            pltpu.VMEM((slots, LANES), F32),
        ],
        compiler_params=pltpu.CompilerParams(vmem_limit_bytes=LIMIT),
        name="moment_rows",
    )(estimate, labels, *places, correction, *begun)


def segments_kernel(across, scale, rows, moments):
    whole = rows[...]
    parts = [whole] + [pltpu.roll(whole, LANES - place * WIDTH, 1) for place in range(1, CAP)]
    values = jnp.concatenate(parts, axis=0)
    ids = values[:, IDS : IDS + 1].astype(jnp.int32)
    spots = lax.broadcasted_iota(jnp.int32, (values.shape[0], NUC_DEV), 1)
    picked = (ids == spots).astype(F32)
    full = lax.dot_general(
        values, picked, (((0,), (0,)), ((), ())),
        precision=lax.Precision.HIGHEST, preferred_element_type=F32,
    )
    mass, high, higher, deep, deep_high, deeper = [full[4 * kind : 4 * kind + 4] for kind in range(6)]
    flat = lambda sums: sums[0:1]
    line = lambda sums: (sums[1:2] + 0.5 * sums[0:1]) * (1.0 / across)
    square = lambda sums: (sums[2:3] + sums[3:4] + sums[1:2] + 0.25 * sums[0:1]) * (1.0 / across**2)
    total = flat(mass)
    sums = jnp.concatenate(
        [
            flat(deep), flat(high), line(mass),
            flat(deeper), flat(higher), square(mass),
            flat(deep_high), line(deep), line(high),
        ],
        axis=0,
    )
    moments[...] = jnp.concatenate([total * scale, sums / jnp.maximum(total, 1.0)], axis=0)


def nucleus_table(across, scale, rows):
    return pl.pallas_call(
        functools.partial(segments_kernel, across, scale),
        out_shape=jax.ShapeDtypeStruct((MOM, NUC_DEV), F32),
        in_specs=[VMEM],
        out_specs=VMEM,
        compiler_params=pltpu.CompilerParams(vmem_limit_bytes=LIMIT),
        cost_estimate=told(10),
        name="nucleus_table",
    )(rows)


def store_of(source, whole, half, part, sem):
    planes, size = whole.shape[0], source.shape[1]
    start = pl.multiple_of(size * (PARTS * half + part), 8)
    return pltpu.make_async_copy(
        source.at[pl.ds(0, planes)], whole.at[:, pl.ds(start, size)], sem
    )


def token_kernel(source, *rest):
    token = rest[-1]
    token[...] = source[0, :8, :LANES]


def token_of(source, after=(), billions=0):
    return pl.pallas_call(
        token_kernel,
        out_shape=jax.ShapeDtypeStruct((8, LANES), F32),
        in_specs=[VMEM] + [ANY] * len(after),
        out_specs=VMEM,
        compiler_params=pltpu.CompilerParams(vmem_limit_bytes=LIMIT),
        cost_estimate=told(billions),
        name="token_of",
    )(source, *after)


def begin_kernel(*refs):
    sources, (whole, sems) = refs[:-2], refs[-2:]
    half = half_of(lax.axis_index("view"))
    copies = [
        store_of(source, whole, half, part, sems.at[part]) for part, source in enumerate(sources)
    ]
    for copy in copies:
        copy.start()
    for copy in copies:
        copy.wait()


def begin_result(shape, mine):
    return pl.pallas_call(
        begin_kernel,
        out_shape=jax.ShapeDtypeStruct(shape, F32),
        in_specs=[VMEM] * len(mine),
        out_specs=ANY,
        scratch_shapes=[pltpu.SemaphoreType.DMA((len(mine),))],
        compiler_params=pltpu.CompilerParams(vmem_limit_bytes=LIMIT),
        name="begin_result",
    )(*mine)


def store_kernel(part, begun, other, whole, sem):
    copy = store_of(other, whole, 1 - half_of(lax.axis_index("view")), part, sem)
    copy.start()
    copy.wait()


def store_part(part, begun, other):
    return pl.pallas_call(
        functools.partial(store_kernel, part),
        out_shape=jax.ShapeDtypeStruct(begun.shape, F32),
        in_specs=[ANY, VMEM],
        out_specs=ANY,
        input_output_aliases={0: 0},
        scratch_shapes=[pltpu.SemaphoreType.DMA],
        compiler_params=pltpu.CompilerParams(vmem_limit_bytes=LIMIT),
        name="store_part",
    )(begun, other)


def on_device(estimate, measured, kernels, labels, label_owner, label_index):
    tiles, views = lax.axis_size("tile"), lax.axis_size("view")
    planes, height, across = estimate.shape
    taps = kernels.shape[2]
    radius = (taps - 1) // 2
    keep = height // 2
    seen = min(height, -(-(keep + radius) // 8) * 8)
    rows = min(height, -(-(keep + 2 * radius) // 16) * 16)
    near_pairs = [(i, i ^ 1) for i in range(tiles)]
    far_pairs = [(i, i + 1) for i in range(1, tiles - 1, 2)]
    far_pairs = far_pairs + [(b, a) for a, b in far_pairs]
    partner = [(i, i ^ 1) for i in range(views)]
    across_pairs = [(i, i ^ 3) for i in range(views)]

    lines = jnp.transpose(kernels, (1, 0, 2))
    blank = blank_rows(across)
    packed = view_out(measured, lines, blank, seen)
    swapped = lax.ppermute(packed, "view", partner)
    to_far, to_near = rims_out(estimate, blank, radius, rows)
    far = lax.ppermute(to_far, "tile", far_pairs)
    near = lax.ppermute(to_near, "tile", near_pairs)
    places = slot_places(tiles, views, label_owner, label_index)
    own = prepare(False, taps, lines, estimate, places[1], rows, seen, keep)
    came = token_of(far, (), 8)
    field_own, *begun = view_field(True, own, far, near, measured, came, ())
    others = prepare(True, taps, swapped, estimate, begun[0], rows, seen, keep)
    field_other, *sends = view_field(False, others, far, near, swapped, came, begun)
    rims = [
        lax.ppermute(send, "tile", pairs) for send, pairs in zip(sends, (far_pairs, near_pairs) * PARTS)
    ]
    inner = own_planes(taps, own[4], others[4], field_own, field_other)
    mine, other, sums = [], [], []
    for part in range(PARTS):
        mine.append(add_rims(inner[part], *rims[2 * part : 2 * part + 2], *sums))
        other.append(lax.ppermute(mine[part], "view", across_pairs))
        sums = [moment_rows(views, tiles, part, estimate, mine[part], labels, places, sums)]
    sent = sums[0]
    got = lax.all_to_all(sent, ("tile", "view"), split_axis=0, concat_axis=0, tiled=True)
    new_mine, new_other, token = [], [], [sent]
    for part in range(PARTS):
        new_mine.append(update(views, part, estimate, mine[part], other[part], token))
        new_other.append(lax.ppermute(new_mine[part], "view", partner))
        token = [token_of(new_mine[part])]
    scale = label_index.shape[1] / (planes * height * across)
    moments = nucleus_table(across, scale, got)
    whole = begin_result(estimate.shape, new_mine)
    for part in range(PARTS):
        whole = store_part(part, whole, new_other[part])
    return whole, moments


def solution(mesh):
    placed = (
        P("tile", None, None),
        P("view", "tile", None, None),
        P("view", None, None),
        P("tile", None, None),
        P("tile", None, None),
        P("tile", None),
    )
    return jax.shard_map(
        on_device,
        mesh=mesh,
        in_specs=placed,
        out_specs=(P("tile", None, None), P(None, "tile")),
        check_vma=False,
    )
```

```python
import functools

import jax
import jax.numpy as jnp
from jax import lax
from jax.experimental import pallas as pl
from jax.experimental.pallas import tpu as pltpu
from jax.sharding import PartitionSpec as P

MOM = 10
CAP = 5
WIDTH = 25
NUC_DEV = 128
LANES = 128
PARTS = 2
TAIL = 24
IDS = 24
F32 = jnp.float32
BF16 = jnp.bfloat16
ANY = pl.BlockSpec(memory_space=pl.ANY)
VMEM = pl.BlockSpec(memory_space=pltpu.VMEM)
LIMIT = 32 * 1024 * 1024


def half_of(view):
    return view & 1


def split(value):
    upper = value.astype(BF16)
    return upper, (value - upper.astype(F32)).astype(BF16)


def band(taps, shape, offset):
    rows = lax.broadcasted_iota(jnp.int32, shape, 0)
    cols = lax.broadcasted_iota(jnp.int32, shape, 1)
    place = cols - rows + offset
    result = jnp.zeros(shape, F32)
    for step, tap in enumerate(taps):
        result = jnp.where(place == step, tap, result)
    return result


def depth_terms(source, weights, first, last, planes, flipped):
    radius = (len(weights) - 1) // 2
    totals = {plane: None for plane in planes}
    for place in range(first, last):
        block = None
        for plane in planes:
            step = plane - place + radius if flipped else place - plane + radius
            if 0 <= step < len(weights):
                block = source(place) if block is None else block
                term = weights[step] * block
                totals[plane] = term if totals[plane] is None else totals[plane] + term
    return totals


def chunks(rows, across):
    return [(slice(row, row + 16), slice(lane, lane + LANES)) for row in range(0, rows, 16) for lane in range(0, across, LANES)]


def rims_out_kernel(estimate, after, to_far, to_near):
    planes, radius, rows = estimate.shape[0], to_far.shape[0], to_far.shape[1]
    odd = lax.axis_index("tile") % 2
    half = half_of(lax.axis_index("view"))
    start = pl.multiple_of((estimate.shape[1] - rows) * half, 8)
    to_far[...] = estimate[pl.ds(odd, radius), pl.ds(start, rows)]
    to_near[...] = estimate[pl.ds(1 - odd, radius), pl.ds(start, rows)]


def rims_out(estimate, after, radius, rows):
    shape = jax.ShapeDtypeStruct((radius, rows, estimate.shape[2]), F32)
    return pl.pallas_call(
        rims_out_kernel,
        out_shape=(shape, shape),
        in_specs=[VMEM, ANY],
        out_specs=(VMEM, VMEM),
        compiler_params=pltpu.CompilerParams(vmem_limit_bytes=LIMIT),
        name="rims_out",
    )(estimate, after)


def blank_kernel(rows):
    rows[...] = jnp.zeros_like(rows)


def blank_rows(across):
    return pl.pallas_call(
        blank_kernel,
        out_shape=jax.ShapeDtypeStruct((TAIL, across), F32),
        out_specs=VMEM,
        compiler_params=pltpu.CompilerParams(vmem_limit_bytes=LIMIT),
        cost_estimate=pl.CostEstimate(flops=8_000_000_000, bytes_accessed=16_000_000, transcendentals=0),
        name="blank_rows",
    )()


def view_out_kernel(seen, measured, taps, blank, packed):
    planes, height = measured.shape[1], measured.shape[2]
    half = half_of(lax.axis_index("view"))
    start = pl.multiple_of((height - seen) * (1 - half), 8)
    for plane in range(planes):
        packed[plane * seen : (plane + 1) * seen] = measured[0, plane, pl.ds(start, seen)]
    packed[planes * seen :] = blank[...]
    for axis in range(taps.shape[0]):
        at = planes * seen + axis
        packed[at : at + 1, : taps.shape[2]] = taps[axis]


def view_out(measured, lines, blank, seen):
    _, planes, _, across = measured.shape
    return pl.pallas_call(
        functools.partial(view_out_kernel, seen),
        out_shape=jax.ShapeDtypeStruct((planes * seen + TAIL, across), F32),
        in_specs=[VMEM] * 3,
        out_specs=VMEM,
        compiler_params=pltpu.CompilerParams(vmem_limit_bytes=LIMIT),
        name="view_out",
    )(measured, lines, blank)


def prepare_kernel(packed, taps, source, estimate, after, wide, tall, back, part, spread):
    half = half_of(lax.axis_index("view"))
    across = wide.shape[-1]
    rows, keep, seen = part.shape[1], back.shape[0], tall.shape[0]
    planes = estimate.shape[0]
    radius = (taps - 1) // 2
    at = source.shape[0] - TAIL
    if packed:
        raw = source[at : at + 3, :taps]
    else:
        raw = jnp.concatenate([source[axis] for axis in range(source.shape[0])], axis=0)
    weights = raw / jnp.sum(raw, axis=-1, keepdims=True)
    deep, high, flat = [[weights[axis : axis + 1, t : t + 1] for t in range(taps)] for axis in range(3)]
    start = pl.multiple_of((2 * keep - rows) * half, 16)
    seen_start = (2 * keep - seen) * half
    near_diagonal = jnp.abs(
        lax.broadcasted_iota(jnp.int32, (across, across), 1)
        - lax.broadcasted_iota(jnp.int32, (across, across), 0)
    ) <= radius
    for turn, line in enumerate((flat[::-1], flat)):
        first_row = jnp.concatenate(
            line[radius:] + [jnp.zeros((1, across - taps), F32)] + line[:radius], axis=1
        )
        square = pltpu.roll(
            jnp.broadcast_to(first_row, (across, across)), 0, 1, stride=1, stride_axis=0
        )
        upper, lower = split(jnp.where(near_diagonal, square, 0.0))
        wide[turn, 0] = upper
        wide[turn, 1] = lower
    upper, lower = split(band(high, (seen, rows), radius + start - seen_start))
    tall[...] = jnp.concatenate([upper, upper, lower], axis=1)
    upper, lower = split(band(high[::-1], (keep, rows), radius + seen_start - keep * half))
    back[...] = jnp.concatenate([upper, upper, lower], axis=1)
    factors = [jnp.broadcast_to(tap, (16, LANES)) for tap in deep]
    spread[...] = jnp.zeros_like(spread)
    for step in range(taps):
        spread[step : step + 1] = factors[step][:1]
    for row, lane in chunks(rows, across):
        where = pl.ds(pl.multiple_of(start + row.start, 16), 16)
        terms = depth_terms(
            lambda place: estimate[place, where, lane], factors, 0, planes, range(planes), False
        )
        for plane, block in terms.items():
            part[plane, row, lane] = block


def prepare(packed, taps, source, estimate, after, rows, seen, keep):
    planes, _, across = estimate.shape
    return pl.pallas_call(
        functools.partial(prepare_kernel, packed, taps),
        out_shape=(
            jax.ShapeDtypeStruct((2, 2, across, across), BF16),
            jax.ShapeDtypeStruct((seen, 3 * rows), BF16),
            jax.ShapeDtypeStruct((keep, 3 * rows), BF16),
            jax.ShapeDtypeStruct((planes, rows, across), F32),
            jax.ShapeDtypeStruct((-(-taps // 8) * 8, LANES), F32),
        ),
        in_specs=[VMEM, VMEM, ANY],
        out_specs=(VMEM,) * 5,
        compiler_params=pltpu.CompilerParams(vmem_limit_bytes=LIMIT),
        name="prepare",
    )(source, estimate, after)


def spread_factors(spread, taps):
    return [jnp.broadcast_to(spread[step : step + 1, :], (16, LANES)) for step in range(taps)]


def fields_kernel(*refs):
    sets, (far, near, measured, swapped), refs = (refs[:5], refs[5:10]), refs[10:14], refs[15:]
    fields, sends, (blur_hi, blur_lo, plane_hi, plane_lo) = refs[:2], refs[2:-4], refs[-4:]
    planes = sets[0][3].shape[0]
    radius, rows, across = near.shape
    keep, seen = sets[0][2].shape[0], sets[0][1].shape[0]
    taps = 2 * radius + 1
    even = lax.axis_index("tile") % 2 == 0
    half = half_of(lax.axis_index("view"))
    seen_start = pl.multiple_of((2 * keep - seen) * half, 8)
    factors = [spread_factors(spread, taps) for _, _, _, _, spread in sets]
    for which, (_, _, _, part, _) in enumerate(sets):
        for row, lane in chunks(rows, across):

            def rim(place):
                if place < 0:
                    at = place + radius
                    return jnp.where(even, far[at, row, lane], near[at, row, lane])
                at = place - planes
                return jnp.where(even, near[at, row, lane], far[at, row, lane])

            below = depth_terms(rim, factors[which], -radius, 0, range(planes), False)
            above = depth_terms(rim, factors[which], planes, planes + radius, range(planes), False)
            for plane in range(planes):
                block = part[plane, row, lane]
                for term in (below[plane], above[plane]):
                    block = block if term is None else block + term
                upper, lower = split(block)
                at = slice(plane * rows + row.start, plane * rows + row.stop)
                blur_hi[which, at, lane] = upper
                blur_lo[which, at, lane] = lower
    lines = []
    for which, (wide, _, _, _, _) in enumerate(sets):
        upper, lower = wide[0, 0], wide[0, 1]
        lines.append(
            jnp.dot(blur_hi[which], upper, preferred_element_type=F32)
            + jnp.dot(blur_lo[which], upper, preferred_element_type=F32)
            + jnp.dot(blur_hi[which], lower, preferred_element_type=F32)
        )
    both = [(which, plane) for which in range(2) for plane in range(planes)]
    forwards = {}
    for which, plane in both:
        hi, lo = split(lines[which][plane * rows : (plane + 1) * rows])
        forwards[which, plane] = jnp.dot(
            sets[which][1][...], jnp.concatenate([hi, lo, hi], axis=0), preferred_element_type=F32
        )
    ratios = {}
    for which, plane in both:
        if which == 0:
            recorded = measured[0, plane, pl.ds(seen_start, seen), :]
        else:
            recorded = swapped[plane * seen : (plane + 1) * seen]
        ratio = recorded / forwards[which, plane]
        if rows > seen:
            ratio = jnp.concatenate([ratio, jnp.zeros((rows - seen, across), F32)], axis=0)
        ratios[which, plane] = split(ratio)
    turned = {}
    for which, plane in both:
        hi, lo = ratios[which, plane]
        turned[which, plane] = jnp.dot(
            sets[which][2][...], jnp.concatenate([hi, lo, hi], axis=0), preferred_element_type=F32
        )
    for which, plane in both:
        hi, lo = split(turned[which, plane])
        plane_hi[which, plane * keep : (plane + 1) * keep] = hi
        plane_lo[which, plane * keep : (plane + 1) * keep] = lo
    for which, (wide, _, _, _, _) in enumerate(sets):
        upper, lower = wide[1, 0], wide[1, 1]
        result = (
            jnp.dot(plane_hi[which], upper, preferred_element_type=F32)
            + jnp.dot(plane_lo[which], upper, preferred_element_type=F32)
            + jnp.dot(plane_hi[which], lower, preferred_element_type=F32)
        )
        fields[which][...] = result.reshape(planes, keep, across)
    for row, lane in chunks(keep, across):
        below, above = [], []
        for which in range(2):
            source = lambda place: fields[which][place, row, lane]
            outer = range(planes, planes + radius)
            below.append(depth_terms(source, factors[which], 0, planes, range(-radius, 0), True))
            above.append(depth_terms(source, factors[which], 0, planes, outer, True))
        part_at, inside = divmod(row.start, keep // PARTS)
        inside = slice(inside, inside + 16)
        for at in range(radius):
            down = below[0][at - radius] + below[1][at - radius]
            up = above[0][at + planes] + above[1][at + planes]
            sends[2 * part_at][at, inside, lane] = jnp.where(even, down, up)
            sends[2 * part_at + 1][at, inside, lane] = jnp.where(even, up, down)


def ratio_fields(own, others, far, near, measured, swapped, after):
    keep, planes = own[2].shape[0], own[3].shape[0]
    radius, rows, across = near.shape
    field = jax.ShapeDtypeStruct((planes, keep, across), F32)
    send = jax.ShapeDtypeStruct((radius, keep // PARTS, across), F32)
    return pl.pallas_call(
        fields_kernel,
        out_shape=(field,) * 2 + (send,) * (2 * PARTS),
        in_specs=[VMEM] * 14 + [ANY],
        out_specs=(VMEM,) * (2 + 2 * PARTS),
        scratch_shapes=[
            pltpu.VMEM((2, planes * rows, across), BF16),
            pltpu.VMEM((2, planes * rows, across), BF16),
            pltpu.VMEM((2, planes * keep, across), BF16),
            pltpu.VMEM((2, planes * keep, across), BF16),
        ],
        compiler_params=pltpu.CompilerParams(vmem_limit_bytes=LIMIT),
        name="ratio_fields",
    )(*own, *others, far, near, measured, swapped, after)


def own_kernel(taps, spread_own, spread_other, field_own, field_other, *inner):
    planes, keep, across = field_own.shape
    factors = [spread_factors(spread, taps) for spread in (spread_own, spread_other)]
    for row, lane in chunks(keep, across):
        parts = [
            depth_terms(
                lambda place: field[place, row, lane], factors[which], 0, planes, range(planes), True
            )
            for which, field in enumerate((field_own, field_other))
        ]
        part_at, inside = divmod(row.start, keep // PARTS)
        for plane in range(planes):
            inner[part_at][plane, inside : inside + 16, lane] = parts[0][plane] + parts[1][plane]


def own_planes(taps, spread_own, spread_other, field_own, field_other):
    planes, keep, across = field_own.shape
    return pl.pallas_call(
        functools.partial(own_kernel, taps),
        out_shape=(jax.ShapeDtypeStruct((planes, keep // PARTS, across), F32),) * PARTS,
        in_specs=[VMEM] * 4,
        out_specs=(VMEM,) * PARTS,
        compiler_params=pltpu.CompilerParams(vmem_limit_bytes=LIMIT),
        name="own_planes",
    )(spread_own, spread_other, field_own, field_other)


def rims_kernel(inner, far, near, *rest):
    correction = rest[-1]
    planes, radius = inner.shape[0], near.shape[0]
    even = lax.axis_index("tile") % 2 == 0
    for plane in range(planes):
        total = inner[plane]
        if plane < radius:
            total += jnp.where(even, far[plane], near[plane])
        if plane >= planes - radius:
            at = plane - planes + radius
            total += jnp.where(even, near[at], far[at])
        correction[plane] = total


def add_rims(inner, far, near, *after):
    return pl.pallas_call(
        rims_kernel,
        out_shape=jax.ShapeDtypeStruct(inner.shape, F32),
        in_specs=[VMEM] * 3 + [ANY] * len(after),
        out_specs=VMEM,
        compiler_params=pltpu.CompilerParams(vmem_limit_bytes=LIMIT),
        name="add_rims",
    )(inner, far, near, *after)


def table_rows(table):
    return jnp.concatenate([table[:8], table[8:]], axis=1)


def update_kernel(views, part, estimate, mine, other, *rest):
    planes, size, across = mine.shape
    result = rest[-1]
    half = half_of(lax.axis_index("view"))
    start = pl.multiple_of(size * (PARTS * half + part), 8)
    for plane in range(planes):
        held = estimate[plane, pl.ds(start, size)]
        at = slice(plane * size, (plane + 1) * size)
        result[at] = held * (mine[plane] + other[plane]) * (1.0 / views)
    spare = result.shape[0] - planes * size
    if spare:
        result[planes * size :] = jnp.zeros((spare, across), F32)


def update(views, part, estimate, mine, other, after):
    planes, size, across = mine.shape
    spare = 8 * (PARTS - 1 - part)
    return pl.pallas_call(
        functools.partial(update_kernel, views, part),
        out_shape=jax.ShapeDtypeStruct((planes * size + spare, across), F32),
        in_specs=[VMEM] * 3 + [ANY] * len(after),
        out_specs=VMEM,
        compiler_params=pltpu.CompilerParams(vmem_limit_bytes=LIMIT),
        name="update",
    )(estimate, mine, other, *after)


def slots_kernel(views, owner_row, index_row, picked, base):
    count = base.shape[0]
    slots = owner_row.shape[1]
    owner = owner_row[...]
    member = (lax.broadcasted_iota(jnp.int32, (count // views, slots), 0) == owner).astype(F32)
    upto = (
        lax.broadcasted_iota(jnp.int32, (slots, slots), 0)
        <= lax.broadcasted_iota(jnp.int32, (slots, slots), 1)
    ).astype(F32)
    running = jnp.dot(member, upto, preferred_element_type=F32)
    rank = jnp.sum(member * running, axis=0, keepdims=True).astype(jnp.int32) - 1
    named = lax.broadcasted_iota(jnp.int32, (count, slots), 0) // views == owner
    index = index_row[...].astype(F32)
    lanes = lax.broadcasted_iota(jnp.int32, (count, LANES), 1)
    result = jnp.zeros((count, LANES), F32)
    for place in range(CAP):
        chosen = named & (rank == place)
        picked[place * count : (place + 1) * count] = chosen.astype(F32)
        ids = jnp.sum(jnp.where(chosen, index, 0.0), axis=1, keepdims=True)
        result = jnp.where(lanes == place * WIDTH + IDS, ids, result)
    base[...] = result


def slot_places(tiles, views, label_owner, label_index):
    slots = label_index.shape[1]
    count = tiles * views
    return pl.pallas_call(
        functools.partial(slots_kernel, views),
        out_shape=(
            jax.ShapeDtypeStruct((CAP * count, slots), F32),
            jax.ShapeDtypeStruct((count, LANES), F32),
        ),
        in_specs=[VMEM, VMEM],
        out_specs=(VMEM, VMEM),
        compiler_params=pltpu.CompilerParams(vmem_limit_bytes=LIMIT),
        name="slot_places",
    )(label_owner.reshape(1, slots), label_index)


def merge_rows(blocks):
    rows = lax.broadcasted_iota(jnp.int32, blocks[0].shape, 0)
    step = 4
    while step:
        low = (rows & step) == 0
        half = len(blocks) // 2
        merged = []
        for one, two in zip(blocks[:half], blocks[half:]):
            kept = jnp.where(low, one, two)
            turned = jnp.where(low, two, one)
            moved = pltpu.roll(turned, step, 0)
            if step < 4:
                moved = jnp.where(low, pltpu.roll(turned, 8 - step, 0), moved)
            merged.append(kept + moved)
        blocks = merged
        step //= 2
    return blocks[0]


def moments_kernel(views, depth_total, part, estimate, labels, picked, base, correction, *refs):
    begun, (sent, held, sums, table) = refs[:-4], refs[-4:]
    planes, size, across = correction.shape
    height_total = estimate.shape[1]
    slots = picked.shape[1]
    half = half_of(lax.axis_index("view"))
    first = (lax.axis_index("tile") * planes).astype(F32) + 0.5
    start = pl.multiple_of(size * (PARTS * half + part), 8)
    held[...] = estimate[:, pl.ds(start, size)] * correction[...] * (1.0 / views)
    group = 16
    spot = lax.broadcasted_iota(jnp.int32, (across, LANES), 0)
    lanes = lax.broadcasted_iota(jnp.int32, (across, LANES), 1)
    low = (spot * spot) & 255
    factors = jnp.where(lanes == 0, 1, jnp.where(lanes == 1, spot, 0))
    factors = jnp.where(lanes == 2, spot * spot - low, jnp.where(lanes == 3, low, factors))
    factors = factors.astype(F32).astype(BF16)
    base_row = lax.broadcasted_iota(jnp.int32, (8, across), 0)

    def one_group(number, carry):
        held_parts = []
        for pair in range(0, group, 2):
            slot = [number * group + pair, number * group + pair + 1]
            parts = [[None] * 6 for _ in slot]
            for row in range(0, size, 8):
                high = ((base_row + (row + start)).astype(F32) + 0.5) * (1.0 / height_total)
                flat, once, twice = [[jnp.zeros((8, across), F32) for _ in slot] for _ in range(3)]
                for plane in reversed(range(planes)):
                    mark = labels[plane, pl.ds(pl.multiple_of(start + row, 8), 8)]
                    value = held[plane, row : row + 8]
                    for at in range(2):
                        flat[at] = flat[at] + jnp.where(mark == slot[at], value, 0.0)
                        if plane > 0:
                            once[at] = once[at] + flat[at]
                            twice[at] = twice[at] + once[at]
                for at in range(2):
                    scaled = flat[at] * high
                    terms = (flat[at], scaled, scaled * high, once[at], once[at] * high, twice[at])
                    parts[at] = [new if old is None else old + new for old, new in zip(parts[at], terms)]
            held_parts += parts
            if len(held_parts) == 8:
                for kind in range(6):
                    row = kind * group + pair + 2 - 8
                    sums[row : row + 8, :] = merge_rows([parts[kind] for parts in held_parts])
                held_parts = []
        whole = sums[...]
        upper, rest = split(whole)
        rest = whole - upper.astype(F32)
        middle, lower = split(rest)
        lines = jnp.dot(
            jnp.concatenate([upper, middle, lower], axis=0), factors, preferred_element_type=F32
        )
        count = 6 * group
        lines = lines[:count] + lines[count : 2 * count] + lines[2 * count :]
        flat, high_flat, square_flat, once, high_once, twice = [
            lines[kind * group : (kind + 1) * group] for kind in range(6)
        ]
        deep = (first * flat + once) * (1.0 / depth_total)
        deep_high = (first * high_flat + high_once) * (1.0 / depth_total)
        deeper = first * (first * flat + 2.0 * once) + (2.0 * twice - once)
        deeper = deeper * (1.0 / depth_total**2)
        total = flat
        for kind, sums_of in enumerate((high_flat, square_flat, deep, deep_high, deeper), 1):
            total += pltpu.roll(sums_of, 4 * kind, 1)
        rows = pl.ds(pl.multiple_of(number * group, group), group)
        target = table if part == PARTS - 1 else sent
        target[rows, :] = total + begun[0][rows, :] if begun else total
        return carry

    lax.fori_loop(0, slots // group, one_group, 0)
    if part < PARTS - 1:
        return
    rows = jnp.dot(
        picked[...], table[...], precision=lax.Precision.HIGHEST, preferred_element_type=F32
    )
    total = base[...]
    count = total.shape[0]
    for place in range(CAP):
        total += pltpu.roll(rows[place * count : (place + 1) * count], place * WIDTH, 1)
    sent[...] = total


def moment_rows(views, tiles, part, estimate, correction, labels, places, begun):
    planes, size, across = correction.shape
    slots = places[0].shape[1]
    count = places[1].shape[0] if part == PARTS - 1 else slots
    return pl.pallas_call(
        functools.partial(moments_kernel, views, tiles * planes, part),
        out_shape=jax.ShapeDtypeStruct((count, LANES), F32),
        in_specs=[VMEM] * (5 + len(begun)),
        out_specs=VMEM,
        scratch_shapes=[
            pltpu.VMEM((planes, size, across), F32),
            pltpu.VMEM((6 * 16, across), F32),
            pltpu.VMEM((slots, LANES), F32),
        ],
        compiler_params=pltpu.CompilerParams(vmem_limit_bytes=LIMIT),
        name="moment_rows",
    )(estimate, labels, *places, correction, *begun)


def segments_kernel(across, scale, rows, moments):
    whole = rows[...]
    parts = [whole] + [pltpu.roll(whole, LANES - place * WIDTH, 1) for place in range(1, CAP)]
    values = jnp.concatenate(parts, axis=0)
    ids = values[:, IDS : IDS + 1].astype(jnp.int32)
    spots = lax.broadcasted_iota(jnp.int32, (values.shape[0], NUC_DEV), 1)
    picked = (ids == spots).astype(F32)
    full = lax.dot_general(
        values, picked, (((0,), (0,)), ((), ())),
        precision=lax.Precision.HIGHEST, preferred_element_type=F32,
    )
    mass, high, higher, deep, deep_high, deeper = [full[4 * kind : 4 * kind + 4] for kind in range(6)]
    flat = lambda sums: sums[0:1]
    line = lambda sums: (sums[1:2] + 0.5 * sums[0:1]) * (1.0 / across)
    square = lambda sums: (sums[2:3] + sums[3:4] + sums[1:2] + 0.25 * sums[0:1]) * (1.0 / across**2)
    total = flat(mass)
    sums = jnp.concatenate(
        [
            flat(deep), flat(high), line(mass),
            flat(deeper), flat(higher), square(mass),
            flat(deep_high), line(deep), line(high),
        ],
        axis=0,
    )
    moments[...] = jnp.concatenate([total * scale, sums / jnp.maximum(total, 1.0)], axis=0)


def nucleus_table(across, scale, rows):
    return pl.pallas_call(
        functools.partial(segments_kernel, across, scale),
        out_shape=jax.ShapeDtypeStruct((MOM, NUC_DEV), F32),
        in_specs=[VMEM],
        out_specs=VMEM,
        compiler_params=pltpu.CompilerParams(vmem_limit_bytes=LIMIT),
        cost_estimate=pl.CostEstimate(flops=10_000_000_000, bytes_accessed=20_000_000, transcendentals=0),
        name="nucleus_table",
    )(rows)


def stores(pieces, sources, whole, half, sems):
    keep = whole.shape[1] // 2
    copies = []
    for number, ((first, size), source) in enumerate(zip(pieces, sources)):
        start = pl.multiple_of(keep * half + first, 8)
        for plane in range(whole.shape[0]):
            copies.append(
                pltpu.make_async_copy(
                    source.at[pl.ds(plane * size, size)],
                    whole.at[plane, pl.ds(start, size)],
                    sems.at[number, plane],
                )
            )
    for copy in copies:
        copy.start()
    return copies


def token_kernel(source, *rest):
    token = rest[-1]
    token[...] = source[:8, :LANES]


def token_of(source, after=(), flops=0):
    return pl.pallas_call(
        token_kernel,
        out_shape=jax.ShapeDtypeStruct((8, LANES), F32),
        in_specs=[VMEM] + [ANY] * len(after),
        out_specs=VMEM,
        compiler_params=pltpu.CompilerParams(vmem_limit_bytes=LIMIT),
        cost_estimate=pl.CostEstimate(flops=flops, bytes_accessed=flops // 500, transcendentals=0),
        name="token_of",
    )(source, *after)


def begin_kernel(pieces, *refs):
    sources, (whole, sems) = refs[:-2], refs[-2:]
    for copy in stores(pieces, sources, whole, half_of(lax.axis_index("view")), sems):
        copy.wait()


def begin_result(pieces, shape, mine):
    return pl.pallas_call(
        functools.partial(begin_kernel, pieces),
        out_shape=jax.ShapeDtypeStruct(shape, F32),
        in_specs=[VMEM] * len(mine),
        out_specs=ANY,
        scratch_shapes=[pltpu.SemaphoreType.DMA((len(pieces), shape[0]))],
        compiler_params=pltpu.CompilerParams(vmem_limit_bytes=LIMIT),
        name="begin_result",
    )(*mine)


def finish_kernel(pieces, begun, *refs):
    others, (whole, sems) = refs[:-2], refs[-2:]
    for copy in stores(pieces, others, whole, 1 - half_of(lax.axis_index("view")), sems):
        copy.wait()


def finish(pieces, begun, others):
    return pl.pallas_call(
        functools.partial(finish_kernel, pieces),
        out_shape=jax.ShapeDtypeStruct(begun.shape, F32),
        in_specs=[ANY] + [VMEM] * len(others),
        out_specs=ANY,
        input_output_aliases={0: 0},
        scratch_shapes=[pltpu.SemaphoreType.DMA((len(pieces), begun.shape[0]))],
        compiler_params=pltpu.CompilerParams(vmem_limit_bytes=LIMIT),
        name="finish",
    )(begun, *others)


def on_device(estimate, measured, kernels, labels, label_owner, label_index):
    tiles, views = lax.axis_size("tile"), lax.axis_size("view")
    planes, height, across = estimate.shape
    taps = kernels.shape[2]
    radius = (taps - 1) // 2
    keep = height // 2
    seen = min(height, -(-(keep + radius) // 8) * 8)
    rows = min(height, -(-(keep + 2 * radius) // 16) * 16)
    near_pairs = [(i, i ^ 1) for i in range(tiles)]
    far_pairs = [(i, i + 1) for i in range(1, tiles - 1, 2)]
    far_pairs = far_pairs + [(b, a) for a, b in far_pairs]
    partner = [(i, i ^ 1) for i in range(views)]
    across_pairs = [(i, i ^ 2) for i in range(views)]

    lines = jnp.transpose(kernels, (1, 0, 2))
    blank = blank_rows(across)
    packed = view_out(measured, lines, blank, seen)
    swapped = lax.ppermute(packed, "view", partner)
    to_far, to_near = rims_out(estimate, blank, radius, rows)
    far = lax.ppermute(to_far, "tile", far_pairs)
    near = lax.ppermute(to_near, "tile", near_pairs)
    places = slot_places(tiles, views, label_owner, label_index)
    own = prepare(False, taps, lines, estimate, places[1], rows, seen, keep)
    others = prepare(True, taps, swapped, estimate, lines, rows, seen, keep)
    came = token_of(far.reshape(radius * rows, across), (others[4],), 0)
    field_own, field_other, *sends = ratio_fields(
        own, others, far, near, measured, swapped, came
    )
    rims = [
        lax.ppermute(send, "tile", pairs) for send, pairs in zip(sends, (far_pairs, near_pairs) * PARTS)
    ]
    inner = own_planes(taps, own[4], others[4], field_own, field_other)
    mine, other, sums = [], [], []
    for part in range(PARTS):
        mine.append(add_rims(inner[part], *rims[2 * part : 2 * part + 2], *sums))
        other.append(lax.ppermute(mine[part], "view", across_pairs))
        sums = [moment_rows(views, tiles, part, estimate, mine[part], labels, places, sums)]
    sent = sums[0]
    got = lax.all_to_all(sent, ("tile", "view"), split_axis=0, concat_axis=0, tiled=True)
    size = keep // PARTS
    pieces = [(part * size, size) for part in range(PARTS)]
    new_mine, new_other, token = [], [], [sent]
    for part in range(PARTS):
        new_mine.append(update(views, part, estimate, mine[part], other[part], token))
        new_other.append(lax.ppermute(new_mine[part], "view", partner))
        token = [token_of(new_mine[part])]
    scale = label_index.shape[1] / (planes * height * across)
    moments = nucleus_table(across, scale, got)
    begun = begin_result(pieces, estimate.shape, new_mine)
    return finish(pieces, begun, new_other), moments


def solution(mesh):
    placed = (
        P("tile", None, None),
        P("view", "tile", None, None),
        P("view", None, None),
        P("tile", None, None),
        P("tile", None, None),
        P("tile", None),
    )
    return jax.shard_map(
        on_device,
        mesh=mesh,
        in_specs=placed,
        out_specs=(P("tile", None, None), P(None, "tile")),
        check_vma=False,
    )
```

```python
import functools

import jax
import jax.numpy as jnp
from jax import lax
from jax.experimental import pallas as pl
from jax.experimental.pallas import tpu as pltpu
from jax.sharding import PartitionSpec as P

MOM = 10
CAP = 5
WIDTH = 25
NUC_DEV = 128
LANES = 128
PARTS = 2
TAIL = 24
IDS = 24
F32 = jnp.float32
BF16 = jnp.bfloat16
ANY = pl.BlockSpec(memory_space=pl.ANY)
VMEM = pl.BlockSpec(memory_space=pltpu.VMEM)
LIMIT = 32 * 1024 * 1024


def half_of(view):
    return (view ^ (view >> 1)) & 1


def split(value):
    upper = value.astype(BF16)
    return upper, (value - upper.astype(F32)).astype(BF16)


def band(taps, shape, offset):
    rows = lax.broadcasted_iota(jnp.int32, shape, 0)
    cols = lax.broadcasted_iota(jnp.int32, shape, 1)
    place = cols - rows + offset
    result = jnp.zeros(shape, F32)
    for step, tap in enumerate(taps):
        result = jnp.where(place == step, tap, result)
    return result


def depth_terms(source, weights, first, last, planes, flipped):
    radius = (len(weights) - 1) // 2
    totals = {plane: None for plane in planes}
    for place in range(first, last):
        block = None
        for plane in planes:
            step = plane - place + radius if flipped else place - plane + radius
            if 0 <= step < len(weights):
                block = source(place) if block is None else block
                term = weights[step] * block
                totals[plane] = term if totals[plane] is None else totals[plane] + term
    return totals


def chunks(rows, across):
    return [(slice(row, row + 16), slice(lane, lane + LANES)) for row in range(0, rows, 16) for lane in range(0, across, LANES)]


def rims_out_kernel(estimate, after, to_far, to_near):
    planes, radius, rows = estimate.shape[0], to_far.shape[0], to_far.shape[1]
    odd = lax.axis_index("tile") % 2
    half = half_of(lax.axis_index("view"))
    start = pl.multiple_of((estimate.shape[1] - rows) * half, 8)
    to_far[...] = estimate[pl.ds(odd, radius), pl.ds(start, rows)]
    to_near[...] = estimate[pl.ds(1 - odd, radius), pl.ds(start, rows)]


def rims_out(estimate, after, radius, rows):
    shape = jax.ShapeDtypeStruct((radius, rows, estimate.shape[2]), F32)
    return pl.pallas_call(
        rims_out_kernel,
        out_shape=(shape, shape),
        in_specs=[VMEM, ANY],
        out_specs=(VMEM, VMEM),
        compiler_params=pltpu.CompilerParams(vmem_limit_bytes=LIMIT),
        name="rims_out",
    )(estimate, after)


def blank_kernel(rows):
    rows[...] = jnp.zeros_like(rows)


def blank_rows(across):
    return pl.pallas_call(
        blank_kernel,
        out_shape=jax.ShapeDtypeStruct((TAIL, across), F32),
        out_specs=VMEM,
        compiler_params=pltpu.CompilerParams(vmem_limit_bytes=LIMIT),
        cost_estimate=pl.CostEstimate(flops=8_000_000_000, bytes_accessed=16_000_000, transcendentals=0),
        name="blank_rows",
    )()


def view_out_kernel(seen, measured, taps, blank, packed):
    planes, height = measured.shape[1], measured.shape[2]
    half = half_of(lax.axis_index("view"))
    start = pl.multiple_of((height - seen) * (1 - half), 8)
    for plane in range(planes):
        packed[plane * seen : (plane + 1) * seen] = measured[0, plane, pl.ds(start, seen)]
    packed[planes * seen :] = blank[...]
    for axis in range(taps.shape[0]):
        at = planes * seen + axis
        packed[at : at + 1, : taps.shape[2]] = taps[axis]


def view_out(measured, lines, blank, seen):
    _, planes, _, across = measured.shape
    return pl.pallas_call(
        functools.partial(view_out_kernel, seen),
        out_shape=jax.ShapeDtypeStruct((planes * seen + TAIL, across), F32),
        in_specs=[VMEM] * 3,
        out_specs=VMEM,
        compiler_params=pltpu.CompilerParams(vmem_limit_bytes=LIMIT),
        name="view_out",
    )(measured, lines, blank)


def prepare_kernel(packed, taps, source, estimate, after, wide, tall, back, part, spread):
    half = half_of(lax.axis_index("view"))
    across = wide.shape[-1]
    rows, keep, seen = part.shape[1], back.shape[0], tall.shape[0]
    planes = estimate.shape[0]
    radius = (taps - 1) // 2
    at = source.shape[0] - TAIL
    if packed:
        raw = source[at : at + 3, :taps]
    else:
        raw = jnp.concatenate([source[axis] for axis in range(source.shape[0])], axis=0)
    weights = raw / jnp.sum(raw, axis=-1, keepdims=True)
    deep, high, flat = [[weights[axis : axis + 1, t : t + 1] for t in range(taps)] for axis in range(3)]
    start = pl.multiple_of((2 * keep - rows) * half, 16)
    seen_start = (2 * keep - seen) * half
    near_diagonal = jnp.abs(
        lax.broadcasted_iota(jnp.int32, (across, across), 1)
        - lax.broadcasted_iota(jnp.int32, (across, across), 0)
    ) <= radius
    for turn, line in enumerate((flat[::-1], flat)):
        first_row = jnp.concatenate(
            line[radius:] + [jnp.zeros((1, across - taps), F32)] + line[:radius], axis=1
        )
        square = pltpu.roll(
            jnp.broadcast_to(first_row, (across, across)), 0, 1, stride=1, stride_axis=0
        )
        upper, lower = split(jnp.where(near_diagonal, square, 0.0))
        wide[turn, 0] = upper
        wide[turn, 1] = lower
    upper, lower = split(band(high, (seen, rows), radius + start - seen_start))
    tall[...] = jnp.concatenate([upper, upper, lower], axis=1)
    upper, lower = split(band(high[::-1], (keep, rows), radius + seen_start - keep * half))
    back[...] = jnp.concatenate([upper, upper, lower], axis=1)
    factors = [jnp.broadcast_to(tap, (16, LANES)) for tap in deep]
    spread[...] = jnp.zeros_like(spread)
    for step in range(taps):
        spread[step : step + 1] = factors[step][:1]
    for row, lane in chunks(rows, across):
        where = pl.ds(pl.multiple_of(start + row.start, 16), 16)
        terms = depth_terms(
            lambda place: estimate[place, where, lane], factors, 0, planes, range(planes), False
        )
        for plane, block in terms.items():
            part[plane, row, lane] = block


def prepare(packed, taps, source, estimate, after, rows, seen, keep):
    planes, _, across = estimate.shape
    return pl.pallas_call(
        functools.partial(prepare_kernel, packed, taps),
        out_shape=(
            jax.ShapeDtypeStruct((2, 2, across, across), BF16),
            jax.ShapeDtypeStruct((seen, 3 * rows), BF16),
            jax.ShapeDtypeStruct((keep, 3 * rows), BF16),
            jax.ShapeDtypeStruct((planes, rows, across), F32),
            jax.ShapeDtypeStruct((-(-taps // 8) * 8, LANES), F32),
        ),
        in_specs=[VMEM, VMEM, ANY],
        out_specs=(VMEM,) * 5,
        compiler_params=pltpu.CompilerParams(vmem_limit_bytes=LIMIT),
        name="prepare",
    )(source, estimate, after)


def spread_factors(spread, taps):
    return [jnp.broadcast_to(spread[step : step + 1, :], (16, LANES)) for step in range(taps)]


def fields_kernel(*refs):
    sets, (far, near, measured, swapped), refs = (refs[:5], refs[5:10]), refs[10:14], refs[15:]
    fields, sends, (blur_hi, blur_lo, plane_hi, plane_lo) = refs[:2], refs[2:-4], refs[-4:]
    planes = sets[0][3].shape[0]
    radius, rows, across = near.shape
    keep, seen = sets[0][2].shape[0], sets[0][1].shape[0]
    taps = 2 * radius + 1
    even = lax.axis_index("tile") % 2 == 0
    half = half_of(lax.axis_index("view"))
    seen_start = pl.multiple_of((2 * keep - seen) * half, 8)
    factors = [spread_factors(spread, taps) for _, _, _, _, spread in sets]
    for which, (_, _, _, part, _) in enumerate(sets):
        for row, lane in chunks(rows, across):

            def rim(place):
                if place < 0:
                    at = place + radius
                    return jnp.where(even, far[at, row, lane], near[at, row, lane])
                at = place - planes
                return jnp.where(even, near[at, row, lane], far[at, row, lane])

            below = depth_terms(rim, factors[which], -radius, 0, range(planes), False)
            above = depth_terms(rim, factors[which], planes, planes + radius, range(planes), False)
            for plane in range(planes):
                block = part[plane, row, lane]
                for term in (below[plane], above[plane]):
                    block = block if term is None else block + term
                upper, lower = split(block)
                at = slice(plane * rows + row.start, plane * rows + row.stop)
                blur_hi[which, at, lane] = upper
                blur_lo[which, at, lane] = lower
    lines = []
    for which, (wide, _, _, _, _) in enumerate(sets):
        upper, lower = wide[0, 0], wide[0, 1]
        lines.append(
            jnp.dot(blur_hi[which], upper, preferred_element_type=F32)
            + jnp.dot(blur_lo[which], upper, preferred_element_type=F32)
            + jnp.dot(blur_hi[which], lower, preferred_element_type=F32)
        )
    both = [(which, plane) for which in range(2) for plane in range(planes)]
    forwards = {}
    for which, plane in both:
        hi, lo = split(lines[which][plane * rows : (plane + 1) * rows])
        forwards[which, plane] = jnp.dot(
            sets[which][1][...], jnp.concatenate([hi, lo, hi], axis=0), preferred_element_type=F32
        )
    ratios = {}
    for which, plane in both:
        if which == 0:
            recorded = measured[0, plane, pl.ds(seen_start, seen), :]
        else:
            recorded = swapped[plane * seen : (plane + 1) * seen]
        ratio = recorded / forwards[which, plane]
        if rows > seen:
            ratio = jnp.concatenate([ratio, jnp.zeros((rows - seen, across), F32)], axis=0)
        ratios[which, plane] = split(ratio)
    turned = {}
    for which, plane in both:
        hi, lo = ratios[which, plane]
        turned[which, plane] = jnp.dot(
            sets[which][2][...], jnp.concatenate([hi, lo, hi], axis=0), preferred_element_type=F32
        )
    for which, plane in both:
        hi, lo = split(turned[which, plane])
        plane_hi[which, plane * keep : (plane + 1) * keep] = hi
        plane_lo[which, plane * keep : (plane + 1) * keep] = lo
    for which, (wide, _, _, _, _) in enumerate(sets):
        upper, lower = wide[1, 0], wide[1, 1]
        result = (
            jnp.dot(plane_hi[which], upper, preferred_element_type=F32)
            + jnp.dot(plane_lo[which], upper, preferred_element_type=F32)
            + jnp.dot(plane_hi[which], lower, preferred_element_type=F32)
        )
        fields[which][...] = result.reshape(planes, keep, across)
    for row, lane in chunks(keep, across):
        below, above = [], []
        for which in range(2):
            source = lambda place: fields[which][place, row, lane]
            outer = range(planes, planes + radius)
            below.append(depth_terms(source, factors[which], 0, planes, range(-radius, 0), True))
            above.append(depth_terms(source, factors[which], 0, planes, outer, True))
        part_at, inside = divmod(row.start, keep // PARTS)
        inside = slice(inside, inside + 16)
        for at in range(radius):
            down = below[0][at - radius] + below[1][at - radius]
            up = above[0][at + planes] + above[1][at + planes]
            sends[2 * part_at][at, inside, lane] = jnp.where(even, down, up)
            sends[2 * part_at + 1][at, inside, lane] = jnp.where(even, up, down)


def ratio_fields(own, others, far, near, measured, swapped, after):
    keep, planes = own[2].shape[0], own[3].shape[0]
    radius, rows, across = near.shape
    field = jax.ShapeDtypeStruct((planes, keep, across), F32)
    send = jax.ShapeDtypeStruct((radius, keep // PARTS, across), F32)
    return pl.pallas_call(
        fields_kernel,
        out_shape=(field,) * 2 + (send,) * (2 * PARTS),
        in_specs=[VMEM] * 14 + [ANY],
        out_specs=(VMEM,) * (2 + 2 * PARTS),
        scratch_shapes=[
            pltpu.VMEM((2, planes * rows, across), BF16),
            pltpu.VMEM((2, planes * rows, across), BF16),
            pltpu.VMEM((2, planes * keep, across), BF16),
            pltpu.VMEM((2, planes * keep, across), BF16),
        ],
        compiler_params=pltpu.CompilerParams(vmem_limit_bytes=LIMIT),
        name="ratio_fields",
    )(*own, *others, far, near, measured, swapped, after)


def own_kernel(taps, spread_own, spread_other, field_own, field_other, *inner):
    planes, keep, across = field_own.shape
    factors = [spread_factors(spread, taps) for spread in (spread_own, spread_other)]
    for row, lane in chunks(keep, across):
        parts = [
            depth_terms(
                lambda place: field[place, row, lane], factors[which], 0, planes, range(planes), True
            )
            for which, field in enumerate((field_own, field_other))
        ]
        part_at, inside = divmod(row.start, keep // PARTS)
        for plane in range(planes):
            inner[part_at][plane, inside : inside + 16, lane] = parts[0][plane] + parts[1][plane]


def own_planes(taps, spread_own, spread_other, field_own, field_other):
    planes, keep, across = field_own.shape
    return pl.pallas_call(
        functools.partial(own_kernel, taps),
        out_shape=(jax.ShapeDtypeStruct((planes, keep // PARTS, across), F32),) * PARTS,
        in_specs=[VMEM] * 4,
        out_specs=(VMEM,) * PARTS,
        compiler_params=pltpu.CompilerParams(vmem_limit_bytes=LIMIT),
        name="own_planes",
    )(spread_own, spread_other, field_own, field_other)


def rims_kernel(inner, far, near, *rest):
    correction = rest[-1]
    planes, radius = inner.shape[0], near.shape[0]
    even = lax.axis_index("tile") % 2 == 0
    for plane in range(planes):
        total = inner[plane]
        if plane < radius:
            total += jnp.where(even, far[plane], near[plane])
        if plane >= planes - radius:
            at = plane - planes + radius
            total += jnp.where(even, near[at], far[at])
        correction[plane] = total


def add_rims(inner, far, near, *after):
    return pl.pallas_call(
        rims_kernel,
        out_shape=jax.ShapeDtypeStruct(inner.shape, F32),
        in_specs=[VMEM] * 3 + [ANY] * len(after),
        out_specs=VMEM,
        compiler_params=pltpu.CompilerParams(vmem_limit_bytes=LIMIT),
        name="add_rims",
    )(inner, far, near, *after)


def table_rows(table):
    return jnp.concatenate([table[:8], table[8:]], axis=1)


def update_kernel(views, part, estimate, mine, other, *rest):
    planes, size, across = mine.shape
    result = rest[-1]
    half = half_of(lax.axis_index("view"))
    start = pl.multiple_of(size * (PARTS * half + part), 8)
    for plane in range(planes):
        held = estimate[plane, pl.ds(start, size)]
        at = slice(plane * size, (plane + 1) * size)
        result[at] = held * (mine[plane] + other[plane]) * (1.0 / views)
    spare = result.shape[0] - planes * size
    if spare:
        result[planes * size :] = jnp.zeros((spare, across), F32)


def update(views, part, estimate, mine, other, after):
    planes, size, across = mine.shape
    spare = 8 * (PARTS - 1 - part)
    return pl.pallas_call(
        functools.partial(update_kernel, views, part),
        out_shape=jax.ShapeDtypeStruct((planes * size + spare, across), F32),
        in_specs=[VMEM] * 3 + [ANY] * len(after),
        out_specs=VMEM,
        compiler_params=pltpu.CompilerParams(vmem_limit_bytes=LIMIT),
        name="update",
    )(estimate, mine, other, *after)


def slots_kernel(views, owner_row, index_row, picked, base):
    count = base.shape[0]
    slots = owner_row.shape[1]
    owner = owner_row[...]
    member = (lax.broadcasted_iota(jnp.int32, (count // views, slots), 0) == owner).astype(F32)
    upto = (
        lax.broadcasted_iota(jnp.int32, (slots, slots), 0)
        <= lax.broadcasted_iota(jnp.int32, (slots, slots), 1)
    ).astype(F32)
    running = jnp.dot(member, upto, preferred_element_type=F32)
    rank = jnp.sum(member * running, axis=0, keepdims=True).astype(jnp.int32) - 1
    named = lax.broadcasted_iota(jnp.int32, (count, slots), 0) // views == owner
    index = index_row[...].astype(F32)
    lanes = lax.broadcasted_iota(jnp.int32, (count, LANES), 1)
    result = jnp.zeros((count, LANES), F32)
    for place in range(CAP):
        chosen = named & (rank == place)
        picked[place * count : (place + 1) * count] = chosen.astype(F32)
        ids = jnp.sum(jnp.where(chosen, index, 0.0), axis=1, keepdims=True)
        result = jnp.where(lanes == place * WIDTH + IDS, ids, result)
    base[...] = result


def slot_places(tiles, views, label_owner, label_index):
    slots = label_index.shape[1]
    count = tiles * views
    return pl.pallas_call(
        functools.partial(slots_kernel, views),
        out_shape=(
            jax.ShapeDtypeStruct((CAP * count, slots), F32),
            jax.ShapeDtypeStruct((count, LANES), F32),
        ),
        in_specs=[VMEM, VMEM],
        out_specs=(VMEM, VMEM),
        compiler_params=pltpu.CompilerParams(vmem_limit_bytes=LIMIT),
        name="slot_places",
    )(label_owner.reshape(1, slots), label_index)


def merge_rows(blocks):
    rows = lax.broadcasted_iota(jnp.int32, blocks[0].shape, 0)
    step = 4
    while step:
        low = (rows & step) == 0
        half = len(blocks) // 2
        merged = []
        for one, two in zip(blocks[:half], blocks[half:]):
            kept = jnp.where(low, one, two)
            turned = jnp.where(low, two, one)
            moved = pltpu.roll(turned, step, 0)
            if step < 4:
                moved = jnp.where(low, pltpu.roll(turned, 8 - step, 0), moved)
            merged.append(kept + moved)
        blocks = merged
        step //= 2
    return blocks[0]


def moments_kernel(views, depth_total, part, estimate, labels, picked, base, correction, *refs):
    begun, (sent, held, sums, table) = refs[:-4], refs[-4:]
    planes, size, across = correction.shape
    height_total = estimate.shape[1]
    slots = picked.shape[1]
    half = half_of(lax.axis_index("view"))
    first = (lax.axis_index("tile") * planes).astype(F32) + 0.5
    start = pl.multiple_of(size * (PARTS * half + part), 8)
    held[...] = estimate[:, pl.ds(start, size)] * correction[...] * (1.0 / views)
    group = 16
    spot = lax.broadcasted_iota(jnp.int32, (across, LANES), 0)
    lanes = lax.broadcasted_iota(jnp.int32, (across, LANES), 1)
    low = (spot * spot) & 255
    factors = jnp.where(lanes == 0, 1, jnp.where(lanes == 1, spot, 0))
    factors = jnp.where(lanes == 2, spot * spot - low, jnp.where(lanes == 3, low, factors))
    factors = factors.astype(F32).astype(BF16)
    base_row = lax.broadcasted_iota(jnp.int32, (8, across), 0)

    def one_group(number, carry):
        held_parts = []
        for pair in range(0, group, 2):
            slot = [number * group + pair, number * group + pair + 1]
            parts = [[None] * 6 for _ in slot]
            for row in range(0, size, 8):
                high = ((base_row + (row + start)).astype(F32) + 0.5) * (1.0 / height_total)
                flat, once, twice = [[jnp.zeros((8, across), F32) for _ in slot] for _ in range(3)]
                for plane in reversed(range(planes)):
                    mark = labels[plane, pl.ds(pl.multiple_of(start + row, 8), 8)]
                    value = held[plane, row : row + 8]
                    for at in range(2):
                        flat[at] = flat[at] + jnp.where(mark == slot[at], value, 0.0)
                        if plane > 0:
                            once[at] = once[at] + flat[at]
                            twice[at] = twice[at] + once[at]
                for at in range(2):
                    scaled = flat[at] * high
                    terms = (flat[at], scaled, scaled * high, once[at], once[at] * high, twice[at])
                    parts[at] = [new if old is None else old + new for old, new in zip(parts[at], terms)]
            held_parts += parts
            if len(held_parts) == 8:
                for kind in range(6):
                    row = kind * group + pair + 2 - 8
                    sums[row : row + 8, :] = merge_rows([parts[kind] for parts in held_parts])
                held_parts = []
        whole = sums[...]
        upper, rest = split(whole)
        rest = whole - upper.astype(F32)
        middle, lower = split(rest)
        lines = jnp.dot(
            jnp.concatenate([upper, middle, lower], axis=0), factors, preferred_element_type=F32
        )
        count = 6 * group
        lines = lines[:count] + lines[count : 2 * count] + lines[2 * count :]
        flat, high_flat, square_flat, once, high_once, twice = [
            lines[kind * group : (kind + 1) * group] for kind in range(6)
        ]
        deep = (first * flat + once) * (1.0 / depth_total)
        deep_high = (first * high_flat + high_once) * (1.0 / depth_total)
        deeper = first * (first * flat + 2.0 * once) + (2.0 * twice - once)
        deeper = deeper * (1.0 / depth_total**2)
        total = flat
        for kind, sums_of in enumerate((high_flat, square_flat, deep, deep_high, deeper), 1):
            total += pltpu.roll(sums_of, 4 * kind, 1)
        rows = pl.ds(pl.multiple_of(number * group, group), group)
        target = table if part == PARTS - 1 else sent
        target[rows, :] = total + begun[0][rows, :] if begun else total
        return carry

    lax.fori_loop(0, slots // group, one_group, 0)
    if part < PARTS - 1:
        return
    rows = jnp.dot(
        picked[...], table[...], precision=lax.Precision.HIGHEST, preferred_element_type=F32
    )
    total = base[...]
    count = total.shape[0]
    for place in range(CAP):
        total += pltpu.roll(rows[place * count : (place + 1) * count], place * WIDTH, 1)
    sent[...] = total


def moment_rows(views, tiles, part, estimate, correction, labels, places, begun):
    planes, size, across = correction.shape
    slots = places[0].shape[1]
    count = places[1].shape[0] if part == PARTS - 1 else slots
    return pl.pallas_call(
        functools.partial(moments_kernel, views, tiles * planes, part),
        out_shape=jax.ShapeDtypeStruct((count, LANES), F32),
        in_specs=[VMEM] * (5 + len(begun)),
        out_specs=VMEM,
        scratch_shapes=[
            pltpu.VMEM((planes, size, across), F32),
            pltpu.VMEM((6 * 16, across), F32),
            pltpu.VMEM((slots, LANES), F32),
        ],
        compiler_params=pltpu.CompilerParams(vmem_limit_bytes=LIMIT),
        name="moment_rows",
    )(estimate, labels, *places, correction, *begun)


def segments_kernel(across, scale, rows, moments):
    whole = rows[...]
    parts = [whole] + [pltpu.roll(whole, LANES - place * WIDTH, 1) for place in range(1, CAP)]
    values = jnp.concatenate(parts, axis=0)
    ids = values[:, IDS : IDS + 1].astype(jnp.int32)
    spots = lax.broadcasted_iota(jnp.int32, (values.shape[0], NUC_DEV), 1)
    picked = (ids == spots).astype(F32)
    full = lax.dot_general(
        values, picked, (((0,), (0,)), ((), ())),
        precision=lax.Precision.HIGHEST, preferred_element_type=F32,
    )
    mass, high, higher, deep, deep_high, deeper = [full[4 * kind : 4 * kind + 4] for kind in range(6)]
    flat = lambda sums: sums[0:1]
    line = lambda sums: (sums[1:2] + 0.5 * sums[0:1]) * (1.0 / across)
    square = lambda sums: (sums[2:3] + sums[3:4] + sums[1:2] + 0.25 * sums[0:1]) * (1.0 / across**2)
    total = flat(mass)
    sums = jnp.concatenate(
        [
            flat(deep), flat(high), line(mass),
            flat(deeper), flat(higher), square(mass),
            flat(deep_high), line(deep), line(high),
        ],
        axis=0,
    )
    moments[...] = jnp.concatenate([total * scale, sums / jnp.maximum(total, 1.0)], axis=0)


def nucleus_table(across, scale, rows):
    return pl.pallas_call(
        functools.partial(segments_kernel, across, scale),
        out_shape=jax.ShapeDtypeStruct((MOM, NUC_DEV), F32),
        in_specs=[VMEM],
        out_specs=VMEM,
        compiler_params=pltpu.CompilerParams(vmem_limit_bytes=LIMIT),
        cost_estimate=pl.CostEstimate(flops=10_000_000_000, bytes_accessed=20_000_000, transcendentals=0),
        name="nucleus_table",
    )(rows)


def stores(pieces, sources, whole, half, sems):
    keep = whole.shape[1] // 2
    copies = []
    for number, ((first, size), source) in enumerate(zip(pieces, sources)):
        start = pl.multiple_of(keep * half + first, 8)
        for plane in range(whole.shape[0]):
            copies.append(
                pltpu.make_async_copy(
                    source.at[pl.ds(plane * size, size)],
                    whole.at[plane, pl.ds(start, size)],
                    sems.at[number, plane],
                )
            )
    for copy in copies:
        copy.start()
    return copies


def token_kernel(source, *rest):
    token = rest[-1]
    token[...] = source[:8, :LANES]


def token_of(source, after=(), flops=0):
    return pl.pallas_call(
        token_kernel,
        out_shape=jax.ShapeDtypeStruct((8, LANES), F32),
        in_specs=[VMEM] + [ANY] * len(after),
        out_specs=VMEM,
        compiler_params=pltpu.CompilerParams(vmem_limit_bytes=LIMIT),
        cost_estimate=pl.CostEstimate(flops=flops, bytes_accessed=flops // 500, transcendentals=0),
        name="token_of",
    )(source, *after)


def begin_kernel(pieces, *refs):
    sources, (whole, sems) = refs[:-2], refs[-2:]
    for copy in stores(pieces, sources, whole, half_of(lax.axis_index("view")), sems):
        copy.wait()


def begin_result(pieces, shape, mine):
    return pl.pallas_call(
        functools.partial(begin_kernel, pieces),
        out_shape=jax.ShapeDtypeStruct(shape, F32),
        in_specs=[VMEM] * len(mine),
        out_specs=ANY,
        scratch_shapes=[pltpu.SemaphoreType.DMA((len(pieces), shape[0]))],
        compiler_params=pltpu.CompilerParams(vmem_limit_bytes=LIMIT),
        name="begin_result",
    )(*mine)


def finish_kernel(pieces, begun, *refs):
    others, (whole, sems) = refs[:-2], refs[-2:]
    for copy in stores(pieces, others, whole, 1 - half_of(lax.axis_index("view")), sems):
        copy.wait()


def finish(pieces, begun, others):
    return pl.pallas_call(
        functools.partial(finish_kernel, pieces),
        out_shape=jax.ShapeDtypeStruct(begun.shape, F32),
        in_specs=[ANY] + [VMEM] * len(others),
        out_specs=ANY,
        input_output_aliases={0: 0},
        scratch_shapes=[pltpu.SemaphoreType.DMA((len(pieces), begun.shape[0]))],
        compiler_params=pltpu.CompilerParams(vmem_limit_bytes=LIMIT),
        name="finish",
    )(begun, *others)


def on_device(estimate, measured, kernels, labels, label_owner, label_index):
    tiles, views = lax.axis_size("tile"), lax.axis_size("view")
    planes, height, across = estimate.shape
    taps = kernels.shape[2]
    radius = (taps - 1) // 2
    keep = height // 2
    seen = min(height, -(-(keep + radius) // 8) * 8)
    rows = min(height, -(-(keep + 2 * radius) // 16) * 16)
    near_pairs = [(i, i ^ 1) for i in range(tiles)]
    far_pairs = [(i, i + 1) for i in range(1, tiles - 1, 2)]
    far_pairs = far_pairs + [(b, a) for a, b in far_pairs]
    partner = [(i, i ^ 1) for i in range(views)]
    across_pairs = [(i, i ^ 3) for i in range(views)]

    lines = jnp.transpose(kernels, (1, 0, 2))
    blank = blank_rows(across)
    packed = view_out(measured, lines, blank, seen)
    swapped = lax.ppermute(packed, "view", partner)
    to_far, to_near = rims_out(estimate, blank, radius, rows)
    far = lax.ppermute(to_far, "tile", far_pairs)
    near = lax.ppermute(to_near, "tile", near_pairs)
    places = slot_places(tiles, views, label_owner, label_index)
    own = prepare(False, taps, lines, estimate, places[1], rows, seen, keep)
    others = prepare(True, taps, swapped, estimate, lines, rows, seen, keep)
    came = token_of(far.reshape(radius * rows, across), (others[4],), 0)
    field_own, field_other, *sends = ratio_fields(
        own, others, far, near, measured, swapped, came
    )
    rims = [
        lax.ppermute(send, "tile", pairs) for send, pairs in zip(sends, (far_pairs, near_pairs) * PARTS)
    ]
    inner = own_planes(taps, own[4], others[4], field_own, field_other)
    mine, other, sums = [], [], []
    for part in range(PARTS):
        mine.append(add_rims(inner[part], *rims[2 * part : 2 * part + 2], *mine[-1:]))
        other.append(lax.ppermute(mine[part], "view", across_pairs))
        sums = [moment_rows(views, tiles, part, estimate, mine[part], labels, places, sums)]
    sent = sums[0]
    got = lax.all_to_all(sent, ("tile", "view"), split_axis=0, concat_axis=0, tiled=True)
    size = keep // PARTS
    pieces = [(part * size, size) for part in range(PARTS)]
    new_mine, new_other, token = [], [], [sent]
    for part in range(PARTS):
        new_mine.append(update(views, part, estimate, mine[part], other[part], token))
        new_other.append(lax.ppermute(new_mine[part], "view", partner))
        token = [token_of(new_mine[part])]
    scale = label_index.shape[1] / (planes * height * across)
    moments = nucleus_table(across, scale, got)
    begun = begin_result(pieces, estimate.shape, new_mine)
    return finish(pieces, begun, new_other), moments


def solution(mesh):
    placed = (
        P("tile", None, None),
        P("view", "tile", None, None),
        P("view", None, None),
        P("tile", None, None),
        P("tile", None, None),
        P("tile", None),
    )
    return jax.shard_map(
        on_device,
        mesh=mesh,
        in_specs=placed,
        out_specs=(P("tile", None, None), P(None, "tile")),
        check_vma=False,
    )
```

```python
import functools

import jax
import jax.numpy as jnp
from jax import lax
from jax.experimental import pallas as pl
from jax.experimental.pallas import tpu as pltpu
from jax.sharding import PartitionSpec as P

MOM = 10
CAP = 5
WIDTH = 25
NUC_DEV = 128
LANES = 128
PARTS = 2
TAIL = 24
IDS = 24
F32 = jnp.float32
BF16 = jnp.bfloat16
ANY = pl.BlockSpec(memory_space=pl.ANY)
VMEM = pl.BlockSpec(memory_space=pltpu.VMEM)
LIMIT = 32 * 1024 * 1024


def half_of(view):
    return (view ^ (view >> 1)) & 1


def split(value):
    upper = value.astype(BF16)
    return upper, (value - upper.astype(F32)).astype(BF16)


def band(taps, shape, offset):
    rows = lax.broadcasted_iota(jnp.int32, shape, 0)
    cols = lax.broadcasted_iota(jnp.int32, shape, 1)
    place = cols - rows + offset
    result = jnp.zeros(shape, F32)
    for step, tap in enumerate(taps):
        result = jnp.where(place == step, tap, result)
    return result


def depth_terms(source, weights, first, last, planes, flipped):
    radius = (len(weights) - 1) // 2
    totals = {plane: None for plane in planes}
    for place in range(first, last):
        block = None
        for plane in planes:
            step = plane - place + radius if flipped else place - plane + radius
            if 0 <= step < len(weights):
                block = source(place) if block is None else block
                term = weights[step] * block
                totals[plane] = term if totals[plane] is None else totals[plane] + term
    return totals


def chunks(rows, across):
    return [(slice(row, row + 16), slice(lane, lane + LANES)) for row in range(0, rows, 16) for lane in range(0, across, LANES)]


def rims_out_kernel(estimate, after, to_far, to_near):
    planes, radius, rows = estimate.shape[0], to_far.shape[0], to_far.shape[1]
    odd = lax.axis_index("tile") % 2
    half = half_of(lax.axis_index("view"))
    start = pl.multiple_of((estimate.shape[1] - rows) * half, 8)
    to_far[...] = estimate[pl.ds(odd, radius), pl.ds(start, rows)]
    to_near[...] = estimate[pl.ds(1 - odd, radius), pl.ds(start, rows)]


def rims_out(estimate, after, radius, rows):
    shape = jax.ShapeDtypeStruct((radius, rows, estimate.shape[2]), F32)
    return pl.pallas_call(
        rims_out_kernel,
        out_shape=(shape, shape),
        in_specs=[VMEM, ANY],
        out_specs=(VMEM, VMEM),
        compiler_params=pltpu.CompilerParams(vmem_limit_bytes=LIMIT),
        name="rims_out",
    )(estimate, after)


def blank_kernel(rows):
    rows[...] = jnp.zeros_like(rows)


def blank_rows(across):
    return pl.pallas_call(
        blank_kernel,
        out_shape=jax.ShapeDtypeStruct((TAIL, across), F32),
        out_specs=VMEM,
        compiler_params=pltpu.CompilerParams(vmem_limit_bytes=LIMIT),
        cost_estimate=pl.CostEstimate(flops=8_000_000_000, bytes_accessed=16_000_000, transcendentals=0),
        name="blank_rows",
    )()


def view_out_kernel(seen, measured, taps, blank, packed):
    planes, height = measured.shape[1], measured.shape[2]
    half = half_of(lax.axis_index("view"))
    start = pl.multiple_of((height - seen) * (1 - half), 8)
    for plane in range(planes):
        packed[plane * seen : (plane + 1) * seen] = measured[0, plane, pl.ds(start, seen)]
    packed[planes * seen :] = blank[...]
    for axis in range(taps.shape[0]):
        at = planes * seen + axis
        packed[at : at + 1, : taps.shape[2]] = taps[axis]


def view_out(measured, lines, blank, seen):
    _, planes, _, across = measured.shape
    return pl.pallas_call(
        functools.partial(view_out_kernel, seen),
        out_shape=jax.ShapeDtypeStruct((planes * seen + TAIL, across), F32),
        in_specs=[VMEM] * 3,
        out_specs=VMEM,
        compiler_params=pltpu.CompilerParams(vmem_limit_bytes=LIMIT),
        name="view_out",
    )(measured, lines, blank)


def prepare_kernel(packed, taps, source, estimate, after, wide, tall, back, part, spread):
    half = half_of(lax.axis_index("view"))
    across = wide.shape[-1]
    rows, keep, seen = part.shape[1], back.shape[0], tall.shape[0]
    planes = estimate.shape[0]
    radius = (taps - 1) // 2
    at = source.shape[0] - TAIL
    if packed:
        raw = source[at : at + 3, :taps]
    else:
        raw = jnp.concatenate([source[axis] for axis in range(source.shape[0])], axis=0)
    weights = raw / jnp.sum(raw, axis=-1, keepdims=True)
    deep, high, flat = [[weights[axis : axis + 1, t : t + 1] for t in range(taps)] for axis in range(3)]
    start = pl.multiple_of((2 * keep - rows) * half, 16)
    seen_start = (2 * keep - seen) * half
    near_diagonal = jnp.abs(
        lax.broadcasted_iota(jnp.int32, (across, across), 1)
        - lax.broadcasted_iota(jnp.int32, (across, across), 0)
    ) <= radius
    for turn, line in enumerate((flat[::-1], flat)):
        first_row = jnp.concatenate(
            line[radius:] + [jnp.zeros((1, across - taps), F32)] + line[:radius], axis=1
        )
        square = pltpu.roll(
            jnp.broadcast_to(first_row, (across, across)), 0, 1, stride=1, stride_axis=0
        )
        upper, lower = split(jnp.where(near_diagonal, square, 0.0))
        wide[turn, 0] = upper
        wide[turn, 1] = lower
    upper, lower = split(band(high, (seen, rows), radius + start - seen_start))
    tall[...] = jnp.concatenate([upper, upper, lower], axis=1)
    upper, lower = split(band(high[::-1], (keep, rows), radius + seen_start - keep * half))
    back[...] = jnp.concatenate([upper, upper, lower], axis=1)
    factors = [jnp.broadcast_to(tap, (16, LANES)) for tap in deep]
    spread[...] = jnp.zeros_like(spread)
    for step in range(taps):
        spread[step : step + 1] = factors[step][:1]
    for row, lane in chunks(rows, across):
        where = pl.ds(pl.multiple_of(start + row.start, 16), 16)
        terms = depth_terms(
            lambda place: estimate[place, where, lane], factors, 0, planes, range(planes), False
        )
        for plane, block in terms.items():
            part[plane, row, lane] = block


def prepare(packed, taps, source, estimate, after, rows, seen, keep):
    planes, _, across = estimate.shape
    return pl.pallas_call(
        functools.partial(prepare_kernel, packed, taps),
        out_shape=(
            jax.ShapeDtypeStruct((2, 2, across, across), BF16),
            jax.ShapeDtypeStruct((seen, 3 * rows), BF16),
            jax.ShapeDtypeStruct((keep, 3 * rows), BF16),
            jax.ShapeDtypeStruct((planes, rows, across), F32),
            jax.ShapeDtypeStruct((-(-taps // 8) * 8, LANES), F32),
        ),
        in_specs=[VMEM, VMEM, ANY],
        out_specs=(VMEM,) * 5,
        compiler_params=pltpu.CompilerParams(vmem_limit_bytes=LIMIT),
        name="prepare",
    )(source, estimate, after)


def spread_factors(spread, taps):
    return [jnp.broadcast_to(spread[step : step + 1, :], (16, LANES)) for step in range(taps)]


def fields_kernel(*refs):
    sets, (far, near, measured, swapped), refs = (refs[:5], refs[5:10]), refs[10:14], refs[15:]
    fields, sends, (blur_hi, blur_lo, plane_hi, plane_lo) = refs[:2], refs[2:-4], refs[-4:]
    planes = sets[0][3].shape[0]
    radius, rows, across = near.shape
    keep, seen = sets[0][2].shape[0], sets[0][1].shape[0]
    taps = 2 * radius + 1
    even = lax.axis_index("tile") % 2 == 0
    half = half_of(lax.axis_index("view"))
    seen_start = pl.multiple_of((2 * keep - seen) * half, 8)
    factors = [spread_factors(spread, taps) for _, _, _, _, spread in sets]
    for which, (_, _, _, part, _) in enumerate(sets):
        for row, lane in chunks(rows, across):

            def rim(place):
                if place < 0:
                    at = place + radius
                    return jnp.where(even, far[at, row, lane], near[at, row, lane])
                at = place - planes
                return jnp.where(even, near[at, row, lane], far[at, row, lane])

            below = depth_terms(rim, factors[which], -radius, 0, range(planes), False)
            above = depth_terms(rim, factors[which], planes, planes + radius, range(planes), False)
            for plane in range(planes):
                block = part[plane, row, lane]
                for term in (below[plane], above[plane]):
                    block = block if term is None else block + term
                upper, lower = split(block)
                at = slice(plane * rows + row.start, plane * rows + row.stop)
                blur_hi[which, at, lane] = upper
                blur_lo[which, at, lane] = lower
    lines = []
    for which, (wide, _, _, _, _) in enumerate(sets):
        upper, lower = wide[0, 0], wide[0, 1]
        lines.append(
            jnp.dot(blur_hi[which], upper, preferred_element_type=F32)
            + jnp.dot(blur_lo[which], upper, preferred_element_type=F32)
            + jnp.dot(blur_hi[which], lower, preferred_element_type=F32)
        )
    both = [(which, plane) for which in range(2) for plane in range(planes)]
    forwards = {}
    for which, plane in both:
        hi, lo = split(lines[which][plane * rows : (plane + 1) * rows])
        forwards[which, plane] = jnp.dot(
            sets[which][1][...], jnp.concatenate([hi, lo, hi], axis=0), preferred_element_type=F32
        )
    ratios = {}
    for which, plane in both:
        if which == 0:
            recorded = measured[0, plane, pl.ds(seen_start, seen), :]
        else:
            recorded = swapped[plane * seen : (plane + 1) * seen]
        ratio = recorded / forwards[which, plane]
        if rows > seen:
            ratio = jnp.concatenate([ratio, jnp.zeros((rows - seen, across), F32)], axis=0)
        ratios[which, plane] = split(ratio)
    turned = {}
    for which, plane in both:
        hi, lo = ratios[which, plane]
        turned[which, plane] = jnp.dot(
            sets[which][2][...], jnp.concatenate([hi, lo, hi], axis=0), preferred_element_type=F32
        )
    for which, plane in both:
        hi, lo = split(turned[which, plane])
        plane_hi[which, plane * keep : (plane + 1) * keep] = hi
        plane_lo[which, plane * keep : (plane + 1) * keep] = lo
    for which, (wide, _, _, _, _) in enumerate(sets):
        upper, lower = wide[1, 0], wide[1, 1]
        result = (
            jnp.dot(plane_hi[which], upper, preferred_element_type=F32)
            + jnp.dot(plane_lo[which], upper, preferred_element_type=F32)
            + jnp.dot(plane_hi[which], lower, preferred_element_type=F32)
        )
        fields[which][...] = result.reshape(planes, keep, across)
    for row, lane in chunks(keep, across):
        below, above = [], []
        for which in range(2):
            source = lambda place: fields[which][place, row, lane]
            outer = range(planes, planes + radius)
            below.append(depth_terms(source, factors[which], 0, planes, range(-radius, 0), True))
            above.append(depth_terms(source, factors[which], 0, planes, outer, True))
        part_at, inside = divmod(row.start, keep // PARTS)
        inside = slice(inside, inside + 16)
        for at in range(radius):
            down = below[0][at - radius] + below[1][at - radius]
            up = above[0][at + planes] + above[1][at + planes]
            sends[2 * part_at][at, inside, lane] = jnp.where(even, down, up)
            sends[2 * part_at + 1][at, inside, lane] = jnp.where(even, up, down)


def ratio_fields(own, others, far, near, measured, swapped, after):
    keep, planes = own[2].shape[0], own[3].shape[0]
    radius, rows, across = near.shape
    field = jax.ShapeDtypeStruct((planes, keep, across), F32)
    send = jax.ShapeDtypeStruct((radius, keep // PARTS, across), F32)
    return pl.pallas_call(
        fields_kernel,
        out_shape=(field,) * 2 + (send,) * (2 * PARTS),
        in_specs=[VMEM] * 14 + [ANY],
        out_specs=(VMEM,) * (2 + 2 * PARTS),
        scratch_shapes=[
            pltpu.VMEM((2, planes * rows, across), BF16),
            pltpu.VMEM((2, planes * rows, across), BF16),
            pltpu.VMEM((2, planes * keep, across), BF16),
            pltpu.VMEM((2, planes * keep, across), BF16),
        ],
        compiler_params=pltpu.CompilerParams(vmem_limit_bytes=LIMIT),
        name="ratio_fields",
    )(*own, *others, far, near, measured, swapped, after)


def own_kernel(taps, spread_own, spread_other, field_own, field_other, *inner):
    planes, keep, across = field_own.shape
    factors = [spread_factors(spread, taps) for spread in (spread_own, spread_other)]
    for row, lane in chunks(keep, across):
        parts = [
            depth_terms(
                lambda place: field[place, row, lane], factors[which], 0, planes, range(planes), True
            )
            for which, field in enumerate((field_own, field_other))
        ]
        part_at, inside = divmod(row.start, keep // PARTS)
        for plane in range(planes):
            inner[part_at][plane, inside : inside + 16, lane] = parts[0][plane] + parts[1][plane]


def own_planes(taps, spread_own, spread_other, field_own, field_other):
    planes, keep, across = field_own.shape
    return pl.pallas_call(
        functools.partial(own_kernel, taps),
        out_shape=(jax.ShapeDtypeStruct((planes, keep // PARTS, across), F32),) * PARTS,
        in_specs=[VMEM] * 4,
        out_specs=(VMEM,) * PARTS,
        compiler_params=pltpu.CompilerParams(vmem_limit_bytes=LIMIT),
        name="own_planes",
    )(spread_own, spread_other, field_own, field_other)


def rims_kernel(inner, far, near, *rest):
    correction = rest[-1]
    planes, radius = inner.shape[0], near.shape[0]
    even = lax.axis_index("tile") % 2 == 0
    for plane in range(planes):
        total = inner[plane]
        if plane < radius:
            total += jnp.where(even, far[plane], near[plane])
        if plane >= planes - radius:
            at = plane - planes + radius
            total += jnp.where(even, near[at], far[at])
        correction[plane] = total


def add_rims(inner, far, near, *after):
    return pl.pallas_call(
        rims_kernel,
        out_shape=jax.ShapeDtypeStruct(inner.shape, F32),
        in_specs=[VMEM] * 3 + [ANY] * len(after),
        out_specs=VMEM,
        compiler_params=pltpu.CompilerParams(vmem_limit_bytes=LIMIT),
        name="add_rims",
    )(inner, far, near, *after)


def table_rows(table):
    return jnp.concatenate([table[:8], table[8:]], axis=1)


def update_kernel(views, part, estimate, mine, other, *rest):
    planes, size, across = mine.shape
    result = rest[-1]
    half = half_of(lax.axis_index("view"))
    start = pl.multiple_of(size * (PARTS * half + part), 8)
    for plane in range(planes):
        held = estimate[plane, pl.ds(start, size)]
        at = slice(plane * size, (plane + 1) * size)
        result[at] = held * (mine[plane] + other[plane]) * (1.0 / views)
    spare = result.shape[0] - planes * size
    if spare:
        result[planes * size :] = jnp.zeros((spare, across), F32)


def update(views, part, estimate, mine, other, after):
    planes, size, across = mine.shape
    spare = 8 * (PARTS - 1 - part)
    return pl.pallas_call(
        functools.partial(update_kernel, views, part),
        out_shape=jax.ShapeDtypeStruct((planes * size + spare, across), F32),
        in_specs=[VMEM] * 3 + [ANY] * len(after),
        out_specs=VMEM,
        compiler_params=pltpu.CompilerParams(vmem_limit_bytes=LIMIT),
        name="update",
    )(estimate, mine, other, *after)


def slots_kernel(views, owner_row, index_row, picked, base):
    count = base.shape[0]
    slots = owner_row.shape[1]
    owner = owner_row[...]
    member = (lax.broadcasted_iota(jnp.int32, (count // views, slots), 0) == owner).astype(F32)
    upto = (
        lax.broadcasted_iota(jnp.int32, (slots, slots), 0)
        <= lax.broadcasted_iota(jnp.int32, (slots, slots), 1)
    ).astype(F32)
    running = jnp.dot(member, upto, preferred_element_type=F32)
    rank = jnp.sum(member * running, axis=0, keepdims=True).astype(jnp.int32) - 1
    named = lax.broadcasted_iota(jnp.int32, (count, slots), 0) // views == owner
    index = index_row[...].astype(F32)
    lanes = lax.broadcasted_iota(jnp.int32, (count, LANES), 1)
    result = jnp.zeros((count, LANES), F32)
    for place in range(CAP):
        chosen = named & (rank == place)
        picked[place * count : (place + 1) * count] = chosen.astype(F32).astype(BF16)
        ids = jnp.sum(jnp.where(chosen, index, 0.0), axis=1, keepdims=True)
        result = jnp.where(lanes == place * WIDTH + IDS, ids, result)
    base[...] = result


def slot_places(tiles, views, label_owner, label_index):
    slots = label_index.shape[1]
    count = tiles * views
    return pl.pallas_call(
        functools.partial(slots_kernel, views),
        out_shape=(
            jax.ShapeDtypeStruct((CAP * count, slots), BF16),
            jax.ShapeDtypeStruct((count, LANES), F32),
        ),
        in_specs=[VMEM, VMEM],
        out_specs=(VMEM, VMEM),
        compiler_params=pltpu.CompilerParams(vmem_limit_bytes=LIMIT),
        name="slot_places",
    )(label_owner.reshape(1, slots), label_index)


def merge_rows(blocks):
    rows = lax.broadcasted_iota(jnp.int32, blocks[0].shape, 0)
    step = 4
    while step:
        low = (rows & step) == 0
        half = len(blocks) // 2
        merged = []
        for one, two in zip(blocks[:half], blocks[half:]):
            kept = jnp.where(low, one, two)
            turned = jnp.where(low, two, one)
            moved = pltpu.roll(turned, step, 0)
            if step < 4:
                moved = jnp.where(low, pltpu.roll(turned, 8 - step, 0), moved)
            merged.append(kept + moved)
        blocks = merged
        step //= 2
    return blocks[0]


def moments_kernel(views, depth_total, part, estimate, labels, picked, base, correction, *refs):
    begun, (sent, held, sums, table) = refs[:-4], refs[-4:]
    planes, size, across = correction.shape
    height_total = estimate.shape[1]
    slots = picked.shape[1]
    half = half_of(lax.axis_index("view"))
    first = (lax.axis_index("tile") * planes).astype(F32) + 0.5
    start = pl.multiple_of(size * (PARTS * half + part), 8)
    held[...] = estimate[:, pl.ds(start, size)] * correction[...] * (1.0 / views)
    group = 16
    spot = lax.broadcasted_iota(jnp.int32, (across, LANES), 0)
    lanes = lax.broadcasted_iota(jnp.int32, (across, LANES), 1)
    low = (spot * spot) & 255
    factors = jnp.where(lanes == 0, 1, jnp.where(lanes == 1, spot, 0))
    factors = jnp.where(lanes == 2, spot * spot - low, jnp.where(lanes == 3, low, factors))
    factors = factors.astype(F32).astype(BF16)
    base_row = lax.broadcasted_iota(jnp.int32, (8, across), 0)

    def one_group(number, carry):
        held_parts = []
        for pair in range(0, group, 2):
            slot = [number * group + pair, number * group + pair + 1]
            parts = [[None] * 6 for _ in slot]
            for row in range(0, size, 8):
                high = ((base_row + (row + start)).astype(F32) + 0.5) * (1.0 / height_total)
                flat, once, twice = [[jnp.zeros((8, across), F32) for _ in slot] for _ in range(3)]
                for plane in reversed(range(planes)):
                    mark = labels[plane, pl.ds(pl.multiple_of(start + row, 8), 8)]
                    value = held[plane, row : row + 8]
                    for at in range(2):
                        flat[at] = flat[at] + jnp.where(mark == slot[at], value, 0.0)
                        if plane > 0:
                            once[at] = once[at] + flat[at]
                            twice[at] = twice[at] + once[at]
                for at in range(2):
                    scaled = flat[at] * high
                    terms = (flat[at], scaled, scaled * high, once[at], once[at] * high, twice[at])
                    parts[at] = [new if old is None else old + new for old, new in zip(parts[at], terms)]
            held_parts += parts
            if len(held_parts) == 8:
                for kind in range(6):
                    row = kind * group + pair + 2 - 8
                    sums[row : row + 8, :] = merge_rows([parts[kind] for parts in held_parts])
                held_parts = []
        whole = sums[...]
        upper, rest = split(whole)
        rest = whole - upper.astype(F32)
        middle, lower = split(rest)
        lines = jnp.dot(
            jnp.concatenate([upper, middle, lower], axis=0), factors, preferred_element_type=F32
        )
        count = 6 * group
        lines = lines[:count] + lines[count : 2 * count] + lines[2 * count :]
        flat, high_flat, square_flat, once, high_once, twice = [
            lines[kind * group : (kind + 1) * group] for kind in range(6)
        ]
        deep = (first * flat + once) * (1.0 / depth_total)
        deep_high = (first * high_flat + high_once) * (1.0 / depth_total)
        deeper = first * (first * flat + 2.0 * once) + (2.0 * twice - once)
        deeper = deeper * (1.0 / depth_total**2)
        total = flat
        for kind, sums_of in enumerate((high_flat, square_flat, deep, deep_high, deeper), 1):
            total += pltpu.roll(sums_of, 4 * kind, 1)
        rows = pl.ds(pl.multiple_of(number * group, group), group)
        target = table if part == PARTS - 1 else sent
        target[rows, :] = total + begun[0][rows, :] if begun else total
        return carry

    lax.fori_loop(0, slots // group, one_group, 0)
    if part < PARTS - 1:
        return
    whole = table[...]
    upper, _ = split(whole)
    middle, lower = split(whole - upper.astype(F32))
    rows = jnp.dot(
        picked[...], jnp.concatenate([upper, middle, lower], axis=1), preferred_element_type=F32
    )
    rows = rows[:, :LANES] + rows[:, LANES : 2 * LANES] + rows[:, 2 * LANES :]
    total = base[...]
    count = total.shape[0]
    for place in range(CAP):
        total += pltpu.roll(rows[place * count : (place + 1) * count], place * WIDTH, 1)
    sent[...] = total


def moment_rows(views, tiles, part, estimate, correction, labels, places, begun):
    planes, size, across = correction.shape
    slots = places[0].shape[1]
    count = places[1].shape[0] if part == PARTS - 1 else slots
    return pl.pallas_call(
        functools.partial(moments_kernel, views, tiles * planes, part),
        out_shape=jax.ShapeDtypeStruct((count, LANES), F32),
        in_specs=[VMEM] * (5 + len(begun)),
        out_specs=VMEM,
        scratch_shapes=[
            pltpu.VMEM((planes, size, across), F32),
            pltpu.VMEM((6 * 16, across), F32),
            pltpu.VMEM((slots, LANES), F32),
        ],
        compiler_params=pltpu.CompilerParams(vmem_limit_bytes=LIMIT),
        name="moment_rows",
    )(estimate, labels, *places, correction, *begun)


def segments_kernel(across, scale, rows, moments):
    whole = rows[...]
    parts = [whole] + [pltpu.roll(whole, LANES - place * WIDTH, 1) for place in range(1, CAP)]
    values = jnp.concatenate(parts, axis=0)
    ids = values[:, IDS : IDS + 1].astype(jnp.int32)
    spots = lax.broadcasted_iota(jnp.int32, (values.shape[0], NUC_DEV), 1)
    picked = (ids == spots).astype(F32)
    full = lax.dot_general(
        values, picked, (((0,), (0,)), ((), ())),
        precision=lax.Precision.HIGHEST, preferred_element_type=F32,
    )
    mass, high, higher, deep, deep_high, deeper = [full[4 * kind : 4 * kind + 4] for kind in range(6)]
    flat = lambda sums: sums[0:1]
    line = lambda sums: (sums[1:2] + 0.5 * sums[0:1]) * (1.0 / across)
    square = lambda sums: (sums[2:3] + sums[3:4] + sums[1:2] + 0.25 * sums[0:1]) * (1.0 / across**2)
    total = flat(mass)
    sums = jnp.concatenate(
        [
            flat(deep), flat(high), line(mass),
            flat(deeper), flat(higher), square(mass),
            flat(deep_high), line(deep), line(high),
        ],
        axis=0,
    )
    moments[...] = jnp.concatenate([total * scale, sums / jnp.maximum(total, 1.0)], axis=0)


def nucleus_table(across, scale, rows):
    return pl.pallas_call(
        functools.partial(segments_kernel, across, scale),
        out_shape=jax.ShapeDtypeStruct((MOM, NUC_DEV), F32),
        in_specs=[VMEM],
        out_specs=VMEM,
        compiler_params=pltpu.CompilerParams(vmem_limit_bytes=LIMIT),
        cost_estimate=pl.CostEstimate(flops=10_000_000_000, bytes_accessed=20_000_000, transcendentals=0),
        name="nucleus_table",
    )(rows)


def stores(pieces, sources, whole, half, sems):
    keep = whole.shape[1] // 2
    copies = []
    for number, ((first, size), source) in enumerate(zip(pieces, sources)):
        start = pl.multiple_of(keep * half + first, 8)
        for plane in range(whole.shape[0]):
            copies.append(
                pltpu.make_async_copy(
                    source.at[pl.ds(plane * size, size)],
                    whole.at[plane, pl.ds(start, size)],
                    sems.at[number, plane],
                )
            )
    for copy in copies:
        copy.start()
    return copies


def token_kernel(source, *rest):
    token = rest[-1]
    token[...] = source[:8, :LANES]


def token_of(source, after=(), flops=0):
    return pl.pallas_call(
        token_kernel,
        out_shape=jax.ShapeDtypeStruct((8, LANES), F32),
        in_specs=[VMEM] + [ANY] * len(after),
        out_specs=VMEM,
        compiler_params=pltpu.CompilerParams(vmem_limit_bytes=LIMIT),
        cost_estimate=pl.CostEstimate(flops=flops, bytes_accessed=flops // 500, transcendentals=0),
        name="token_of",
    )(source, *after)


def begin_kernel(pieces, *refs):
    sources, (whole, sems) = refs[:-2], refs[-2:]
    for copy in stores(pieces, sources, whole, half_of(lax.axis_index("view")), sems):
        copy.wait()


def begin_result(pieces, shape, mine):
    return pl.pallas_call(
        functools.partial(begin_kernel, pieces),
        out_shape=jax.ShapeDtypeStruct(shape, F32),
        in_specs=[VMEM] * len(mine),
        out_specs=ANY,
        scratch_shapes=[pltpu.SemaphoreType.DMA((len(pieces), shape[0]))],
        compiler_params=pltpu.CompilerParams(vmem_limit_bytes=LIMIT),
        name="begin_result",
    )(*mine)


def finish_kernel(pieces, begun, *refs):
    others, (whole, sems) = refs[:-2], refs[-2:]
    for copy in stores(pieces, others, whole, 1 - half_of(lax.axis_index("view")), sems):
        copy.wait()


def finish(pieces, begun, others):
    return pl.pallas_call(
        functools.partial(finish_kernel, pieces),
        out_shape=jax.ShapeDtypeStruct(begun.shape, F32),
        in_specs=[ANY] + [VMEM] * len(others),
        out_specs=ANY,
        input_output_aliases={0: 0},
        scratch_shapes=[pltpu.SemaphoreType.DMA((len(pieces), begun.shape[0]))],
        compiler_params=pltpu.CompilerParams(vmem_limit_bytes=LIMIT),
        name="finish",
    )(begun, *others)


def on_device(estimate, measured, kernels, labels, label_owner, label_index):
    tiles, views = lax.axis_size("tile"), lax.axis_size("view")
    planes, height, across = estimate.shape
    taps = kernels.shape[2]
    radius = (taps - 1) // 2
    keep = height // 2
    seen = min(height, -(-(keep + radius) // 8) * 8)
    rows = min(height, -(-(keep + 2 * radius) // 16) * 16)
    near_pairs = [(i, i ^ 1) for i in range(tiles)]
    far_pairs = [(i, i + 1) for i in range(1, tiles - 1, 2)]
    far_pairs = far_pairs + [(b, a) for a, b in far_pairs]
    partner = [(i, i ^ 1) for i in range(views)]
    across_pairs = [(i, i ^ 3) for i in range(views)]

    lines = jnp.transpose(kernels, (1, 0, 2))
    blank = blank_rows(across)
    packed = view_out(measured, lines, blank, seen)
    swapped = lax.ppermute(packed, "view", partner)
    to_far, to_near = rims_out(estimate, blank, radius, rows)
    far = lax.ppermute(to_far, "tile", far_pairs)
    near = lax.ppermute(to_near, "tile", near_pairs)
    places = slot_places(tiles, views, label_owner, label_index)
    own = prepare(False, taps, lines, estimate, places[1], rows, seen, keep)
    others = prepare(True, taps, swapped, estimate, lines, rows, seen, keep)
    came = token_of(far.reshape(radius * rows, across), (others[4],), 0)
    field_own, field_other, *sends = ratio_fields(
        own, others, far, near, measured, swapped, came
    )
    rims = [
        lax.ppermute(send, "tile", pairs) for send, pairs in zip(sends, (far_pairs, near_pairs) * PARTS)
    ]
    inner = own_planes(taps, own[4], others[4], field_own, field_other)
    mine, other, sums = [], [], []
    for part in range(PARTS):
        mine.append(add_rims(inner[part], *rims[2 * part : 2 * part + 2], *sums))
        other.append(lax.ppermute(mine[part], "view", across_pairs))
        sums = [moment_rows(views, tiles, part, estimate, mine[part], labels, places, sums)]
    sent = sums[0]
    got = lax.all_to_all(sent, ("tile", "view"), split_axis=0, concat_axis=0, tiled=True)
    size = keep // PARTS
    pieces = [(part * size, size) for part in range(PARTS)]
    new_mine, new_other, token = [], [], [sent]
    for part in range(PARTS):
        new_mine.append(update(views, part, estimate, mine[part], other[part], token))
        new_other.append(lax.ppermute(new_mine[part], "view", partner))
        token = [token_of(new_mine[part])]
    scale = label_index.shape[1] / (planes * height * across)
    moments = nucleus_table(across, scale, got)
    begun = begin_result(pieces, estimate.shape, new_mine)
    return finish(pieces, begun, new_other), moments


def solution(mesh):
    placed = (
        P("tile", None, None),
        P("view", "tile", None, None),
        P("view", None, None),
        P("tile", None, None),
        P("tile", None, None),
        P("tile", None),
    )
    return jax.shard_map(
        on_device,
        mesh=mesh,
        in_specs=placed,
        out_specs=(P("tile", None, None), P(None, "tile")),
        check_vma=False,
    )
```

```python
import functools

import jax
import jax.numpy as jnp
from jax import lax
from jax.experimental import pallas as pl
from jax.experimental.pallas import tpu as pltpu
from jax.sharding import PartitionSpec as P

MOM = 10
CAP = 5
WIDTH = 25
NUC_DEV = 128
LANES = 128
PARTS = 2
TAIL = 16
IDS = 24
F32 = jnp.float32
BF16 = jnp.bfloat16
ANY = pl.BlockSpec(memory_space=pl.ANY)
VMEM = pl.BlockSpec(memory_space=pltpu.VMEM)
LIMIT = 32 * 1024 * 1024


def half_of(view):
    return (view ^ (view >> 1)) & 1


def split(value):
    upper = value.astype(BF16)
    return upper, (value - upper.astype(F32)).astype(BF16)


def band(taps, shape, offset):
    rows = lax.broadcasted_iota(jnp.int32, shape, 0)
    cols = lax.broadcasted_iota(jnp.int32, shape, 1)
    place = cols - rows + offset
    result = jnp.zeros(shape, F32)
    for step, tap in enumerate(taps):
        result = jnp.where(place == step, tap, result)
    return result


def depth_terms(source, weights, first, last, planes, flipped):
    radius = (len(weights) - 1) // 2
    totals = {plane: None for plane in planes}
    for place in range(first, last):
        block = None
        for plane in planes:
            step = plane - place + radius if flipped else place - plane + radius
            if 0 <= step < len(weights):
                block = source(place) if block is None else block
                term = weights[step] * block
                totals[plane] = term if totals[plane] is None else totals[plane] + term
    return totals


def chunks(rows, across):
    return [(slice(row, row + 16), slice(lane, lane + LANES)) for row in range(0, rows, 16) for lane in range(0, across, LANES)]


def rims_out_kernel(estimate, after, to_far, to_near):
    planes, radius, rows = estimate.shape[0], to_far.shape[0], to_far.shape[1]
    odd = lax.axis_index("tile") % 2
    half = half_of(lax.axis_index("view"))
    start = pl.multiple_of((estimate.shape[1] - rows) * half, 8)
    to_far[...] = estimate[pl.ds(odd, radius), pl.ds(start, rows)]
    to_near[...] = estimate[pl.ds(1 - odd, radius), pl.ds(start, rows)]


def rims_out(estimate, after, radius, rows):
    shape = jax.ShapeDtypeStruct((radius, rows, estimate.shape[2]), F32)
    return pl.pallas_call(
        rims_out_kernel,
        out_shape=(shape, shape),
        in_specs=[VMEM, ANY],
        out_specs=(VMEM, VMEM),
        compiler_params=pltpu.CompilerParams(vmem_limit_bytes=LIMIT),
        name="rims_out",
    )(estimate, after)


def blank_kernel(rows):
    rows[...] = jnp.zeros_like(rows)


def blank_rows(across):
    return pl.pallas_call(
        blank_kernel,
        out_shape=jax.ShapeDtypeStruct((TAIL, across), F32),
        out_specs=VMEM,
        compiler_params=pltpu.CompilerParams(vmem_limit_bytes=LIMIT),
        cost_estimate=pl.CostEstimate(flops=8_000_000_000, bytes_accessed=16_000_000, transcendentals=0),
        name="blank_rows",
    )()


def view_out_kernel(seen, measured, taps, blank, packed):
    planes, height = measured.shape[1], measured.shape[2]
    half = half_of(lax.axis_index("view"))
    start = pl.multiple_of((height - seen) * (1 - half), 8)
    for plane in range(planes):
        packed[plane * seen : (plane + 1) * seen] = measured[0, plane, pl.ds(start, seen)]
    packed[planes * seen :] = blank[...]
    for axis in range(taps.shape[0]):
        at = planes * seen + axis
        packed[at : at + 1, : taps.shape[2]] = taps[axis]


def view_out(measured, lines, blank, seen):
    _, planes, _, across = measured.shape
    return pl.pallas_call(
        functools.partial(view_out_kernel, seen),
        out_shape=jax.ShapeDtypeStruct((planes * seen + TAIL, across), F32),
        in_specs=[VMEM] * 3,
        out_specs=VMEM,
        compiler_params=pltpu.CompilerParams(vmem_limit_bytes=LIMIT),
        name="view_out",
    )(measured, lines, blank)


def prepare_kernel(packed, taps, source, estimate, after, wide, tall, back, part, spread):
    half = half_of(lax.axis_index("view"))
    across = wide.shape[-1]
    rows, keep, seen = part.shape[1], back.shape[0], tall.shape[0]
    planes = estimate.shape[0]
    radius = (taps - 1) // 2
    at = source.shape[0] - TAIL
    if packed:
        raw = source[at : at + 3, :taps]
    else:
        raw = jnp.concatenate([source[axis] for axis in range(source.shape[0])], axis=0)
    weights = raw / jnp.sum(raw, axis=-1, keepdims=True)
    deep, high, flat = [[weights[axis : axis + 1, t : t + 1] for t in range(taps)] for axis in range(3)]
    start = pl.multiple_of((2 * keep - rows) * half, 16)
    seen_start = (2 * keep - seen) * half
    near_diagonal = jnp.abs(
        lax.broadcasted_iota(jnp.int32, (across, across), 1)
        - lax.broadcasted_iota(jnp.int32, (across, across), 0)
    ) <= radius
    for turn, line in enumerate((flat[::-1], flat)):
        first_row = jnp.concatenate(
            line[radius:] + [jnp.zeros((1, across - taps), F32)] + line[:radius], axis=1
        )
        square = pltpu.roll(
            jnp.broadcast_to(first_row, (across, across)), 0, 1, stride=1, stride_axis=0
        )
        upper, lower = split(jnp.where(near_diagonal, square, 0.0))
        wide[turn, 0] = upper
        wide[turn, 1] = lower
    upper, lower = split(band(high, (seen, rows), radius + start - seen_start))
    tall[...] = jnp.concatenate([upper, upper, lower], axis=1)
    upper, lower = split(band(high[::-1], (keep, rows), radius + seen_start - keep * half))
    back[...] = jnp.concatenate([upper, upper, lower], axis=1)
    factors = [jnp.broadcast_to(tap, (16, LANES)) for tap in deep]
    spread[...] = jnp.zeros_like(spread)
    for step in range(taps):
        spread[step : step + 1] = factors[step][:1]
    for row, lane in chunks(rows, across):
        where = pl.ds(pl.multiple_of(start + row.start, 16), 16)
        terms = depth_terms(
            lambda place: estimate[place, where, lane], factors, 0, planes, range(planes), False
        )
        for plane, block in terms.items():
            part[plane, row, lane] = block


def prepare(packed, taps, source, estimate, after, rows, seen, keep):
    planes, _, across = estimate.shape
    return pl.pallas_call(
        functools.partial(prepare_kernel, packed, taps),
        out_shape=(
            jax.ShapeDtypeStruct((2, 2, across, across), BF16),
            jax.ShapeDtypeStruct((seen, 3 * rows), BF16),
            jax.ShapeDtypeStruct((keep, 3 * rows), BF16),
            jax.ShapeDtypeStruct((planes, rows, across), F32),
            jax.ShapeDtypeStruct((-(-taps // 8) * 8, LANES), F32),
        ),
        in_specs=[VMEM, VMEM, ANY],
        out_specs=(VMEM,) * 5,
        compiler_params=pltpu.CompilerParams(vmem_limit_bytes=LIMIT),
        name="prepare",
    )(source, estimate, after)


def spread_factors(spread, taps):
    return [jnp.broadcast_to(spread[step : step + 1, :], (16, LANES)) for step in range(taps)]


def fields_kernel(*refs):
    sets, (far, near, measured, swapped), refs = (refs[:5], refs[5:10]), refs[10:14], refs[15:]
    fields, sends, (blur_hi, blur_lo, plane_hi, plane_lo) = refs[:2], refs[2:-4], refs[-4:]
    planes = sets[0][3].shape[0]
    radius, rows, across = near.shape
    keep, seen = sets[0][2].shape[0], sets[0][1].shape[0]
    taps = 2 * radius + 1
    even = lax.axis_index("tile") % 2 == 0
    half = half_of(lax.axis_index("view"))
    seen_start = pl.multiple_of((2 * keep - seen) * half, 8)
    factors = [spread_factors(spread, taps) for _, _, _, _, spread in sets]
    for which, (_, _, _, part, _) in enumerate(sets):
        for row, lane in chunks(rows, across):

            def rim(place):
                if place < 0:
                    at = place + radius
                    return jnp.where(even, far[at, row, lane], near[at, row, lane])
                at = place - planes
                return jnp.where(even, near[at, row, lane], far[at, row, lane])

            below = depth_terms(rim, factors[which], -radius, 0, range(planes), False)
            above = depth_terms(rim, factors[which], planes, planes + radius, range(planes), False)
            for plane in range(planes):
                block = part[plane, row, lane]
                for term in (below[plane], above[plane]):
                    block = block if term is None else block + term
                upper, lower = split(block)
                at = slice(plane * rows + row.start, plane * rows + row.stop)
                blur_hi[which, at, lane] = upper
                blur_lo[which, at, lane] = lower
    lines = []
    for which, (wide, _, _, _, _) in enumerate(sets):
        upper, lower = wide[0, 0], wide[0, 1]
        lines.append(
            jnp.dot(blur_hi[which], upper, preferred_element_type=F32)
            + jnp.dot(blur_lo[which], upper, preferred_element_type=F32)
            + jnp.dot(blur_hi[which], lower, preferred_element_type=F32)
        )
    both = [(which, plane) for which in range(2) for plane in range(planes)]
    forwards = {}
    for which, plane in both:
        hi, lo = split(lines[which][plane * rows : (plane + 1) * rows])
        forwards[which, plane] = jnp.dot(
            sets[which][1][...], jnp.concatenate([hi, lo, hi], axis=0), preferred_element_type=F32
        )
    ratios = {}
    for which, plane in both:
        if which == 0:
            recorded = measured[0, plane, pl.ds(seen_start, seen), :]
        else:
            recorded = swapped[plane * seen : (plane + 1) * seen]
        ratio = recorded / forwards[which, plane]
        if rows > seen:
            ratio = jnp.concatenate([ratio, jnp.zeros((rows - seen, across), F32)], axis=0)
        ratios[which, plane] = split(ratio)
    turned = {}
    for which, plane in both:
        hi, lo = ratios[which, plane]
        turned[which, plane] = jnp.dot(
            sets[which][2][...], jnp.concatenate([hi, lo, hi], axis=0), preferred_element_type=F32
        )
    for which, plane in both:
        hi, lo = split(turned[which, plane])
        plane_hi[which, plane * keep : (plane + 1) * keep] = hi
        plane_lo[which, plane * keep : (plane + 1) * keep] = lo
    for which, (wide, _, _, _, _) in enumerate(sets):
        upper, lower = wide[1, 0], wide[1, 1]
        result = (
            jnp.dot(plane_hi[which], upper, preferred_element_type=F32)
            + jnp.dot(plane_lo[which], upper, preferred_element_type=F32)
            + jnp.dot(plane_hi[which], lower, preferred_element_type=F32)
        )
        fields[which][...] = result.reshape(planes, keep, across)
    for row, lane in chunks(keep, across):
        below, above = [], []
        for which in range(2):
            source = lambda place: fields[which][place, row, lane]
            outer = range(planes, planes + radius)
            below.append(depth_terms(source, factors[which], 0, planes, range(-radius, 0), True))
            above.append(depth_terms(source, factors[which], 0, planes, outer, True))
        part_at, inside = divmod(row.start, keep // PARTS)
        inside = slice(inside, inside + 16)
        for at in range(radius):
            down = below[0][at - radius] + below[1][at - radius]
            up = above[0][at + planes] + above[1][at + planes]
            sends[2 * part_at][at, inside, lane] = jnp.where(even, down, up)
            sends[2 * part_at + 1][at, inside, lane] = jnp.where(even, up, down)


def ratio_fields(own, others, far, near, measured, swapped, after):
    keep, planes = own[2].shape[0], own[3].shape[0]
    radius, rows, across = near.shape
    field = jax.ShapeDtypeStruct((planes, keep, across), F32)
    send = jax.ShapeDtypeStruct((radius, keep // PARTS, across), F32)
    return pl.pallas_call(
        fields_kernel,
        out_shape=(field,) * 2 + (send,) * (2 * PARTS),
        in_specs=[VMEM] * 14 + [ANY],
        out_specs=(VMEM,) * (2 + 2 * PARTS),
        scratch_shapes=[
            pltpu.VMEM((2, planes * rows, across), BF16),
            pltpu.VMEM((2, planes * rows, across), BF16),
            pltpu.VMEM((2, planes * keep, across), BF16),
            pltpu.VMEM((2, planes * keep, across), BF16),
        ],
        compiler_params=pltpu.CompilerParams(vmem_limit_bytes=LIMIT),
        name="ratio_fields",
    )(*own, *others, far, near, measured, swapped, after)


def own_kernel(taps, spread_own, spread_other, field_own, field_other, *inner):
    planes, keep, across = field_own.shape
    factors = [spread_factors(spread, taps) for spread in (spread_own, spread_other)]
    for row, lane in chunks(keep, across):
        parts = [
            depth_terms(
                lambda place: field[place, row, lane], factors[which], 0, planes, range(planes), True
            )
            for which, field in enumerate((field_own, field_other))
        ]
        part_at, inside = divmod(row.start, keep // PARTS)
        for plane in range(planes):
            inner[part_at][plane, inside : inside + 16, lane] = parts[0][plane] + parts[1][plane]


def own_planes(taps, spread_own, spread_other, field_own, field_other):
    planes, keep, across = field_own.shape
    return pl.pallas_call(
        functools.partial(own_kernel, taps),
        out_shape=(jax.ShapeDtypeStruct((planes, keep // PARTS, across), F32),) * PARTS,
        in_specs=[VMEM] * 4,
        out_specs=(VMEM,) * PARTS,
        compiler_params=pltpu.CompilerParams(vmem_limit_bytes=LIMIT),
        name="own_planes",
    )(spread_own, spread_other, field_own, field_other)


def rims_kernel(inner, far, near, *rest):
    correction = rest[-1]
    planes, radius = inner.shape[0], near.shape[0]
    even = lax.axis_index("tile") % 2 == 0
    for plane in range(planes):
        total = inner[plane]
        if plane < radius:
            total += jnp.where(even, far[plane], near[plane])
        if plane >= planes - radius:
            at = plane - planes + radius
            total += jnp.where(even, near[at], far[at])
        correction[plane] = total


def add_rims(inner, far, near, *after):
    return pl.pallas_call(
        rims_kernel,
        out_shape=jax.ShapeDtypeStruct(inner.shape, F32),
        in_specs=[VMEM] * 3 + [ANY] * len(after),
        out_specs=VMEM,
        compiler_params=pltpu.CompilerParams(vmem_limit_bytes=LIMIT),
        name="add_rims",
    )(inner, far, near, *after)


def table_rows(table):
    return jnp.concatenate([table[:8], table[8:]], axis=1)


def update_kernel(views, part, estimate, mine, other, *rest):
    planes, size, across = mine.shape
    result = rest[-1]
    half = half_of(lax.axis_index("view"))
    start = pl.multiple_of(size * (PARTS * half + part), 8)
    for plane in range(planes):
        held = estimate[plane, pl.ds(start, size)]
        at = slice(plane * size, (plane + 1) * size)
        result[at] = held * (mine[plane] + other[plane]) * (1.0 / views)
    spare = result.shape[0] - planes * size
    if spare:
        result[planes * size :] = jnp.zeros((spare, across), F32)


def update(views, part, estimate, mine, other, after):
    planes, size, across = mine.shape
    spare = 8 * (PARTS - 1 - part)
    return pl.pallas_call(
        functools.partial(update_kernel, views, part),
        out_shape=jax.ShapeDtypeStruct((planes * size + spare, across), F32),
        in_specs=[VMEM] * 3 + [ANY] * len(after),
        out_specs=VMEM,
        compiler_params=pltpu.CompilerParams(vmem_limit_bytes=LIMIT),
        name="update",
    )(estimate, mine, other, *after)


def slots_kernel(views, owner_row, index_row, picked, base):
    count = base.shape[0]
    slots = owner_row.shape[1]
    owner = owner_row[...]
    member = (lax.broadcasted_iota(jnp.int32, (count // views, slots), 0) == owner).astype(F32)
    upto = (
        lax.broadcasted_iota(jnp.int32, (slots, slots), 0)
        <= lax.broadcasted_iota(jnp.int32, (slots, slots), 1)
    ).astype(F32)
    running = jnp.dot(member, upto, preferred_element_type=F32)
    rank = jnp.sum(member * running, axis=0, keepdims=True).astype(jnp.int32) - 1
    named = lax.broadcasted_iota(jnp.int32, (count, slots), 0) // views == owner
    index = index_row[...].astype(F32)
    lanes = lax.broadcasted_iota(jnp.int32, (count, LANES), 1)
    result = jnp.zeros((count, LANES), F32)
    for place in range(CAP):
        chosen = named & (rank == place)
        picked[place * count : (place + 1) * count] = chosen.astype(F32).astype(BF16)
        ids = jnp.sum(jnp.where(chosen, index, 0.0), axis=1, keepdims=True)
        result = jnp.where(lanes == place * WIDTH + IDS, ids, result)
    base[...] = result


def slot_places(tiles, views, label_owner, label_index):
    slots = label_index.shape[1]
    count = tiles * views
    return pl.pallas_call(
        functools.partial(slots_kernel, views),
        out_shape=(
            jax.ShapeDtypeStruct((CAP * count, slots), BF16),
            jax.ShapeDtypeStruct((count, LANES), F32),
        ),
        in_specs=[VMEM, VMEM],
        out_specs=(VMEM, VMEM),
        compiler_params=pltpu.CompilerParams(vmem_limit_bytes=LIMIT),
        name="slot_places",
    )(label_owner.reshape(1, slots), label_index)


def merge_rows(blocks):
    rows = lax.broadcasted_iota(jnp.int32, blocks[0].shape, 0)
    step = 4
    while step:
        low = (rows & step) == 0
        half = len(blocks) // 2
        merged = []
        for one, two in zip(blocks[:half], blocks[half:]):
            kept = jnp.where(low, one, two)
            turned = jnp.where(low, two, one)
            moved = pltpu.roll(turned, step, 0)
            if step < 4:
                moved = jnp.where(low, pltpu.roll(turned, 8 - step, 0), moved)
            merged.append(kept + moved)
        blocks = merged
        step //= 2
    return blocks[0]


def moments_kernel(views, depth_total, part, estimate, labels, picked, base, correction, *refs):
    begun, (sent, held, sums, table) = refs[:-4], refs[-4:]
    planes, size, across = correction.shape
    height_total = estimate.shape[1]
    slots = picked.shape[1]
    half = half_of(lax.axis_index("view"))
    first = (lax.axis_index("tile") * planes).astype(F32) + 0.5
    start = pl.multiple_of(size * (PARTS * half + part), 8)
    held[...] = estimate[:, pl.ds(start, size)] * correction[...] * (1.0 / views)
    group = 16
    spot = lax.broadcasted_iota(jnp.int32, (across, LANES), 0)
    lanes = lax.broadcasted_iota(jnp.int32, (across, LANES), 1)
    low = (spot * spot) & 255
    factors = jnp.where(lanes == 0, 1, jnp.where(lanes == 1, spot, 0))
    factors = jnp.where(lanes == 2, spot * spot - low, jnp.where(lanes == 3, low, factors))
    factors = factors.astype(F32).astype(BF16)
    base_row = lax.broadcasted_iota(jnp.int32, (8, across), 0)

    def one_group(number, carry):
        held_parts = []
        for pair in range(0, group, 2):
            slot = [number * group + pair, number * group + pair + 1]
            parts = [[None] * 6 for _ in slot]
            for row in range(0, size, 8):
                high = ((base_row + (row + start)).astype(F32) + 0.5) * (1.0 / height_total)
                flat, once, twice = [[jnp.zeros((8, across), F32) for _ in slot] for _ in range(3)]
                for plane in reversed(range(planes)):
                    mark = labels[plane, pl.ds(pl.multiple_of(start + row, 8), 8)]
                    value = held[plane, row : row + 8]
                    for at in range(2):
                        flat[at] = flat[at] + jnp.where(mark == slot[at], value, 0.0)
                        if plane > 0:
                            once[at] = once[at] + flat[at]
                            twice[at] = twice[at] + once[at]
                for at in range(2):
                    scaled = flat[at] * high
                    terms = (flat[at], scaled, scaled * high, once[at], once[at] * high, twice[at])
                    parts[at] = [new if old is None else old + new for old, new in zip(parts[at], terms)]
            held_parts += parts
            if len(held_parts) == 8:
                for kind in range(6):
                    row = kind * group + pair + 2 - 8
                    sums[row : row + 8, :] = merge_rows([parts[kind] for parts in held_parts])
                held_parts = []
        whole = sums[...]
        upper, rest = split(whole)
        rest = whole - upper.astype(F32)
        middle, lower = split(rest)
        lines = jnp.dot(
            jnp.concatenate([upper, middle, lower], axis=0), factors, preferred_element_type=F32
        )
        count = 6 * group
        lines = lines[:count] + lines[count : 2 * count] + lines[2 * count :]
        flat, high_flat, square_flat, once, high_once, twice = [
            lines[kind * group : (kind + 1) * group] for kind in range(6)
        ]
        deep = (first * flat + once) * (1.0 / depth_total)
        deep_high = (first * high_flat + high_once) * (1.0 / depth_total)
        deeper = first * (first * flat + 2.0 * once) + (2.0 * twice - once)
        deeper = deeper * (1.0 / depth_total**2)
        total = flat
        for kind, sums_of in enumerate((high_flat, square_flat, deep, deep_high, deeper), 1):
            total += pltpu.roll(sums_of, 4 * kind, 1)
        rows = pl.ds(pl.multiple_of(number * group, group), group)
        target = table if part == PARTS - 1 else sent
        target[rows, :] = total + begun[0][rows, :] if begun else total
        return carry

    lax.fori_loop(0, slots // group, one_group, 0)
    if part < PARTS - 1:
        return
    whole = table[...]
    upper, _ = split(whole)
    middle, lower = split(whole - upper.astype(F32))
    rows = jnp.dot(
        picked[...], jnp.concatenate([upper, middle, lower], axis=1), preferred_element_type=F32
    )
    rows = rows[:, :LANES] + rows[:, LANES : 2 * LANES] + rows[:, 2 * LANES :]
    total = base[...]
    count = total.shape[0]
    for place in range(CAP):
        total += pltpu.roll(rows[place * count : (place + 1) * count], place * WIDTH, 1)
    sent[...] = total


def moment_rows(views, tiles, part, estimate, correction, labels, places, begun):
    planes, size, across = correction.shape
    slots = places[0].shape[1]
    count = places[1].shape[0] if part == PARTS - 1 else slots
    return pl.pallas_call(
        functools.partial(moments_kernel, views, tiles * planes, part),
        out_shape=jax.ShapeDtypeStruct((count, LANES), F32),
        in_specs=[VMEM] * (5 + len(begun)),
        out_specs=VMEM,
        scratch_shapes=[
            pltpu.VMEM((planes, size, across), F32),
            pltpu.VMEM((6 * 16, across), F32),
            pltpu.VMEM((slots, LANES), F32),
        ],
        compiler_params=pltpu.CompilerParams(vmem_limit_bytes=LIMIT),
        name="moment_rows",
    )(estimate, labels, *places, correction, *begun)


def segments_kernel(across, scale, rows, moments):
    whole = rows[...]
    parts = [whole] + [pltpu.roll(whole, LANES - place * WIDTH, 1) for place in range(1, CAP)]
    values = jnp.concatenate(parts, axis=0)
    ids = values[:, IDS : IDS + 1].astype(jnp.int32)
    spots = lax.broadcasted_iota(jnp.int32, (values.shape[0], NUC_DEV), 1)
    picked = (ids == spots).astype(F32)
    full = lax.dot_general(
        values, picked, (((0,), (0,)), ((), ())),
        precision=lax.Precision.HIGHEST, preferred_element_type=F32,
    )
    mass, high, higher, deep, deep_high, deeper = [full[4 * kind : 4 * kind + 4] for kind in range(6)]
    flat = lambda sums: sums[0:1]
    line = lambda sums: (sums[1:2] + 0.5 * sums[0:1]) * (1.0 / across)
    square = lambda sums: (sums[2:3] + sums[3:4] + sums[1:2] + 0.25 * sums[0:1]) * (1.0 / across**2)
    total = flat(mass)
    sums = jnp.concatenate(
        [
            flat(deep), flat(high), line(mass),
            flat(deeper), flat(higher), square(mass),
            flat(deep_high), line(deep), line(high),
        ],
        axis=0,
    )
    moments[...] = jnp.concatenate([total * scale, sums / jnp.maximum(total, 1.0)], axis=0)


def nucleus_table(across, scale, rows):
    return pl.pallas_call(
        functools.partial(segments_kernel, across, scale),
        out_shape=jax.ShapeDtypeStruct((MOM, NUC_DEV), F32),
        in_specs=[VMEM],
        out_specs=VMEM,
        compiler_params=pltpu.CompilerParams(vmem_limit_bytes=LIMIT),
        cost_estimate=pl.CostEstimate(flops=10_000_000_000, bytes_accessed=20_000_000, transcendentals=0),
        name="nucleus_table",
    )(rows)


def stores(pieces, sources, whole, half, sems):
    keep = whole.shape[1] // 2
    copies = []
    for number, ((first, size), source) in enumerate(zip(pieces, sources)):
        start = pl.multiple_of(keep * half + first, 8)
        for plane in range(whole.shape[0]):
            copies.append(
                pltpu.make_async_copy(
                    source.at[pl.ds(plane * size, size)],
                    whole.at[plane, pl.ds(start, size)],
                    sems.at[number, plane],
                )
            )
    for copy in copies:
        copy.start()
    return copies


def token_kernel(source, *rest):
    token = rest[-1]
    token[...] = source[:8, :LANES]


def token_of(source, after=(), flops=0):
    return pl.pallas_call(
        token_kernel,
        out_shape=jax.ShapeDtypeStruct((8, LANES), F32),
        in_specs=[VMEM] + [ANY] * len(after),
        out_specs=VMEM,
        compiler_params=pltpu.CompilerParams(vmem_limit_bytes=LIMIT),
        cost_estimate=pl.CostEstimate(flops=flops, bytes_accessed=flops // 500, transcendentals=0),
        name="token_of",
    )(source, *after)


def begin_kernel(pieces, *refs):
    sources, (whole, sems) = refs[:-2], refs[-2:]
    for copy in stores(pieces, sources, whole, half_of(lax.axis_index("view")), sems):
        copy.wait()


def begin_result(pieces, shape, mine):
    return pl.pallas_call(
        functools.partial(begin_kernel, pieces),
        out_shape=jax.ShapeDtypeStruct(shape, F32),
        in_specs=[VMEM] * len(mine),
        out_specs=ANY,
        scratch_shapes=[pltpu.SemaphoreType.DMA((len(pieces), shape[0]))],
        compiler_params=pltpu.CompilerParams(vmem_limit_bytes=LIMIT),
        name="begin_result",
    )(*mine)


def finish_kernel(pieces, begun, *refs):
    others, (whole, sems) = refs[:-2], refs[-2:]
    for copy in stores(pieces, others, whole, 1 - half_of(lax.axis_index("view")), sems):
        copy.wait()


def finish(pieces, begun, others):
    return pl.pallas_call(
        functools.partial(finish_kernel, pieces),
        out_shape=jax.ShapeDtypeStruct(begun.shape, F32),
        in_specs=[ANY] + [VMEM] * len(others),
        out_specs=ANY,
        input_output_aliases={0: 0},
        scratch_shapes=[pltpu.SemaphoreType.DMA((len(pieces), begun.shape[0]))],
        compiler_params=pltpu.CompilerParams(vmem_limit_bytes=LIMIT),
        name="finish",
    )(begun, *others)


def on_device(estimate, measured, kernels, labels, label_owner, label_index):
    tiles, views = lax.axis_size("tile"), lax.axis_size("view")
    planes, height, across = estimate.shape
    taps = kernels.shape[2]
    radius = (taps - 1) // 2
    keep = height // 2
    seen = min(height, -(-(keep + radius) // 8) * 8)
    rows = min(height, -(-(keep + 2 * radius) // 16) * 16)
    near_pairs = [(i, i ^ 1) for i in range(tiles)]
    far_pairs = [(i, i + 1) for i in range(1, tiles - 1, 2)]
    far_pairs = far_pairs + [(b, a) for a, b in far_pairs]
    partner = [(i, i ^ 1) for i in range(views)]
    across_pairs = [(i, i ^ 3) for i in range(views)]

    lines = jnp.transpose(kernels, (1, 0, 2))
    blank = blank_rows(across)
    packed = view_out(measured, lines, blank, seen)
    swapped = lax.ppermute(packed, "view", partner)
    to_far, to_near = rims_out(estimate, blank, radius, rows)
    far = lax.ppermute(to_far, "tile", far_pairs)
    near = lax.ppermute(to_near, "tile", near_pairs)
    places = slot_places(tiles, views, label_owner, label_index)
    own = prepare(False, taps, lines, estimate, places[1], rows, seen, keep)
    others = prepare(True, taps, swapped, estimate, lines, rows, seen, keep)
    came = token_of(far.reshape(radius * rows, across), (others[4],), 0)
    field_own, field_other, *sends = ratio_fields(
        own, others, far, near, measured, swapped, came
    )
    rims = [
        lax.ppermute(send, "tile", pairs) for send, pairs in zip(sends, (far_pairs, near_pairs) * PARTS)
    ]
    inner = own_planes(taps, own[4], others[4], field_own, field_other)
    mine, other, sums = [], [], []
    for part in range(PARTS):
        mine.append(add_rims(inner[part], *rims[2 * part : 2 * part + 2], *sums))
        other.append(lax.ppermute(mine[part], "view", across_pairs))
        sums = [moment_rows(views, tiles, part, estimate, mine[part], labels, places, sums)]
    sent = sums[0]
    got = lax.all_to_all(sent, ("tile", "view"), split_axis=0, concat_axis=0, tiled=True)
    size = keep // PARTS
    pieces = [(part * size, size) for part in range(PARTS)]
    new_mine, new_other, token = [], [], [sent]
    for part in range(PARTS):
        new_mine.append(update(views, part, estimate, mine[part], other[part], token))
        new_other.append(lax.ppermute(new_mine[part], "view", partner))
        token = [token_of(new_mine[part])]
    scale = label_index.shape[1] / (planes * height * across)
    moments = nucleus_table(across, scale, got)
    begun = begin_result(pieces, estimate.shape, new_mine)
    return finish(pieces, begun, new_other), moments


def solution(mesh):
    placed = (
        P("tile", None, None),
        P("view", "tile", None, None),
        P("view", None, None),
        P("tile", None, None),
        P("tile", None, None),
        P("tile", None),
    )
    return jax.shard_map(
        on_device,
        mesh=mesh,
        in_specs=placed,
        out_specs=(P("tile", None, None), P(None, "tile")),
        check_vma=False,
    )
```
